256 devices in a mesh: dp: 32 (over z, y_hi, core), head: 8 (over x, y_lo).
Axes of the slice: x: 4, y: 4 (y_hi: 2, y_lo: 2; y = y_hi * 2 + y_lo), z: 8, core: 2. Of those that a mesh axis runs over, the one named last changes fastest.
Arguments:
- hidden: bfloat16 [8192, 4096], P('dp', 'head'), may hold values from -6 to 6
- value_proj: bfloat16 [4096, 8192], P('dp', 'head'), may hold values from -0.09375 to 0.09375
- state_proj: bfloat16 [4096, 2048], P('dp', 'head'), may hold values from -0.01171875 to 0.01171875
- step_proj: bfloat16 [4096, 128], P('dp', 'head'), may hold values from -0.09375 to 0.09375
- step_bias: float32 [128], P('head'), may hold values from -3 to -0.5
- decay_rate: float32 [128], P('head'), may hold values from 6.1035157e-06 to 0.3
- skip_gain: float32 [128], P('head'), may hold values from 0.5 to 1.5
- out_grad: bfloat16 [8192, 8192], P('dp', 'head'), may hold values from -0.3984375 to 0.3984375
Outputs:
- mixer_out: bfloat16 [8192, 8192], P('dp', 'head')
- hidden_grad: bfloat16 [8192, 4096], P('dp', 'head')
- value_proj_grad: float32 [4096, 8192], P('dp', 'head')
- state_proj_grad: float32 [4096, 2048], P('dp', 'head')
- step_proj_grad: float32 [4096, 128], P('dp', 'head')
The draws below stay inside these ranges and needn't reach their ends.
All inputs are finite; a program needn't handle non-finite values.
Results may differ from the reference program's by a relative error of at most 0.02.
Values may be sent and summed in bfloat16 or wider, within the bound.
No kernel may reach another device: no remote copies, remote signals or barrier semaphores. Data moves between devices by JAX's collectives and lax.ppermute only.
A program may use at most 256 MiB of HBM per device.

```python
import math
import jax
import jax.numpy as jnp
from jax import lax

D = 4096
HEADS = 128
HEAD_DIM = 64
STATE = 128
GROUPS = 8
SPAN = 128
TOK_DEV = 256
LENGTH = 8192
VALUE_W = 8192
STATE_W = 2048
N_DP = 32


def block_levels(own_key, dims, cuts, smallest, largest):
    def one(axis_at, parts):
        heights = jax.random.uniform(jax.random.fold_in(jax.random.fold_in(own_key, 6), axis_at), (parts,), jnp.float32, smallest / len(cuts), largest / len(cuts))
        return jnp.repeat(jnp.exp(heights), dims[axis_at] // parts).reshape((-1,) + (1,) * (len(dims) - axis_at - 1))

    loudness = one(*cuts[0])
    for cut in cuts[1:]:
        loudness = loudness * one(*cut)
    return loudness


def scatter_about(stream_key, shape, scale, reach, pieces=(), held_as=jnp.bfloat16):
    values = jax.random.normal(stream_key, shape, jnp.float32) * scale
    if len(pieces) > 0:
        values = block_levels(stream_key, shape, pieces, -0.22, 0.18) * values
    return jnp.clip(values, min=-reach, max=reach).astype(held_as)


def setup_inputs(seed: int = 0) -> dict:
    arg_keys = jax.random.split(jax.random.key(seed), 9)
    hidden = scatter_about(arg_keys[0], (LENGTH, D), 1.0, 6.0, ((0, 32), (1, 8)))
    value_proj = scatter_about(arg_keys[1], (D, VALUE_W), D ** -0.5, 0.09375, ((0, 32), (1, 8)))
    state_proj = scatter_about(arg_keys[2], (D, STATE_W), (64 * D) ** -0.5, 0.01171875, ((0, 32), (1, 8)))
    step_proj = scatter_about(arg_keys[3], (D, HEADS), D ** -0.5, 0.09375, ((0, 32), (1, 8)))
    step_bias = jnp.clip(-3.0 + 2.5 * jax.random.uniform(arg_keys[4], (HEADS,), jnp.float32) ** block_levels(arg_keys[4], (HEADS,), ((0, 8),), -0.2, 0.2), -3.0, -0.5)
    decay_rate = jnp.clip(jnp.exp(math.log(0.3) - 10.8026728 * jax.random.uniform(arg_keys[5], (HEADS,), jnp.float32) ** block_levels(arg_keys[5], (HEADS,), ((0, 8),), -0.2, 0.2)), 6.10351571594947e-06, 0.3)
    skip_gain = jnp.clip(0.5 + 1.0 * jax.random.uniform(arg_keys[6], (HEADS,), jnp.float32) ** block_levels(arg_keys[6], (HEADS,), ((0, 8),), -0.2, 0.2), 0.5, 1.5)
    out_grad = scatter_about(arg_keys[7], (LENGTH, VALUE_W), 0.05, 0.3984375, ((0, 32), (1, 8)))
    return {"hidden": hidden, "value_proj": value_proj, "state_proj": state_proj, "step_proj": step_proj, "step_bias": step_bias, "decay_rate": decay_rate, "skip_gain": skip_gain, "out_grad": out_grad}


highest = lax.Precision.HIGHEST

def span_step(state, blocks):
    values, b_mat, c_mat, log_decay, step = blocks
    length = values.shape[0]
    cum_log = jnp.cumsum(log_decay, axis=0)
    diff = cum_log[:, None] - cum_log[None, :]
    lower = lax.broadcasted_iota(jnp.int32, (length, length), 0) >= lax.broadcasted_iota(jnp.int32, (length, length), 1)
    decay = jnp.where(lower[:, :, None, None], jnp.exp(jnp.minimum(diff, 0.0)), 0.0)
    scores = jnp.einsum('tgn,sgn->tsg', c_mat, b_mat, precision=highest)
    mixing = scores[:, :, :, None] * decay * step[None]
    inner = jnp.einsum('tsge,sgep->tgep', mixing, values, precision=highest)
    carried = jnp.einsum('tgn,gepn->tgep', c_mat, state, precision=highest) * jnp.exp(cum_log)[..., None]
    last_log = cum_log[-1]
    tail = jnp.exp(last_log[None] - cum_log) * step
    fresh = jnp.einsum('sge,sgep,sgn->gepn', tail, values, b_mat, precision=highest)
    new_state = jnp.exp(last_log)[:, :, None, None] * state + fresh
    return (new_state, inner + carried)

def scan_spans(values, b_mat, c_mat, step, rate, gain, span):
    tokens, groups, each, width = values.shape
    state_dim = b_mat.shape[2]
    count = tokens // span
    log_decay = -step * rate[None]
    blocks = (values.reshape(count, span, groups, each, width), b_mat.reshape(count, span, groups, state_dim), c_mat.reshape(count, span, groups, state_dim), log_decay.reshape(count, span, groups, each), step.reshape(count, span, groups, each))
    start = jnp.zeros((groups, each, width, state_dim), jnp.float32)
    final, outputs = lax.scan(jax.checkpoint(span_step), start, blocks)
    mixed = outputs.reshape(tokens, groups, each, width) + gain[None, :, :, None] * values
    return (mixed, final, log_decay)

def reference(hidden, value_proj, state_proj, step_proj, step_bias, decay_rate, skip_gain, out_grad):
    each = HEADS // GROUPS
    pre_value = jnp.dot(hidden, value_proj, preferred_element_type=jnp.float32)
    pre_state = jnp.dot(hidden, state_proj, preferred_element_type=jnp.float32)
    pre_step = jnp.dot(hidden, step_proj, preferred_element_type=jnp.float32) + step_bias[None]
    values = lax.optimization_barrier(pre_value.astype(jnp.bfloat16)).astype(jnp.float32)
    projections = lax.optimization_barrier(pre_state.astype(jnp.bfloat16)).astype(jnp.float32)
    step = jax.nn.softplus(pre_step)
    values_four = values.reshape(LENGTH, GROUPS, each, HEAD_DIM)
    pairs = projections.reshape(LENGTH, GROUPS, 2, STATE)
    b_mat = pairs[:, :, 0]
    c_mat = pairs[:, :, 1]
    step_three = step.reshape(LENGTH, GROUPS, each)
    rate = decay_rate.reshape(GROUPS, each)
    gain = skip_gain.reshape(GROUPS, each)

    def mixer(values_in, b_in, c_in, step_in):
        return scan_spans(values_in, b_in, c_in, step_in, rate, gain, SPAN)[0]
    mixed, pullback = jax.vjp(mixer, values_four, b_mat, c_mat, step_three)
    cotangent = out_grad.astype(jnp.float32).reshape(mixed.shape)
    d_values, d_b, d_c, d_step = pullback(cotangent)
    value_back = d_values.reshape(LENGTH, VALUE_W).astype(jnp.bfloat16)
    state_back = jnp.stack([d_b, d_c], axis=2).reshape(LENGTH, STATE_W).astype(jnp.bfloat16)
    step_back = (d_step.reshape(LENGTH, HEADS) * jax.nn.sigmoid(pre_step)).astype(jnp.bfloat16)
    hidden_grad = (jnp.dot(value_back, value_proj.T, preferred_element_type=jnp.float32) + jnp.dot(state_back, state_proj.T, preferred_element_type=jnp.float32) + jnp.dot(step_back, step_proj.T, preferred_element_type=jnp.float32)).astype(jnp.bfloat16)
    backs = jnp.concatenate([value_back, state_back, step_back], axis=1)

    def block_term(total, index):
        rows_in = lax.dynamic_slice_in_dim(hidden, index * TOK_DEV, TOK_DEV, 0)
        back_rows = lax.dynamic_slice_in_dim(backs, index * TOK_DEV, TOK_DEV, 0)
        term = lax.dot_general(rows_in, back_rows, (((0,), (0,)), ((), ())), preferred_element_type=jnp.float32)
        rounded = lax.optimization_barrier(term.astype(jnp.bfloat16)).astype(jnp.float32)
        return (total + rounded, None)
    total, _ = lax.scan(block_term, jnp.zeros((D, VALUE_W + STATE_W + HEADS), jnp.float32), jnp.arange(N_DP).astype(jnp.int32))
    mixer_out = mixed.reshape(LENGTH, VALUE_W).astype(jnp.bfloat16)
    return (mixer_out, hidden_grad, total[:, :VALUE_W], total[:, VALUE_W:VALUE_W + STATE_W], total[:, VALUE_W + STATE_W:])
```

```python
import jax
import jax.numpy as jnp
from jax import lax
from jax.experimental import pallas as pl
from jax.experimental.pallas import tpu as pltpu
from jax.sharding import Mesh, PartitionSpec as P

HEAD_DIM = 64
STATE = 128
Q = 128
EACH = 4
VW = EACH * HEAD_DIM
NZ, NX, NY = 8, 4, 4
f32, bf16 = jnp.float32, jnp.bfloat16
HI = lax.Precision.HIGHEST


def shift(value, axis, by, count, wrap=True):
    pairs = [(i, (i + by) % count) for i in range(count) if wrap or 0 <= i + by < count]
    return lax.ppermute(value, axis, pairs)


def dot(left, right, dims, precision=None):
    return lax.dot_general(
        left, right, (dims, ((), ())), preferred_element_type=f32, precision=precision
    )


def iota(shape, dim):
    return lax.broadcasted_iota(jnp.int32, shape, dim)


def consts():
    low = (iota((Q, Q), 0) >= iota((Q, Q), 1)).astype(f32)
    spread = (iota((EACH, VW), 1) // HEAD_DIM == iota((EACH, VW), 0)).astype(f32)
    return low, spread


def state_kernel(x_ref, bc_ref, g_ref, step_ref, rate_ref, fresh_ref, seed_ref, ends_ref, sum_ref, run):
    k = pl.program_id(0)
    low, spread = consts()
    step = step_ref[...]
    cum = dot(low, -step * rate_ref[...], ((1,), (0,)), HI)
    cum_wide = dot(cum, spread, ((1,), (0,)), HI)
    step_wide = dot(step, spread, ((1,), (0,)), HI)
    last_wide = cum_wide[Q - 1 :, :]
    last_col = dot(spread, cum[Q - 1 :, :], ((0,), (1,)), HI)
    tail = (x_ref[...].astype(f32) * (jnp.exp(last_wide - cum_wide) * step_wide)).astype(bf16)
    grown = (g_ref[...].astype(f32) * jnp.exp(cum_wide)).astype(bf16)
    fresh = dot(tail, bc_ref[:, :STATE], ((0,), (0,)))
    seed = dot(grown, bc_ref[:, STATE:], ((0,), (0,)))
    fresh_ref[0] = fresh
    seed_ref[0] = seed

    @pl.when(k == 0)
    def _():
        ends_ref[...] = jnp.zeros_like(ends_ref)
        run[...] = jnp.zeros_like(run)

    sum_ref[0] = jnp.broadcast_to(last_col, (VW, STATE))
    ends_ref[0, :VW] = jnp.exp(last_col) * ends_ref[0, :VW] + fresh
    ends_ref[1, :VW] = ends_ref[1, :VW] + jnp.exp(run[...]) * seed
    run[...] = run[...] + last_col
    total = jnp.broadcast_to(jnp.exp(run[...]), (VW, STATE))
    ends_ref[0, VW:] = total
    ends_ref[1, VW:] = total


def scan_kernel(
    x_ref, bc_ref, g_ref, step_ref, stept_ref, sigt_ref, rate_ref, ratet_ref, gain_ref,
    fresh_ref, seed_ref, sum_ref, in_ref, later_ref,
    y_ref, back_ref, dstep_ref, held, grads,
):
    k = pl.program_id(0)
    count = pl.num_programs(0)

    @pl.when(k == 0)
    def _():
        def ahead(i, state):
            held[i] = state
            return jnp.exp(sum_ref[i]) * state + fresh_ref[i]

        held[count] = lax.fori_loop(0, count, ahead, in_ref[...])

        def behind(i, state):
            j = count - 1 - i
            grads[j] = state
            return jnp.exp(sum_ref[j]) * state + seed_ref[j]

        lax.fori_loop(0, count, behind, later_ref[...])

    low, spread = consts()
    mask = low > 0.0
    step = step_ref[...]
    decay = -step * rate_ref[...]
    cum = dot(low, decay, ((1,), (0,)), HI)
    cum_t = dot(decay, low, ((0,), (1,)), HI)
    step_t = stept_ref[...]
    cum_wide = dot(cum, spread, ((1,), (0,)), HI)
    step_wide = dot(step, spread, ((1,), (0,)), HI)
    gain_wide = dot(gain_ref[...], spread, ((1,), (0,)), HI)
    growth = jnp.exp(cum_wide)
    rest = jnp.exp(cum_wide[Q - 1 :, :] - cum_wide)
    x, g = x_ref[...], g_ref[...]
    xf, gf = x.astype(f32), g.astype(f32)
    b_mat, c_mat = bc_ref[:, :STATE], bc_ref[:, STATE:]
    state, nxt, grad = held[k], held[k + 1], grads[k]
    state_b, grad_b = state.astype(bf16), grad.astype(bf16)

    scores = jnp.where(mask, dot(c_mat, b_mat, ((1,), (1,))), 0.0)
    mixed, moved = [], []
    pairs = jnp.zeros((Q, Q), f32)
    lane = iota((Q, EACH), 1)
    row = iota((EACH, Q), 0)
    out_sum = jnp.zeros((Q, EACH), f32)
    in_sum = jnp.zeros((EACH, Q), f32)
    for e in range(EACH):
        cut = slice(e * HEAD_DIM, (e + 1) * HEAD_DIM)
        fade = jnp.exp(jnp.minimum(cum[:, e : e + 1] - cum_t[e : e + 1, :], 0.0))
        weight = scores * fade
        step_row = step_t[e : e + 1, :]
        mixing = (weight * step_row).astype(bf16)
        mixed.append(dot(mixing, x[:, cut], ((1,), (0,))))
        moved.append(dot(mixing, g[:, cut], ((0,), (0,))))
        outer = dot(g[:, cut], x[:, cut], ((1,), (1,)))
        pairs = pairs + outer * fade * step_row
        both = weight * outer
        in_sum = in_sum + jnp.where(row == e, jnp.sum(both, axis=0, keepdims=True), 0.0)
        out_sum = out_sum + jnp.where(
            lane == e, jnp.sum(both * step_row, axis=1, keepdims=True), 0.0
        )
    pairs = jnp.where(mask, pairs, 0.0).astype(bf16)

    from_state = growth * dot(c_mat, state_b, ((1,), (1,)))
    from_later = rest * dot(b_mat, grad_b, ((1,), (1,)))
    y = jnp.concatenate(mixed, axis=1) + from_state + gain_wide * xf
    y_ref[...] = y.astype(bf16)
    d_x = jnp.concatenate(moved, axis=1) + step_wide * from_later + gain_wide * gf
    d_b = dot(pairs, c_mat, ((0,), (0,))) + dot(
        (xf * (rest * step_wide)).astype(bf16), grad_b, ((1,), (0,))
    )
    d_c = dot(pairs, b_mat, ((1,), (0,))) + dot(
        (gf * growth).astype(bf16), state_b, ((1,), (0,))
    )
    back_ref[:, :VW] = d_x.astype(bf16)
    back_ref[:, VW : VW + STATE] = d_b.astype(bf16)
    back_ref[:, VW + STATE :] = d_c.astype(bf16)

    direct = in_sum + dot(spread, xf * from_later, ((1,), (1,)), HI)
    out_t = dot(spread, gf * from_state, ((1,), (1,)), HI)
    crossing = dot(spread, jnp.sum(grad * nxt, axis=1, keepdims=True), ((1,), (0,)), HI)
    d_decay = (
        dot(out_sum, low, ((0,), (0,)), HI)
        + dot(out_t - direct * step_t, low, ((1,), (0,)), HI)
        + crossing
    )
    d_step = direct - ratet_ref[...] * d_decay
    dstep_ref[...] = d_step * sigt_ref[...]


def put(whole, part, where):
    return lax.dynamic_update_slice(whole, part, where)


def local(hidden, value_proj, state_proj, step_proj, step_bias, decay_rate, skip_gain, out_grad):
    z, yh, c, x, yl = (lax.axis_index(a) for a in ("z", "yh", "c", "x", "yl"))
    y_axis = ("yh", "yl")
    y = yh * 2 + yl
    tok = hidden.shape[0]
    tokens = 4 * tok
    blocks = tokens // Q
    rows = value_proj.shape[0]
    half = 2 * VW
    cols = half + 2 * STATE + 2 * EACH

    value_t = value_proj.T
    state_t = state_proj.T
    step_tr = step_proj.T

    def chosen(which):
        return jnp.concatenate(
            [
                lax.dynamic_slice_in_dim(value_t, which * half, half, 0),
                state_t,
                lax.dynamic_slice_in_dim(step_tr, which * 2 * EACH, 2 * EACH, 0),
            ],
            axis=0,
        )

    mine, theirs = chosen(yh), shift(chosen(1 - yh), "yh", 1, 2)
    chunk = jnp.where(
        yh == 0,
        jnp.concatenate([mine, theirs], axis=1),
        jnp.concatenate([theirs, mine], axis=1),
    )
    parts = hidden.reshape(tok, 2, 2, 128)
    keep = lax.dynamic_index_in_dim(parts, c, 2, False).reshape(tok, 256)
    give = lax.dynamic_index_in_dim(parts, 1 - c, 2, False).reshape(tok, 256)
    got = shift(give, "c", 1, 2)
    first = jnp.where(c == 0, keep, got)
    second = jnp.where(c == 0, got, keep)

    hid = jnp.zeros((NX, 2, 2, 2, tok, 256), bf16)
    whole_w = jnp.zeros((NZ, cols, 256), bf16)
    whole_w = put(whole_w, chunk[None], (z, 0, 0))
    up = down = chunk
    a_y = jnp.zeros((2, 2, tok, 256), bf16)
    b_x = jnp.zeros((NX, tok, 256), bf16)
    a_y = put(a_y, first[None, None], (yl, yh, 0, 0))
    b_x = put(b_x, second[None], (x, 0, 0))
    for by in (1, -1, 2):
        from_y = (y - by) % NY
        a_y = put(a_y, shift(first, y_axis, by, NY)[None, None], (from_y % 2, from_y // 2, 0, 0))
        b_x = put(b_x, shift(second, "x", by, NX)[None], ((x - by) % NX, 0, 0))
    hid = put(hid, a_y[None, :, :, None], (x, 0, 0, 0, 0, 0))
    hid = put(hid, b_x[:, None, None, None], (0, yl, yh, 1, 0, 0))
    for by in (1, -1, 2):
        from_x, from_y = (x - by) % NX, (y - by) % NY
        hid = put(hid, shift(a_y, "x", by, NX)[None, :, :, None], (from_x, 0, 0, 0, 0, 0))
        hid = put(
            hid,
            shift(b_x, y_axis, by, NY)[:, None, None, None],
            (0, from_y % 2, from_y // 2, 1, 0, 0),
        )
    for step in range(1, NZ // 2 + 1):
        up = shift(up, "z", 1, NZ)
        whole_w = put(whole_w, up[None], ((z - step) % NZ, 0, 0))
        if step < NZ // 2:
            down = shift(down, "z", -1, NZ)
            whole_w = put(whole_w, down[None], ((z + step) % NZ, 0, 0))
    hid = hid.reshape(NZ, tokens, 256)

    def to_heads(value):
        value = value.reshape(tok, 2, 2, VW)
        pair = shift(lax.dynamic_index_in_dim(value, 1 - c, 2, False), "c", 1, 2)
        own = lax.dynamic_index_in_dim(value, c, 2, False)
        value = jnp.where(c == 0, jnp.stack([own, pair]), jnp.stack([pair, own]))
        pair = shift(lax.dynamic_index_in_dim(value, 1 - yh, 2, False), "yh", 1, 2)
        own = lax.dynamic_index_in_dim(value, yh, 2, False)
        value = jnp.where(yh == 0, jnp.stack([own, pair]), jnp.stack([pair, own]))
        return value.reshape(tokens, VW)

    def to_tokens(value):
        value = value.reshape(2, 2, tok, VW)
        pair = shift(lax.dynamic_index_in_dim(value, 1 - yh, 0, False), "yh", 1, 2)
        own = lax.dynamic_index_in_dim(value, yh, 0, False)
        value = jnp.where(yh == 0, jnp.stack([own, pair], 2), jnp.stack([pair, own], 2))
        pair = shift(lax.dynamic_index_in_dim(value, 1 - c, 0, False), "c", 1, 2)
        own = lax.dynamic_index_in_dim(value, c, 0, False)
        value = jnp.where(c == 0, jnp.stack([own, pair], 2), jnp.stack([pair, own], 2))
        return value.reshape(tok, 4 * VW)

    cot = to_heads(out_grad)

    def project(weights):
        return dot(hid, weights, ((0, 2), (0, 2)))

    w_own = lax.dynamic_slice_in_dim(whole_w, c * VW, VW, 1)
    w_other = lax.dynamic_slice_in_dim(whole_w, (1 - c) * VW, VW, 1)
    w_rest = whole_w[:, half:]
    p_rest = project(w_rest)
    p_other = project(w_other)
    p_own = project(w_own)
    p_bc, p_step = p_rest[:, : 2 * STATE], p_rest[:, 2 * STATE :]
    bc = (p_bc + shift(p_bc, "c", 1, 2)).astype(bf16)
    pre_step = p_step + shift(p_step, "c", 1, 2)
    values = (p_own + shift(p_other, "c", 1, 2)).astype(bf16)
    place = yh * 2 + c
    pre_step = lax.dynamic_slice_in_dim(pre_step, c * EACH, EACH, 1)
    bias, rate, gain = (
        lax.dynamic_slice_in_dim(v, place * EACH, EACH, 0)[None]
        for v in (step_bias, decay_rate, skip_gain)
    )
    pre_step = pre_step + bias
    step = jax.nn.softplus(pre_step)
    sig_t = jax.nn.sigmoid(pre_step).T
    step_t = step.T

    def blocked(width):
        return pl.BlockSpec((Q, width), lambda k: (k, 0))

    def whole(*shape):
        return pl.BlockSpec(shape, lambda k: (0,) * len(shape))

    params = pltpu.CompilerParams(vmem_limit_bytes=32 * 1024 * 1024)
    per_block = pl.BlockSpec((1, VW, STATE), lambda k: (k, 0, 0))
    stack = jax.ShapeDtypeStruct((blocks, VW, STATE), f32)
    fresh, seed, ends, sums = pl.pallas_call(
        state_kernel,
        grid=(blocks,),
        in_specs=[blocked(VW), blocked(2 * STATE), blocked(VW), blocked(EACH), whole(1, EACH)],
        out_specs=[per_block, per_block, whole(2, 2 * VW, STATE), per_block],
        out_shape=[stack, stack, jax.ShapeDtypeStruct((2, 2 * VW, STATE), f32), stack],
        scratch_shapes=[pltpu.VMEM((VW, 1), f32)],
        compiler_params=params,
        name="states",
    )(values, bc, cot, step, rate)

    def windows(start, sign):
        short = shift(start, "z", sign, NZ, False)
        for by in (1, 2, 4):
            far = shift(short, "z", sign * by, NZ, False)
            short = jnp.concatenate(
                [short[:VW] + short[VW:] * far[:VW], short[VW:] * far[VW:]], axis=0
            )
        return short[:VW]

    state_in = windows(ends[0], 1)
    later = windows(ends[1], -1)

    mixed, back, d_step = pl.pallas_call(
        scan_kernel,
        grid=(blocks,),
        in_specs=[
            blocked(VW), blocked(2 * STATE), blocked(VW), blocked(EACH),
            pl.BlockSpec((EACH, Q), lambda k: (0, k)), pl.BlockSpec((EACH, Q), lambda k: (0, k)),
            whole(1, EACH), whole(EACH, 1), whole(1, EACH),
            whole(blocks, VW, STATE), whole(blocks, VW, STATE), whole(blocks, VW, STATE),
            whole(VW, STATE), whole(VW, STATE),
        ],
        out_specs=[
            blocked(VW), blocked(VW + 2 * STATE), pl.BlockSpec((EACH, Q), lambda k: (0, k)),
        ],
        out_shape=[
            jax.ShapeDtypeStruct((tokens, VW), bf16),
            jax.ShapeDtypeStruct((tokens, VW + 2 * STATE), bf16),
            jax.ShapeDtypeStruct((EACH, tokens), f32),
        ],
        scratch_shapes=[
            pltpu.VMEM((blocks + 1, VW, STATE), f32), pltpu.VMEM((blocks, VW, STATE), f32),
        ],
        compiler_params=params,
        name="scan",
    )(values, bc, cot, step, step_t, sig_t, rate, rate.T, gain, fresh, seed, sums, state_in, later)

    mixer_out = to_tokens(mixed)

    back_other = shift(back, "c", 1, 2)
    step_back = d_step.T.astype(bf16)
    step_other = shift(step_back, "c", 1, 2)
    d_own, d_other = back[:, :VW], back_other[:, :VW]
    d_bc = (back[:, VW:].astype(f32) + back_other[:, VW:].astype(f32)).astype(bf16)
    backs = jnp.where(
        c == 0,
        jnp.concatenate([d_own, d_other, d_bc, step_back, step_other], axis=1),
        jnp.concatenate([d_other, d_own, d_bc, step_other, step_back], axis=1),
    )

    def term(at):
        block = lax.dynamic_index_in_dim(hid, at % NZ, 0, False)
        return dot(backs, block, ((0,), (0,)))

    up = term(z + NZ // 2).astype(bf16)
    down = term(z + NZ // 2 + 1).astype(bf16)
    for hop in range(1, NZ // 2 + 1):
        up = shift(up, "z", 1, NZ)
        if hop < NZ // 2:
            up = (up.astype(f32) + term(z + NZ // 2 - hop)).astype(bf16)
            down = shift(down, "z", -1, NZ)
            if hop < NZ // 2 - 1:
                down = (down.astype(f32) + term(z + NZ // 2 + 1 + hop)).astype(bf16)
    summed = up.astype(f32) + down.astype(f32) + term(z)
    pair = summed.reshape(cols, 2, 128)
    own = lax.dynamic_index_in_dim(pair, yh, 1, False)
    other = shift(lax.dynamic_index_in_dim(pair, 1 - yh, 1, False).astype(bf16), "yh", 1, 2)
    other = other.astype(f32)
    low_part, high_part = jnp.where(yh == 0, own, other), jnp.where(yh == 0, other, own)
    value_grad = jnp.concatenate([low_part[:half], high_part[:half]], axis=0).T
    state_grad = (own[half : half + 2 * STATE] + other[half : half + 2 * STATE]).T
    step_grad = jnp.concatenate(
        [low_part[half + 2 * STATE :], high_part[half + 2 * STATE :]], axis=0
    ).T

    spread = lax.dot_general(
        backs, whole_w, (((1,), (1,)), ((), ())), preferred_element_type=f32
    )
    spread = spread.reshape(2, 2, tok, NX, 2, 256)
    spread = spread.transpose(1, 3, 4, 0, 2, 5)
    a_part, b_part = spread[0], spread[1]

    def pick_x(value, by):
        return lax.dynamic_index_in_dim(value, (x + by) % NX, 0, False)

    def pick_y(value, by):
        at = (y + by) % NY
        value = lax.dynamic_index_in_dim(value, at % 2, value.ndim - 4, False)
        return lax.dynamic_index_in_dim(value, at // 2, value.ndim - 3, False)

    a_sum, b_sum = pick_x(a_part, 0), pick_y(b_part, 0)
    for by in (2, 1, -1):
        a_sum = a_sum + shift(pick_x(a_part, by).astype(bf16), "x", by, NX).astype(f32)
        b_sum = b_sum + shift(pick_y(b_part, by).astype(bf16), y_axis, by, NY).astype(f32)
    a_out, b_out = pick_y(a_sum, 0), pick_x(b_sum, 0)
    for by in (2, 1, -1):
        a_out = a_out + shift(pick_y(a_sum, by).astype(bf16), y_axis, by, NY).astype(f32)
        b_out = b_out + shift(pick_x(b_sum, by).astype(bf16), "x", by, NX).astype(f32)
    a_out, b_out = a_out.astype(bf16), b_out.astype(bf16)
    keep = jnp.where(c == 0, a_out, b_out).reshape(tok, 2, 128)
    got = shift(jnp.where(c == 0, b_out, a_out), "c", 1, 2).reshape(tok, 2, 128)
    hidden_grad = jnp.where(
        c == 0, jnp.stack([keep, got], axis=2), jnp.stack([got, keep], axis=2)
    ).reshape(tok, 512)
    return mixer_out, hidden_grad, value_grad, state_grad, step_grad


def solution(mesh):
    fine = Mesh(mesh.devices.reshape(NZ, 2, 2, NX, 2), ("z", "yh", "c", "x", "yl"))
    split = P(("z", "yh", "c"), ("x", "yl"))
    by_head = P(("x", "yl"))
    return jax.shard_map(
        local,
        mesh=fine,
        in_specs=(split,) * 4 + (by_head,) * 3 + (split,),
        out_specs=(split,) * 5,
        check_vma=False,
    )
```

```python
import jax
import jax.numpy as jnp
from jax import lax
from jax.experimental import pallas as pl
from jax.experimental.pallas import tpu as pltpu
from jax.sharding import Mesh, PartitionSpec as P

HEAD_DIM = 64
STATE = 128
Q = 128
EACH = 4
VW = EACH * HEAD_DIM
BC = 2 * STATE
MAIN = 2 * VW + BC
STEPS = 16
COLS = MAIN + STEPS
FEAT = 256
NZ, NX, NY = 8, 4, 4
PARTS = 4
f32, bf16 = jnp.float32, jnp.bfloat16
HI = lax.Precision.HIGHEST


def vmem(mebibytes):
    return pltpu.CompilerParams(vmem_limit_bytes=mebibytes * 1024 * 1024)


def shift(value, axis, by, count, wrap=True):
    pairs = [(i, (i + by) % count) for i in range(count) if wrap or 0 <= i + by < count]
    return lax.ppermute(value, axis, pairs)


def both_x(value):
    pairs = [(c * NX + i, c * NX + (i + 1 - 2 * c) % NX) for c in range(2) for i in range(NX)]
    return lax.ppermute(value, ("c", "x"), pairs)


def both_y(value):
    def at(c, y):
        return (y // 2) * 4 + c * 2 + y % 2

    pairs = [(at(c, y), at(c, (y + 1 - 2 * c) % NY)) for c in range(2) for y in range(NY)]
    return lax.ppermute(value, ("yh", "c", "yl"), pairs)


def swap(value):
    return shift(value, "c", 1, 2)


def dot(left, right, dims, precision=None):
    return lax.dot_general(
        left, right, (dims, ((), ())), preferred_element_type=f32, precision=precision
    )


NN, NT, TN = ((1,), (0,)), ((1,), (1,)), ((0,), (0,))


def iota(shape, dim):
    return lax.broadcasted_iota(jnp.int32, shape, dim)


def consts():
    low = (iota((Q, Q), 0) >= iota((Q, Q), 1)).astype(f32)
    spread = (iota((EACH, VW), 1) // HEAD_DIM == iota((EACH, VW), 0)).astype(f32)
    return low, spread


def project_first(at_ref, *refs):
    x, y, z, way = (at_ref[i] for i in range(4))
    a_refs, b_refs, w_refs = refs[:NX], refs[NX : NX + NY], refs[NX + NY : NX + NY + NZ]
    hid_ref, w_ref, other_ref, bc_ref, step_ref = refs[NX + NY + NZ :]
    tok = a_refs[0].shape[1]
    for j in range(NX):
        x_at = (x - way * j) & (NX - 1)
        for i in range(NY):
            y_at = (y - way * i) & (NY - 1)
            lanes = pl.ds(pl.multiple_of((2 * x_at + (y_at & 1)) * FEAT, FEAT), FEAT)
            row = (y_at >> 1) * 2
            hid_ref[row, :, lanes] = a_refs[j][i]
            hid_ref[row + 1, :, lanes] = b_refs[i][j]
    for i in range(NZ):
        z_at = (z + offset(i)) & (NZ - 1)
        w_ref[:, pl.ds(pl.multiple_of(z_at * FEAT, FEAT), FEAT)] = w_refs[i][...]
    for i in range(4):
        rows = slice(i * tok, (i + 1) * tok)
        block = hid_ref[i]
        bc_ref[rows, :] = dot(block, w_ref[2 * VW : MAIN, :], NT)
        other_ref[rows, :] = dot(block, w_ref[VW : 2 * VW, :], NT)
        step_ref[:, rows] = dot(w_ref[MAIN:, :], block, NT)


def offset(i):
    return i // 2 if i % 2 == 0 else -(i + 1) // 2


def project_own(hid_ref, w_ref, own_ref):
    own_ref[...] = dot(hid_ref[0], w_ref[...], NT)


def state_kernel(
    own_ref, pair_ref, bc_own_ref, bc_pair_ref, g_ref, step_ref, rate_ref,
    x_ref, bc_ref, held_ref, grads_ref, cross_ref, ends_ref, cum_ref, fresh, seeds,
):
    count = x_ref.shape[0] // Q
    low, spread = consts()
    total = jnp.zeros((EACH, 1), f32)
    lasts = []
    for k in range(count):
        rows = slice(k * Q, (k + 1) * Q)
        x = (own_ref[rows, :] + pair_ref[rows, :]).astype(bf16)
        bc = (bc_own_ref[rows, :] + bc_pair_ref[rows, :]).astype(bf16)
        x_ref[rows, :] = x
        bc_ref[rows, :] = bc
        step = step_ref[:, rows]
        cum = dot(-step * rate_ref[...], low, NT, HI)
        cum_ref[:, rows] = cum + total
        last = cum[:, Q - 1 :]
        rest = jnp.exp(last - cum) * step
        rest_wide = dot(rest, spread, TN, HI)
        growth_wide = dot(jnp.exp(cum), spread, TN, HI)
        tail = (x.astype(f32) * rest_wide).astype(bf16)
        grown = (g_ref[rows, :].astype(f32) * growth_wide).astype(bf16)
        fresh[k] = dot(tail, bc[:, :STATE], TN)
        seeds[k] = dot(grown, bc[:, STATE:], TN)
        lasts.append(dot(spread, jnp.exp(last), TN, HI))
        total = total + last
    state = jnp.zeros((VW, STATE), f32)
    for k in range(count):
        held_ref[k] = state.astype(bf16)
        state = lasts[k] * state + fresh[k]
        fresh[k] = state
    grad = jnp.zeros((VW, STATE), f32)
    for k in range(count - 1, -1, -1):
        grads_ref[k] = grad.astype(bf16)
        cross = jnp.sum(grad * fresh[k], axis=1, keepdims=True)
        cross_ref[k] = jnp.broadcast_to(dot(spread, cross, NN, HI), (EACH, Q))
        grad = lasts[k] * grad + seeds[k]
    eye = (iota((EACH, STATE), 0) == iota((EACH, STATE), 1)).astype(f32)
    decay = dot(jnp.broadcast_to(jnp.exp(total), (EACH, STEPS)), eye, TN, HI)
    high = decay.astype(bf16).astype(f32)
    mid = (decay - high).astype(bf16).astype(f32)
    least = decay - high - mid
    row = iota((STEPS, STATE), 0)
    pieces = jnp.where(row == 0, high, jnp.where(row == 1, mid, jnp.where(row == 2, least, 0.0)))
    ends_ref[0, :VW] = state.astype(bf16)
    ends_ref[1, :VW] = grad.astype(bf16)
    ends_ref[0, VW:] = pieces.astype(bf16)
    ends_ref[1, VW:] = pieces.astype(bf16)


def scan_kernel(
    x_ref, bc_ref, g_ref, step_ref, rate_ref, gain_ref, held_ref, grads_ref, cross_ref,
    out_ref, dstep_ref,
):
    low, spread = consts()
    mask = low > 0.0
    step_t = step_ref[...]
    cum_t = dot(-step_t * rate_ref[...], low, NT, HI)
    cum_wide = dot(cum_t, spread, TN, HI)
    step_wide = dot(step_t, spread, TN, HI)
    gain_wide = dot(gain_ref[...], spread, TN, HI)
    growth = jnp.exp(cum_wide)
    rest = jnp.exp(cum_wide[Q - 1 :, :] - cum_wide)
    x, g = x_ref[...], g_ref[...]
    xf, gf = x.astype(f32), g.astype(f32)
    b_mat, c_mat = bc_ref[:, :STATE], bc_ref[:, STATE:]
    state, grad = held_ref[0], grads_ref[0]

    scores = jnp.where(mask, dot(c_mat, b_mat, NT), 0.0)
    mixed, moved = [], []
    pairs = jnp.zeros((Q, Q), f32)
    lane = iota((Q, EACH), 1)
    row = iota((EACH, Q), 0)
    out_sum = jnp.zeros((Q, EACH), f32)
    in_sum = jnp.zeros((EACH, Q), f32)
    for e in range(EACH):
        cut = slice(e * HEAD_DIM, (e + 1) * HEAD_DIM)
        first = slice(e * HEAD_DIM, e * HEAD_DIM + 1)
        fade = jnp.exp(jnp.minimum(cum_wide[:, first] - cum_t[e : e + 1, :], 0.0))
        weight = scores * fade
        step_row = step_t[e : e + 1, :]
        mixing = (weight * step_row).astype(bf16)
        mixed.append(dot(mixing, x[:, cut], NN))
        moved.append(dot(mixing, g[:, cut], TN))
        outer = dot(g[:, cut], x[:, cut], NT)
        pairs = pairs + outer * fade * step_row
        both = weight * outer
        in_sum = in_sum + jnp.where(row == e, jnp.sum(both, axis=0, keepdims=True), 0.0)
        out_sum = out_sum + jnp.where(
            lane == e, jnp.sum(both * step_row, axis=1, keepdims=True), 0.0
        )
    pairs = jnp.where(mask, pairs, 0.0).astype(bf16)

    from_state = growth * dot(c_mat, state, NT)
    from_later = rest * dot(b_mat, grad, NT)
    out_ref[:, :VW] = jnp.concatenate(mixed, axis=1) + from_state + gain_wide * xf
    out_ref[:, VW : 2 * VW] = (
        jnp.concatenate(moved, axis=1) + step_wide * from_later + gain_wide * gf
    )
    out_ref[:, 2 * VW : 2 * VW + STATE] = dot(pairs, c_mat, TN) + dot(
        (xf * (rest * step_wide)).astype(bf16), grad, NN
    )
    out_ref[:, 2 * VW + STATE :] = dot(pairs, b_mat, NN) + dot(
        (gf * growth).astype(bf16), state, NN
    )
    direct = in_sum + dot(spread, xf * from_later, NT, HI)
    out_t = dot(spread, gf * from_state, NT, HI)
    d_decay = (
        dot(out_sum, low, TN, HI) + dot(out_t - direct * step_t, low, NN, HI) + cross_ref[0]
    )
    dstep_ref[...] = direct - rate_ref[...] * d_decay


def join_kernel(
    x_ref, bc_ref, g_ref, step_ref, sig_ref, rate_ref, cum_ref, in_ref, later_ref, *refs
):
    parts, dsteps = refs[:PARTS], refs[PARTS : 2 * PARTS]
    y_ref, back_ref, dstep_ref = refs[2 * PARTS :]
    low, spread = consts()
    tokens = x_ref.shape[0]
    size = tokens // PARTS
    count = tokens // Q
    state_b, later_b = in_ref[...], later_ref[...]
    state, later = state_b.astype(f32), later_b.astype(f32)
    last = cum_ref[:, tokens - 1 :]
    decay = dot(spread, jnp.exp(last), TN, HI)
    cross = dot(
        spread, jnp.sum(later * (decay * state), axis=1, keepdims=True), NN, HI
    )
    outs, directs = [], []
    for i in range(PARTS):
        rows = slice(i * size, (i + 1) * size)
        cum, step = cum_ref[:, rows], step_ref[:, rows]
        growth = dot(jnp.exp(cum), spread, TN, HI)
        rest = dot(jnp.exp(last - cum), spread, TN, HI)
        step_wide = dot(step, spread, TN, HI)
        xf, gf = x_ref[rows, :].astype(f32), g_ref[rows, :].astype(f32)
        b_mat, c_mat = bc_ref[rows, :STATE], bc_ref[rows, STATE:]
        from_state = growth * dot(c_mat, state_b, NT)
        from_later = rest * dot(b_mat, later_b, NT)
        part = parts[i]
        y_ref[rows, :] = (part[:, :VW] + from_state).astype(bf16)
        back_ref[rows, :VW] = (part[:, VW : 2 * VW] + step_wide * from_later).astype(bf16)
        back_ref[rows, VW : VW + STATE] = (
            part[:, 2 * VW : 2 * VW + STATE]
            + dot((xf * (rest * step_wide)).astype(bf16), later_b, NN)
        ).astype(bf16)
        back_ref[rows, VW + STATE :] = (
            part[:, 2 * VW + STATE :] + dot((gf * growth).astype(bf16), state_b, NN)
        ).astype(bf16)
        directs.append(dot(spread, xf * from_later, NT, HI))
        outs.append(dot(spread, gf * from_state, NT, HI))
    direct = jnp.concatenate(directs, axis=1)
    out = jnp.concatenate(outs, axis=1)
    came = direct * step_ref[...]
    behind = [None] * count
    run = cross
    for k in range(count - 1, -1, -1):
        piece = out[:, k * Q : (k + 1) * Q]
        behind[k] = dot(piece, low, NN, HI) + run
        run = run + jnp.sum(piece, axis=1, keepdims=True)
    run = jnp.zeros((EACH, 1), f32)
    dstep_ref[...] = jnp.zeros_like(dstep_ref)
    for k in range(count):
        rows = slice(k * Q, (k + 1) * Q)
        piece = came[:, rows]
        ahead = dot(piece, low, NT, HI) - piece + run
        run = run + jnp.sum(piece, axis=1, keepdims=True)
        i, j = k * Q // size, k * Q % size
        raw = dsteps[i][:, j : j + Q] + direct[:, rows] - rate_ref[...] * (behind[k] + ahead)
        dstep_ref[:EACH, rows] = (raw * sig_ref[:, rows]).astype(bf16)


def both_bc(back_ref, pair_ref):
    return (back_ref[:, VW:].astype(f32) + pair_ref[:, VW:].astype(f32)).astype(bf16)


def term_kernel(at_ref, back_ref, pair_ref, steps_ref, hid_ref, *refs):
    out_ref = refs[-1]
    hid = hid_ref[...].reshape(-1, FEAT)
    main = jnp.concatenate([back_ref[:, :VW], pair_ref[:, :VW], both_bc(back_ref, pair_ref)], axis=1)
    rows = dot(hid, main, TN)
    steps = dot(steps_ref[...], hid, NN)
    for ref in refs[:-1]:
        rows = rows + ref[:FEAT, :].astype(f32)
        steps = steps + ref[FEAT:, :FEAT].astype(f32)
    out_ref[:FEAT, :] = rows.astype(out_ref.dtype)
    out_ref[FEAT:, :FEAT] = steps.astype(out_ref.dtype)
    out_ref[FEAT:, FEAT:] = jnp.zeros((STEPS, MAIN - FEAT), out_ref.dtype)


def input_kernel(back_ref, pair_ref, steps_ref, w_ref, a_ref, b_ref, bc):
    @pl.when(pl.program_id(0) == 0)
    def _():
        bc[...] = both_bc(back_ref, pair_ref)

    size = a_ref.shape[3]
    for i in range(4):
        rows = slice(i * size, (i + 1) * size)
        total = (
            dot(back_ref[rows, :VW], w_ref[:VW, :], NN)
            + dot(pair_ref[rows, :VW], w_ref[VW : 2 * VW, :], NN)
            + dot(bc[rows, :], w_ref[2 * VW : MAIN, :], NN)
            + dot(steps_ref[:, rows], w_ref[MAIN:, :], TN)
        ).astype(bf16)
        if i % 2 == 0:
            a_ref[0, 0, i // 2] = total
        else:
            b_ref[i // 2, 0, 0] = total


def take_kernel(at_ref, table_ref, *refs):
    value = table_ref[...].reshape(refs[-1].shape)
    if len(refs) > 1:
        value = value.astype(f32) + refs[0][...].astype(f32)
    refs[-1][...] = value.astype(bf16)


def take(table, at, *sums):
    shape = table.shape[1:]
    full = pl.BlockSpec(shape, lambda k, at: (0,) * len(shape))
    block = pl.BlockSpec((1,) + shape, lambda k, at: (at[0],) + (0,) * len(shape))
    return pl.pallas_call(
        take_kernel,
        grid_spec=pltpu.PrefetchScalarGridSpec(
            num_scalar_prefetch=1,
            grid=(1,),
            in_specs=[block] + [full] * len(sums),
            out_specs=full,
        ),
        out_shape=jax.ShapeDtypeStruct(shape, bf16),
        compiler_params=vmem(6),
        cost_estimate=cost(1e6, 6 * table.size // table.shape[0]),
        name="take",
    )(at[None], table, *sums)


def pick(value, at, dim):
    return lax.dynamic_index_in_dim(value, at, dim, False)


def tie(*values):
    return lax.optimization_barrier(values)


def cost(flops, moved):
    return pl.CostEstimate(flops=int(flops), bytes_accessed=int(moved), transcendentals=0)


def local(hidden, value_proj, state_proj, step_proj, step_bias, decay_rate, skip_gain, out_grad):
    z, yh, c, x, yl = (lax.axis_index(a) for a in ("z", "yh", "c", "x", "yl"))
    y = yh * 2 + yl
    way = 1 - 2 * c
    tok = hidden.shape[0]
    tokens = 4 * tok
    blocks = tokens // Q

    value_t, state_t, step_tr = value_proj.T, state_proj.T, step_proj.T
    none = jnp.zeros((EACH, value_proj.shape[0]), bf16)

    def chosen(which):
        def some(array, wide, core):
            return lax.dynamic_slice_in_dim(array, (which * 2 + core) * wide, wide, 0)

        return jnp.concatenate(
            [
                some(value_t, VW, c), some(value_t, VW, 1 - c), state_t,
                some(step_tr, EACH, c), none, some(step_tr, EACH, 1 - c), none,
            ],
            axis=0,
        )

    mine, theirs = chosen(yh), shift(chosen(1 - yh), "yh", 1, 2)
    chunk = jnp.where(
        yh == 0,
        jnp.concatenate([mine, theirs], axis=1),
        jnp.concatenate([theirs, mine], axis=1),
    )
    parts = hidden.reshape(tok, 2, 2, 128)
    keep = pick(parts, c, 2).reshape(tok, FEAT)
    got = swap(pick(parts, 1 - c, 2).reshape(tok, FEAT))
    first = jnp.where(c == 0, keep, got)
    second = jnp.where(c == 0, got, keep)

    def pairwise(own, pair, place, dim):
        return jnp.where(
            place == 0, jnp.stack([own, pair], dim), jnp.stack([pair, own], dim)
        )

    out_grad, chunk = tie(out_grad, chunk)
    cot = out_grad.reshape(tok, 2, 2, VW)
    cot = pairwise(pick(cot, c, 2), swap(pick(cot, 1 - c, 2)), c, 0)

    weights = [chunk, shift(chunk, "z", 1, NZ), shift(chunk, "z", -1, NZ)]
    a_blocks, b_blocks = [first], [second]
    for hop in range(1, 4):
        a_blocks.append(both_y(a_blocks[-1]))
        b_blocks.append(both_x(b_blocks[-1]))
    a_blocks, b_blocks = [jnp.stack(a_blocks)], [jnp.stack(b_blocks)]
    weights[1], weights[2], a_blocks[0], b_blocks[0], cot = tie(
        weights[1], weights[2], a_blocks[0], b_blocks[0], cot
    )
    cot = pairwise(pick(cot, yh, 2), shift(pick(cot, 1 - yh, 2), "yh", 1, 2), yh, 0)
    cot = cot.reshape(tokens, VW)
    for hop in range(1, 4):
        weights.append(shift(weights[-2], "z", 1, NZ))
        if hop < 3:
            weights.append(shift(weights[-2], "z", -1, NZ))
        a_blocks.append(both_x(a_blocks[-1]))
        b_blocks.append(both_y(b_blocks[-1]))
        if hop < 3:
            weights[-1], weights[-2], a_blocks[-1], b_blocks[-1] = tie(
                weights[-1], weights[-2], a_blocks[-1], b_blocks[-1]
            )

    def whole(*shape):
        return pl.BlockSpec(shape, lambda *k: (0,) * len(shape))

    def shaped(dtype, *shape):
        return jax.ShapeDtypeStruct(shape, dtype)

    places = jnp.stack([x, y, z, way]).astype(jnp.int32)
    wide = NZ * FEAT
    hid, whole_w, p_other, p_bc, p_step = pl.pallas_call(
        project_first,
        in_specs=[pl.BlockSpec(memory_space=pltpu.SMEM)]
        + [pl.BlockSpec(memory_space=pltpu.VMEM)] * (NX + NY + NZ),
        out_shape=[
            shaped(bf16, 4, tok, wide), shaped(bf16, COLS, wide),
            shaped(f32, tokens, VW), shaped(f32, tokens, BC), shaped(f32, STEPS, tokens),
        ],
        compiler_params=vmem(28),
        name="project_first",
    )(places, *a_blocks, *b_blocks, *weights)
    p_step_pair, p_bc_pair, p_pair = swap(p_step), swap(p_bc), swap(p_other)
    p_own = pl.pallas_call(
        project_own,
        grid=(4,),
        in_specs=[pl.BlockSpec((1, tok, wide), lambda k: (k, 0, 0)), whole(VW, wide)],
        out_specs=pl.BlockSpec((tok, VW), lambda k: (k, 0)),
        out_shape=shaped(f32, tokens, VW),
        compiler_params=vmem(8),
        cost_estimate=cost(2 * tokens * wide * VW, 6 << 20),
        name="project_own",
    )(hid, whole_w)
    place = (yh * 2 + c) * EACH
    bias, rate, gain = (
        lax.dynamic_slice_in_dim(v, place, EACH, 0)[:, None]
        for v in (step_bias, decay_rate, skip_gain)
    )
    pre_step = p_step[:EACH] + p_step_pair[STEPS // 2 : STEPS // 2 + EACH] + bias
    step = jax.nn.softplus(pre_step)
    sig = jax.nn.sigmoid(pre_step)

    values, bc, held, grads, cross, ends, cum = pl.pallas_call(
        state_kernel,
        out_shape=[
            shaped(bf16, tokens, VW), shaped(bf16, tokens, BC),
            shaped(bf16, blocks, VW, STATE), shaped(bf16, blocks, VW, STATE),
            shaped(f32, blocks, EACH, Q), shaped(bf16, 2, VW + STEPS, STATE),
            shaped(f32, EACH, tokens),
        ],
        scratch_shapes=[
            pltpu.VMEM((blocks, VW, STATE), f32), pltpu.VMEM((blocks, VW, STATE), f32),
        ],
        compiler_params=vmem(16),
        name="states",
    )(p_own, p_pair, p_bc, p_bc_pair, cot, step, rate)

    def scan_part(i, values):
        each = blocks // PARTS

        def rows(width):
            return pl.BlockSpec((Q, width), lambda k: (i * each + k, 0))

        def lanes():
            return pl.BlockSpec((EACH, Q), lambda k: (0, i * each + k))

        def stack(*shape):
            return pl.BlockSpec((1,) + shape, lambda k: (i * each + k, 0, 0))

        return pl.pallas_call(
            scan_kernel,
            grid=(each,),
            in_specs=[
                rows(VW), rows(BC), rows(VW), lanes(), whole(EACH, 1), whole(EACH, 1),
                stack(VW, STATE), stack(VW, STATE), stack(EACH, Q),
            ],
            out_specs=[
                pl.BlockSpec((Q, 2 * VW + BC), lambda k: (k, 0)),
                pl.BlockSpec((EACH, Q), lambda k: (0, k)),
            ],
            out_shape=[shaped(f32, tokens // PARTS, 2 * VW + BC), shaped(f32, EACH, tokens // PARTS)],
            compiler_params=vmem(6),
            cost_estimate=cost(3e9, 4 << 20),
            name="scan",
        )(values, bc, cot, step, rate, gain, held, grads, cross)

    def unpack(packed):
        state = packed[:VW].astype(f32)
        decay = jnp.sum(packed[VW:].astype(f32), axis=0)[:EACH]
        return state, decay

    def times(decay, state):
        return (decay[:, None, None] * state.reshape(EACH, HEAD_DIM, STATE)).reshape(VW, STATE)

    def pack(state, decay):
        high = lax.reduce_precision(decay, 8, 7)
        mid = lax.reduce_precision(decay - high, 8, 7)
        pieces = jnp.stack([high, mid, decay - high - mid])
        pieces = jnp.pad(pieces, ((0, STEPS - 3), (0, STATE - EACH)))
        return jnp.concatenate([state, pieces], axis=0).astype(bf16)

    def along(packed, by):
        pairs = [
            (i * 2 + core, (i + by * (1 - 2 * core)) * 2 + core)
            for i in range(NZ)
            for core in range(2)
            if 0 <= i + by * (1 - 2 * core) < NZ
        ]
        return lax.ppermute(packed, ("z", "c"), pairs)

    def join(near, far):
        return near[0] + times(near[1], far[0]), near[1] * far[1]

    def unpack_both(packed):
        return [unpack(packed[0]), unpack(packed[1])]

    def pack_both(windows):
        return jnp.stack([pack(*w) for w in windows])

    start = jnp.stack([pick(ends, c, 0), swap(pick(ends, 1 - c, 0))])
    start, late_values = tie(start, values)
    local_parts = [scan_part(i, late_values) for i in range(PARTS)]
    window = [
        join(near, far)
        for near, far in zip(unpack_both(along(start, 1)), unpack_both(along(start, 2)))
    ]
    for by in (2, 4):
        far = unpack_both(along(pack_both(window), by))
        window = [join(w, f) for w, f in zip(window, far)]
    kept, given = window[0][0].astype(bf16), window[1][0].astype(bf16)
    other_way = swap(given)
    state_in = jnp.where(c == 0, kept, other_way)
    later = jnp.where(c == 0, other_way, kept)

    mixed, back, steps = pl.pallas_call(
        join_kernel,
        out_shape=[
            shaped(bf16, tokens, VW), shaped(bf16, tokens, VW + BC), shaped(bf16, STEPS, tokens),
        ],
        compiler_params=vmem(20),
        name="join",
    )(
        values, bc, cot, step, sig, rate, cum, state_in, later,
        *(p[0] for p in local_parts), *(p[1] for p in local_parts),
    )

    back_pair, steps_pair = swap(back), swap(steps)
    steps = jnp.concatenate([steps[: STEPS // 2], steps_pair[: STEPS // 2]], axis=0)

    def term(at, *sums, last=False):
        full = [whole(tokens, VW + BC)] * 2 + [whole(STEPS, tokens)]
        return pl.pallas_call(
            term_kernel,
            grid_spec=pltpu.PrefetchScalarGridSpec(
                num_scalar_prefetch=1,
                grid=(1,),
                in_specs=full
                + [pl.BlockSpec((4, tok, FEAT), lambda k, at: (0, 0, at[0]))]
                + [whole(FEAT + STEPS, MAIN)] * len(sums),
                out_specs=whole(FEAT + STEPS, MAIN),
            ),
            out_shape=shaped(f32 if last else bf16, FEAT + STEPS, MAIN),
            compiler_params=vmem(14),
            cost_estimate=cost(2 * tokens * COLS * FEAT, 4 << 20),
            name="term",
        )((at % NZ)[None], back, back_pair, steps, hid, *sums)

    up, down = term(z + NZ // 2), term(z + NZ // 2 + 1)
    up, down, late_back = tie(up, down, back)

    a_part, b_part = pl.pallas_call(
        input_kernel,
        grid=(NZ,),
        in_specs=[
            whole(tokens, VW + BC), whole(tokens, VW + BC), whole(STEPS, tokens),
            pl.BlockSpec((COLS, FEAT), lambda k: (0, k)),
        ],
        out_specs=[
            pl.BlockSpec((1, 1, 2, tok, FEAT), lambda k: (k // 2, k % 2, 0, 0, 0)),
            pl.BlockSpec((2, 1, 1, tok, FEAT), lambda k: (0, k % 2, k // 2, 0, 0)),
        ],
        out_shape=[shaped(bf16, NX, 2, 2, tok, FEAT), shaped(bf16, 2, 2, NX, tok, FEAT)],
        scratch_shapes=[pltpu.VMEM((tokens, BC), bf16)],
        compiler_params=vmem(14),
        cost_estimate=cost(2 * tokens * COLS * FEAT * NZ, 8 << 20),
        name="input",
    )(late_back, back_pair, steps, whole_w)
    a_part = a_part.reshape(NX, NY, tok, FEAT)
    b_part = b_part.reshape(NY, NX, tok, FEAT)

    def x_at(hop):
        return (x - way * hop) % NX

    def y_at(hop):
        return (y - way * hop) % NY

    def y_turned(hop):
        at = y_at(hop)
        return at % 2 * 2 + at // 2

    a_sum, b_sum = take(a_part, x_at(1)), take(b_part, y_at(1))
    for hop in range(1, 4):
        up = shift(up, "z", 1, NZ)
        down = shift(down, "z", -1, NZ)
        a_sum = take(a_part, x_at(hop + 1), both_x(a_sum))
        b_sum = take(b_part, y_at(hop + 1), both_y(b_sum))
        up = term(z + NZ // 2 - hop, up)
        if hop < 3:
            down = term(z + NZ // 2 + 1 + hop, down)
            up, down, a_sum, b_sum = tie(up, down, a_sum, b_sum)
    up = shift(up, "z", 1, NZ)
    a_all, b_all = a_sum, b_sum
    a_sum, b_sum = take(a_all, y_turned(1)), take(b_all, x_at(1))
    for hop in range(1, 4):
        a_sum = take(a_all, y_turned(hop + 1), both_y(a_sum))
        b_sum = take(b_all, x_at(hop + 1), both_x(b_sum))
    keep = jnp.where(c == 0, a_sum, b_sum).reshape(tok, 2, 128)
    got = swap(jnp.where(c == 0, b_sum, a_sum)).reshape(tok, 2, 128)
    hidden_grad = pairwise(keep, got, c, 2).reshape(tok, 2 * FEAT)

    mixed, back_pair = tie(mixed, back_pair)
    mixed = mixed.reshape(2, 2, tok, VW)
    mixed = pairwise(pick(mixed, yh, 0), shift(pick(mixed, 1 - yh, 0), "yh", 1, 2), yh, 2)
    mixed = pairwise(pick(mixed, c, 0), swap(pick(mixed, 1 - c, 0)), c, 2)
    mixer_out = mixed.reshape(tok, 4 * VW)

    summed = term(z, up, down, last=True)
    half = FEAT // 2
    main, step_rows = summed[:FEAT].reshape(2, half, MAIN), summed[FEAT:, :FEAT]
    step_rows = step_rows.reshape(STEPS, 2, half)
    give = jnp.concatenate(
        [pick(main, 1 - yh, 0), jnp.pad(pick(step_rows, 1 - yh, 1), ((0, 0), (0, MAIN - half)))],
        axis=0,
    )
    other = shift(give.astype(bf16), "yh", 1, 2).astype(f32)
    own, own_step = pick(main, yh, 0), pick(step_rows, yh, 1)
    other_step = other[half:, :half]
    other = other[:half]
    state_grad = own[:, 2 * VW :] + other[:, 2 * VW :]

    def ordered(own, other, wide, gap):
        def cores(value):
            mine, pair = value[:, :wide], value[:, gap : gap + wide]
            return jnp.where(
                c == 0,
                jnp.concatenate([mine, pair], axis=1),
                jnp.concatenate([pair, mine], axis=1),
            )

        own, other = cores(own), cores(other)
        return jnp.where(
            yh == 0,
            jnp.concatenate([own, other], axis=1),
            jnp.concatenate([other, own], axis=1),
        )

    value_grad = ordered(own, other, VW, VW)
    step_grad = ordered(own_step.T, other_step.T, EACH, STEPS // 2)
    return mixer_out, hidden_grad, value_grad, state_grad, step_grad


def solution(mesh):
    fine = Mesh(mesh.devices.reshape(NZ, 2, 2, NX, 2), ("z", "yh", "c", "x", "yl"))
    split = P(("z", "yh", "c"), ("x", "yl"))
    by_head = P(("x", "yl"))
    return jax.shard_map(
        local,
        mesh=fine,
        in_specs=(split,) * 4 + (by_head,) * 3 + (split,),
        out_specs=(split,) * 5,
        check_vma=False,
    )
```

```python
import jax
import jax.numpy as jnp
from jax import lax
from jax.experimental import pallas as pl
from jax.experimental.pallas import tpu as pltpu
from jax.sharding import Mesh, PartitionSpec as P

HEAD_DIM = 64
STATE = 128
Q = 128
EACH = 4
VW = EACH * HEAD_DIM
BC = 2 * STATE
MAIN = 2 * VW + BC
STEPS = 16
COLS = MAIN + STEPS
FEAT = 256
NZ, NX, NY = 8, 4, 4
SPLIT = 400
f32, bf16 = jnp.float32, jnp.bfloat16
HI = lax.Precision.HIGHEST


def vmem(mebibytes):
    return pltpu.CompilerParams(vmem_limit_bytes=mebibytes * 1024 * 1024)


def shift(value, axis, by, count, wrap=True):
    pairs = [(i, (i + by) % count) for i in range(count) if wrap or 0 <= i + by < count]
    return lax.ppermute(value, axis, pairs)


def both_x(value):
    pairs = [(c * NX + i, c * NX + (i + 1 - 2 * c) % NX) for c in range(2) for i in range(NX)]
    return lax.ppermute(value, ("c", "x"), pairs)


def both_y(value):
    def at(c, y):
        return (y // 2) * 4 + c * 2 + y % 2

    pairs = [(at(c, y), at(c, (y + 1 - 2 * c) % NY)) for c in range(2) for y in range(NY)]
    return lax.ppermute(value, ("yh", "c", "yl"), pairs)


def swap(value):
    return shift(value, "c", 1, 2)


def dot(left, right, dims, precision=None):
    return lax.dot_general(
        left, right, (dims, ((), ())), preferred_element_type=f32, precision=precision
    )


NN, NT, TN = ((1,), (0,)), ((1,), (1,)), ((0,), (0,))


def iota(shape, dim):
    return lax.broadcasted_iota(jnp.int32, shape, dim)


def consts():
    low = (iota((Q, Q), 0) >= iota((Q, Q), 1)).astype(f32)
    spread = (iota((EACH, VW), 1) // HEAD_DIM == iota((EACH, VW), 0)).astype(f32)
    return low, spread


def project_kernel(at_ref, *refs):
    x, y, z, way = (at_ref[i] for i in range(4))
    a_refs, b_refs, w_refs = refs[:NX], refs[NX : NX + NY], refs[NX + NY : NX + NY + NZ]
    part_ref, hid_out, w_out, own_ref, send_ref, hid, weights, sems = refs[NX + NY + NZ :]
    tok = hid.shape[1]
    copies = []

    def copy(source, target):
        copies.append(pltpu.make_async_copy(source, target, sems.at[len(copies)]))
        copies[-1].start()

    for j in range(NX):
        x_at = (x - way * j) & (NX - 1)
        for i in range(NY):
            y_at = (y - way * i) & (NY - 1)
            lanes = pl.ds(pl.multiple_of((2 * x_at + (y_at & 1)) * FEAT, FEAT), FEAT)
            row = (y_at >> 1) * 2
            copy(a_refs[j].at[i], hid.at[row, :, lanes])
            copy(b_refs[i].at[j], hid.at[row + 1, :, lanes])
    for i in range(NZ):
        z_at = (z + offset(i)) & (NZ - 1)
        lanes = pl.ds(pl.multiple_of(z_at * FEAT, FEAT), FEAT)
        copy(w_refs[i], weights.at[SPLIT:, lanes])
        copy(part_ref.at[i], weights.at[:SPLIT, i * FEAT : (i + 1) * FEAT])
    for one in copies:
        one.wait()
    hid_back = pltpu.make_async_copy(hid, hid_out, sems.at[len(copies)])
    w_back = pltpu.make_async_copy(weights, w_out, sems.at[len(copies) + 1])
    hid_back.start()
    w_back.start()
    half = 2 * tok
    for i in range(4):
        rows = slice(i * tok, (i + 1) * tok)
        block = hid[i]
        own_ref[rows, :] = dot(block, weights[:VW, :], NT)
        send_ref[rows, :VW] = dot(block, weights[VW : 2 * VW, :], NT)
        send_ref[rows, VW:] = dot(block, weights[2 * VW : MAIN, :], NT)
        low = 4 * tok + STEPS * (i * tok // half)
        send_ref[low : low + STEPS, i * tok % half : i * tok % half + tok] = dot(
            weights[MAIN:, :], block, NT
        )
    hid_back.wait()
    w_back.wait()


def offset(i):
    return i // 2 if i % 2 == 0 else -(i + 1) // 2


def state_kernel(
    own_ref, send_ref, recv_ref, g_ref, step_ref, rate_ref,
    x_ref, bc_ref, fresh_ref, seed_ref, last_ref, ends_ref,
):
    tokens = x_ref.shape[0]
    count = tokens // Q
    low, spread = consts()
    cum = dot(-step_ref[...] * rate_ref[...], low, NT, HI)
    twice = jnp.concatenate(
        [jnp.concatenate([spread, jnp.zeros_like(spread)], axis=1),
         jnp.concatenate([jnp.zeros_like(spread), spread], axis=1)], axis=0)
    lane = iota((EACH, count), 1)
    ends = jnp.zeros((EACH, count), f32)
    for k in range(count):
        rows = slice(k * Q, (k + 1) * Q)
        x = (own_ref[rows, :] + recv_ref[rows, :VW]).astype(bf16)
        bc = (send_ref[rows, VW:] + recv_ref[rows, VW:]).astype(bf16)
        x_ref[rows, :] = x
        bc_ref[rows, :] = bc
        here = cum[k * EACH : (k + 1) * EACH]
        last = here[:, Q - 1 :]
        ends = ends + jnp.where(lane == k, last, 0.0)
        rest = jnp.exp(last - here) * step_ref[k * EACH : (k + 1) * EACH, :]
        both = dot(jnp.concatenate([rest, jnp.exp(here)], axis=0), twice, TN, HI)
        tail = (x.astype(f32) * both[:, :VW]).astype(bf16)
        grown = (g_ref[rows, :].astype(f32) * both[:, VW:]).astype(bf16)
        fresh_ref[k] = dot(tail, bc[:, :STATE], TN)
        seed_ref[k] = dot(grown, bc[:, STATE:], TN)
    lasts = dot(spread, jnp.exp(ends), TN, HI)
    last_ref[...] = lasts
    state = jnp.zeros((VW, STATE), f32)
    grad = jnp.zeros((VW, STATE), f32)
    for k in range(count):
        state = lasts[:, k : k + 1] * state + fresh_ref[k]
        back = count - 1 - k
        grad = lasts[:, back : back + 1] * grad + seed_ref[back]
    eye = (iota((EACH, STATE), 0) == iota((EACH, STATE), 1)).astype(f32)
    total = jnp.exp(jnp.sum(ends, axis=1, keepdims=True))
    pieces = split_decay(dot(jnp.broadcast_to(total, (EACH, STEPS)), eye, TN, HI)).astype(bf16)
    ends_ref[0, :VW] = state.astype(bf16)
    ends_ref[1, :VW] = grad.astype(bf16)
    ends_ref[0, VW:] = pieces
    ends_ref[1, VW:] = pieces


def split_decay(decay):
    high = decay.astype(bf16).astype(f32)
    mid = (decay - high).astype(bf16).astype(f32)
    least = decay - high - mid
    row = iota((STEPS, STATE), 0)
    return jnp.where(row == 0, high, jnp.where(row == 1, mid, jnp.where(row == 2, least, 0.0)))


def window_kernel(near_ref, far_ref, out_ref):
    spread = (iota((VW, STATE), 0) // HEAD_DIM == iota((VW, STATE), 1)).astype(bf16)
    for i in range(2):
        near = near_ref[i, VW:]
        column = jnp.sum(dot(spread, near, NT), axis=1, keepdims=True)
        out_ref[i, :VW] = (
            near_ref[i, :VW].astype(f32) + column * far_ref[i, :VW].astype(f32)
        ).astype(bf16)
        decay = jnp.sum(near.astype(f32), axis=0, keepdims=True) * jnp.sum(
            far_ref[i, VW:].astype(f32), axis=0, keepdims=True
        )
        out_ref[i, VW:] = split_decay(jnp.broadcast_to(decay, (STEPS, STATE))).astype(bf16)


def scan_kernel(
    x_ref, bc_ref, g_ref, step_ref, sig_ref, rate_ref, gain_ref,
    fresh_ref, seed_ref, last_ref, in_ref, later_ref,
    y_ref, back_ref, dstep_ref, held, grads,
):
    at = pl.program_id(0)
    count = fresh_ref.shape[0]

    @pl.when(at == 0)
    def _():
        lasts = last_ref[...]
        state = in_ref[...].astype(f32)
        grad = later_ref[...].astype(f32)
        for k in range(count):
            held[k] = state
            state = lasts[:, k : k + 1] * state + fresh_ref[k]
            back = count - 1 - k
            grads[back] = grad
            grad = lasts[:, back : back + 1] * grad + seed_ref[back]
        held[count] = state

    low, spread = consts()
    mask = low > 0.0
    zero = jnp.zeros_like(spread)
    twice = jnp.concatenate(
        [jnp.concatenate([spread, zero], axis=1), jnp.concatenate([zero, spread], axis=1)], axis=0)
    lane = iota((Q, EACH), 1)
    row = iota((EACH, Q), 0)
    gain_wide = gain_ref[...]
    for sub in range(step_ref.shape[0]):
        k = at * step_ref.shape[0] + sub
        rows = slice(sub * Q, (sub + 1) * Q)
        step_t = step_ref[sub]
        cum_t = dot(-step_t * rate_ref[...], low, NT, HI)
        both_wide = dot(jnp.concatenate([cum_t, step_t], axis=0), twice, TN, HI)
        cum_wide, step_wide = both_wide[:, :VW], both_wide[:, VW:]
        growth = jnp.exp(cum_wide)
        rest = jnp.exp(cum_wide[Q - 1 :, :] - cum_wide)
        x, g = x_ref[rows, :], g_ref[rows, :]
        xf, gf = x.astype(f32), g.astype(f32)
        b_mat, c_mat = bc_ref[rows, :STATE], bc_ref[rows, STATE:]
        state, nxt, grad = held[k], held[k + 1], grads[k]
        state_b, grad_b = state.astype(bf16), grad.astype(bf16)

        scores = jnp.where(mask, dot(c_mat, b_mat, NT), 0.0)
        mixed, moved = [], []
        pairs = jnp.zeros((Q, Q), f32)
        out_sum = jnp.zeros((Q, EACH), f32)
        in_sum = jnp.zeros((EACH, Q), f32)
        for e in range(EACH):
            cut = slice(e * HEAD_DIM, (e + 1) * HEAD_DIM)
            first = slice(e * HEAD_DIM, e * HEAD_DIM + 1)
            fade = jnp.exp(jnp.minimum(cum_wide[:, first] - cum_t[e : e + 1, :], 0.0))
            weight = scores * fade
            step_row = step_t[e : e + 1, :]
            mixing = (weight * step_row).astype(bf16)
            mixed.append(dot(mixing, x[:, cut], NN))
            moved.append(dot(mixing, g[:, cut], TN))
            outer = dot(g[:, cut], x[:, cut], NT)
            pairs = pairs + outer * fade * step_row
            both = weight * outer
            in_sum = in_sum + jnp.where(row == e, jnp.sum(both, axis=0, keepdims=True), 0.0)
            out_sum = out_sum + jnp.where(
                lane == e, jnp.sum(both * step_row, axis=1, keepdims=True), 0.0
            )
        pairs = jnp.where(mask, pairs, 0.0).astype(bf16)

        from_state = growth * dot(c_mat, state_b, NT)
        from_later = rest * dot(b_mat, grad_b, NT)
        y_ref[rows, :] = (
            jnp.concatenate(mixed, axis=1) + from_state + gain_wide * xf
        ).astype(bf16)
        back_ref[rows, :VW] = (
            jnp.concatenate(moved, axis=1) + step_wide * from_later + gain_wide * gf
        ).astype(bf16)
        back_ref[rows, VW : VW + STATE] = (
            dot(pairs, c_mat, TN) + dot((xf * (rest * step_wide)).astype(bf16), grad_b, NN)
        ).astype(bf16)
        back_ref[rows, VW + STATE :] = (
            dot(pairs, b_mat, NN) + dot((gf * growth).astype(bf16), state_b, NN)
        ).astype(bf16)

        direct = in_sum + dot(spread, xf * from_later, NT, HI)
        out_t = dot(spread, gf * from_state, NT, HI)
        crossing = dot(spread, jnp.sum(grad * nxt, axis=1, keepdims=True), NN, HI)
        d_decay = (
            dot(out_sum, low, TN, HI) + dot(out_t - direct * step_t, low, NN, HI) + crossing
        )
        d_step = (direct - rate_ref[...] * d_decay) * sig_ref[sub]
        dstep_ref[:, rows] = jnp.concatenate(
            [d_step, jnp.zeros((STEPS - EACH, Q), f32)], axis=0
        ).astype(bf16)


def both_bc(back_ref, pair_ref):
    return (back_ref[:, VW:].astype(f32) + pair_ref[:, VW:].astype(f32)).astype(bf16)


def term_kernel(at_ref, back_ref, pair_ref, steps_ref, hid_ref, *refs):
    outs, blocks, sems = refs[:-2], refs[-2], refs[-1]
    copies = []
    for i in range(len(outs)):
        lanes = pl.ds(pl.multiple_of(at_ref[i] * FEAT, FEAT), FEAT)
        copies.append(pltpu.make_async_copy(hid_ref.at[:, :, lanes], blocks.at[i], sems.at[i]))
        copies[-1].start()
    main = jnp.concatenate([back_ref[:, :VW], pair_ref[:, :VW], both_bc(back_ref, pair_ref)], axis=1)
    for i, out_ref in enumerate(outs):
        copies[i].wait()
        block = blocks[i].reshape(-1, FEAT)
        out_ref[:FEAT, :] = dot(block, main, TN).astype(bf16)
        out_ref[FEAT:, :FEAT] = dot(steps_ref[...], block, NN).astype(bf16)
        out_ref[FEAT:, FEAT:] = jnp.zeros((STEPS, MAIN - FEAT), bf16)


def input_kernel(back_ref, pair_ref, steps_ref, w_ref, a_ref, b_ref, bc, weights, sems):
    at = pl.program_id(0)

    def fetch(i):
        return pltpu.make_async_copy(
            w_ref.at[:, i * FEAT : (i + 1) * FEAT], weights.at[i], sems.at[i]
        )

    @pl.when(at == 0)
    def _():
        for i in range(NZ):
            fetch(i).start()
        bc[...] = both_bc(back_ref, pair_ref)

    for i in range(NZ):

        @pl.when(at == i)
        def _():
            fetch(i).wait()

    size = a_ref.shape[3]
    for i in range(4):
        rows = slice(i * size, (i + 1) * size)
        total = (
            dot(back_ref[rows, :VW], weights[at, :VW, :], NN)
            + dot(pair_ref[rows, :VW], weights[at, VW : 2 * VW, :], NN)
            + dot(bc[rows, :], weights[at, 2 * VW : MAIN, :], NN)
            + dot(steps_ref[:, rows], weights[at, MAIN:, :], TN)
        ).astype(bf16)
        if i % 2 == 0:
            a_ref[0, 0, i // 2] = total
        else:
            b_ref[i // 2, 0, 0] = total


def take_kernel(at_ref, table_ref, *refs):
    sums, out_ref, block, sem = refs[:-3], refs[-3], refs[-2], refs[-1]
    copy = pltpu.make_async_copy(table_ref.at[at_ref[0]], block, sem)
    copy.start()
    copy.wait()
    value = block[...]
    if sums:
        value = (value.astype(f32) + sums[0][...].astype(f32)).astype(bf16)
    out_ref[...] = value


def take(table, at, *sums):
    shape = table.shape[1:]
    return pl.pallas_call(
        take_kernel,
        in_specs=[pl.BlockSpec(memory_space=pltpu.SMEM), pl.BlockSpec(memory_space=pltpu.HBM)]
        + [pl.BlockSpec(memory_space=pltpu.VMEM)] * len(sums),
        out_shape=jax.ShapeDtypeStruct(shape, bf16),
        scratch_shapes=[pltpu.VMEM(shape, bf16), pltpu.SemaphoreType.DMA],
        compiler_params=vmem(4),
        cost_estimate=TINY,
        name="take",
    )(at[None].astype(jnp.int32), table, *sums)


def cores_kernel(at_ref, own_ref, pair_ref, out_ref):
    c = at_ref[0]
    for i in range(2):
        part = slice(i * 128, (i + 1) * 128)
        out_ref[:, pl.ds(pl.multiple_of((2 * i + c) * 128, 128), 128)] = own_ref[:, part]
        out_ref[:, pl.ds(pl.multiple_of((2 * i + 1 - c) * 128, 128), 128)] = pair_ref[:, part]


def heads_kernel(at_ref, own_ref, pair_ref, cross_ref, out_ref):
    yh, c = at_ref[0], at_ref[1]

    def to(first, second, value):
        lanes = pl.ds(pl.multiple_of((first * 2 + second) * VW, VW), VW)
        out_ref[:, lanes] = value

    to(yh, c, own_ref[c])
    to(1 - yh, c, pair_ref[c])
    to(yh, 1 - c, cross_ref[0])
    to(1 - yh, 1 - c, cross_ref[1])


def pick(value, at, dim):
    return lax.dynamic_index_in_dim(value, at, dim, False)


def tie(*values):
    return lax.optimization_barrier(values)


TINY = pl.CostEstimate(flops=1024, bytes_accessed=1024, transcendentals=0)


def local(hidden, value_proj, state_proj, step_proj, step_bias, decay_rate, skip_gain, out_grad):
    z, yh, c, x, yl = (lax.axis_index(a) for a in ("z", "yh", "c", "x", "yl"))
    y = yh * 2 + yl
    way = 1 - 2 * c
    tok = hidden.shape[0]
    tokens = 4 * tok
    blocks = tokens // Q

    value_t, state_t, step_tr = value_proj.T, state_proj.T, step_proj.T
    none = jnp.zeros((EACH, value_proj.shape[0]), bf16)

    def chosen(which):
        def some(array, wide, core):
            return lax.dynamic_slice_in_dim(array, (which * 2 + core) * wide, wide, 0)

        return jnp.concatenate(
            [
                some(value_t, VW, c), some(value_t, VW, 1 - c), state_t,
                some(step_tr, EACH, c), none, some(step_tr, EACH, 1 - c), none,
            ],
            axis=0,
        )

    mine, theirs = chosen(yh), shift(chosen(1 - yh), "yh", 1, 2)
    chunk = jnp.where(
        yh == 0,
        jnp.concatenate([mine, theirs], axis=1),
        jnp.concatenate([theirs, mine], axis=1),
    )
    parts = hidden.reshape(tok, 2, 2, 128)
    keep = pick(parts, c, 2).reshape(tok, FEAT)
    got = swap(pick(parts, 1 - c, 2).reshape(tok, FEAT))
    first = jnp.where(c == 0, keep, got)
    second = jnp.where(c == 0, got, keep)

    def pairwise(own, pair, place, dim):
        return jnp.where(
            place == 0, jnp.stack([own, pair], dim), jnp.stack([pair, own], dim)
        )

    out_grad, chunk = tie(out_grad, chunk)
    cot = out_grad.reshape(tok, 2, 2, VW)
    cot = pairwise(pick(cot, c, 2), swap(pick(cot, 1 - c, 2)), c, 0)

    brought = lax.all_gather(chunk[:SPLIT], "z")
    ring = chunk[SPLIT:]
    weights = [ring, shift(ring, "z", 1, NZ), shift(ring, "z", -1, NZ)]
    a_blocks, b_blocks = [first], [second]
    for hop in range(1, 4):
        a_blocks.append(both_y(a_blocks[-1]))
        b_blocks.append(both_x(b_blocks[-1]))
    a_blocks, b_blocks = [jnp.stack(a_blocks)], [jnp.stack(b_blocks)]
    weights[1], weights[2], a_blocks[0], b_blocks[0], cot = tie(
        weights[1], weights[2], a_blocks[0], b_blocks[0], cot
    )
    cot = pairwise(pick(cot, yh, 2), shift(pick(cot, 1 - yh, 2), "yh", 1, 2), yh, 0)
    cot = cot.reshape(tokens, VW)
    for hop in range(1, 4):
        weights.append(shift(weights[-2], "z", 1, NZ))
        if hop < 3:
            weights.append(shift(weights[-2], "z", -1, NZ))
        a_blocks.append(both_x(a_blocks[-1]))
        b_blocks.append(both_y(b_blocks[-1]))
        if hop < 3:
            weights[-1], weights[-2], a_blocks[-1], b_blocks[-1] = tie(
                weights[-1], weights[-2], a_blocks[-1], b_blocks[-1]
            )

    def whole(*shape):
        return pl.BlockSpec(shape, lambda *k: (0,) * len(shape))

    def shaped(dtype, *shape):
        return jax.ShapeDtypeStruct(shape, dtype)

    places = jnp.stack([x, y, z, way]).astype(jnp.int32)
    wide = NZ * FEAT
    in_hbm = pl.BlockSpec(memory_space=pltpu.HBM)
    in_vmem = pl.BlockSpec(memory_space=pltpu.VMEM)
    in_smem = pl.BlockSpec(memory_space=pltpu.SMEM)
    hid, whole_w, p_own, p_send = pl.pallas_call(
        project_kernel,
        in_specs=[in_smem] + [in_hbm] * (NX + NY + NZ + 1),
        out_specs=[in_hbm, in_hbm, in_vmem, in_vmem],
        out_shape=[
            shaped(bf16, 4, tok, wide), shaped(bf16, COLS, wide),
            shaped(f32, tokens, VW), shaped(f32, tokens + 2 * STEPS, VW + BC),
        ],
        scratch_shapes=[
            pltpu.VMEM((4, tok, wide), bf16), pltpu.VMEM((COLS, wide), bf16),
            pltpu.SemaphoreType.DMA((2 * NX * NY + 2 * NZ + 2,)),
        ],
        compiler_params=vmem(20),
        name="project",
    )(places, *a_blocks, *b_blocks, *weights, brought)
    p_recv = swap(p_send)

    def step_rows(packed):
        packed = packed[tokens:]
        return jnp.concatenate([packed[:STEPS], packed[STEPS:]], axis=1)

    place = (yh * 2 + c) * EACH
    bias, rate, gain = (
        lax.dynamic_slice_in_dim(v, place, EACH, 0)[:, None]
        for v in (step_bias, decay_rate, skip_gain)
    )
    pre_step = (
        step_rows(p_send)[:EACH] + step_rows(p_recv)[STEPS // 2 : STEPS // 2 + EACH] + bias
    )
    pre_step = pre_step.reshape(EACH, blocks, Q).transpose(1, 0, 2)
    step = jax.nn.softplus(pre_step)
    sig = jax.nn.sigmoid(pre_step)

    states = shaped(f32, blocks, VW, STATE)
    values, bc, fresh, seeds, lasts, ends = pl.pallas_call(
        state_kernel,
        out_shape=[
            shaped(bf16, tokens, VW), shaped(bf16, tokens, BC), states, states,
            shaped(f32, VW, blocks), shaped(bf16, 2, VW + STEPS, STATE),
        ],
        compiler_params=vmem(14),
        name="states",
    )(p_own, p_send, p_recv, cot, step.reshape(blocks * EACH, Q), jnp.tile(rate, (blocks, 1)))

    def along(packed, by):
        pairs = [
            (i * 2 + core, (i + by * (1 - 2 * core)) * 2 + core)
            for i in range(NZ)
            for core in range(2)
            if 0 <= i + by * (1 - 2 * core) < NZ
        ]
        return lax.ppermute(packed, ("z", "c"), pairs)

    def joined(near, far):
        return pl.pallas_call(
            window_kernel,
            out_shape=shaped(bf16, 2, VW + STEPS, STATE),
            compiler_params=vmem(2),
            cost_estimate=TINY,
            name="window",
        )(near, far)

    start = jnp.stack([pick(ends, c, 0), swap(pick(ends, 1 - c, 0))])
    window = joined(along(start, 1), along(start, 2))
    for by in (2, 4):
        window = joined(window, along(window, by))
    kept, given = window[0, :VW], window[1, :VW]
    other_way = swap(given)
    state_in = jnp.where(c == 0, kept, other_way)
    later = jnp.where(c == 0, other_way, kept)

    each = 2

    def rows(width):
        return pl.BlockSpec((each * Q, width), lambda k: (k, 0))

    lanes = pl.BlockSpec((each, EACH, Q), lambda k: (k, 0, 0))
    mixed, back, steps = pl.pallas_call(
        scan_kernel,
        grid=(blocks // each,),
        in_specs=[
            rows(VW), rows(BC), rows(VW), lanes, lanes, whole(EACH, 1), whole(1, VW),
            whole(blocks, VW, STATE), whole(blocks, VW, STATE), whole(VW, blocks),
            whole(VW, STATE), whole(VW, STATE),
        ],
        out_specs=[
            rows(VW), rows(VW + BC), pl.BlockSpec((STEPS, each * Q), lambda k: (0, k)),
        ],
        out_shape=[
            shaped(bf16, tokens, VW), shaped(bf16, tokens, VW + BC), shaped(bf16, STEPS, tokens),
        ],
        scratch_shapes=[
            pltpu.VMEM((blocks + 1, VW, STATE), f32), pltpu.VMEM((blocks, VW, STATE), f32),
        ],
        compiler_params=vmem(14),
        name="scan",
    )(
        values, bc, cot, step, sig, rate, jnp.repeat(gain, HEAD_DIM, axis=0).T,
        fresh, seeds, lasts, state_in, later,
    )

    back_pair, steps_pair = swap(back), swap(steps)
    steps = jnp.concatenate([steps[: STEPS // 2], steps_pair[: STEPS // 2]], axis=0)

    def terms(*offsets):
        count = len(offsets)
        at = jnp.stack([(z + i) % NZ for i in offsets]).astype(jnp.int32)
        return pl.pallas_call(
            term_kernel,
            in_specs=[in_smem, in_vmem, in_vmem, in_vmem, in_hbm],
            out_shape=[shaped(bf16, FEAT + STEPS, MAIN)] * count,
            scratch_shapes=[
                pltpu.VMEM((count, 4, tok, FEAT), bf16), pltpu.SemaphoreType.DMA((count,)),
            ],
            compiler_params=vmem(16),
            cost_estimate=TINY,
            name="term",
        )(at, back, back_pair, steps, hid)

    def more(sums, *parts):
        total = sums.astype(f32)
        for part in parts:
            total = total + part.astype(f32)
        return total

    up, down = terms(4, 5)
    up, down, late_back = tie(up, down, back)

    a_part, b_part = pl.pallas_call(
        input_kernel,
        grid=(NZ,),
        in_specs=[
            whole(tokens, VW + BC), whole(tokens, VW + BC), whole(STEPS, tokens), in_hbm,
        ],
        out_specs=[
            pl.BlockSpec((1, 1, 2, tok, FEAT), lambda k: (k // 2, k % 2, 0, 0, 0)),
            pl.BlockSpec((2, 1, 1, tok, FEAT), lambda k: (0, k % 2, k // 2, 0, 0)),
        ],
        out_shape=[shaped(bf16, NX, 2, 2, tok, FEAT), shaped(bf16, 2, 2, NX, tok, FEAT)],
        scratch_shapes=[
            pltpu.VMEM((tokens, BC), bf16), pltpu.VMEM((NZ, COLS, FEAT), bf16),
            pltpu.SemaphoreType.DMA((NZ,)),
        ],
        compiler_params=vmem(16),
        cost_estimate=TINY,
        name="input",
    )(late_back, back_pair, steps, whole_w)
    a_part = a_part.reshape(NX, NY, tok, FEAT)
    b_part = b_part.reshape(NY, NX, tok, FEAT)

    def x_at(hop):
        return (x - way * hop) % NX

    def y_at(hop):
        return (y - way * hop) % NY

    def y_turned(hop):
        at = y_at(hop)
        return at % 2 * 2 + at // 2

    a_sum, b_sum = take(a_part, x_at(1)), take(b_part, y_at(1))
    add_3, add_2, add_1, add_0, add_6, add_7 = terms(3, 2, 1, 0, 6, 7)
    for hop in range(1, 4):
        up = shift(up, "z", 1, NZ)
        down = shift(down, "z", -1, NZ)
        a_sum = take(a_part, x_at(hop + 1), both_x(a_sum))
        b_sum = take(b_part, y_at(hop + 1), both_y(b_sum))
        up = more(up, (add_3, add_2, add_1)[hop - 1]).astype(bf16)
        if hop < 3:
            down = more(down, (add_6, add_7)[hop - 1]).astype(bf16)
            up, down, a_sum, b_sum = tie(up, down, a_sum, b_sum)
    up = shift(up, "z", 1, NZ)
    a_all, b_all = a_sum, b_sum
    a_sum, b_sum = take(a_all, y_turned(1)), take(b_all, x_at(1))
    for hop in range(1, 4):
        a_sum = take(a_all, y_turned(hop + 1), both_y(a_sum))
        b_sum = take(b_all, x_at(hop + 1), both_x(b_sum))
    keep = jnp.where(c == 0, a_sum, b_sum)
    got = swap(jnp.where(c == 0, b_sum, a_sum))
    hidden_grad = pl.pallas_call(
        cores_kernel,
        in_specs=[in_smem, in_vmem, in_vmem],
        out_shape=shaped(bf16, tok, 2 * FEAT),
        compiler_params=vmem(4),
        cost_estimate=TINY,
        name="by_core",
    )(c[None].astype(jnp.int32), keep, got)

    mixed, back_pair = tie(mixed, back_pair)
    mixed = mixed.reshape(2, 2, tok, VW)
    own = pick(mixed, yh, 0)
    pair = shift(pick(mixed, 1 - yh, 0), "yh", 1, 2)
    crossed = swap(jnp.stack([pick(own, 1 - c, 0), pick(pair, 1 - c, 0)]))
    mixer_out = pl.pallas_call(
        heads_kernel,
        in_specs=[in_smem, in_vmem, in_vmem, in_vmem],
        out_shape=shaped(bf16, tok, 4 * VW),
        compiler_params=vmem(4),
        cost_estimate=TINY,
        name="by_head",
    )(jnp.stack([yh, c]).astype(jnp.int32), own, pair, crossed)

    summed = more(add_0, up, down)
    half = FEAT // 2
    main, step_part = summed[:FEAT].reshape(2, half, MAIN), summed[FEAT:, :FEAT]
    step_part = step_part.reshape(STEPS, 2, half)
    give = jnp.concatenate(
        [pick(main, 1 - yh, 0), jnp.pad(pick(step_part, 1 - yh, 1), ((0, 0), (0, MAIN - half)))],
        axis=0,
    )
    other = shift(give.astype(bf16), "yh", 1, 2).astype(f32)
    own, own_step = pick(main, yh, 0), pick(step_part, yh, 1)
    other_step = other[half:, :half]
    other = other[:half]
    state_grad = own[:, 2 * VW :] + other[:, 2 * VW :]

    def ordered(own, other, wide, gap):
        def cores(value):
            mine, pair = value[:, :wide], value[:, gap : gap + wide]
            return jnp.where(
                c == 0,
                jnp.concatenate([mine, pair], axis=1),
                jnp.concatenate([pair, mine], axis=1),
            )

        own, other = cores(own), cores(other)
        return jnp.where(
            yh == 0,
            jnp.concatenate([own, other], axis=1),
            jnp.concatenate([other, own], axis=1),
        )

    value_grad = ordered(own, other, VW, VW)
    step_grad = ordered(own_step.T, other_step.T, EACH, STEPS // 2)
    return mixer_out, hidden_grad, value_grad, state_grad, step_grad


def solution(mesh):
    fine = Mesh(mesh.devices.reshape(NZ, 2, 2, NX, 2), ("z", "yh", "c", "x", "yl"))
    split = P(("z", "yh", "c"), ("x", "yl"))
    by_head = P(("x", "yl"))
    return jax.shard_map(
        local,
        mesh=fine,
        in_specs=(split,) * 4 + (by_head,) * 3 + (split,),
        out_specs=(split,) * 5,
        check_vma=False,
    )
```

```python
import jax
import jax.numpy as jnp
from jax import lax
from jax.experimental import pallas as pl
from jax.experimental.pallas import tpu as pltpu
from jax.sharding import Mesh, PartitionSpec as P

HEAD_DIM = 64
STATE = 128
Q = 128
EACH = 4
VW = EACH * HEAD_DIM
BC = 2 * STATE
MAIN = 2 * VW + BC
STEPS = 16
COLS = MAIN + STEPS
FEAT = 256
NZ, NX, NY = 8, 4, 4
SPLIT = 528
f32, bf16 = jnp.float32, jnp.bfloat16
HI = lax.Precision.HIGHEST


def vmem(mebibytes):
    return pltpu.CompilerParams(vmem_limit_bytes=mebibytes * 1024 * 1024)


ALL = vmem(60)


def shift(value, axis, by, count, wrap=True):
    pairs = [(i, (i + by) % count) for i in range(count) if wrap or 0 <= i + by < count]
    return lax.ppermute(value, axis, pairs)


def both_x(value):
    pairs = [(c * NX + i, c * NX + (i + 1 - 2 * c) % NX) for c in range(2) for i in range(NX)]
    return lax.ppermute(value, ("c", "x"), pairs)


def both_y(value):
    def at(c, y):
        return (y // 2) * 4 + c * 2 + y % 2

    pairs = [(at(c, y), at(c, (y + 1 - 2 * c) % NY)) for c in range(2) for y in range(NY)]
    return lax.ppermute(value, ("yh", "c", "yl"), pairs)


def swap(value):
    return shift(value, "c", 1, 2)


def dot(left, right, dims, precision=None):
    return lax.dot_general(
        left, right, (dims, ((), ())), preferred_element_type=f32, precision=precision
    )


NN, NT, TN = ((1,), (0,)), ((1,), (1,)), ((0,), (0,))


def iota(shape, dim):
    return lax.broadcasted_iota(jnp.int32, shape, dim)


def consts():
    low = (iota((Q, Q), 0) >= iota((Q, Q), 1)).astype(f32)
    spread = (iota((EACH, VW), 1) // HEAD_DIM == iota((EACH, VW), 0)).astype(f32)
    return low, spread


def pieces(rows):
    high = rows.astype(bf16).astype(f32)
    mid = (rows - high).astype(bf16).astype(f32)
    return jnp.concatenate([high, mid, rows - high - mid], axis=0).astype(bf16)


def exact(rows, right, dims):
    n = rows.shape[0]
    out = dot(pieces(rows), right.astype(bf16), dims)
    return out[:n] + out[n : 2 * n] + out[2 * n :]


def widen(rows, right):
    right = right.astype(bf16)
    return dot(pieces(rows), jnp.concatenate([right] * 3, axis=0), TN)


def project_kernel(at_ref, *refs):
    x, y, z, way = (at_ref[i] for i in range(4))
    a_refs, b_refs, w_refs = refs[:NX], refs[NX : NX + NY], refs[NX + NY : NX + NY + NZ]
    part_ref, hid_out, w_out, own_ref, send_ref, hid, weights, sems = refs[NX + NY + NZ :]
    tok = hid.shape[1]
    copies = []

    def copy(source, target):
        copies.append(pltpu.make_async_copy(source, target, sems.at[len(copies)]))
        copies[-1].start()

    for j in range(NX):
        x_at = (x - way * j) & (NX - 1)
        for i in range(NY):
            y_at = (y - way * i) & (NY - 1)
            lanes = pl.ds(pl.multiple_of((2 * x_at + (y_at & 1)) * FEAT, FEAT), FEAT)
            row = (y_at >> 1) * 2
            copy(a_refs[j].at[i], hid.at[row, :, lanes])
            copy(b_refs[i].at[j], hid.at[row + 1, :, lanes])
    for i in range(NZ):
        z_at = (z + offset(i)) & (NZ - 1)
        lanes = pl.ds(pl.multiple_of(z_at * FEAT, FEAT), FEAT)
        copy(w_refs[i], weights.at[SPLIT:, lanes])
        copy(part_ref.at[i], weights.at[:SPLIT, i * FEAT : (i + 1) * FEAT])
    for one in copies:
        one.wait()
    hid_back = pltpu.make_async_copy(hid, hid_out, sems.at[len(copies)])
    w_back = pltpu.make_async_copy(weights, w_out, sems.at[len(copies) + 1])
    hid_back.start()
    w_back.start()
    half = 2 * tok
    for i in range(4):
        rows = slice(i * tok, (i + 1) * tok)
        block = hid[i]
        own_ref[rows, :] = dot(block, weights[:VW, :], NT)
        send_ref[rows, :VW] = dot(block, weights[VW : 2 * VW, :], NT)
        send_ref[rows, VW:] = dot(block, weights[2 * VW : MAIN, :], NT)
        low = 4 * tok + STEPS * (i * tok // half)
        send_ref[low : low + STEPS, i * tok % half : i * tok % half + tok] = dot(
            weights[MAIN:, :], block, NT
        )
    hid_back.wait()
    w_back.wait()


def offset(i):
    return i // 2 if i % 2 == 0 else -(i + 1) // 2


def state_kernel(
    own_ref, send_ref, recv_ref, g_ref, step_ref, rate_ref,
    x_ref, bc_ref, fresh_ref, seed_ref, last_ref, ends_ref,
):
    tokens = x_ref.shape[0]
    count = tokens // Q
    low, spread = consts()
    cum = exact(-step_ref[...] * rate_ref[...], low, NT)
    twice = jnp.concatenate(
        [jnp.concatenate([spread, jnp.zeros_like(spread)], axis=1),
         jnp.concatenate([jnp.zeros_like(spread), spread], axis=1)], axis=0)
    lane = iota((EACH, count), 1)
    ends = jnp.zeros((EACH, count), f32)
    for k in range(count):
        rows = slice(k * Q, (k + 1) * Q)
        x = (own_ref[rows, :] + recv_ref[rows, :VW]).astype(bf16)
        bc = (send_ref[rows, VW:] + recv_ref[rows, VW:]).astype(bf16)
        x_ref[rows, :] = x
        bc_ref[rows, :] = bc
        here = cum[k * EACH : (k + 1) * EACH]
        last = here[:, Q - 1 :]
        ends = ends + jnp.where(lane == k, last, 0.0)
        rest = jnp.exp(last - here) * step_ref[k * EACH : (k + 1) * EACH, :]
        both = widen(jnp.concatenate([rest, jnp.exp(here)], axis=0), twice)
        tail = (x.astype(f32) * both[:, :VW]).astype(bf16)
        grown = (g_ref[rows, :].astype(f32) * both[:, VW:]).astype(bf16)
        fresh_ref[k] = dot(tail, bc[:, :STATE], TN)
        seed_ref[k] = dot(grown, bc[:, STATE:], TN)
    lasts = dot(spread, jnp.exp(ends), TN, HI)
    last_ref[...] = lasts
    state = jnp.zeros((VW, STATE), f32)
    grad = jnp.zeros((VW, STATE), f32)
    for k in range(count):
        state = lasts[:, k : k + 1] * state + fresh_ref[k]
        back = count - 1 - k
        grad = lasts[:, back : back + 1] * grad + seed_ref[back]
    eye = (iota((EACH, STATE), 0) == iota((EACH, STATE), 1)).astype(f32)
    total = jnp.exp(jnp.sum(ends, axis=1, keepdims=True))
    pieces = split_decay(dot(jnp.broadcast_to(total, (EACH, STEPS)), eye, TN, HI)).astype(bf16)
    ends_ref[0, :VW] = state.astype(bf16)
    ends_ref[1, :VW] = grad.astype(bf16)
    ends_ref[0, VW:] = pieces
    ends_ref[1, VW:] = pieces


def split_decay(decay):
    high = decay.astype(bf16).astype(f32)
    mid = (decay - high).astype(bf16).astype(f32)
    least = decay - high - mid
    row = iota((STEPS, STATE), 0)
    return jnp.where(row == 0, high, jnp.where(row == 1, mid, jnp.where(row == 2, least, 0.0)))


def window_kernel(near_ref, far_ref, out_ref):
    spread = (iota((VW, STATE), 0) // HEAD_DIM == iota((VW, STATE), 1)).astype(bf16)
    for i in range(2):
        near = near_ref[i, VW:]
        column = jnp.sum(dot(spread, near, NT), axis=1, keepdims=True)
        out_ref[i, :VW] = (
            near_ref[i, :VW].astype(f32) + column * far_ref[i, :VW].astype(f32)
        ).astype(bf16)
        decay = jnp.sum(near.astype(f32), axis=0, keepdims=True) * jnp.sum(
            far_ref[i, VW:].astype(f32), axis=0, keepdims=True
        )
        out_ref[i, VW:] = split_decay(jnp.broadcast_to(decay, (STEPS, STATE))).astype(bf16)


def scan_kernel(
    x_ref, bc_ref, g_ref, step_ref, sig_ref, rate_ref, gain_ref,
    fresh_ref, seed_ref, last_ref, in_ref, later_ref,
    y_ref, back_ref, dstep_ref, held, grads,
):
    at = pl.program_id(0)
    count = fresh_ref.shape[0]

    @pl.when(at == 0)
    def _():
        lasts = last_ref[...]
        state = in_ref[...].astype(f32)
        grad = later_ref[...].astype(f32)
        for k in range(count):
            held[k] = state
            state = lasts[:, k : k + 1] * state + fresh_ref[k]
            back = count - 1 - k
            grads[back] = grad
            grad = lasts[:, back : back + 1] * grad + seed_ref[back]
        held[count] = state

    low, spread = consts()
    mask = low > 0.0
    zero = jnp.zeros_like(spread)
    twice = jnp.concatenate(
        [jnp.concatenate([spread, zero], axis=1), jnp.concatenate([zero, spread], axis=1)], axis=0)
    lane = iota((Q, EACH), 1)
    row = iota((EACH, Q), 0)
    gain_wide = gain_ref[...]
    for sub in range(step_ref.shape[0]):
        k = at * step_ref.shape[0] + sub
        rows = slice(sub * Q, (sub + 1) * Q)
        step_t = step_ref[sub]
        cum_t = exact(-step_t * rate_ref[...], low, NT)
        both_wide = widen(jnp.concatenate([cum_t, step_t], axis=0), twice)
        cum_wide, step_wide = both_wide[:, :VW], both_wide[:, VW:]
        growth = jnp.exp(cum_wide)
        rest = jnp.exp(cum_wide[Q - 1 :, :] - cum_wide)
        x, g = x_ref[rows, :], g_ref[rows, :]
        xf, gf = x.astype(f32), g.astype(f32)
        b_mat, c_mat = bc_ref[rows, :STATE], bc_ref[rows, STATE:]
        state, nxt, grad = held[k], held[k + 1], grads[k]
        state_b, grad_b = state.astype(bf16), grad.astype(bf16)

        scores = jnp.where(mask, dot(c_mat, b_mat, NT), 0.0)
        mixed, moved = [], []
        pairs = jnp.zeros((Q, Q), f32)
        out_sum = jnp.zeros((Q, EACH), f32)
        in_sum = jnp.zeros((EACH, Q), f32)
        for e in range(EACH):
            cut = slice(e * HEAD_DIM, (e + 1) * HEAD_DIM)
            first = slice(e * HEAD_DIM, e * HEAD_DIM + 1)
            fade = jnp.exp(jnp.minimum(cum_wide[:, first] - cum_t[e : e + 1, :], 0.0))
            weight = scores * fade
            step_row = step_t[e : e + 1, :]
            mixing = (weight * step_row).astype(bf16)
            mixed.append(dot(mixing, x[:, cut], NN))
            moved.append(dot(mixing, g[:, cut], TN))
            outer = dot(g[:, cut], x[:, cut], NT)
            pairs = pairs + outer * fade * step_row
            both = weight * outer
            in_sum = in_sum + jnp.where(row == e, jnp.sum(both, axis=0, keepdims=True), 0.0)
            out_sum = out_sum + jnp.where(
                lane == e, jnp.sum(both * step_row, axis=1, keepdims=True), 0.0
            )
        pairs = jnp.where(mask, pairs, 0.0).astype(bf16)

        from_state = growth * dot(c_mat, state_b, NT)
        from_later = rest * dot(b_mat, grad_b, NT)
        y_ref[rows, :] = (
            jnp.concatenate(mixed, axis=1) + from_state + gain_wide * xf
        ).astype(bf16)
        back_ref[rows, :VW] = (
            jnp.concatenate(moved, axis=1) + step_wide * from_later + gain_wide * gf
        ).astype(bf16)
        back_ref[rows, VW : VW + STATE] = (
            dot(pairs, c_mat, TN) + dot((xf * (rest * step_wide)).astype(bf16), grad_b, NN)
        ).astype(bf16)
        back_ref[rows, VW + STATE :] = (
            dot(pairs, b_mat, NN) + dot((gf * growth).astype(bf16), state_b, NN)
        ).astype(bf16)

        direct = in_sum + dot(spread.astype(bf16), (xf * from_later).astype(bf16), NT)
        out_t = dot(spread.astype(bf16), (gf * from_state).astype(bf16), NT)
        crossing = dot(spread, jnp.sum(grad * nxt, axis=1, keepdims=True), NN, HI)
        d_decay = (
            dot(out_sum, low, TN, HI) + exact(out_t - direct * step_t, low, NN) + crossing
        )
        d_step = (direct - rate_ref[...] * d_decay) * sig_ref[sub]
        dstep_ref[:, rows] = jnp.concatenate(
            [d_step, jnp.zeros((STEPS - EACH, Q), f32)], axis=0
        ).astype(bf16)


def both_bc(back_ref, pair_ref):
    return (back_ref[:, VW:].astype(f32) + pair_ref[:, VW:].astype(f32)).astype(bf16)


def term_kernel(at_ref, back_ref, pair_ref, steps_ref, hid_ref, *refs):
    outs, blocks, sems = refs[:-2], refs[-2], refs[-1]
    copies = []
    for i in range(len(outs)):
        lanes = pl.ds(pl.multiple_of(at_ref[i] * FEAT, FEAT), FEAT)
        copies.append(pltpu.make_async_copy(hid_ref.at[:, :, lanes], blocks.at[i], sems.at[i]))
        copies[-1].start()
    main = jnp.concatenate([back_ref[:, :VW], pair_ref[:, :VW], both_bc(back_ref, pair_ref)], axis=1)
    for i, out_ref in enumerate(outs):
        copies[i].wait()
        block = blocks[i].reshape(-1, FEAT)
        out_ref[:FEAT, :] = dot(block, main, TN).astype(bf16)
        out_ref[FEAT:, :FEAT] = dot(steps_ref[...], block, NN).astype(bf16)
        out_ref[FEAT:, FEAT:] = jnp.zeros((STEPS, MAIN - FEAT), bf16)


def input_kernel(back_ref, pair_ref, steps_ref, w_ref, a_ref, b_ref, bc, weights, sems):
    at = pl.program_id(0)

    def fetch(i):
        return pltpu.make_async_copy(
            w_ref.at[:, i * FEAT : (i + 1) * FEAT], weights.at[i], sems.at[i]
        )

    @pl.when(at == 0)
    def _():
        for i in range(NZ):
            fetch(i).start()
        bc[...] = both_bc(back_ref, pair_ref)

    for i in range(NZ):

        @pl.when(at == i)
        def _():
            fetch(i).wait()

    size = a_ref.shape[3]
    for i in range(4):
        rows = slice(i * size, (i + 1) * size)
        total = (
            dot(back_ref[rows, :VW], weights[at, :VW, :], NN)
            + dot(pair_ref[rows, :VW], weights[at, VW : 2 * VW, :], NN)
            + dot(bc[rows, :], weights[at, 2 * VW : MAIN, :], NN)
            + dot(steps_ref[:, rows], weights[at, MAIN:, :], TN)
        ).astype(bf16)
        if i % 2 == 0:
            a_ref[0, 0, i // 2] = total
        else:
            b_ref[i // 2, 0, 0] = total


def take_kernel(at_ref, table_ref, *refs):
    sums, out_ref, block, sem = refs[:-3], refs[-3], refs[-2], refs[-1]
    copy = pltpu.make_async_copy(table_ref.at[at_ref[0]], block, sem)
    copy.start()
    copy.wait()
    value = block[...]
    if sums:
        value = (value.astype(f32) + sums[0][...].astype(f32)).astype(bf16)
    out_ref[...] = value


def take(table, at, *sums):
    shape = table.shape[1:]
    return pl.pallas_call(
        take_kernel,
        in_specs=[pl.BlockSpec(memory_space=pltpu.SMEM), pl.BlockSpec(memory_space=pltpu.HBM)]
        + [pl.BlockSpec(memory_space=pltpu.VMEM)] * len(sums),
        out_shape=jax.ShapeDtypeStruct(shape, bf16),
        scratch_shapes=[pltpu.VMEM(shape, bf16), pltpu.SemaphoreType.DMA],
        compiler_params=vmem(4),
        cost_estimate=TINY,
        name="take",
    )(at[None].astype(jnp.int32), table, *sums)


def add_kernel(left_ref, right_ref, out_ref):
    out_ref[...] = (left_ref[...].astype(f32) + right_ref[...].astype(f32)).astype(bf16)


def added(left, right):
    return pl.pallas_call(
        add_kernel,
        out_shape=jax.ShapeDtypeStruct(left.shape, bf16),
        compiler_params=vmem(3),
        cost_estimate=TINY,
        name="add",
    )(left, right)


def cores_kernel(at_ref, own_ref, pair_ref, out_ref):
    c = at_ref[0]
    for i in range(2):
        part = slice(i * 128, (i + 1) * 128)
        out_ref[:, pl.ds(pl.multiple_of((2 * i + c) * 128, 128), 128)] = own_ref[:, part]
        out_ref[:, pl.ds(pl.multiple_of((2 * i + 1 - c) * 128, 128), 128)] = pair_ref[:, part]


def heads_kernel(at_ref, own_ref, pair_ref, cross_ref, out_ref):
    yh, c = at_ref[0], at_ref[1]

    def to(first, second, value):
        lanes = pl.ds(pl.multiple_of((first * 2 + second) * VW, VW), VW)
        out_ref[:, lanes] = value

    to(yh, c, own_ref[c])
    to(1 - yh, c, pair_ref[c])
    to(yh, 1 - c, cross_ref[0])
    to(1 - yh, 1 - c, cross_ref[1])


def pick(value, at, dim):
    return lax.dynamic_index_in_dim(value, at, dim, False)


def tie(*values):
    return lax.optimization_barrier(values)


TINY = pl.CostEstimate(flops=1024, bytes_accessed=1024, transcendentals=0)


def local(hidden, value_proj, state_proj, step_proj, step_bias, decay_rate, skip_gain, out_grad):
    z, yh, c, x, yl = (lax.axis_index(a) for a in ("z", "yh", "c", "x", "yl"))
    y = yh * 2 + yl
    way = 1 - 2 * c
    tok = hidden.shape[0]
    tokens = 4 * tok
    blocks = tokens // Q

    parts = hidden.reshape(tok, 2, 2, 128)
    keep = pick(parts, c, 2).reshape(tok, FEAT)
    got = swap(pick(parts, 1 - c, 2).reshape(tok, FEAT))
    first = jnp.where(c == 0, keep, got)
    second = jnp.where(c == 0, got, keep)

    value_proj, state_proj, step_proj, first, second = tie(
        value_proj, state_proj, step_proj, first, second
    )
    value_t, state_t, step_tr = value_proj.T, state_proj.T, step_proj.T
    none = jnp.zeros((EACH, value_proj.shape[0]), bf16)

    def chosen(which):
        def some(array, wide, core):
            return lax.dynamic_slice_in_dim(array, (which * 2 + core) * wide, wide, 0)

        return jnp.concatenate(
            [
                some(value_t, VW, c), some(value_t, VW, 1 - c), state_t,
                some(step_tr, EACH, c), none, some(step_tr, EACH, 1 - c), none,
            ],
            axis=0,
        )

    mine, theirs = chosen(yh), shift(chosen(1 - yh), "yh", 1, 2)
    chunk = jnp.where(
        yh == 0,
        jnp.concatenate([mine, theirs], axis=1),
        jnp.concatenate([theirs, mine], axis=1),
    )
    def pairwise(own, pair, place, dim):
        return jnp.where(
            place == 0, jnp.stack([own, pair], dim), jnp.stack([pair, own], dim)
        )

    out_grad, chunk = tie(out_grad, chunk)
    cot = out_grad.reshape(tok, 2, 2, VW)
    cot = pairwise(pick(cot, c, 2), swap(pick(cot, 1 - c, 2)), c, 0)

    brought = lax.all_gather(chunk[:SPLIT], "z")
    ring = chunk[SPLIT:]
    weights = [ring, shift(ring, "z", 1, NZ), shift(ring, "z", -1, NZ)]
    a_blocks, b_blocks = [first], [second]
    for hop in range(1, 4):
        a_blocks.append(both_y(a_blocks[-1]))
        b_blocks.append(both_x(b_blocks[-1]))
    a_blocks, b_blocks = [jnp.stack(a_blocks)], [jnp.stack(b_blocks)]
    weights[1], weights[2], a_blocks[0], b_blocks[0], cot = tie(
        weights[1], weights[2], a_blocks[0], b_blocks[0], cot
    )
    cot = pairwise(pick(cot, yh, 2), shift(pick(cot, 1 - yh, 2), "yh", 1, 2), yh, 0)
    cot = cot.reshape(tokens, VW)
    for hop in range(1, 4):
        weights.append(shift(weights[-2], "z", 1, NZ))
        if hop < 3:
            weights.append(shift(weights[-2], "z", -1, NZ))
        a_blocks.append(both_x(a_blocks[-1]))
        b_blocks.append(both_y(b_blocks[-1]))
        if hop < 3:
            weights[-1], weights[-2], a_blocks[-1], b_blocks[-1] = tie(
                weights[-1], weights[-2], a_blocks[-1], b_blocks[-1]
            )
        if hop == 2:
            a_blocks[-1], b_blocks[-1], cot = tie(a_blocks[-1], b_blocks[-1], cot)

    def whole(*shape):
        return pl.BlockSpec(shape, lambda *k: (0,) * len(shape))

    def shaped(dtype, *shape):
        return jax.ShapeDtypeStruct(shape, dtype)

    places = jnp.stack([x, y, z, way]).astype(jnp.int32)
    wide = NZ * FEAT
    in_hbm = pl.BlockSpec(memory_space=pltpu.HBM)
    in_vmem = pl.BlockSpec(memory_space=pltpu.VMEM)
    in_smem = pl.BlockSpec(memory_space=pltpu.SMEM)
    hid, whole_w, p_own, p_send = pl.pallas_call(
        project_kernel,
        in_specs=[in_smem] + [in_hbm] * (NX + NY + NZ + 1),
        out_specs=[in_hbm, in_hbm, in_vmem, in_vmem],
        out_shape=[
            shaped(bf16, 4, tok, wide), shaped(bf16, COLS, wide),
            shaped(f32, tokens, VW), shaped(f32, tokens + 2 * STEPS, VW + BC),
        ],
        scratch_shapes=[
            pltpu.VMEM((4, tok, wide), bf16), pltpu.VMEM((COLS, wide), bf16),
            pltpu.SemaphoreType.DMA((2 * NX * NY + 2 * NZ + 2,)),
        ],
        compiler_params=ALL,
        name="project",
    )(places, *a_blocks, *b_blocks, *weights, brought)
    p_recv = swap(p_send)

    def step_rows(packed):
        packed = packed[tokens:]
        return jnp.concatenate([packed[:STEPS], packed[STEPS:]], axis=1)

    place = (yh * 2 + c) * EACH
    bias, rate, gain = (
        lax.dynamic_slice_in_dim(v, place, EACH, 0)[:, None]
        for v in (step_bias, decay_rate, skip_gain)
    )
    pre_step = (
        step_rows(p_send)[:EACH] + step_rows(p_recv)[STEPS // 2 : STEPS // 2 + EACH] + bias
    )
    pre_step = pre_step.reshape(EACH, blocks, Q).transpose(1, 0, 2)
    step = jax.nn.softplus(pre_step)
    sig = jax.nn.sigmoid(pre_step)

    states = shaped(f32, blocks, VW, STATE)
    values, bc, fresh, seeds, lasts, ends = pl.pallas_call(
        state_kernel,
        out_shape=[
            shaped(bf16, tokens, VW), shaped(bf16, tokens, BC), states, states,
            shaped(f32, VW, blocks), shaped(bf16, 2, VW + STEPS, STATE),
        ],
        compiler_params=vmem(16),
        name="states",
    )(p_own, p_send, p_recv, cot, step.reshape(blocks * EACH, Q), jnp.tile(rate, (blocks, 1)))

    def along(packed, by):
        pairs = [
            (i * 2 + core, (i + by * (1 - 2 * core)) * 2 + core)
            for i in range(NZ)
            for core in range(2)
            if 0 <= i + by * (1 - 2 * core) < NZ
        ]
        return lax.ppermute(packed, ("z", "c"), pairs)

    def joined(near, far):
        return pl.pallas_call(
            window_kernel,
            out_shape=shaped(bf16, 2, VW + STEPS, STATE),
            compiler_params=vmem(2),
            cost_estimate=TINY,
            name="window",
        )(near, far)

    start = jnp.stack([pick(ends, c, 0), swap(pick(ends, 1 - c, 0))])
    window = joined(along(start, 1), along(start, 2))
    for by in (2, 4):
        window = joined(window, along(window, by))
    kept, given = window[0, :VW], window[1, :VW]
    other_way = swap(given)
    state_in = jnp.where(c == 0, kept, other_way)
    later = jnp.where(c == 0, other_way, kept)

    each = 2

    def rows(width):
        return pl.BlockSpec((each * Q, width), lambda k: (k, 0))

    lanes = pl.BlockSpec((each, EACH, Q), lambda k: (k, 0, 0))
    mixed, back, steps = pl.pallas_call(
        scan_kernel,
        grid=(blocks // each,),
        in_specs=[
            rows(VW), rows(BC), rows(VW), lanes, lanes, whole(EACH, 1), whole(1, VW),
            whole(blocks, VW, STATE), whole(blocks, VW, STATE), whole(VW, blocks),
            whole(VW, STATE), whole(VW, STATE),
        ],
        out_specs=[
            rows(VW), rows(VW + BC), pl.BlockSpec((STEPS, each * Q), lambda k: (0, k)),
        ],
        out_shape=[
            shaped(bf16, tokens, VW), shaped(bf16, tokens, VW + BC), shaped(bf16, STEPS, tokens),
        ],
        scratch_shapes=[
            pltpu.VMEM((blocks + 1, VW, STATE), f32), pltpu.VMEM((blocks, VW, STATE), f32),
        ],
        compiler_params=vmem(16),
        name="scan",
    )(
        values, bc, cot, step, sig, rate, jnp.repeat(gain, HEAD_DIM, axis=0).T,
        fresh, seeds, lasts, state_in, later,
    )

    back_pair, steps_pair = swap(back), swap(steps)
    steps = jnp.concatenate([steps[: STEPS // 2], steps_pair[: STEPS // 2]], axis=0)

    def terms(*offsets):
        count = len(offsets)
        at = jnp.stack([(z + i) % NZ for i in offsets]).astype(jnp.int32)
        return pl.pallas_call(
            term_kernel,
            in_specs=[in_smem, in_vmem, in_vmem, in_vmem, in_hbm],
            out_shape=[shaped(bf16, FEAT + STEPS, MAIN)] * count,
            scratch_shapes=[
                pltpu.VMEM((count, 4, tok, FEAT), bf16), pltpu.SemaphoreType.DMA((count,)),
            ],
            compiler_params=ALL,
            cost_estimate=TINY,
            name="term",
        )(at, back, back_pair, steps, hid)

    def more(sums, *parts):
        total = sums.astype(f32)
        for part in parts:
            total = total + part.astype(f32)
        return total

    up, down, add_3, add_2, add_1, add_0, add_6, add_7 = terms(4, 5, 3, 2, 1, 0, 6, 7)
    up, down, late_back = tie(up, down, back)

    a_part, b_part = pl.pallas_call(
        input_kernel,
        grid=(NZ,),
        in_specs=[
            whole(tokens, VW + BC), whole(tokens, VW + BC), whole(STEPS, tokens), in_hbm,
        ],
        out_specs=[
            pl.BlockSpec((1, 1, 2, tok, FEAT), lambda k: (k // 2, k % 2, 0, 0, 0)),
            pl.BlockSpec((2, 1, 1, tok, FEAT), lambda k: (0, k % 2, k // 2, 0, 0)),
        ],
        out_shape=[shaped(bf16, NX, 2, 2, tok, FEAT), shaped(bf16, 2, 2, NX, tok, FEAT)],
        scratch_shapes=[
            pltpu.VMEM((tokens, BC), bf16), pltpu.VMEM((NZ, COLS, FEAT), bf16),
            pltpu.SemaphoreType.DMA((NZ,)),
        ],
        compiler_params=ALL,
        cost_estimate=TINY,
        name="input",
    )(late_back, back_pair, steps, whole_w)
    a_part = a_part.reshape(NX, NY, tok, FEAT)
    b_part = b_part.reshape(NY, NX, tok, FEAT)

    def x_at(hop):
        return (x - way * hop) % NX

    def y_at(hop):
        return (y - way * hop) % NY

    def y_turned(hop):
        at = y_at(hop)
        return at % 2 * 2 + at // 2

    a_sum, b_sum = take(a_part, x_at(1)), take(b_part, y_at(1))
    for hop in range(1, 4):
        up = shift(up, "z", 1, NZ)
        down = shift(down, "z", -1, NZ)
        a_sum = take(a_part, x_at(hop + 1), both_x(a_sum))
        b_sum = take(b_part, y_at(hop + 1), both_y(b_sum))
        up = added(up, (add_3, add_2, add_1)[hop - 1])
        if hop < 3:
            down = added(down, (add_6, add_7)[hop - 1])
            up, down, a_sum, b_sum = tie(up, down, a_sum, b_sum)
    up = shift(up, "z", 1, NZ)
    a_all, b_all = a_sum, b_sum
    a_sum, b_sum = take(a_all, y_turned(1)), take(b_all, x_at(1))
    for hop in range(1, 4):
        a_sum = take(a_all, y_turned(hop + 1), both_y(a_sum))
        b_sum = take(b_all, x_at(hop + 1), both_x(b_sum))
    keep = jnp.where(c == 0, a_sum, b_sum)
    got = swap(jnp.where(c == 0, b_sum, a_sum))
    hidden_grad = pl.pallas_call(
        cores_kernel,
        in_specs=[in_smem, in_vmem, in_vmem],
        out_shape=shaped(bf16, tok, 2 * FEAT),
        compiler_params=vmem(3),
        cost_estimate=TINY,
        name="by_core",
    )(c[None].astype(jnp.int32), keep, got)

    mixed, back_pair = tie(mixed, back_pair)
    mixed = mixed.reshape(2, 2, tok, VW)
    own = pick(mixed, yh, 0)
    pair = shift(pick(mixed, 1 - yh, 0), "yh", 1, 2)
    crossed = swap(jnp.stack([pick(own, 1 - c, 0), pick(pair, 1 - c, 0)]))
    mixer_out = pl.pallas_call(
        heads_kernel,
        in_specs=[in_smem, in_vmem, in_vmem, in_vmem],
        out_shape=shaped(bf16, tok, 4 * VW),
        compiler_params=vmem(4),
        cost_estimate=TINY,
        name="by_head",
    )(jnp.stack([yh, c]).astype(jnp.int32), own, pair, crossed)

    summed = more(add_0, up, down)
    half = FEAT // 2
    main, step_part = summed[:FEAT].reshape(2, half, MAIN), summed[FEAT:, :FEAT]
    step_part = step_part.reshape(STEPS, 2, half)
    give = jnp.concatenate(
        [pick(main, 1 - yh, 0), jnp.pad(pick(step_part, 1 - yh, 1), ((0, 0), (0, MAIN - half)))],
        axis=0,
    )
    other = shift(give.astype(bf16), "yh", 1, 2).astype(f32)
    own, own_step = pick(main, yh, 0), pick(step_part, yh, 1)
    other_step = other[half:, :half]
    other = other[:half]
    state_grad = own[:, 2 * VW :] + other[:, 2 * VW :]

    def ordered(own, other, wide, gap):
        def cores(value):
            mine, pair = value[:, :wide], value[:, gap : gap + wide]
            return jnp.where(
                c == 0,
                jnp.concatenate([mine, pair], axis=1),
                jnp.concatenate([pair, mine], axis=1),
            )

        own, other = cores(own), cores(other)
        return jnp.where(
            yh == 0,
            jnp.concatenate([own, other], axis=1),
            jnp.concatenate([other, own], axis=1),
        )

    value_grad = ordered(own, other, VW, VW)
    step_grad = ordered(own_step.T, other_step.T, EACH, STEPS // 2)
    return mixer_out, hidden_grad, value_grad, state_grad, step_grad


def solution(mesh):
    fine = Mesh(mesh.devices.reshape(NZ, 2, 2, NX, 2), ("z", "yh", "c", "x", "yl"))
    split = P(("z", "yh", "c"), ("x", "yl"))
    by_head = P(("x", "yl"))
    return jax.shard_map(
        local,
        mesh=fine,
        in_specs=(split,) * 4 + (by_head,) * 3 + (split,),
        out_specs=(split,) * 5,
        check_vma=False,
    )
```

```python
import jax
import jax.numpy as jnp
from jax import lax
from jax.experimental import pallas as pl
from jax.experimental.pallas import tpu as pltpu
from jax.sharding import Mesh, PartitionSpec as P

HEAD_DIM = 64
STATE = 128
Q = 128
EACH = 4
VW = EACH * HEAD_DIM
BC = 2 * STATE
MAIN = 2 * VW + BC
STEPS = 16
COLS = MAIN + STEPS
FEAT = 256
NZ, NX, NY = 8, 4, 4
SPLIT = 0
f32, bf16 = jnp.float32, jnp.bfloat16
HI = lax.Precision.HIGHEST


def vmem(mebibytes):
    return pltpu.CompilerParams(vmem_limit_bytes=mebibytes * 1024 * 1024)


ALL = vmem(60)


def shift(value, axis, by, count, wrap=True):
    pairs = [(i, (i + by) % count) for i in range(count) if wrap or 0 <= i + by < count]
    return lax.ppermute(value, axis, pairs)


def both_x(value):
    pairs = [(c * NX + i, c * NX + (i + 1 - 2 * c) % NX) for c in range(2) for i in range(NX)]
    return lax.ppermute(value, ("c", "x"), pairs)


def both_y(value):
    def at(c, y):
        return (y // 2) * 4 + c * 2 + y % 2

    pairs = [(at(c, y), at(c, (y + 1 - 2 * c) % NY)) for c in range(2) for y in range(NY)]
    return lax.ppermute(value, ("yh", "c", "yl"), pairs)


def swap(value):
    return shift(value, "c", 1, 2)


def dot(left, right, dims, precision=None):
    return lax.dot_general(
        left, right, (dims, ((), ())), preferred_element_type=f32, precision=precision
    )


NN, NT, TN = ((1,), (0,)), ((1,), (1,)), ((0,), (0,))


def iota(shape, dim):
    return lax.broadcasted_iota(jnp.int32, shape, dim)


def consts():
    low = (iota((Q, Q), 0) >= iota((Q, Q), 1)).astype(f32)
    spread = (iota((EACH, VW), 1) // HEAD_DIM == iota((EACH, VW), 0)).astype(f32)
    return low, spread


def pieces(rows):
    high = rows.astype(bf16).astype(f32)
    mid = (rows - high).astype(bf16).astype(f32)
    return jnp.concatenate([high, mid, rows - high - mid], axis=0).astype(bf16)


def exact(rows, right, dims):
    n = rows.shape[0]
    out = dot(pieces(rows), right.astype(bf16), dims)
    return out[:n] + out[n : 2 * n] + out[2 * n :]


def widen(rows, right):
    right = right.astype(bf16)
    return dot(pieces(rows), jnp.concatenate([right] * 3, axis=0), TN)


def project_kernel(at_ref, *refs):
    x, y, z, way = (at_ref[i] for i in range(4))
    a_refs, b_refs, w_refs = refs[:NX], refs[NX : NX + NY], refs[NX + NY : NX + NY + NZ]
    hid_out, w_out, own_ref, send_ref, hid, weights, sems = refs[-7:]
    tok = hid.shape[1]
    copies = []

    def copy(source, target):
        copies.append(pltpu.make_async_copy(source, target, sems.at[len(copies)]))
        copies[-1].start()

    def place(source, x_at, y_at, core):
        x_at, y_at = x_at & (NX - 1), y_at & (NY - 1)
        lanes = pl.ds(pl.multiple_of((2 * x_at + (y_at & 1)) * FEAT, FEAT), FEAT)
        copy(source, hid.at[(y_at >> 1) * 2 + core, :, lanes])

    for j in range(NX):
        for i in range(NY):
            place(a_refs[j].at[i], x - way * j, y - i, 0)
            place(b_refs[i].at[j], x - j, y - way * i, 1)
    for i in range(NZ):
        z_at = (z + offset(i)) & (NZ - 1)
        lanes = pl.ds(pl.multiple_of(z_at * FEAT, FEAT), FEAT)
        copy(w_refs[i], weights.at[SPLIT:, lanes])
        if SPLIT:
            part_ref = refs[NX + NY + NZ]
            copy(part_ref.at[i], weights.at[:SPLIT, i * FEAT : (i + 1) * FEAT])
    for one in copies:
        one.wait()
    hid_back = pltpu.make_async_copy(hid, hid_out, sems.at[len(copies)])
    w_back = pltpu.make_async_copy(weights, w_out, sems.at[len(copies) + 1])
    hid_back.start()
    w_back.start()
    block = hid[...].reshape(4 * tok, NZ * FEAT)
    send_ref[: 4 * tok, VW:] = dot(block, weights[2 * VW : MAIN, :], NT)
    send_ref[: 4 * tok, :VW] = dot(block, weights[VW : 2 * VW, :], NT)
    steps = dot(weights[MAIN:, :], block, NT)
    send_ref[4 * tok : 4 * tok + STEPS, :] = steps[:, : 2 * tok]
    send_ref[4 * tok + STEPS :, :] = steps[:, 2 * tok :]
    own_ref[...] = dot(block, weights[:VW, :], NT)
    hid_back.wait()
    w_back.wait()


def offset(i):
    return i // 2 if i % 2 == 0 else -(i + 1) // 2


def state_kernel(
    own_ref, send_ref, recv_ref, g_ref, step_ref, rate_ref,
    x_ref, bc_ref, fresh_ref, seed_ref, last_ref, ends_ref,
):
    tokens = x_ref.shape[0]
    count = tokens // Q
    low, spread = consts()
    cum = exact(-step_ref[...] * rate_ref[...], low, NT)
    twice = jnp.concatenate(
        [jnp.concatenate([spread, jnp.zeros_like(spread)], axis=1),
         jnp.concatenate([jnp.zeros_like(spread), spread], axis=1)], axis=0)
    lane = iota((EACH, count), 1)
    ends = jnp.zeros((EACH, count), f32)
    for k in range(count):
        rows = slice(k * Q, (k + 1) * Q)
        x = (own_ref[rows, :] + recv_ref[rows, :VW]).astype(bf16)
        bc = (send_ref[rows, VW:] + recv_ref[rows, VW:]).astype(bf16)
        x_ref[rows, :] = x
        bc_ref[rows, :] = bc
        here = cum[k * EACH : (k + 1) * EACH]
        last = here[:, Q - 1 :]
        ends = ends + jnp.where(lane == k, last, 0.0)
        rest = jnp.exp(last - here) * step_ref[k * EACH : (k + 1) * EACH, :]
        both = widen(jnp.concatenate([rest, jnp.exp(here)], axis=0), twice)
        tail = (x.astype(f32) * both[:, :VW]).astype(bf16)
        grown = (g_ref[rows, :].astype(f32) * both[:, VW:]).astype(bf16)
        fresh_ref[k] = dot(tail, bc[:, :STATE], TN)
        seed_ref[k] = dot(grown, bc[:, STATE:], TN)
    lasts = dot(spread, jnp.exp(ends), TN, HI)
    last_ref[...] = lasts
    state = jnp.zeros((VW, STATE), f32)
    grad = jnp.zeros((VW, STATE), f32)
    for k in range(count):
        state = lasts[:, k : k + 1] * state + fresh_ref[k]
        back = count - 1 - k
        grad = lasts[:, back : back + 1] * grad + seed_ref[back]
    eye = (iota((EACH, STATE), 0) == iota((EACH, STATE), 1)).astype(f32)
    total = jnp.exp(jnp.sum(ends, axis=1, keepdims=True))
    pieces = split_decay(dot(jnp.broadcast_to(total, (EACH, STEPS)), eye, TN, HI)).astype(bf16)
    ends_ref[0, :VW] = state.astype(bf16)
    ends_ref[1, :VW] = grad.astype(bf16)
    ends_ref[0, VW:] = pieces
    ends_ref[1, VW:] = pieces


def split_decay(decay):
    high = decay.astype(bf16).astype(f32)
    mid = (decay - high).astype(bf16).astype(f32)
    least = decay - high - mid
    row = iota((STEPS, STATE), 0)
    return jnp.where(row == 0, high, jnp.where(row == 1, mid, jnp.where(row == 2, least, 0.0)))


def window_kernel(near_ref, far_ref, out_ref):
    spread = (iota((VW, STATE), 0) // HEAD_DIM == iota((VW, STATE), 1)).astype(bf16)
    for i in range(2):
        near = near_ref[i, VW:]
        column = jnp.sum(dot(spread, near, NT), axis=1, keepdims=True)
        out_ref[i, :VW] = (
            near_ref[i, :VW].astype(f32) + column * far_ref[i, :VW].astype(f32)
        ).astype(bf16)
        decay = jnp.sum(near.astype(f32), axis=0, keepdims=True) * jnp.sum(
            far_ref[i, VW:].astype(f32), axis=0, keepdims=True
        )
        out_ref[i, VW:] = split_decay(jnp.broadcast_to(decay, (STEPS, STATE))).astype(bf16)


def scan_kernel(
    x_ref, bc_ref, g_ref, step_ref, sig_ref, rate_ref, gain_ref,
    fresh_ref, seed_ref, last_ref, in_ref, later_ref,
    y_ref, back_ref, dstep_ref, held, grads,
):
    at = pl.program_id(0)
    count = fresh_ref.shape[0]

    @pl.when(at == 0)
    def _():
        lasts = last_ref[...]
        state = in_ref[...].astype(f32)
        grad = later_ref[...].astype(f32)
        for k in range(count):
            held[k] = state
            state = lasts[:, k : k + 1] * state + fresh_ref[k]
            back = count - 1 - k
            grads[back] = grad
            grad = lasts[:, back : back + 1] * grad + seed_ref[back]
        held[count] = state

    low, spread = consts()
    mask = low > 0.0
    zero = jnp.zeros_like(spread)
    twice = jnp.concatenate(
        [jnp.concatenate([spread, zero], axis=1), jnp.concatenate([zero, spread], axis=1)], axis=0)
    lane = iota((Q, EACH), 1)
    row = iota((EACH, Q), 0)
    gain_wide = gain_ref[...]
    for sub in range(step_ref.shape[0]):
        k = at * step_ref.shape[0] + sub
        rows = slice(sub * Q, (sub + 1) * Q)
        step_t = step_ref[sub]
        cum_t = exact(-step_t * rate_ref[...], low, NT)
        both_wide = widen(jnp.concatenate([cum_t, step_t], axis=0), twice)
        cum_wide, step_wide = both_wide[:, :VW], both_wide[:, VW:]
        growth = jnp.exp(cum_wide)
        rest = jnp.exp(cum_wide[Q - 1 :, :] - cum_wide)
        x, g = x_ref[rows, :], g_ref[rows, :]
        xf, gf = x.astype(f32), g.astype(f32)
        b_mat, c_mat = bc_ref[rows, :STATE], bc_ref[rows, STATE:]
        state, nxt, grad = held[k], held[k + 1], grads[k]
        state_b, grad_b = state.astype(bf16), grad.astype(bf16)

        scores = jnp.where(mask, dot(c_mat, b_mat, NT), 0.0)
        mixed, moved = [], []
        pairs = jnp.zeros((Q, Q), f32)
        out_sum = jnp.zeros((Q, EACH), f32)
        in_sum = jnp.zeros((EACH, Q), f32)
        for e in range(EACH):
            cut = slice(e * HEAD_DIM, (e + 1) * HEAD_DIM)
            first = slice(e * HEAD_DIM, e * HEAD_DIM + 1)
            fade = jnp.exp(jnp.minimum(cum_wide[:, first] - cum_t[e : e + 1, :], 0.0))
            weight = scores * fade
            step_row = step_t[e : e + 1, :]
            mixing = (weight * step_row).astype(bf16)
            mixed.append(dot(mixing, x[:, cut], NN))
            moved.append(dot(mixing, g[:, cut], TN))
            outer = dot(g[:, cut], x[:, cut], NT)
            pairs = pairs + outer * fade * step_row
            both = weight * outer
            in_sum = in_sum + jnp.where(row == e, jnp.sum(both, axis=0, keepdims=True), 0.0)
            out_sum = out_sum + jnp.where(
                lane == e, jnp.sum(both * step_row, axis=1, keepdims=True), 0.0
            )
        pairs = jnp.where(mask, pairs, 0.0).astype(bf16)

        from_state = growth * dot(c_mat, state_b, NT)
        from_later = rest * dot(b_mat, grad_b, NT)
        y_ref[rows, :] = (
            jnp.concatenate(mixed, axis=1) + from_state + gain_wide * xf
        ).astype(bf16)
        back_ref[rows, :VW] = (
            jnp.concatenate(moved, axis=1) + step_wide * from_later + gain_wide * gf
        ).astype(bf16)
        back_ref[rows, VW : VW + STATE] = (
            dot(pairs, c_mat, TN) + dot((xf * (rest * step_wide)).astype(bf16), grad_b, NN)
        ).astype(bf16)
        back_ref[rows, VW + STATE :] = (
            dot(pairs, b_mat, NN) + dot((gf * growth).astype(bf16), state_b, NN)
        ).astype(bf16)

        direct = in_sum + dot(spread.astype(bf16), (xf * from_later).astype(bf16), NT)
        out_t = dot(spread.astype(bf16), (gf * from_state).astype(bf16), NT)
        crossing = dot(spread, jnp.sum(grad * nxt, axis=1, keepdims=True), NN, HI)
        d_decay = (
            dot(out_sum, low, TN, HI) + exact(out_t - direct * step_t, low, NN) + crossing
        )
        d_step = (direct - rate_ref[...] * d_decay) * sig_ref[sub]
        dstep_ref[:, rows] = jnp.concatenate(
            [d_step, jnp.zeros((STEPS - EACH, Q), f32)], axis=0
        ).astype(bf16)


def both_bc(back_ref, pair_ref):
    return (back_ref[:, VW:].astype(f32) + pair_ref[:, VW:].astype(f32)).astype(bf16)


def term_kernel(at_ref, back_ref, pair_ref, steps_ref, hid_ref, main_ref, *refs):
    outs, blocks, sems = refs[:-2], refs[-2], refs[-1]
    copies = []
    for i in range(len(outs)):
        lanes = pl.ds(pl.multiple_of(at_ref[i] * FEAT, FEAT), FEAT)
        copies.append(pltpu.make_async_copy(hid_ref.at[:, :, lanes], blocks.at[i], sems.at[i]))
        copies[-1].start()
    bc = (back_ref[:, VW:].astype(f32) + pair_ref[:, VW:].astype(f32)).astype(bf16)
    main = jnp.concatenate([back_ref[:, :VW], pair_ref[:, :VW], bc], axis=1)
    eye = (iota((STEPS, STATE), 0) == iota((STEPS, STATE), 1)).astype(bf16)
    main_ref[:, :MAIN] = main
    main_ref[:, MAIN:] = dot(steps_ref[...], eye, TN).astype(bf16)
    for i, out_ref in enumerate(outs):
        copies[i].wait()
        block = blocks[i].reshape(-1, FEAT)
        out_ref[:FEAT, :] = dot(block, main, TN).astype(bf16)
        out_ref[FEAT:, :FEAT] = dot(steps_ref[...], block, NN).astype(bf16)
        out_ref[FEAT:, FEAT:] = jnp.zeros((STEPS, MAIN - FEAT), bf16)


def input_kernel(
    at_ref, main_ref, w_ref, a_ref, b_ref, a_first_ref, b_first_ref, weights, sems
):
    k = pl.program_id(0)
    x_first, y_first = at_ref[0], at_ref[1]

    def fetch(i):
        return pltpu.make_async_copy(
            w_ref.at[:, i * FEAT : (i + 1) * FEAT], weights.at[i, :COLS], sems.at[i]
        )

    @pl.when(k == 0)
    def _():
        for i in range(NZ):
            fetch(i).start()
            weights[i, COLS:] = jnp.zeros((MAIN + STATE - COLS, FEAT), bf16)

    for i in range(NZ):

        @pl.when(k == i)
        def _():
            fetch(i).wait()

    size = a_ref.shape[3]
    total = dot(main_ref[...], weights[k], NN).astype(bf16).reshape(2, 2, size, FEAT)
    x_at, yl_at = k // 2, k % 2
    a_ref[0, 0] = total[:, 0]
    b_ref[:, 0, 0] = total[:, 1]

    @pl.when(x_at == x_first)
    def _():
        a_first_ref[yl_at] = total[:, 0]

    for i in range(2):

        @pl.when(y_first == 2 * i + yl_at)
        def _():
            b_first_ref[x_at] = total[i, 1]


def hop_kernel(final, at_ref, *refs):
    count = 3 if final else 4
    x_at, y_at, x, y = (at_ref[i] for i in range(4))
    ins, outs = refs[: 2 * count], refs[2 * count : -2 * count - 1]
    held, sems = refs[-2 * count - 1 : -1], refs[-1]
    copies = []
    for i in range(2 * count):
        source = ins[i]
        if i == 1:
            source = source.at[x_at]
        if i == 3:
            source = source.at[y_at]
        copies.append(pltpu.make_async_copy(source, held[i], sems.at[i]))
        copies[-1].start()
    for i in range(count):
        copies[2 * i].wait()
        copies[2 * i + 1].wait()
        value = (held[2 * i][...].astype(f32) + held[2 * i + 1][...].astype(f32)).astype(bf16)
        if i >= 2 or not final:
            outs[i - 2 if final else i][...] = value
        else:
            held[2 * i][...] = value
    if final:
        for i in range(NY):
            at = (y + i) & (NY - 1)
            outs[1 + i][...] = held[0][(at & 1) * 2 + (at >> 1)]
            outs[1 + NY + i][...] = held[2][(x + i) & (NX - 1)]


def close_kernel(at_ref, *refs):
    a_refs, b_refs, keep_ref, give_ref = refs[:NY], refs[NY : NY + NX], refs[-2], refs[-1]
    sums = []
    for parts in (a_refs, b_refs):
        total = parts[0][...].astype(f32)
        for part in parts[1:]:
            total = total + part[...].astype(f32)
        sums.append(total)
    mine = at_ref[0] == 0
    keep_ref[...] = jnp.where(mine, sums[0], sums[1]).astype(bf16)
    give_ref[...] = jnp.where(mine, sums[1], sums[0]).astype(bf16)


def cores_kernel(at_ref, own_ref, pair_ref, out_ref):
    c = at_ref[0]
    for i in range(2):
        part = slice(i * 128, (i + 1) * 128)
        out_ref[:, pl.ds(pl.multiple_of((2 * i + c) * 128, 128), 128)] = own_ref[:, part]
        out_ref[:, pl.ds(pl.multiple_of((2 * i + 1 - c) * 128, 128), 128)] = pair_ref[:, part]


def heads_kernel(at_ref, own_ref, pair_ref, cross_ref, out_ref):
    yh, c = at_ref[0], at_ref[1]

    def to(first, second, value):
        lanes = pl.ds(pl.multiple_of((first * 2 + second) * VW, VW), VW)
        out_ref[:, lanes] = value

    to(yh, c, own_ref[c])
    to(1 - yh, c, pair_ref[c])
    to(yh, 1 - c, cross_ref[0])
    to(1 - yh, 1 - c, cross_ref[1])


def pick(value, at, dim):
    return lax.dynamic_index_in_dim(value, at, dim, False)


def tie(*values):
    return lax.optimization_barrier(values)


TINY = pl.CostEstimate(flops=1024, bytes_accessed=1024, transcendentals=0)


def local(hidden, value_proj, state_proj, step_proj, step_bias, decay_rate, skip_gain, out_grad):
    z, yh, c, x, yl = (lax.axis_index(a) for a in ("z", "yh", "c", "x", "yl"))
    y = yh * 2 + yl
    way = 1 - 2 * c
    tok = hidden.shape[0]
    tokens = 4 * tok
    blocks = tokens // Q

    parts = hidden.reshape(tok, 2, 2, 128)
    keep = pick(parts, c, 2).reshape(tok, FEAT)
    got = swap(pick(parts, 1 - c, 2).reshape(tok, FEAT))
    first = jnp.where(c == 0, keep, got)
    second = jnp.where(c == 0, got, keep)

    value_proj, state_proj, step_proj, first, second = tie(
        value_proj, state_proj, step_proj, first, second
    )
    value_t, state_t, step_tr = value_proj.T, state_proj.T, step_proj.T
    none = jnp.zeros((EACH, value_proj.shape[0]), bf16)

    def chosen(which):
        def some(array, wide, core):
            return lax.dynamic_slice_in_dim(array, (which * 2 + core) * wide, wide, 0)

        return jnp.concatenate(
            [
                some(value_t, VW, c), some(value_t, VW, 1 - c), state_t,
                some(step_tr, EACH, c), none, some(step_tr, EACH, 1 - c), none,
            ],
            axis=0,
        )

    mine, theirs = chosen(yh), shift(chosen(1 - yh), "yh", 1, 2)
    chunk = jnp.where(
        yh == 0,
        jnp.concatenate([mine, theirs], axis=1),
        jnp.concatenate([theirs, mine], axis=1),
    )
    def pairwise(own, pair, place, dim):
        return jnp.where(
            place == 0, jnp.stack([own, pair], dim), jnp.stack([pair, own], dim)
        )

    out_grad, chunk = tie(out_grad, chunk)
    cot = out_grad.reshape(tok, 2, 2, VW)
    cot = pairwise(pick(cot, c, 2), swap(pick(cot, 1 - c, 2)), c, 0)

    brought = [lax.all_gather(chunk[:SPLIT], "z")] if SPLIT else []
    ring = chunk[SPLIT:]
    weights = [ring, shift(ring, "z", 1, NZ), shift(ring, "z", -1, NZ)]
    a_blocks = [jnp.stack([first] + [shift(first, ("yh", "yl"), i, NY) for i in range(1, NY)])]
    b_blocks = [jnp.stack([second] + [shift(second, "x", i, NX) for i in range(1, NX)])]
    weights[1], weights[2], a_blocks[0], b_blocks[0], cot = tie(
        weights[1], weights[2], a_blocks[0], b_blocks[0], cot
    )
    cot = pairwise(pick(cot, yh, 2), shift(pick(cot, 1 - yh, 2), "yh", 1, 2), yh, 0)
    cot = cot.reshape(tokens, VW)
    for hop in range(1, 4):
        weights.append(shift(weights[-2], "z", 1, NZ))
        if hop < 3:
            weights.append(shift(weights[-2], "z", -1, NZ))
        a_blocks.append(both_x(a_blocks[-1]))
        b_blocks.append(both_y(b_blocks[-1]))
        if hop < 3:
            weights[-1], weights[-2], a_blocks[-1], b_blocks[-1] = tie(
                weights[-1], weights[-2], a_blocks[-1], b_blocks[-1]
            )

    def whole(*shape):
        return pl.BlockSpec(shape, lambda *k: (0,) * len(shape))

    def shaped(dtype, *shape):
        return jax.ShapeDtypeStruct(shape, dtype)

    places = jnp.stack([x, y, z, way]).astype(jnp.int32)
    wide = NZ * FEAT
    in_hbm = pl.BlockSpec(memory_space=pltpu.HBM)
    in_vmem = pl.BlockSpec(memory_space=pltpu.VMEM)
    in_smem = pl.BlockSpec(memory_space=pltpu.SMEM)
    hid, whole_w, p_own, p_send = pl.pallas_call(
        project_kernel,
        in_specs=[in_smem] + [in_hbm] * (NX + NY + NZ + len(brought)),
        out_specs=[in_hbm, in_hbm, in_vmem, in_vmem],
        out_shape=[
            shaped(bf16, 4, tok, wide), shaped(bf16, COLS, wide),
            shaped(f32, tokens, VW), shaped(f32, tokens + 2 * STEPS, VW + BC),
        ],
        scratch_shapes=[
            pltpu.VMEM((4, tok, wide), bf16), pltpu.VMEM((COLS, wide), bf16),
            pltpu.SemaphoreType.DMA((2 * NX * NY + 2 * NZ + 2,)),
        ],
        compiler_params=ALL,
        cost_estimate=pl.CostEstimate(
            flops=10 * 2**30, bytes_accessed=32 * 2**20, transcendentals=0
        ),
        name="project",
    )(places, *a_blocks, *b_blocks, *weights, *brought)
    p_send, cot = tie(p_send, cot)
    p_recv = swap(p_send)

    def step_rows(packed):
        packed = packed[tokens:]
        return jnp.concatenate([packed[:STEPS], packed[STEPS:]], axis=1)

    place = (yh * 2 + c) * EACH
    bias, rate, gain = (
        lax.dynamic_slice_in_dim(v, place, EACH, 0)[:, None]
        for v in (step_bias, decay_rate, skip_gain)
    )
    pre_step = (
        step_rows(p_send)[:EACH] + step_rows(p_recv)[STEPS // 2 : STEPS // 2 + EACH] + bias
    )
    pre_step = pre_step.reshape(EACH, blocks, Q).transpose(1, 0, 2)
    step = jax.nn.softplus(pre_step)
    sig = jax.nn.sigmoid(pre_step)

    states = shaped(f32, blocks, VW, STATE)
    values, bc, fresh, seeds, lasts, ends = pl.pallas_call(
        state_kernel,
        out_shape=[
            shaped(bf16, tokens, VW), shaped(bf16, tokens, BC), states, states,
            shaped(f32, VW, blocks), shaped(bf16, 2, VW + STEPS, STATE),
        ],
        compiler_params=ALL,
        name="states",
    )(p_own, p_send, p_recv, cot, step.reshape(blocks * EACH, Q), jnp.tile(rate, (blocks, 1)))

    def along(packed, by):
        pairs = [
            (i * 2 + core, (i + by * (1 - 2 * core)) * 2 + core)
            for i in range(NZ)
            for core in range(2)
            if 0 <= i + by * (1 - 2 * core) < NZ
        ]
        return lax.ppermute(packed, ("z", "c"), pairs)

    def joined(near, far):
        return pl.pallas_call(
            window_kernel,
            out_shape=shaped(bf16, 2, VW + STEPS, STATE),
            compiler_params=vmem(2),
            cost_estimate=TINY,
            name="window",
        )(near, far)

    start = jnp.stack([pick(ends, c, 0), swap(pick(ends, 1 - c, 0))])
    window = joined(along(start, 1), along(start, 2))
    for by in (2, 4):
        window = joined(window, along(window, by))
    kept, given = window[0, :VW], window[1, :VW]
    other_way = swap(given)
    state_in = jnp.where(c == 0, kept, other_way)
    later = jnp.where(c == 0, other_way, kept)

    each = 2

    def rows(width):
        return pl.BlockSpec((each * Q, width), lambda k: (k, 0))

    lanes = pl.BlockSpec((each, EACH, Q), lambda k: (k, 0, 0))
    mixed, back, steps = pl.pallas_call(
        scan_kernel,
        grid=(blocks // each,),
        in_specs=[
            rows(VW), rows(BC), rows(VW), lanes, lanes, whole(EACH, 1), whole(1, VW),
            whole(blocks, VW, STATE), whole(blocks, VW, STATE), whole(VW, blocks),
            whole(VW, STATE), whole(VW, STATE),
        ],
        out_specs=[
            rows(VW), rows(VW + BC), pl.BlockSpec((STEPS, each * Q), lambda k: (0, k)),
        ],
        out_shape=[
            shaped(bf16, tokens, VW), shaped(bf16, tokens, VW + BC), shaped(bf16, STEPS, tokens),
        ],
        scratch_shapes=[
            pltpu.VMEM((blocks + 1, VW, STATE), f32), pltpu.VMEM((blocks, VW, STATE), f32),
        ],
        compiler_params=ALL,
        name="scan",
    )(
        values, bc, cot, step, sig, rate, jnp.repeat(gain, HEAD_DIM, axis=0).T,
        fresh, seeds, lasts, state_in, later,
    )

    back_pair, steps_pair = swap(back), swap(steps)
    steps = jnp.concatenate([steps[: STEPS // 2], steps_pair[: STEPS // 2]], axis=0)

    order = (4, 5, 3, 2, 1, 0, 6, 7)
    main, up, down, *adds = pl.pallas_call(
        term_kernel,
        in_specs=[in_smem, in_vmem, in_vmem, in_vmem, in_hbm],
        out_shape=[shaped(bf16, tokens, MAIN + STATE)]
        + [shaped(bf16, FEAT + STEPS, MAIN)] * NZ,
        scratch_shapes=[
            pltpu.VMEM((NZ, 4, tok, FEAT), bf16), pltpu.SemaphoreType.DMA((NZ,)),
        ],
        compiler_params=ALL,
        cost_estimate=TINY,
        name="term",
    )(jnp.stack([(z + i) % NZ for i in order]).astype(jnp.int32), back, back_pair, steps, hid)
    add_3, add_2, add_1, add_0, add_6, add_7 = adds

    def more(sums, *parts):
        total = sums.astype(f32)
        for part in parts:
            total = total + part.astype(f32)
        return total

    def x_at(hop):
        return (x - way * hop) % NX

    def y_at(hop):
        return (y - way * hop) % NY

    a_part, b_part, a_sum, b_sum = pl.pallas_call(
        input_kernel,
        grid=(NZ,),
        in_specs=[in_smem, whole(tokens, MAIN + STATE), in_hbm],
        out_specs=[
            pl.BlockSpec((1, 1, 2, tok, FEAT), lambda k: (k // 2, k % 2, 0, 0, 0)),
            pl.BlockSpec((2, 1, 1, tok, FEAT), lambda k: (0, k % 2, k // 2, 0, 0)),
            whole(2, 2, tok, FEAT), whole(NX, tok, FEAT),
        ],
        out_shape=[
            shaped(bf16, NX, 2, 2, tok, FEAT), shaped(bf16, 2, 2, NX, tok, FEAT),
            shaped(bf16, 2, 2, tok, FEAT), shaped(bf16, NX, tok, FEAT),
        ],
        scratch_shapes=[
            pltpu.VMEM((NZ, MAIN + STATE, FEAT), bf16), pltpu.SemaphoreType.DMA((NZ,)),
        ],
        compiler_params=ALL,
        cost_estimate=TINY,
        name="input",
    )(jnp.stack([x_at(1), y_at(1)]).astype(jnp.int32), main, whole_w)
    a_part = a_part.reshape(NX, NY, tok, FEAT)
    b_part = b_part.reshape(NY, NX, tok, FEAT)
    a_sum = a_sum.reshape(NY, tok, FEAT)

    def add_hop(hop, a_sum, b_sum, *sums):
        final = hop == 3
        tables = [a_sum, a_part, b_sum, b_part, *sums]
        wide_block, block = (NX, tok, FEAT), (tok, FEAT)
        grad = (FEAT + STEPS, MAIN)
        shapes = [wide_block] * 4 + [grad] * len(sums)
        outs = [grad] + [block] * (NX + NY) if final else [wide_block] * 2 + [grad] * 2
        return pl.pallas_call(
            lambda *refs: hop_kernel(final, *refs),
            in_specs=[in_smem] + [in_hbm] * len(tables),
            out_shape=[shaped(bf16, *shape) for shape in outs],
            scratch_shapes=[pltpu.VMEM(shape, bf16) for shape in shapes]
            + [pltpu.SemaphoreType.DMA((len(tables),))],
            compiler_params=ALL,
            cost_estimate=TINY,
            name="hop",
        )(jnp.stack([x_at(hop + 1), y_at(hop + 1), x, y]).astype(jnp.int32), *tables)

    for hop in range(1, 3):
        a_sum, b_sum, up, down = add_hop(
            hop, both_x(a_sum), both_y(b_sum),
            shift(up, "z", 1, NZ), (add_3, add_2)[hop - 1],
            shift(down, "z", -1, NZ), (add_6, add_7)[hop - 1],
        )
    up, *last = add_hop(3, both_x(a_sum), both_y(b_sum), shift(up, "z", 1, NZ), add_1)
    down = shift(down, "z", -1, NZ)
    up = shift(up, "z", 1, NZ)
    a_last = [last[0]] + [shift(last[i], ("yh", "yl"), i, NY) for i in range(1, NY)]
    b_last = [last[NY]] + [shift(last[NY + i], "x", i, NX) for i in range(1, NX)]
    keep, give = pl.pallas_call(
        close_kernel,
        in_specs=[in_smem] + [in_vmem] * (NX + NY),
        out_shape=[shaped(bf16, tok, FEAT)] * 2,
        compiler_params=vmem(4),
        cost_estimate=TINY,
        name="close",
    )(c[None].astype(jnp.int32), *a_last, *b_last)
    hidden_grad = pl.pallas_call(
        cores_kernel,
        in_specs=[in_smem, in_vmem, in_vmem],
        out_shape=shaped(bf16, tok, 2 * FEAT),
        compiler_params=vmem(3),
        cost_estimate=TINY,
        name="by_core",
    )(c[None].astype(jnp.int32), keep, swap(give))

    mixed, back_pair = tie(mixed, back_pair)
    mixed = mixed.reshape(2, 2, tok, VW)
    own = pick(mixed, yh, 0)
    pair = shift(pick(mixed, 1 - yh, 0), "yh", 1, 2)
    crossed = swap(jnp.stack([pick(own, 1 - c, 0), pick(pair, 1 - c, 0)]))
    mixer_out = pl.pallas_call(
        heads_kernel,
        in_specs=[in_smem, in_vmem, in_vmem, in_vmem],
        out_shape=shaped(bf16, tok, 4 * VW),
        compiler_params=vmem(4),
        cost_estimate=TINY,
        name="by_head",
    )(jnp.stack([yh, c]).astype(jnp.int32), own, pair, crossed)

    summed = more(add_0, up, down)
    half = FEAT // 2
    main, step_part = summed[:FEAT].reshape(2, half, MAIN), summed[FEAT:, :FEAT]
    step_part = step_part.reshape(STEPS, 2, half)
    give = jnp.concatenate(
        [pick(main, 1 - yh, 0), jnp.pad(pick(step_part, 1 - yh, 1), ((0, 0), (0, MAIN - half)))],
        axis=0,
    )
    other = shift(give.astype(bf16), "yh", 1, 2).astype(f32)
    own, own_step = pick(main, yh, 0), pick(step_part, yh, 1)
    other_step = other[half:, :half]
    other = other[:half]
    state_grad = own[:, 2 * VW :] + other[:, 2 * VW :]

    def ordered(own, other, wide, gap):
        def cores(value):
            mine, pair = value[:, :wide], value[:, gap : gap + wide]
            return jnp.where(
                c == 0,
                jnp.concatenate([mine, pair], axis=1),
                jnp.concatenate([pair, mine], axis=1),
            )

        own, other = cores(own), cores(other)
        return jnp.where(
            yh == 0,
            jnp.concatenate([own, other], axis=1),
            jnp.concatenate([other, own], axis=1),
        )

    value_grad = ordered(own, other, VW, VW)
    step_grad = ordered(own_step.T, other_step.T, EACH, STEPS // 2)
    return mixer_out, hidden_grad, value_grad, state_grad, step_grad


def solution(mesh):
    fine = Mesh(mesh.devices.reshape(NZ, 2, 2, NX, 2), ("z", "yh", "c", "x", "yl"))
    split = P(("z", "yh", "c"), ("x", "yl"))
    by_head = P(("x", "yl"))
    return jax.shard_map(
        local,
        mesh=fine,
        in_specs=(split,) * 4 + (by_head,) * 3 + (split,),
        out_specs=(split,) * 5,
        check_vma=False,
    )
```

```python
import jax
import jax.numpy as jnp
from jax import lax
from jax.experimental import pallas as pl
from jax.experimental.pallas import tpu as pltpu
from jax.sharding import Mesh, PartitionSpec as P

HEAD_DIM = 64
STATE = 128
Q = 128
EACH = 4
VW = EACH * HEAD_DIM
BC = 2 * STATE
MAIN = 2 * VW + BC
STEPS = 16
COLS = MAIN + STEPS
FEAT = 256
NZ, NX, NY = 8, 4, 4
SPLIT = 0
f32, bf16 = jnp.float32, jnp.bfloat16
HI = lax.Precision.HIGHEST


def vmem(mebibytes):
    return pltpu.CompilerParams(vmem_limit_bytes=mebibytes * 1024 * 1024)


ALL = vmem(60)


def shift(value, axis, by, count, wrap=True):
    pairs = [(i, (i + by) % count) for i in range(count) if wrap or 0 <= i + by < count]
    return lax.ppermute(value, axis, pairs)


def both_x(value):
    pairs = [(c * NX + i, c * NX + (i + 1 - 2 * c) % NX) for c in range(2) for i in range(NX)]
    return lax.ppermute(value, ("c", "x"), pairs)


def both_y(value):
    def at(c, y):
        return (y // 2) * 4 + c * 2 + y % 2

    pairs = [(at(c, y), at(c, (y + 1 - 2 * c) % NY)) for c in range(2) for y in range(NY)]
    return lax.ppermute(value, ("yh", "c", "yl"), pairs)


def swap(value):
    return shift(value, "c", 1, 2)


def dot(left, right, dims, precision=None):
    return lax.dot_general(
        left, right, (dims, ((), ())), preferred_element_type=f32, precision=precision
    )


NN, NT, TN = ((1,), (0,)), ((1,), (1,)), ((0,), (0,))


def iota(shape, dim):
    return lax.broadcasted_iota(jnp.int32, shape, dim)


def consts():
    low = (iota((Q, Q), 0) >= iota((Q, Q), 1)).astype(f32)
    spread = (iota((EACH, VW), 1) // HEAD_DIM == iota((EACH, VW), 0)).astype(f32)
    return low, spread


def pieces(rows):
    high = rows.astype(bf16).astype(f32)
    mid = (rows - high).astype(bf16).astype(f32)
    return jnp.concatenate([high, mid, rows - high - mid], axis=0).astype(bf16)


def exact(rows, right, dims):
    n = rows.shape[0]
    out = dot(pieces(rows), right.astype(bf16), dims)
    return out[:n] + out[n : 2 * n] + out[2 * n :]


def widen(rows, right):
    right = right.astype(bf16)
    return dot(pieces(rows), jnp.concatenate([right] * 3, axis=0), TN)


def project_kernel(at_ref, *refs):
    x, y, z, way = (at_ref[i] for i in range(4))
    a_refs, b_refs, w_refs = refs[:NX], refs[NX : NX + NY], refs[NX + NY : NX + NY + NZ]
    hid_out, w_out, own_ref, send_ref, hid, weights, sems = refs[-7:]
    tok = hid.shape[1]
    copies = []

    def copy(source, target):
        copies.append(pltpu.make_async_copy(source, target, sems.at[len(copies)]))
        copies[-1].start()

    def place(source, x_at, y_at, core):
        x_at, y_at = x_at & (NX - 1), y_at & (NY - 1)
        lanes = pl.ds(pl.multiple_of((2 * x_at + (y_at & 1)) * FEAT, FEAT), FEAT)
        copy(source, hid.at[(y_at >> 1) * 2 + core, :, lanes])

    for j in range(NX):
        for i in range(NY):
            place(a_refs[j].at[i], x - way * j, y - i, 0)
            place(b_refs[i].at[j], x - j, y - way * i, 1)
    for i in range(NZ):
        z_at = (z + offset(i)) & (NZ - 1)
        lanes = pl.ds(pl.multiple_of(z_at * FEAT, FEAT), FEAT)
        copy(w_refs[i], weights.at[SPLIT:, lanes])
        if SPLIT:
            part_ref = refs[NX + NY + NZ]
            copy(part_ref.at[i], weights.at[:SPLIT, i * FEAT : (i + 1) * FEAT])
    for one in copies:
        one.wait()
    hid_back = pltpu.make_async_copy(hid, hid_out, sems.at[len(copies)])
    w_back = pltpu.make_async_copy(weights, w_out, sems.at[len(copies) + 1])
    hid_back.start()
    w_back.start()
    block = hid[...].reshape(4 * tok, NZ * FEAT)
    send_ref[: 4 * tok, VW:] = dot(block, weights[2 * VW : MAIN, :], NT)
    send_ref[: 4 * tok, :VW] = dot(block, weights[VW : 2 * VW, :], NT)
    steps = dot(weights[MAIN:, :], block, NT)
    send_ref[4 * tok : 4 * tok + STEPS, :] = steps[:, : 2 * tok]
    send_ref[4 * tok + STEPS :, :] = steps[:, 2 * tok :]
    own_ref[...] = dot(block, weights[:VW, :], NT)
    hid_back.wait()
    w_back.wait()


def offset(i):
    return i // 2 if i % 2 == 0 else -(i + 1) // 2


def state_kernel(
    own_ref, send_ref, recv_ref, g_ref, step_ref, rate_ref,
    x_ref, bc_ref, fresh_ref, seed_ref, last_ref, ends_ref,
):
    tokens = x_ref.shape[0]
    count = tokens // Q
    low, spread = consts()
    cum = exact(-step_ref[...] * rate_ref[...], low, NT)
    twice = jnp.concatenate(
        [jnp.concatenate([spread, jnp.zeros_like(spread)], axis=1),
         jnp.concatenate([jnp.zeros_like(spread), spread], axis=1)], axis=0)
    lane = iota((EACH, count), 1)
    ends = jnp.zeros((EACH, count), f32)
    for k in range(count):
        rows = slice(k * Q, (k + 1) * Q)
        x = (own_ref[rows, :] + recv_ref[rows, :VW]).astype(bf16)
        bc = (send_ref[rows, VW:] + recv_ref[rows, VW:]).astype(bf16)
        x_ref[rows, :] = x
        bc_ref[rows, :] = bc
        here = cum[k * EACH : (k + 1) * EACH]
        last = here[:, Q - 1 :]
        ends = ends + jnp.where(lane == k, last, 0.0)
        rest = jnp.exp(last - here) * step_ref[k * EACH : (k + 1) * EACH, :]
        both = widen(jnp.concatenate([rest, jnp.exp(here)], axis=0), twice)
        tail = (x.astype(f32) * both[:, :VW]).astype(bf16)
        grown = (g_ref[rows, :].astype(f32) * both[:, VW:]).astype(bf16)
        fresh_ref[k] = dot(tail, bc[:, :STATE], TN)
        seed_ref[k] = dot(grown, bc[:, STATE:], TN)
    lasts = dot(spread, jnp.exp(ends), TN, HI)
    last_ref[...] = lasts
    state = jnp.zeros((VW, STATE), f32)
    grad = jnp.zeros((VW, STATE), f32)
    for k in range(count):
        state = lasts[:, k : k + 1] * state + fresh_ref[k]
        back = count - 1 - k
        grad = lasts[:, back : back + 1] * grad + seed_ref[back]
    eye = (iota((EACH, STATE), 0) == iota((EACH, STATE), 1)).astype(f32)
    total = jnp.exp(jnp.sum(ends, axis=1, keepdims=True))
    pieces = split_decay(dot(jnp.broadcast_to(total, (EACH, STEPS)), eye, TN, HI)).astype(bf16)
    ends_ref[0, :VW] = state.astype(bf16)
    ends_ref[1, :VW] = grad.astype(bf16)
    ends_ref[0, VW:] = pieces
    ends_ref[1, VW:] = pieces


def split_decay(decay):
    high = decay.astype(bf16).astype(f32)
    mid = (decay - high).astype(bf16).astype(f32)
    least = decay - high - mid
    row = iota((STEPS, STATE), 0)
    return jnp.where(row == 0, high, jnp.where(row == 1, mid, jnp.where(row == 2, least, 0.0)))


def window_kernel(near_ref, far_ref, out_ref):
    spread = (iota((VW, STATE), 0) // HEAD_DIM == iota((VW, STATE), 1)).astype(bf16)
    for i in range(2):
        near = near_ref[i, VW:]
        column = jnp.sum(dot(spread, near, NT), axis=1, keepdims=True)
        out_ref[i, :VW] = (
            near_ref[i, :VW].astype(f32) + column * far_ref[i, :VW].astype(f32)
        ).astype(bf16)
        decay = jnp.sum(near.astype(f32), axis=0, keepdims=True) * jnp.sum(
            far_ref[i, VW:].astype(f32), axis=0, keepdims=True
        )
        out_ref[i, VW:] = split_decay(jnp.broadcast_to(decay, (STEPS, STATE))).astype(bf16)


def scan_kernel(
    x_ref, bc_ref, g_ref, step_ref, sig_ref, rate_ref, gain_ref,
    fresh_ref, seed_ref, last_ref, in_ref, later_ref,
    y_ref, back_ref, dstep_ref, held, grads,
):
    at = pl.program_id(0)
    count = fresh_ref.shape[0]

    @pl.when(at == 0)
    def _():
        lasts = last_ref[...]
        state = in_ref[...].astype(f32)
        grad = later_ref[...].astype(f32)
        for k in range(count):
            held[k] = state
            state = lasts[:, k : k + 1] * state + fresh_ref[k]
            back = count - 1 - k
            grads[back] = grad
            grad = lasts[:, back : back + 1] * grad + seed_ref[back]
        held[count] = state

    low, spread = consts()
    mask = low > 0.0
    zero = jnp.zeros_like(spread)
    twice = jnp.concatenate(
        [jnp.concatenate([spread, zero], axis=1), jnp.concatenate([zero, spread], axis=1)], axis=0)
    lane = iota((Q, EACH), 1)
    row = iota((EACH, Q), 0)
    gain_wide = gain_ref[...]
    for sub in range(step_ref.shape[0]):
        k = at * step_ref.shape[0] + sub
        rows = slice(sub * Q, (sub + 1) * Q)
        step_t = step_ref[sub]
        cum_t = exact(-step_t * rate_ref[...], low, NT)
        both_wide = widen(jnp.concatenate([cum_t, step_t], axis=0), twice)
        cum_wide, step_wide = both_wide[:, :VW], both_wide[:, VW:]
        growth = jnp.exp(cum_wide)
        rest = jnp.exp(cum_wide[Q - 1 :, :] - cum_wide)
        x, g = x_ref[rows, :], g_ref[rows, :]
        xf, gf = x.astype(f32), g.astype(f32)
        b_mat, c_mat = bc_ref[rows, :STATE], bc_ref[rows, STATE:]
        state, nxt, grad = held[k], held[k + 1], grads[k]
        state_b, grad_b = state.astype(bf16), grad.astype(bf16)

        scores = jnp.where(mask, dot(c_mat, b_mat, NT), 0.0)
        mixed, moved = [], []
        pairs = jnp.zeros((Q, Q), f32)
        out_sum = jnp.zeros((Q, EACH), f32)
        in_sum = jnp.zeros((EACH, Q), f32)
        for e in range(EACH):
            cut = slice(e * HEAD_DIM, (e + 1) * HEAD_DIM)
            first = slice(e * HEAD_DIM, e * HEAD_DIM + 1)
            fade = jnp.exp(jnp.minimum(cum_wide[:, first] - cum_t[e : e + 1, :], 0.0))
            weight = scores * fade
            step_row = step_t[e : e + 1, :]
            mixing = (weight * step_row).astype(bf16)
            mixed.append(dot(mixing, x[:, cut], NN))
            moved.append(dot(mixing, g[:, cut], TN))
            outer = dot(g[:, cut], x[:, cut], NT)
            pairs = pairs + outer * fade * step_row
            both = weight * outer
            in_sum = in_sum + jnp.where(row == e, jnp.sum(both, axis=0, keepdims=True), 0.0)
            out_sum = out_sum + jnp.where(
                lane == e, jnp.sum(both * step_row, axis=1, keepdims=True), 0.0
            )
        pairs = jnp.where(mask, pairs, 0.0).astype(bf16)

        from_state = growth * dot(c_mat, state_b, NT)
        from_later = rest * dot(b_mat, grad_b, NT)
        y_ref[rows, :] = (
            jnp.concatenate(mixed, axis=1) + from_state + gain_wide * xf
        ).astype(bf16)
        back_ref[rows, :VW] = (
            jnp.concatenate(moved, axis=1) + step_wide * from_later + gain_wide * gf
        ).astype(bf16)
        back_ref[rows, VW : VW + STATE] = (
            dot(pairs, c_mat, TN) + dot((xf * (rest * step_wide)).astype(bf16), grad_b, NN)
        ).astype(bf16)
        back_ref[rows, VW + STATE :] = (
            dot(pairs, b_mat, NN) + dot((gf * growth).astype(bf16), state_b, NN)
        ).astype(bf16)

        direct = in_sum + dot(spread.astype(bf16), (xf * from_later).astype(bf16), NT)
        out_t = dot(spread.astype(bf16), (gf * from_state).astype(bf16), NT)
        crossing = dot(spread, jnp.sum(grad * nxt, axis=1, keepdims=True), NN, HI)
        d_decay = (
            dot(out_sum, low, TN, HI) + exact(out_t - direct * step_t, low, NN) + crossing
        )
        d_step = (direct - rate_ref[...] * d_decay) * sig_ref[sub]
        dstep_ref[:, rows] = jnp.concatenate(
            [d_step, jnp.zeros((STEPS - EACH, Q), f32)], axis=0
        ).astype(bf16)


def both_bc(back_ref, pair_ref):
    return (back_ref[:, VW:].astype(f32) + pair_ref[:, VW:].astype(f32)).astype(bf16)


def fetch_blocks(at_ref, hid_ref, blocks, sems):
    copies = []
    for i in range(blocks.shape[0]):
        lanes = pl.ds(pl.multiple_of(at_ref[i] * FEAT, FEAT), FEAT)
        copies.append(pltpu.make_async_copy(hid_ref.at[:, :, lanes], blocks.at[i], sems.at[i]))
        copies[-1].start()
    return copies


def write_terms(copies, blocks, main, steps, outs):
    for i, out_ref in enumerate(outs):
        copies[i].wait()
        block = blocks[i].reshape(-1, FEAT)
        out_ref[:FEAT, :] = dot(block, main, TN).astype(bf16)
        out_ref[FEAT:, :FEAT] = dot(steps, block, NN).astype(bf16)
        out_ref[FEAT:, FEAT:] = jnp.zeros((STEPS, MAIN - FEAT), bf16)


def first_kernel(at_ref, back_ref, pair_ref, steps_ref, hid_ref, main_ref, *refs):
    outs, blocks, sems = refs[:-2], refs[-2], refs[-1]
    copies = fetch_blocks(at_ref, hid_ref, blocks, sems)
    bc = (back_ref[:, VW:].astype(f32) + pair_ref[:, VW:].astype(f32)).astype(bf16)
    main = jnp.concatenate([back_ref[:, :VW], pair_ref[:, :VW], bc], axis=1)
    eye = (iota((STEPS, STATE), 0) == iota((STEPS, STATE), 1)).astype(bf16)
    main_ref[:, :MAIN] = main
    main_ref[:, MAIN:] = dot(steps_ref[...], eye, TN).astype(bf16)
    write_terms(copies, blocks, main, steps_ref[...], outs)


def term_kernel(at_ref, main_ref, steps_ref, hid_ref, *refs):
    outs, blocks, sems = refs[:-2], refs[-2], refs[-1]
    copies = fetch_blocks(at_ref, hid_ref, blocks, sems)
    write_terms(copies, blocks, main_ref[:, :MAIN], steps_ref[...], outs)


def input_kernel(
    at_ref, main_ref, w_ref, a_ref, b_ref, a_first_ref, b_first_ref, weights, sems
):
    k = pl.program_id(0)
    x_first, y_first = at_ref[0], at_ref[1]

    def fetch(i):
        return pltpu.make_async_copy(
            w_ref.at[:, i * FEAT : (i + 1) * FEAT], weights.at[i, :COLS], sems.at[i]
        )

    @pl.when(k == 0)
    def _():
        for i in range(NZ):
            fetch(i).start()
            weights[i, COLS:] = jnp.zeros((MAIN + STATE - COLS, FEAT), bf16)

    for i in range(NZ):

        @pl.when(k == i)
        def _():
            fetch(i).wait()

    size = a_ref.shape[3]
    total = dot(main_ref[...], weights[k], NN).astype(bf16).reshape(2, 2, size, FEAT)
    x_at, yl_at = k // 2, k % 2
    a_ref[0, 0] = total[:, 0]
    b_ref[:, 0, 0] = total[:, 1]

    @pl.when(x_at == x_first)
    def _():
        a_first_ref[yl_at] = total[:, 0]

    for i in range(2):

        @pl.when(y_first == 2 * i + yl_at)
        def _():
            b_first_ref[x_at] = total[i, 1]


def hop_kernel(final, at_ref, *refs):
    count = 4
    x_at, y_at, x, y = (at_ref[i] for i in range(4))
    ins, outs = refs[: 2 * count], refs[2 * count : -2 * count - 1]
    held, sems = refs[-2 * count - 1 : -1], refs[-1]
    copies = []
    for i in range(2 * count):
        source = ins[i]
        if i == 1:
            source = source.at[x_at]
        if i == 3:
            source = source.at[y_at]
        copies.append(pltpu.make_async_copy(source, held[i], sems.at[i]))
        copies[-1].start()
    for i in range(count):
        copies[2 * i].wait()
        copies[2 * i + 1].wait()
        value = (held[2 * i][...].astype(f32) + held[2 * i + 1][...].astype(f32)).astype(bf16)
        if final:
            held[2 * i][...] = value
        else:
            outs[i][...] = value
    if final:
        for i in range(NY):
            at = (y + i) & (NY - 1)
            outs[i][...] = held[0][(at & 1) * 2 + (at >> 1)]
            outs[NY + i][...] = held[2][(x + i) & (NX - 1)]
        half = FEAT // 2
        for i in range(2):
            for j in range(2):
                at = pl.multiple_of(((y >> 1) ^ j) * half, half)
                out_ref = outs[NY + NX + 2 * i + j]
                out_ref[:half, :] = held[4 + 2 * i][pl.ds(at, half), :]
                out_ref[half:, :half] = held[4 + 2 * i][FEAT:, pl.ds(at, half)]
                out_ref[half:, half:] = jnp.zeros((STEPS, MAIN - half), bf16)


def close_kernel(at_ref, *refs):
    a_refs, b_refs, keep_ref, give_ref = refs[:NY], refs[NY : NY + NX], refs[-2], refs[-1]
    sums = []
    for parts in (a_refs, b_refs):
        total = parts[0][...].astype(f32)
        for part in parts[1:]:
            total = total + part[...].astype(f32)
        sums.append(total)
    mine = at_ref[0] == 0
    keep_ref[...] = jnp.where(mine, sums[0], sums[1]).astype(bf16)
    give_ref[...] = jnp.where(mine, sums[1], sums[0]).astype(bf16)


def cores_kernel(at_ref, own_ref, pair_ref, out_ref):
    c = at_ref[0]
    for i in range(2):
        part = slice(i * 128, (i + 1) * 128)
        out_ref[:, pl.ds(pl.multiple_of((2 * i + c) * 128, 128), 128)] = own_ref[:, part]
        out_ref[:, pl.ds(pl.multiple_of((2 * i + 1 - c) * 128, 128), 128)] = pair_ref[:, part]


def heads_kernel(at_ref, own_ref, pair_ref, cross_ref, out_ref):
    yh, c = at_ref[0], at_ref[1]

    def to(first, second, value):
        lanes = pl.ds(pl.multiple_of((first * 2 + second) * VW, VW), VW)
        out_ref[:, lanes] = value

    to(yh, c, own_ref[c])
    to(1 - yh, c, pair_ref[c])
    to(yh, 1 - c, cross_ref[0])
    to(1 - yh, 1 - c, cross_ref[1])


def pick(value, at, dim):
    return lax.dynamic_index_in_dim(value, at, dim, False)


def tie(*values):
    return lax.optimization_barrier(values)


LONG = pl.CostEstimate(flops=10 * 2**30, bytes_accessed=32 * 2**20, transcendentals=0)
TINY = pl.CostEstimate(flops=1024, bytes_accessed=1024, transcendentals=0)


def local(hidden, value_proj, state_proj, step_proj, step_bias, decay_rate, skip_gain, out_grad):
    z, yh, c, x, yl = (lax.axis_index(a) for a in ("z", "yh", "c", "x", "yl"))
    y = yh * 2 + yl
    way = 1 - 2 * c
    tok = hidden.shape[0]
    tokens = 4 * tok
    blocks = tokens // Q

    parts = hidden.reshape(tok, 2, 2, 128)
    keep = pick(parts, c, 2).reshape(tok, FEAT)
    got = swap(pick(parts, 1 - c, 2).reshape(tok, FEAT))
    first = jnp.where(c == 0, keep, got)
    second = jnp.where(c == 0, got, keep)

    value_proj, state_proj, step_proj, first, second = tie(
        value_proj, state_proj, step_proj, first, second
    )
    value_t, state_t, step_tr = value_proj.T, state_proj.T, step_proj.T
    none = jnp.zeros((EACH, value_proj.shape[0]), bf16)

    def chosen(which):
        def some(array, wide, core):
            return lax.dynamic_slice_in_dim(array, (which * 2 + core) * wide, wide, 0)

        return jnp.concatenate(
            [
                some(value_t, VW, c), some(value_t, VW, 1 - c), state_t,
                some(step_tr, EACH, c), none, some(step_tr, EACH, 1 - c), none,
            ],
            axis=0,
        )

    mine, theirs = chosen(yh), shift(chosen(1 - yh), "yh", 1, 2)
    chunk = jnp.where(
        yh == 0,
        jnp.concatenate([mine, theirs], axis=1),
        jnp.concatenate([theirs, mine], axis=1),
    )
    def pairwise(own, pair, place, dim):
        return jnp.where(
            place == 0, jnp.stack([own, pair], dim), jnp.stack([pair, own], dim)
        )

    out_grad, chunk = tie(out_grad, chunk)
    cot = out_grad.reshape(tok, 2, 2, VW)
    cot = pairwise(pick(cot, c, 2), swap(pick(cot, 1 - c, 2)), c, 0)

    brought = [lax.all_gather(chunk[:SPLIT], "z")] if SPLIT else []
    ring = chunk[SPLIT:]
    weights = [ring, shift(ring, "z", 1, NZ), shift(ring, "z", -1, NZ)]
    a_blocks = [jnp.stack([first] + [shift(first, ("yh", "yl"), i, NY) for i in range(1, NY)])]
    b_blocks = [jnp.stack([second] + [shift(second, "x", i, NX) for i in range(1, NX)])]
    weights[1], weights[2], a_blocks[0], b_blocks[0], cot = tie(
        weights[1], weights[2], a_blocks[0], b_blocks[0], cot
    )
    cot = pairwise(pick(cot, yh, 2), shift(pick(cot, 1 - yh, 2), "yh", 1, 2), yh, 0)
    cot = cot.reshape(tokens, VW)
    for hop in range(1, 4):
        weights.append(shift(weights[-2], "z", 1, NZ))
        if hop < 3:
            weights.append(shift(weights[-2], "z", -1, NZ))
        a_blocks.append(both_x(a_blocks[-1]))
        b_blocks.append(both_y(b_blocks[-1]))
        if hop == 1:
            a_blocks[-1], b_blocks[-1], cot = tie(a_blocks[-1], b_blocks[-1], cot)
        if hop < 3:
            weights[-1], weights[-2], a_blocks[-1], b_blocks[-1] = tie(
                weights[-1], weights[-2], a_blocks[-1], b_blocks[-1]
            )

    def whole(*shape):
        return pl.BlockSpec(shape, lambda *k: (0,) * len(shape))

    def shaped(dtype, *shape):
        return jax.ShapeDtypeStruct(shape, dtype)

    places = jnp.stack([x, y, z, way]).astype(jnp.int32)
    wide = NZ * FEAT
    in_hbm = pl.BlockSpec(memory_space=pltpu.HBM)
    in_vmem = pl.BlockSpec(memory_space=pltpu.VMEM)
    in_smem = pl.BlockSpec(memory_space=pltpu.SMEM)
    hid, whole_w, p_own, p_send = pl.pallas_call(
        project_kernel,
        in_specs=[in_smem] + [in_hbm] * (NX + NY + NZ + len(brought)),
        out_specs=[in_hbm, in_hbm, in_vmem, in_vmem],
        out_shape=[
            shaped(bf16, 4, tok, wide), shaped(bf16, COLS, wide),
            shaped(f32, tokens, VW), shaped(f32, tokens + 2 * STEPS, VW + BC),
        ],
        scratch_shapes=[
            pltpu.VMEM((4, tok, wide), bf16), pltpu.VMEM((COLS, wide), bf16),
            pltpu.SemaphoreType.DMA((2 * NX * NY + 2 * NZ + 2,)),
        ],
        compiler_params=ALL,
        cost_estimate=LONG,
        name="project",
    )(places, *a_blocks, *b_blocks, *weights, *brought)
    p_recv = swap(p_send)

    def step_rows(packed):
        packed = packed[tokens:]
        return jnp.concatenate([packed[:STEPS], packed[STEPS:]], axis=1)

    place = (yh * 2 + c) * EACH
    bias, rate, gain = (
        lax.dynamic_slice_in_dim(v, place, EACH, 0)[:, None]
        for v in (step_bias, decay_rate, skip_gain)
    )
    pre_step = (
        step_rows(p_send)[:EACH] + step_rows(p_recv)[STEPS // 2 : STEPS // 2 + EACH] + bias
    )
    pre_step = pre_step.reshape(EACH, blocks, Q).transpose(1, 0, 2)
    step = jax.nn.softplus(pre_step)
    sig = jax.nn.sigmoid(pre_step)

    states = shaped(f32, blocks, VW, STATE)
    values, bc, fresh, seeds, lasts, ends = pl.pallas_call(
        state_kernel,
        out_shape=[
            shaped(bf16, tokens, VW), shaped(bf16, tokens, BC), states, states,
            shaped(f32, VW, blocks), shaped(bf16, 2, VW + STEPS, STATE),
        ],
        compiler_params=ALL,
        name="states",
    )(p_own, p_send, p_recv, cot, step.reshape(blocks * EACH, Q), jnp.tile(rate, (blocks, 1)))

    def along(packed, by):
        pairs = [
            (i * 2 + core, (i + by * (1 - 2 * core)) * 2 + core)
            for i in range(NZ)
            for core in range(2)
            if 0 <= i + by * (1 - 2 * core) < NZ
        ]
        return lax.ppermute(packed, ("z", "c"), pairs)

    def joined(near, far):
        return pl.pallas_call(
            window_kernel,
            out_shape=shaped(bf16, 2, VW + STEPS, STATE),
            compiler_params=vmem(2),
            cost_estimate=TINY,
            name="window",
        )(near, far)

    start = jnp.stack([pick(ends, c, 0), swap(pick(ends, 1 - c, 0))])
    window = joined(along(start, 1), along(start, 2))
    for by in (2, 4):
        window = joined(window, along(window, by))
    kept, given = window[0, :VW], window[1, :VW]
    other_way = swap(given)
    state_in = jnp.where(c == 0, kept, other_way)
    later = jnp.where(c == 0, other_way, kept)

    each = 2

    def rows(width):
        return pl.BlockSpec((each * Q, width), lambda k: (k, 0))

    lanes = pl.BlockSpec((each, EACH, Q), lambda k: (k, 0, 0))
    mixed, back, steps = pl.pallas_call(
        scan_kernel,
        grid=(blocks // each,),
        in_specs=[
            rows(VW), rows(BC), rows(VW), lanes, lanes, whole(EACH, 1), whole(1, VW),
            whole(blocks, VW, STATE), whole(blocks, VW, STATE), whole(VW, blocks),
            whole(VW, STATE), whole(VW, STATE),
        ],
        out_specs=[
            rows(VW), rows(VW + BC), pl.BlockSpec((STEPS, each * Q), lambda k: (0, k)),
        ],
        out_shape=[
            shaped(bf16, tokens, VW), shaped(bf16, tokens, VW + BC), shaped(bf16, STEPS, tokens),
        ],
        scratch_shapes=[
            pltpu.VMEM((blocks + 1, VW, STATE), f32), pltpu.VMEM((blocks, VW, STATE), f32),
        ],
        compiler_params=ALL,
        name="scan",
    )(
        values, bc, cot, step, sig, rate, jnp.repeat(gain, HEAD_DIM, axis=0).T,
        fresh, seeds, lasts, state_in, later,
    )

    back_pair, steps_pair = swap(back), swap(steps)
    steps = jnp.concatenate([steps[: STEPS // 2], steps_pair[: STEPS // 2]], axis=0)

    def hid_at(*offsets):
        return jnp.stack([(z + i) % NZ for i in offsets]).astype(jnp.int32)

    def fetched(count):
        return [pltpu.VMEM((count, 4, tok, FEAT), bf16), pltpu.SemaphoreType.DMA((count,))]

    grad_block = shaped(bf16, FEAT + STEPS, MAIN)
    main, up, down = pl.pallas_call(
        first_kernel,
        in_specs=[in_smem, in_vmem, in_vmem, in_vmem, in_hbm],
        out_shape=[shaped(bf16, tokens, MAIN + STATE)] + [grad_block] * 2,
        scratch_shapes=fetched(2),
        compiler_params=ALL,
        cost_estimate=TINY,
        name="first",
    )(hid_at(4, 5), back, back_pair, steps, hid)
    add_3, add_6, add_2, add_7, add_1, add_0 = pl.pallas_call(
        term_kernel,
        in_specs=[in_smem, in_vmem, in_vmem, in_hbm],
        out_shape=[grad_block] * 6,
        scratch_shapes=fetched(6),
        compiler_params=ALL,
        cost_estimate=LONG,
        name="term",
    )(hid_at(3, 6, 2, 7, 1, 0), main, steps, hid)

    def more(sums, *parts):
        total = sums.astype(f32)
        for part in parts:
            total = total + part.astype(f32)
        return total

    def x_at(hop):
        return (x - way * hop) % NX

    def y_at(hop):
        return (y - way * hop) % NY

    a_part, b_part, a_sum, b_sum = pl.pallas_call(
        input_kernel,
        grid=(NZ,),
        in_specs=[in_smem, whole(tokens, MAIN + STATE), in_hbm],
        out_specs=[
            pl.BlockSpec((1, 1, 2, tok, FEAT), lambda k: (k // 2, k % 2, 0, 0, 0)),
            pl.BlockSpec((2, 1, 1, tok, FEAT), lambda k: (0, k % 2, k // 2, 0, 0)),
            whole(2, 2, tok, FEAT), whole(NX, tok, FEAT),
        ],
        out_shape=[
            shaped(bf16, NX, 2, 2, tok, FEAT), shaped(bf16, 2, 2, NX, tok, FEAT),
            shaped(bf16, 2, 2, tok, FEAT), shaped(bf16, NX, tok, FEAT),
        ],
        scratch_shapes=[
            pltpu.VMEM((NZ, MAIN + STATE, FEAT), bf16), pltpu.SemaphoreType.DMA((NZ,)),
        ],
        compiler_params=ALL,
        cost_estimate=LONG,
        name="input",
    )(jnp.stack([x_at(1), y_at(1)]).astype(jnp.int32), main, whole_w)
    mixed = mixed.reshape(2, 2, tok, VW)
    heads_own = pick(mixed, yh, 0)
    pair = shift(pick(mixed, 1 - yh, 0), "yh", 1, 2)
    a_sum, b_sum, pair = tie(a_sum, b_sum, pair)
    crossed = swap(jnp.stack([pick(heads_own, 1 - c, 0), pick(pair, 1 - c, 0)]))
    a_part = a_part.reshape(NX, NY, tok, FEAT)
    b_part = b_part.reshape(NY, NX, tok, FEAT)
    a_sum = a_sum.reshape(NY, tok, FEAT)

    def add_hop(hop, a_sum, b_sum, *sums):
        final = hop == 3
        tables = [a_sum, a_part, b_sum, b_part, *sums]
        wide_block, block = (NX, tok, FEAT), (tok, FEAT)
        grad = (FEAT + STEPS, MAIN)
        shapes = [wide_block] * 4 + [grad] * len(sums)
        outs = [wide_block] * 2 + [grad] * 2
        if final:
            outs = [block] * (NX + NY) + [(FEAT // 2 + STEPS, MAIN)] * 4
        return pl.pallas_call(
            lambda *refs: hop_kernel(final, *refs),
            in_specs=[in_smem] + [in_hbm] * len(tables),
            out_shape=[shaped(bf16, *shape) for shape in outs],
            scratch_shapes=[pltpu.VMEM(shape, bf16) for shape in shapes]
            + [pltpu.SemaphoreType.DMA((len(tables),))],
            compiler_params=ALL,
            cost_estimate=TINY,
            name="hop",
        )(jnp.stack([x_at(hop + 1), y_at(hop + 1), x, y]).astype(jnp.int32), *tables)

    for hop in range(1, 4):
        a_sum, b_sum, up, down, *last = add_hop(
            hop, both_x(a_sum), both_y(b_sum),
            shift(up, "z", 1, NZ), (add_3, add_2, add_1)[hop - 1],
            shift(down, "z", -1, NZ), (add_6, add_7, add_0)[hop - 1],
        )
        if hop == 1:
            a_sum, b_sum, crossed = tie(a_sum, b_sum, crossed)
    mixer_out = pl.pallas_call(
        heads_kernel,
        in_specs=[in_smem, in_vmem, in_vmem, in_vmem],
        out_shape=shaped(bf16, tok, 4 * VW),
        compiler_params=vmem(4),
        cost_estimate=TINY,
        name="by_head",
    )(jnp.stack([yh, c]).astype(jnp.int32), heads_own, pair, crossed)
    last = [a_sum, b_sum, up, down] + last
    ends = last[NX + NY :]
    across = [(2 * i + j, 2 * ((i + 1) % NZ) + 1 - j) for i in range(NZ) for j in range(2)]
    own = more(ends[2], shift(ends[0], "z", 1, NZ))
    other = more(
        shift(ends[3], "yh", 1, 2), lax.ppermute(ends[1], ("z", "yh"), across)
    )
    a_last = [last[0]] + [shift(last[i], ("yh", "yl"), i, NY) for i in range(1, NY)]
    b_last = [last[NY]] + [shift(last[NY + i], "x", i, NX) for i in range(1, NX)]
    keep, give = pl.pallas_call(
        close_kernel,
        in_specs=[in_smem] + [in_vmem] * (NX + NY),
        out_shape=[shaped(bf16, tok, FEAT)] * 2,
        compiler_params=vmem(4),
        cost_estimate=TINY,
        name="close",
    )(c[None].astype(jnp.int32), *a_last, *b_last)
    hidden_grad = pl.pallas_call(
        cores_kernel,
        in_specs=[in_smem, in_vmem, in_vmem],
        out_shape=shaped(bf16, tok, 2 * FEAT),
        compiler_params=vmem(3),
        cost_estimate=TINY,
        name="by_core",
    )(c[None].astype(jnp.int32), keep, swap(give))

    half = FEAT // 2
    own_step, other_step = own[half:, :half], other[half:, :half]
    own, other = own[:half], other[:half]
    state_grad = own[:, 2 * VW :] + other[:, 2 * VW :]

    def ordered(own, other, wide, gap):
        def cores(value):
            mine, pair = value[:, :wide], value[:, gap : gap + wide]
            return jnp.where(
                c == 0,
                jnp.concatenate([mine, pair], axis=1),
                jnp.concatenate([pair, mine], axis=1),
            )

        own, other = cores(own), cores(other)
        return jnp.where(
            yh == 0,
            jnp.concatenate([own, other], axis=1),
            jnp.concatenate([other, own], axis=1),
        )

    value_grad = ordered(own, other, VW, VW)
    step_grad = ordered(own_step.T, other_step.T, EACH, STEPS // 2)
    return mixer_out, hidden_grad, value_grad, state_grad, step_grad


def solution(mesh):
    fine = Mesh(mesh.devices.reshape(NZ, 2, 2, NX, 2), ("z", "yh", "c", "x", "yl"))
    split = P(("z", "yh", "c"), ("x", "yl"))
    by_head = P(("x", "yl"))
    return jax.shard_map(
        local,
        mesh=fine,
        in_specs=(split,) * 4 + (by_head,) * 3 + (split,),
        out_specs=(split,) * 5,
        check_vma=False,
    )
```

```python
import jax
import jax.numpy as jnp
from jax import lax
from jax.experimental import pallas as pl
from jax.experimental.pallas import tpu as pltpu
from jax.sharding import Mesh, PartitionSpec as P

HEAD_DIM = 64
STATE = 128
Q = 128
EACH = 4
VW = EACH * HEAD_DIM
BC = 2 * STATE
MAIN = 2 * VW + BC
STEPS = 16
COLS = MAIN + STEPS
FEAT = 256
NZ, NX, NY = 8, 4, 4
SPLIT = 0
f32, bf16 = jnp.float32, jnp.bfloat16
HI = lax.Precision.HIGHEST


def vmem(mebibytes):
    return pltpu.CompilerParams(vmem_limit_bytes=mebibytes * 1024 * 1024)


ALL = vmem(60)


def shift(value, axis, by, count, wrap=True):
    pairs = [(i, (i + by) % count) for i in range(count) if wrap or 0 <= i + by < count]
    return lax.ppermute(value, axis, pairs)


def both_x(value):
    pairs = [(c * NX + i, c * NX + (i + 1 - 2 * c) % NX) for c in range(2) for i in range(NX)]
    return lax.ppermute(value, ("c", "x"), pairs)


def both_y(value):
    def at(c, y):
        return (y // 2) * 4 + c * 2 + y % 2

    pairs = [(at(c, y), at(c, (y + 1 - 2 * c) % NY)) for c in range(2) for y in range(NY)]
    return lax.ppermute(value, ("yh", "c", "yl"), pairs)


def swap(value):
    return shift(value, "c", 1, 2)


def dot(left, right, dims, precision=None):
    return lax.dot_general(
        left, right, (dims, ((), ())), preferred_element_type=f32, precision=precision
    )


NN, NT, TN = ((1,), (0,)), ((1,), (1,)), ((0,), (0,))


def iota(shape, dim):
    return lax.broadcasted_iota(jnp.int32, shape, dim)


def consts():
    low = (iota((Q, Q), 0) >= iota((Q, Q), 1)).astype(f32)
    spread = (iota((EACH, VW), 1) // HEAD_DIM == iota((EACH, VW), 0)).astype(f32)
    return low, spread


def pieces(rows):
    high = rows.astype(bf16).astype(f32)
    mid = (rows - high).astype(bf16).astype(f32)
    return jnp.concatenate([high, mid, rows - high - mid], axis=0).astype(bf16)


def exact(rows, right, dims):
    n = rows.shape[0]
    out = dot(pieces(rows), right.astype(bf16), dims)
    return out[:n] + out[n : 2 * n] + out[2 * n :]


def widen(rows, right):
    right = right.astype(bf16)
    return dot(pieces(rows), jnp.concatenate([right] * 3, axis=0), TN)


def project_kernel(at_ref, *refs):
    x, y, z, way = (at_ref[i] for i in range(4))
    a_refs, b_refs, w_refs = refs[:NX], refs[NX : NX + NY], refs[NX + NY : NX + NY + NZ]
    hid_out, w_out, own_ref, send_ref, hid, weights, sems = refs[-7:]
    tok = hid.shape[1]
    copies = []

    def copy(source, target):
        copies.append(pltpu.make_async_copy(source, target, sems.at[len(copies)]))
        copies[-1].start()

    def place(source, x_at, y_at, core):
        x_at, y_at = x_at & (NX - 1), y_at & (NY - 1)
        lanes = pl.ds(pl.multiple_of((2 * x_at + (y_at & 1)) * FEAT, FEAT), FEAT)
        copy(source, hid.at[(y_at >> 1) * 2 + core, :, lanes])

    for j in range(NX):
        for i in range(NY):
            place(a_refs[j].at[i], x - way * j, y - i, 0)
            place(b_refs[i].at[j], x - j, y - way * i, 1)
    for i in range(NZ):
        z_at = (z + offset(i)) & (NZ - 1)
        lanes = pl.ds(pl.multiple_of(z_at * FEAT, FEAT), FEAT)
        copy(w_refs[i], weights.at[SPLIT:, lanes])
        if SPLIT:
            part_ref = refs[NX + NY + NZ]
            copy(part_ref.at[i], weights.at[:SPLIT, i * FEAT : (i + 1) * FEAT])
    for one in copies:
        one.wait()
    hid_back = pltpu.make_async_copy(hid, hid_out, sems.at[len(copies)])
    w_back = pltpu.make_async_copy(weights, w_out, sems.at[len(copies) + 1])
    hid_back.start()
    w_back.start()
    block = hid[...].reshape(4 * tok, NZ * FEAT)
    send_ref[: 4 * tok, VW:] = dot(block, weights[2 * VW : MAIN, :], NT)
    send_ref[: 4 * tok, :VW] = dot(block, weights[VW : 2 * VW, :], NT)
    steps = dot(weights[MAIN:, :], block, NT)
    send_ref[4 * tok : 4 * tok + STEPS, :] = steps[:, : 2 * tok]
    send_ref[4 * tok + STEPS :, :] = steps[:, 2 * tok :]
    own_ref[...] = dot(block, weights[:VW, :], NT)
    hid_back.wait()
    w_back.wait()


def offset(i):
    return i // 2 if i % 2 == 0 else -(i + 1) // 2


def state_kernel(
    at_ref, own_ref, send_ref, recv_ref, g_ref, head_ref,
    x_ref, bc_ref, step_ref, sig_ref, fresh_ref, seed_ref, last_ref, keep_ref, give_ref,
):
    tokens = x_ref.shape[0]
    count = tokens // Q
    low, spread = consts()
    bias, rate = head_ref[:, 0:1], head_ref[:, 1:2]
    pre = []
    for i in range(2):
        base = tokens + i * STEPS
        mine = send_ref[base : base + EACH, :]
        pair = recv_ref[base + STEPS // 2 : base + STEPS // 2 + EACH, :]
        rows = mine + pair + bias
        pre += [rows[:, k * Q : (k + 1) * Q] for k in range(rows.shape[1] // Q)]
    pre = jnp.concatenate(pre, axis=0)
    small = jnp.exp(-jnp.abs(pre))
    above = 1.0 + small
    log_above = jnp.where(
        above == 1.0, small, jnp.log(above) * (small / jnp.where(above == 1.0, 1.0, above - 1.0))
    )
    step = jnp.maximum(pre, 0.0) + log_above
    sig = jnp.where(pre >= 0.0, 1.0, small) / above
    for k in range(count):
        step_ref[k] = step[k * EACH : (k + 1) * EACH]
        sig_ref[k] = sig[k * EACH : (k + 1) * EACH]
    cum = exact(-step * jnp.concatenate([rate] * count, axis=0), low, NT)
    twice = jnp.concatenate(
        [jnp.concatenate([spread, jnp.zeros_like(spread)], axis=1),
         jnp.concatenate([jnp.zeros_like(spread), spread], axis=1)], axis=0)
    lane = iota((EACH, count), 1)
    ends = jnp.zeros((EACH, count), f32)
    for k in range(count):
        rows = slice(k * Q, (k + 1) * Q)
        x = (own_ref[rows, :] + recv_ref[rows, :VW]).astype(bf16)
        bc = (send_ref[rows, VW:] + recv_ref[rows, VW:]).astype(bf16)
        x_ref[rows, :] = x
        bc_ref[rows, :] = bc
        here = cum[k * EACH : (k + 1) * EACH]
        last = here[:, Q - 1 :]
        ends = ends + jnp.where(lane == k, last, 0.0)
        rest = jnp.exp(last - here) * step[k * EACH : (k + 1) * EACH]
        both = widen(jnp.concatenate([rest, jnp.exp(here)], axis=0), twice)
        tail = (x.astype(f32) * both[:, :VW]).astype(bf16)
        grown = (g_ref[rows, :].astype(f32) * both[:, VW:]).astype(bf16)
        fresh_ref[k] = dot(tail, bc[:, :STATE], TN)
        seed_ref[k] = dot(grown, bc[:, STATE:], TN)
    lasts = dot(spread, jnp.exp(ends), TN, HI)
    last_ref[...] = lasts
    state = jnp.zeros((VW, STATE), f32)
    grad = jnp.zeros((VW, STATE), f32)
    for k in range(count):
        state = lasts[:, k : k + 1] * state + fresh_ref[k]
        back = count - 1 - k
        grad = lasts[:, back : back + 1] * grad + seed_ref[back]
    eye = (iota((EACH, STATE), 0) == iota((EACH, STATE), 1)).astype(f32)
    total = jnp.exp(jnp.sum(ends, axis=1, keepdims=True))
    parts = split_decay(dot(jnp.broadcast_to(total, (EACH, STEPS)), eye, TN, HI)).astype(bf16)
    up_core = at_ref[5] == 0
    keep_ref[:VW] = jnp.where(up_core, state, grad).astype(bf16)
    give_ref[:VW] = jnp.where(up_core, grad, state).astype(bf16)
    keep_ref[VW:] = parts
    give_ref[VW:] = parts


def split_decay(decay):
    high = decay.astype(bf16).astype(f32)
    mid = (decay - high).astype(bf16).astype(f32)
    least = decay - high - mid
    row = iota((STEPS, STATE), 0)
    return jnp.where(row == 0, high, jnp.where(row == 1, mid, jnp.where(row == 2, least, 0.0)))


def window_kernel(near_ref, far_ref, *out_refs):
    spread = (iota((VW, STATE), 0) // HEAD_DIM == iota((VW, STATE), 1)).astype(bf16)
    for i in range(2):
        out_ref = out_refs[i] if len(out_refs) == 2 else out_refs[0].at[i]
        near = near_ref[i, VW:]
        column = jnp.sum(dot(spread, near, NT), axis=1, keepdims=True)
        out_ref[:VW] = (
            near_ref[i, :VW].astype(f32) + column * far_ref[i, :VW].astype(f32)
        ).astype(bf16)
        decay = jnp.sum(near.astype(f32), axis=0, keepdims=True) * jnp.sum(
            far_ref[i, VW:].astype(f32), axis=0, keepdims=True
        )
        out_ref[VW:] = split_decay(jnp.broadcast_to(decay, (STEPS, STATE))).astype(bf16)


def scan_kernel(
    at_ref, x_ref, bc_ref, g_ref, step_ref, sig_ref, head_ref,
    fresh_ref, seed_ref, last_ref, kept_ref, other_ref,
    y_ref, back_ref, dstep_ref, held, grads,
):
    at = pl.program_id(0)
    count = fresh_ref.shape[0]

    @pl.when(at == 0)
    def _():
        lasts = last_ref[...]
        kept, other = kept_ref[:VW].astype(f32), other_ref[:VW].astype(f32)
        up_core = at_ref[5] == 0
        state, grad = jnp.where(up_core, kept, other), jnp.where(up_core, other, kept)
        for k in range(count):
            held[k] = state
            state = lasts[:, k : k + 1] * state + fresh_ref[k]
            back = count - 1 - k
            grads[back] = grad
            grad = lasts[:, back : back + 1] * grad + seed_ref[back]
        held[count] = state

    low, spread = consts()
    mask = low > 0.0
    zero = jnp.zeros_like(spread)
    twice = jnp.concatenate(
        [jnp.concatenate([spread, zero], axis=1), jnp.concatenate([zero, spread], axis=1)], axis=0)
    lane = iota((Q, EACH), 1)
    row = iota((EACH, Q), 0)
    rate = head_ref[:, 1:2]
    gain_wide = jnp.sum(head_ref[:, 2:3] * spread, axis=0, keepdims=True)
    for sub in range(step_ref.shape[0]):
        k = at * step_ref.shape[0] + sub
        rows = slice(sub * Q, (sub + 1) * Q)
        step_t = step_ref[sub]
        cum_t = exact(-step_t * rate, low, NT)
        both_wide = widen(jnp.concatenate([cum_t, step_t], axis=0), twice)
        cum_wide, step_wide = both_wide[:, :VW], both_wide[:, VW:]
        growth = jnp.exp(cum_wide)
        rest = jnp.exp(cum_wide[Q - 1 :, :] - cum_wide)
        x, g = x_ref[rows, :], g_ref[rows, :]
        xf, gf = x.astype(f32), g.astype(f32)
        b_mat, c_mat = bc_ref[rows, :STATE], bc_ref[rows, STATE:]
        state, nxt, grad = held[k], held[k + 1], grads[k]
        state_b, grad_b = state.astype(bf16), grad.astype(bf16)

        scores = jnp.where(mask, dot(c_mat, b_mat, NT), 0.0)
        mixed, moved = [], []
        pairs = jnp.zeros((Q, Q), f32)
        out_sum = jnp.zeros((Q, EACH), f32)
        in_sum = jnp.zeros((EACH, Q), f32)
        for e in range(EACH):
            cut = slice(e * HEAD_DIM, (e + 1) * HEAD_DIM)
            first = slice(e * HEAD_DIM, e * HEAD_DIM + 1)
            fade = jnp.exp(jnp.minimum(cum_wide[:, first] - cum_t[e : e + 1, :], 0.0))
            weight = scores * fade
            step_row = step_t[e : e + 1, :]
            mixing = (weight * step_row).astype(bf16)
            mixed.append(dot(mixing, x[:, cut], NN))
            moved.append(dot(mixing, g[:, cut], TN))
            outer = dot(g[:, cut], x[:, cut], NT)
            pairs = pairs + outer * fade * step_row
            both = weight * outer
            in_sum = in_sum + jnp.where(row == e, jnp.sum(both, axis=0, keepdims=True), 0.0)
            out_sum = out_sum + jnp.where(
                lane == e, jnp.sum(both * step_row, axis=1, keepdims=True), 0.0
            )
        pairs = jnp.where(mask, pairs, 0.0).astype(bf16)

        from_state = growth * dot(c_mat, state_b, NT)
        from_later = rest * dot(b_mat, grad_b, NT)
        y_ref[rows, :] = (
            jnp.concatenate(mixed, axis=1) + from_state + gain_wide * xf
        ).astype(bf16)
        back_ref[rows, :VW] = (
            jnp.concatenate(moved, axis=1) + step_wide * from_later + gain_wide * gf
        ).astype(bf16)
        back_ref[rows, VW : VW + STATE] = (
            dot(pairs, c_mat, TN) + dot((xf * (rest * step_wide)).astype(bf16), grad_b, NN)
        ).astype(bf16)
        back_ref[rows, VW + STATE :] = (
            dot(pairs, b_mat, NN) + dot((gf * growth).astype(bf16), state_b, NN)
        ).astype(bf16)

        direct = in_sum + dot(spread.astype(bf16), (xf * from_later).astype(bf16), NT)
        out_t = dot(spread.astype(bf16), (gf * from_state).astype(bf16), NT)
        crossing = dot(spread, jnp.sum(grad * nxt, axis=1, keepdims=True), NN, HI)
        d_decay = (
            dot(out_sum, low, TN, HI) + exact(out_t - direct * step_t, low, NN) + crossing
        )
        d_step = (direct - rate * d_decay) * sig_ref[sub]
        dstep_ref[:, rows] = jnp.concatenate(
            [d_step, jnp.zeros((STEPS - EACH, Q), f32)], axis=0
        ).astype(bf16)


def both_bc(back_ref, pair_ref):
    return (back_ref[:, VW:].astype(f32) + pair_ref[:, VW:].astype(f32)).astype(bf16)


def fetch_blocks(at_ref, offsets, hid_ref, blocks, sems):
    copies = []
    for i in range(blocks.shape[0]):
        lanes = pl.ds(pl.multiple_of(at_ref[14 + offsets[i]] * FEAT, FEAT), FEAT)
        copies.append(pltpu.make_async_copy(hid_ref.at[:, :, lanes], blocks.at[i], sems.at[i]))
        copies[-1].start()
    return copies


def write_terms(copies, blocks, main, steps, outs):
    for i, out_ref in enumerate(outs):
        copies[i].wait()
        block = blocks[i].reshape(-1, FEAT)
        out_ref[:FEAT, :] = dot(block, main, TN).astype(bf16)
        out_ref[FEAT:, :FEAT] = dot(steps, block, NN).astype(bf16)
        out_ref[FEAT:, FEAT:] = jnp.zeros((STEPS, MAIN - FEAT), bf16)


def first_kernel(at_ref, back_ref, pair_ref, own_ref, other_ref, hid_ref, main_ref, steps_ref, *refs):
    outs, blocks, sems = refs[:-2], refs[-2], refs[-1]
    copies = fetch_blocks(at_ref, FIRST, hid_ref, blocks, sems)
    bc = (back_ref[:, VW:].astype(f32) + pair_ref[:, VW:].astype(f32)).astype(bf16)
    main = jnp.concatenate([back_ref[:, :VW], pair_ref[:, :VW], bc], axis=1)
    half = STEPS // 2
    steps = jnp.concatenate(
        [own_ref[...].astype(f32)[:half], other_ref[...].astype(f32)[:half]], axis=0
    ).astype(bf16)
    eye = (iota((STEPS, STATE), 0) == iota((STEPS, STATE), 1)).astype(bf16)
    main_ref[:, :MAIN] = main
    main_ref[:, MAIN:] = dot(steps, eye, TN).astype(bf16)
    steps_ref[...] = steps
    write_terms(copies, blocks, main, steps, outs)


def term_kernel(at_ref, main_ref, steps_ref, hid_ref, *refs):
    outs, blocks, sems = refs[:-2], refs[-2], refs[-1]
    copies = fetch_blocks(at_ref, LATER, hid_ref, blocks, sems)
    write_terms(copies, blocks, main_ref[:, :MAIN], steps_ref[...], outs)


def input_kernel(
    at_ref, main_ref, w_ref, a_ref, b_ref, a_first_ref, b_first_ref, weights, sems
):
    k = pl.program_id(0)
    x_first, y_first = at_ref[6], at_ref[10]

    def fetch(i):
        return pltpu.make_async_copy(
            w_ref.at[:, i * FEAT : (i + 1) * FEAT], weights.at[i, :COLS], sems.at[i]
        )

    @pl.when(k == 0)
    def _():
        for i in range(NZ):
            fetch(i).start()
            weights[i, COLS:] = jnp.zeros((MAIN + STATE - COLS, FEAT), bf16)

    for i in range(NZ):

        @pl.when(k == i)
        def _():
            fetch(i).wait()

    size = a_ref.shape[3]
    total = dot(main_ref[...], weights[k], NN).astype(bf16).reshape(2, 2, size, FEAT)
    x_at, yl_at = k // 2, k % 2
    a_ref[0, 0] = total[:, 0]
    b_ref[:, 0, 0] = total[:, 1]

    @pl.when(x_at == x_first)
    def _():
        a_first_ref[yl_at] = total[:, 0]

    for i in range(2):

        @pl.when(y_first == 2 * i + yl_at)
        def _():
            b_first_ref[x_at] = total[i, 1]


def hop_kernel(hop, final, count, ends, at_ref, *refs):
    x, y = at_ref[0], at_ref[1]
    ins, held, sems = refs[: 2 * count], refs[-2 * count - 1 : -1], refs[-1]
    outs = list(refs[2 * count : -2 * count - 1])
    copies = []
    for i in range(2 * count):
        source = ins[i]
        if hop and i == 1:
            source = source.at[at_ref[6 + hop]]
        if hop and i == 3:
            source = source.at[at_ref[10 + hop]]
        copies.append(pltpu.make_async_copy(source, held[i], sems.at[i]))
        copies[-1].start()
    for i in range(count):
        copies[2 * i].wait()
        copies[2 * i + 1].wait()
        value = (held[2 * i][...].astype(f32) + held[2 * i + 1][...].astype(f32)).astype(bf16)
        if (final and i < 2) or (ends and i >= 2):
            held[2 * i][...] = value
        else:
            outs.pop(0)[...] = value
    if final:
        for i in range(NY):
            at = (y + i) & (NY - 1)
            outs[i][...] = held[0][(at & 1) * 2 + (at >> 1)]
            outs[NY + i][...] = held[2][(x + i) & (NX - 1)]
    if ends:
        half = FEAT // 2
        for i in range(2):
            for j in range(2):
                at = pl.multiple_of(((y >> 1) ^ j) * half, half)
                out_ref = outs[2 * i + j]
                out_ref[:half, :] = held[4 + 2 * i][pl.ds(at, half), :]
                out_ref[half:, :half] = held[4 + 2 * i][FEAT:, pl.ds(at, half)]
                out_ref[half:, half:] = jnp.zeros((STEPS, MAIN - half), bf16)


def close_kernel(at_ref, *refs):
    a_refs, b_refs, keep_ref, give_ref = refs[:NY], refs[NY : NY + NX], refs[-2], refs[-1]
    sums = []
    for parts in (a_refs, b_refs):
        total = parts[0][...].astype(f32)
        for part in parts[1:]:
            total = total + part[...].astype(f32)
        sums.append(total)
    mine = at_ref[5] == 0
    keep_ref[...] = jnp.where(mine, sums[0], sums[1]).astype(bf16)
    give_ref[...] = jnp.where(mine, sums[1], sums[0]).astype(bf16)


def cores_kernel(at_ref, own_ref, pair_ref, out_ref):
    c = at_ref[5]
    for i in range(2):
        part = slice(i * 128, (i + 1) * 128)
        out_ref[:, pl.ds(pl.multiple_of((2 * i + c) * 128, 128), 128)] = own_ref[:, part]
        out_ref[:, pl.ds(pl.multiple_of((2 * i + 1 - c) * 128, 128), 128)] = pair_ref[:, part]


def heads_kernel(at_ref, own_ref, pair_ref, cross_ref, out_ref):
    yh, c = at_ref[4], at_ref[5]

    def to(first, second, value):
        lanes = pl.ds(pl.multiple_of((first * 2 + second) * VW, VW), VW)
        out_ref[:, lanes] = value

    to(yh, c, own_ref[c])
    to(1 - yh, c, pair_ref[c])
    to(yh, 1 - c, cross_ref[0])
    to(1 - yh, 1 - c, cross_ref[1])


def pick(value, at, dim):
    return lax.dynamic_index_in_dim(value, at, dim, False)


def tie(*values):
    return lax.optimization_barrier(values)


FIRST, LATER = (4, 5), (3, 6, 2, 7, 1, 0)
LONG = pl.CostEstimate(flops=10 * 2**30, bytes_accessed=32 * 2**20, transcendentals=0)
TINY = pl.CostEstimate(flops=1024, bytes_accessed=1024, transcendentals=0)


def local(hidden, value_proj, state_proj, step_proj, step_bias, decay_rate, skip_gain, out_grad):
    z, yh, c, x, yl = (lax.axis_index(a) for a in ("z", "yh", "c", "x", "yl"))
    y = yh * 2 + yl
    way = 1 - 2 * c
    tok = hidden.shape[0]
    tokens = 4 * tok
    blocks = tokens // Q

    parts = hidden.reshape(tok, 2, 2, 128)
    keep = pick(parts, c, 2).reshape(tok, FEAT)
    got = swap(pick(parts, 1 - c, 2).reshape(tok, FEAT))
    first = jnp.where(c == 0, keep, got)
    second = jnp.where(c == 0, got, keep)

    value_proj, state_proj, step_proj, first, second = tie(
        value_proj, state_proj, step_proj, first, second
    )
    def x_at(hop):
        return (x - way * hop) % NX

    def y_at(hop):
        return (y - way * hop) % NY

    places = jnp.stack(
        [x, y, z, way, yh, c]
        + [x_at(i) for i in range(1, 5)]
        + [y_at(i) for i in range(1, 5)]
        + [(z + i) % NZ for i in range(NZ)]
    ).astype(jnp.int32)
    heads = jnp.stack(
        [
            lax.dynamic_slice_in_dim(v, (yh * 2 + c) * EACH, EACH, 0)
            for v in (step_bias, decay_rate, skip_gain)
        ],
        axis=1,
    )

    value_t, state_t, step_tr = value_proj.T, state_proj.T, step_proj.T
    none = jnp.zeros((EACH, value_proj.shape[0]), bf16)

    def chosen(which):
        def some(array, wide, core):
            return lax.dynamic_slice_in_dim(array, (which * 2 + core) * wide, wide, 0)

        return jnp.concatenate(
            [
                some(value_t, VW, c), some(value_t, VW, 1 - c), state_t,
                some(step_tr, EACH, c), none, some(step_tr, EACH, 1 - c), none,
            ],
            axis=0,
        )

    mine, theirs = chosen(yh), shift(chosen(1 - yh), "yh", 1, 2)
    chunk = jnp.where(
        yh == 0,
        jnp.concatenate([mine, theirs], axis=1),
        jnp.concatenate([theirs, mine], axis=1),
    )
    def pairwise(own, pair, place, dim):
        return jnp.where(
            place == 0, jnp.stack([own, pair], dim), jnp.stack([pair, own], dim)
        )

    out_grad, chunk = tie(out_grad, chunk)
    cot = out_grad.reshape(tok, 2, 2, VW)
    cot = pairwise(pick(cot, c, 2), swap(pick(cot, 1 - c, 2)), c, 0)

    brought = [lax.all_gather(chunk[:SPLIT], "z")] if SPLIT else []
    ring = chunk[SPLIT:]
    weights = [ring, shift(ring, "z", 1, NZ), shift(ring, "z", -1, NZ)]
    a_blocks = [jnp.stack([first] + [shift(first, ("yh", "yl"), i, NY) for i in range(1, NY)])]
    b_blocks = [jnp.stack([second] + [shift(second, "x", i, NX) for i in range(1, NX)])]
    weights[1], weights[2], a_blocks[0], b_blocks[0], cot = tie(
        weights[1], weights[2], a_blocks[0], b_blocks[0], cot
    )
    cot = pairwise(pick(cot, yh, 2), shift(pick(cot, 1 - yh, 2), "yh", 1, 2), yh, 0)
    cot = cot.reshape(tokens, VW)
    for hop in range(1, 4):
        weights.append(shift(weights[-2], "z", 1, NZ))
        if hop < 3:
            weights.append(shift(weights[-2], "z", -1, NZ))
        a_blocks.append(both_x(a_blocks[-1]))
        b_blocks.append(both_y(b_blocks[-1]))
        if hop == 1:
            a_blocks[-1], b_blocks[-1], cot = tie(a_blocks[-1], b_blocks[-1], cot)
        if hop < 3:
            weights[-1], weights[-2], a_blocks[-1], b_blocks[-1] = tie(
                weights[-1], weights[-2], a_blocks[-1], b_blocks[-1]
            )

    def whole(*shape):
        return pl.BlockSpec(shape, lambda *k: (0,) * len(shape))

    def shaped(dtype, *shape):
        return jax.ShapeDtypeStruct(shape, dtype)

    wide = NZ * FEAT
    in_hbm = pl.BlockSpec(memory_space=pltpu.HBM)
    in_vmem = pl.BlockSpec(memory_space=pltpu.VMEM)
    in_smem = pl.BlockSpec(memory_space=pltpu.SMEM)
    hid, whole_w, p_own, p_send = pl.pallas_call(
        project_kernel,
        in_specs=[in_smem] + [in_hbm] * (NX + NY + NZ + len(brought)),
        out_specs=[in_hbm, in_hbm, in_vmem, in_vmem],
        out_shape=[
            shaped(bf16, 4, tok, wide), shaped(bf16, COLS, wide),
            shaped(f32, tokens, VW), shaped(f32, tokens + 2 * STEPS, VW + BC),
        ],
        scratch_shapes=[
            pltpu.VMEM((4, tok, wide), bf16), pltpu.VMEM((COLS, wide), bf16),
            pltpu.SemaphoreType.DMA((2 * NX * NY + 2 * NZ + 2,)),
        ],
        compiler_params=ALL,
        cost_estimate=LONG,
        name="project",
    )(places, *a_blocks, *b_blocks, *weights, *brought)
    p_recv = swap(p_send)

    states = shaped(f32, blocks, VW, STATE)
    by_lanes = shaped(f32, blocks, EACH, Q)
    packed = shaped(bf16, VW + STEPS, STATE)
    values, bc, step, sig, fresh, seeds, lasts, keep, give = pl.pallas_call(
        state_kernel,
        in_specs=[in_smem] + [in_vmem] * 5,
        out_shape=[
            shaped(bf16, tokens, VW), shaped(bf16, tokens, BC), by_lanes, by_lanes,
            states, states, shaped(f32, VW, blocks), packed, packed,
        ],
        compiler_params=ALL,
        name="states",
    )(places, p_own, p_send, p_recv, cot, heads)

    def along(packed, by):
        pairs = [
            (i * 2 + core, (i + by * (1 - 2 * core)) * 2 + core)
            for i in range(NZ)
            for core in range(2)
            if 0 <= i + by * (1 - 2 * core) < NZ
        ]
        return lax.ppermute(packed, ("z", "c"), pairs)

    def joined(near, far, split=False):
        return pl.pallas_call(
            window_kernel,
            out_shape=[packed] * 2 if split else shaped(bf16, 2, VW + STEPS, STATE),
            compiler_params=vmem(2),
            cost_estimate=TINY,
            name="window",
        )(near, far)

    start = jnp.stack([keep, swap(give)])
    window = joined(along(start, 1), along(start, 2))
    window = joined(window, along(window, 2))
    kept, given = joined(window, along(window, 4), True)
    other_way = swap(given)

    each = 2

    def rows(width):
        return pl.BlockSpec((each * Q, width), lambda k: (k, 0))

    lanes = pl.BlockSpec((each, EACH, Q), lambda k: (k, 0, 0))
    mixed, back, steps = pl.pallas_call(
        scan_kernel,
        grid=(blocks // each,),
        in_specs=[
            in_smem, rows(VW), rows(BC), rows(VW), lanes, lanes, whole(EACH, 3),
            whole(blocks, VW, STATE), whole(blocks, VW, STATE), whole(VW, blocks),
            whole(VW + STEPS, STATE), whole(VW + STEPS, STATE),
        ],
        out_specs=[
            rows(VW), rows(VW + BC), pl.BlockSpec((STEPS, each * Q), lambda k: (0, k)),
        ],
        out_shape=[
            shaped(bf16, tokens, VW), shaped(bf16, tokens, VW + BC), shaped(bf16, STEPS, tokens),
        ],
        scratch_shapes=[
            pltpu.VMEM((blocks + 1, VW, STATE), f32), pltpu.VMEM((blocks, VW, STATE), f32),
        ],
        compiler_params=ALL,
        name="scan",
    )(
        places, values, bc, cot, step, sig, heads, fresh, seeds, lasts, kept, other_way,
    )

    back_pair, steps_pair = swap(back), swap(steps)

    def fetched(count):
        return [pltpu.VMEM((count, 4, tok, FEAT), bf16), pltpu.SemaphoreType.DMA((count,))]

    grad_block = shaped(bf16, FEAT + STEPS, MAIN)
    main, both_steps, up, down = pl.pallas_call(
        first_kernel,
        in_specs=[in_smem] + [in_vmem] * 4 + [in_hbm],
        out_shape=[shaped(bf16, tokens, MAIN + STATE), shaped(bf16, STEPS, tokens)]
        + [grad_block] * 2,
        scratch_shapes=fetched(2),
        compiler_params=ALL,
        cost_estimate=TINY,
        name="first",
    )(places, back, back_pair, steps, steps_pair, hid)
    add_3, add_6, add_2, add_7, add_1, add_0 = pl.pallas_call(
        term_kernel,
        in_specs=[in_smem, in_vmem, in_vmem, in_hbm],
        out_shape=[grad_block] * 6,
        scratch_shapes=fetched(6),
        compiler_params=ALL,
        cost_estimate=LONG,
        name="term",
    )(places, main, both_steps, hid)

    def add_hop(hop, *tables):
        final = hop == 3
        wide_block, block = (NX, tok, FEAT), (tok, FEAT)
        grad = (FEAT + STEPS, MAIN)
        count = len(tables) // 2
        ends = hop == 1
        shapes = ([wide_block] * 4 if hop else []) + [grad] * (len(tables) - (4 if hop else 0))
        outs = [shape for shape in shapes[::2]]
        if final:
            outs = [block] * (NX + NY)
        if ends:
            outs = [wide_block] * 2 + [(FEAT // 2 + STEPS, MAIN)] * 4
        return pl.pallas_call(
            lambda *refs: hop_kernel(hop, final, count, ends, *refs),
            in_specs=[in_smem] + [in_hbm] * len(tables),
            out_shape=[shaped(bf16, *shape) for shape in outs],
            scratch_shapes=[pltpu.VMEM(shape, bf16) for shape in shapes]
            + [pltpu.SemaphoreType.DMA((len(tables),))],
            compiler_params=ALL,
            cost_estimate=TINY,
            name="hop",
        )(places, *tables)

    def ring_on(up, down):
        return shift(up, "z", 1, NZ), shift(down, "z", -1, NZ)

    come_up, come_down = ring_on(up, down)
    up, down = add_hop(0, come_up, add_3, come_down, add_6)
    up, down, main = tie(up, down, main)
    come_up, come_down = ring_on(up, down)

    def more(sums, *parts):
        total = sums.astype(f32)
        for part in parts:
            total = total + part.astype(f32)
        return total

    a_part, b_part, a_sum, b_sum = pl.pallas_call(
        input_kernel,
        grid=(NZ,),
        in_specs=[in_smem, whole(tokens, MAIN + STATE), in_hbm],
        out_specs=[
            pl.BlockSpec((1, 1, 2, tok, FEAT), lambda k: (k // 2, k % 2, 0, 0, 0)),
            pl.BlockSpec((2, 1, 1, tok, FEAT), lambda k: (0, k % 2, k // 2, 0, 0)),
            whole(2, 2, tok, FEAT), whole(NX, tok, FEAT),
        ],
        out_shape=[
            shaped(bf16, NX, 2, 2, tok, FEAT), shaped(bf16, 2, 2, NX, tok, FEAT),
            shaped(bf16, 2, 2, tok, FEAT), shaped(bf16, NX, tok, FEAT),
        ],
        scratch_shapes=[
            pltpu.VMEM((NZ, MAIN + STATE, FEAT), bf16), pltpu.SemaphoreType.DMA((NZ,)),
        ],
        compiler_params=ALL,
        cost_estimate=LONG,
        name="input",
    )(places, main, whole_w)
    mixed = mixed.reshape(2, 2, tok, VW)
    heads_own = pick(mixed, yh, 0)
    pair = shift(pick(mixed, 1 - yh, 0), "yh", 1, 2)
    a_sum, b_sum, pair, come_up, come_down = tie(a_sum, b_sum, pair, come_up, come_down)
    up, down = add_hop(0, come_up, add_2, come_down, add_7)
    crossed = swap(jnp.stack([pick(heads_own, 1 - c, 0), pick(pair, 1 - c, 0)]))
    a_part = a_part.reshape(NX, NY, tok, FEAT)
    b_part = b_part.reshape(NY, NX, tok, FEAT)
    a_sum = a_sum.reshape(NY, tok, FEAT)

    come_up, come_down = ring_on(up, down)
    a_sum, b_sum, *ends = add_hop(
        1, both_x(a_sum), a_part, both_y(b_sum), b_part, come_up, add_1, come_down, add_0
    )
    a_sum, b_sum, crossed = tie(a_sum, b_sum, crossed)
    mixer_out = pl.pallas_call(
        heads_kernel,
        in_specs=[in_smem, in_vmem, in_vmem, in_vmem],
        out_shape=shaped(bf16, tok, 4 * VW),
        compiler_params=vmem(4),
        cost_estimate=TINY,
        name="by_head",
    )(places, heads_own, pair, crossed)
    across = [(2 * i + j, 2 * ((i + 1) % NZ) + 1 - j) for i in range(NZ) for j in range(2)]
    own = more(ends[2], shift(ends[0], "z", 1, NZ))
    other = more(
        shift(ends[3], "yh", 1, 2), lax.ppermute(ends[1], ("z", "yh"), across)
    )
    a_sum, b_sum = add_hop(2, both_x(a_sum), a_part, both_y(b_sum), b_part)
    last = add_hop(3, both_x(a_sum), a_part, both_y(b_sum), b_part)
    a_last = [last[0]] + [shift(last[i], ("yh", "yl"), i, NY) for i in range(1, NY)]
    b_last = [last[NY]] + [shift(last[NY + i], "x", i, NX) for i in range(1, NX)]
    keep, give = pl.pallas_call(
        close_kernel,
        in_specs=[in_smem] + [in_vmem] * (NX + NY),
        out_shape=[shaped(bf16, tok, FEAT)] * 2,
        compiler_params=vmem(4),
        cost_estimate=TINY,
        name="close",
    )(places, *a_last, *b_last)
    hidden_grad = pl.pallas_call(
        cores_kernel,
        in_specs=[in_smem, in_vmem, in_vmem],
        out_shape=shaped(bf16, tok, 2 * FEAT),
        compiler_params=vmem(3),
        cost_estimate=TINY,
        name="by_core",
    )(places, keep, swap(give))

    half = FEAT // 2
    own_step, other_step = own[half:, :half], other[half:, :half]
    own, other = own[:half], other[:half]
    state_grad = own[:, 2 * VW :] + other[:, 2 * VW :]

    def ordered(own, other, wide, gap):
        def cores(value):
            mine, pair = value[:, :wide], value[:, gap : gap + wide]
            return jnp.where(
                c == 0,
                jnp.concatenate([mine, pair], axis=1),
                jnp.concatenate([pair, mine], axis=1),
            )

        own, other = cores(own), cores(other)
        return jnp.where(
            yh == 0,
            jnp.concatenate([own, other], axis=1),
            jnp.concatenate([other, own], axis=1),
        )

    value_grad = ordered(own, other, VW, VW)
    step_grad = ordered(own_step.T, other_step.T, EACH, STEPS // 2)
    return mixer_out, hidden_grad, value_grad, state_grad, step_grad


def solution(mesh):
    fine = Mesh(mesh.devices.reshape(NZ, 2, 2, NX, 2), ("z", "yh", "c", "x", "yl"))
    split = P(("z", "yh", "c"), ("x", "yl"))
    by_head = P(("x", "yl"))
    return jax.shard_map(
        local,
        mesh=fine,
        in_specs=(split,) * 4 + (by_head,) * 3 + (split,),
        out_specs=(split,) * 5,
        check_vma=False,
    )
```

```python
import jax
import jax.numpy as jnp
from jax import lax
from jax.experimental import pallas as pl
from jax.experimental.pallas import tpu as pltpu
from jax.sharding import Mesh, PartitionSpec as P

HEAD_DIM = 64
STATE = 128
Q = 128
EACH = 4
VW = EACH * HEAD_DIM
BC = 2 * STATE
MAIN = 2 * VW + BC
STEPS = 16
COLS = MAIN + STEPS
FEAT = 256
NZ, NX, NY = 8, 4, 4
SPLIT = 0
f32, bf16 = jnp.float32, jnp.bfloat16
HI = lax.Precision.HIGHEST


def vmem(mebibytes):
    return pltpu.CompilerParams(vmem_limit_bytes=mebibytes * 1024 * 1024)


ALL = vmem(60)


def shift(value, axis, by, count, wrap=True):
    pairs = [(i, (i + by) % count) for i in range(count) if wrap or 0 <= i + by < count]
    return lax.ppermute(value, axis, pairs)


def both_x(value):
    pairs = [(c * NX + i, c * NX + (i + 1 - 2 * c) % NX) for c in range(2) for i in range(NX)]
    return lax.ppermute(value, ("c", "x"), pairs)


def both_y(value):
    def at(c, y):
        return (y // 2) * 4 + c * 2 + y % 2

    pairs = [(at(c, y), at(c, (y + 1 - 2 * c) % NY)) for c in range(2) for y in range(NY)]
    return lax.ppermute(value, ("yh", "c", "yl"), pairs)


def swap(value):
    return shift(value, "c", 1, 2)


def dot(left, right, dims, precision=None):
    return lax.dot_general(
        left, right, (dims, ((), ())), preferred_element_type=f32, precision=precision
    )


NN, NT, TN = ((1,), (0,)), ((1,), (1,)), ((0,), (0,))


def iota(shape, dim):
    return lax.broadcasted_iota(jnp.int32, shape, dim)


def consts():
    low = (iota((Q, Q), 0) >= iota((Q, Q), 1)).astype(f32)
    spread = (iota((EACH, VW), 1) // HEAD_DIM == iota((EACH, VW), 0)).astype(f32)
    return low, spread


def pieces(rows):
    high = rows.astype(bf16).astype(f32)
    mid = (rows - high).astype(bf16).astype(f32)
    return jnp.concatenate([high, mid, rows - high - mid], axis=0).astype(bf16)


def exact(rows, right, dims):
    n = rows.shape[0]
    out = dot(pieces(rows), right.astype(bf16), dims)
    return out[:n] + out[n : 2 * n] + out[2 * n :]


def widen(rows, right):
    right = right.astype(bf16)
    return dot(pieces(rows), jnp.concatenate([right] * 3, axis=0), TN)


def project_kernel(at_ref, *refs):
    x, y, z, way = (at_ref[i] for i in range(4))
    a_refs, b_refs, w_refs = refs[:NX], refs[NX : NX + NY], refs[NX + NY : NX + NY + NZ]
    hid_out, w_out, own_ref, send_ref, hid, weights, sems = refs[-7:]
    tok = hid.shape[1]
    copies = []

    def copy(source, target):
        copies.append(pltpu.make_async_copy(source, target, sems.at[len(copies)]))
        copies[-1].start()

    def place(source, x_at, y_at, core):
        x_at, y_at = x_at & (NX - 1), y_at & (NY - 1)
        lanes = pl.ds(pl.multiple_of((2 * x_at + (y_at & 1)) * FEAT, FEAT), FEAT)
        copy(source, hid.at[(y_at >> 1) * 2 + core, :, lanes])

    for j in range(NX):
        for i in range(NY):
            place(a_refs[j].at[i], x - way * j, y - i, 0)
            place(b_refs[i].at[j], x - j, y - way * i, 1)
    for i in range(NZ):
        z_at = (z + offset(i)) & (NZ - 1)
        lanes = pl.ds(pl.multiple_of(z_at * FEAT, FEAT), FEAT)
        copy(w_refs[i], weights.at[SPLIT:, lanes])
        if SPLIT:
            part_ref = refs[NX + NY + NZ]
            copy(part_ref.at[i], weights.at[:SPLIT, i * FEAT : (i + 1) * FEAT])
    for one in copies:
        one.wait()
    hid_back = pltpu.make_async_copy(hid, hid_out, sems.at[len(copies)])
    w_back = pltpu.make_async_copy(weights, w_out, sems.at[len(copies) + 1])
    hid_back.start()
    w_back.start()
    block = hid[...].reshape(4 * tok, NZ * FEAT)
    send_ref[: 4 * tok, VW:] = dot(block, weights[2 * VW : MAIN, :], NT)
    send_ref[: 4 * tok, :VW] = dot(block, weights[VW : 2 * VW, :], NT)
    steps = dot(weights[MAIN:, :], block, NT)
    send_ref[4 * tok : 4 * tok + STEPS, :] = steps[:, : 2 * tok]
    send_ref[4 * tok + STEPS :, :] = steps[:, 2 * tok :]
    own_ref[...] = dot(block, weights[:VW, :], NT)
    hid_back.wait()
    w_back.wait()


def offset(i):
    return i // 2 if i % 2 == 0 else -(i + 1) // 2


def state_kernel(
    at_ref, own_ref, send_ref, recv_ref, g_ref, head_ref,
    x_ref, bc_ref, step_ref, sig_ref, fresh_ref, seed_ref, last_ref, keep_ref, give_ref,
):
    tokens = x_ref.shape[0]
    count = tokens // Q
    low, spread = consts()
    bias, rate = head_ref[:, 0:1], head_ref[:, 1:2]
    pre = []
    for i in range(2):
        base = tokens + i * STEPS
        mine = send_ref[base : base + EACH, :]
        pair = recv_ref[base + STEPS // 2 : base + STEPS // 2 + EACH, :]
        rows = mine + pair + bias
        pre += [rows[:, k * Q : (k + 1) * Q] for k in range(rows.shape[1] // Q)]
    pre = jnp.concatenate(pre, axis=0)
    small = jnp.exp(-jnp.abs(pre))
    above = 1.0 + small
    log_above = jnp.where(
        above == 1.0, small, jnp.log(above) * (small / jnp.where(above == 1.0, 1.0, above - 1.0))
    )
    step = jnp.maximum(pre, 0.0) + log_above
    sig = jnp.where(pre >= 0.0, 1.0, small) / above
    for k in range(count):
        step_ref[k] = step[k * EACH : (k + 1) * EACH]
        sig_ref[k] = sig[k * EACH : (k + 1) * EACH]
    cum = exact(-step * jnp.concatenate([rate] * count, axis=0), low, NT)
    twice = jnp.concatenate(
        [jnp.concatenate([spread, jnp.zeros_like(spread)], axis=1),
         jnp.concatenate([jnp.zeros_like(spread), spread], axis=1)], axis=0)
    lane = iota((EACH, count), 1)
    ends = jnp.zeros((EACH, count), f32)
    for k in range(count):
        rows = slice(k * Q, (k + 1) * Q)
        x = (own_ref[rows, :] + recv_ref[rows, :VW]).astype(bf16)
        bc = (send_ref[rows, VW:] + recv_ref[rows, VW:]).astype(bf16)
        x_ref[rows, :] = x
        bc_ref[rows, :] = bc
        here = cum[k * EACH : (k + 1) * EACH]
        last = here[:, Q - 1 :]
        ends = ends + jnp.where(lane == k, last, 0.0)
        rest = jnp.exp(last - here) * step[k * EACH : (k + 1) * EACH]
        both = widen(jnp.concatenate([rest, jnp.exp(here)], axis=0), twice)
        tail = (x.astype(f32) * both[:, :VW]).astype(bf16)
        grown = (g_ref[rows, :].astype(f32) * both[:, VW:]).astype(bf16)
        fresh_ref[k] = dot(tail, bc[:, :STATE], TN)
        seed_ref[k] = dot(grown, bc[:, STATE:], TN)
    lasts = dot(spread, jnp.exp(ends), TN, HI)
    last_ref[...] = lasts
    state = jnp.zeros((VW, STATE), f32)
    grad = jnp.zeros((VW, STATE), f32)
    for k in range(count):
        state = lasts[:, k : k + 1] * state + fresh_ref[k]
        back = count - 1 - k
        grad = lasts[:, back : back + 1] * grad + seed_ref[back]
    eye = (iota((EACH, STATE), 0) == iota((EACH, STATE), 1)).astype(f32)
    total = jnp.exp(jnp.sum(ends, axis=1, keepdims=True))
    parts = split_decay(dot(jnp.broadcast_to(total, (EACH, STEPS)), eye, TN, HI)).astype(bf16)
    up_core = at_ref[5] == 0
    keep_ref[:VW] = jnp.where(up_core, state, grad).astype(bf16)
    give_ref[:VW] = jnp.where(up_core, grad, state).astype(bf16)
    keep_ref[VW:] = parts
    give_ref[VW:] = parts


def split_decay(decay):
    high = decay.astype(bf16).astype(f32)
    mid = (decay - high).astype(bf16).astype(f32)
    least = decay - high - mid
    row = iota((STEPS, STATE), 0)
    return jnp.where(row == 0, high, jnp.where(row == 1, mid, jnp.where(row == 2, least, 0.0)))


def window_kernel(near_ref, far_ref, *out_refs):
    spread = (iota((VW, STATE), 0) // HEAD_DIM == iota((VW, STATE), 1)).astype(bf16)
    for i in range(2):
        out_ref = out_refs[i] if len(out_refs) == 2 else out_refs[0].at[i]
        near = near_ref[i, VW:]
        column = jnp.sum(dot(spread, near, NT), axis=1, keepdims=True)
        out_ref[:VW] = (
            near_ref[i, :VW].astype(f32) + column * far_ref[i, :VW].astype(f32)
        ).astype(bf16)
        decay = jnp.sum(near.astype(f32), axis=0, keepdims=True) * jnp.sum(
            far_ref[i, VW:].astype(f32), axis=0, keepdims=True
        )
        out_ref[VW:] = split_decay(jnp.broadcast_to(decay, (STEPS, STATE))).astype(bf16)


def scan_kernel(
    at_ref, x_ref, bc_ref, g_ref, step_ref, sig_ref, head_ref,
    fresh_ref, seed_ref, last_ref, kept_ref, other_ref,
    y_ref, back_ref, dstep_ref, held, grads,
):
    at = pl.program_id(0)
    count = fresh_ref.shape[0]

    @pl.when(at == 0)
    def _():
        lasts = last_ref[...]
        kept, other = kept_ref[:VW].astype(f32), other_ref[:VW].astype(f32)
        up_core = at_ref[5] == 0
        state, grad = jnp.where(up_core, kept, other), jnp.where(up_core, other, kept)
        for k in range(count):
            held[k] = state
            state = lasts[:, k : k + 1] * state + fresh_ref[k]
            back = count - 1 - k
            grads[back] = grad
            grad = lasts[:, back : back + 1] * grad + seed_ref[back]
        held[count] = state

    low, spread = consts()
    mask = low > 0.0
    zero = jnp.zeros_like(spread)
    twice = jnp.concatenate(
        [jnp.concatenate([spread, zero], axis=1), jnp.concatenate([zero, spread], axis=1)], axis=0)
    lane = iota((Q, EACH), 1)
    row = iota((EACH, Q), 0)
    rate = head_ref[:, 1:2]
    gain_wide = jnp.sum(head_ref[:, 2:3] * spread, axis=0, keepdims=True)
    for sub in range(step_ref.shape[0]):
        k = at * step_ref.shape[0] + sub
        rows = slice(sub * Q, (sub + 1) * Q)
        step_t = step_ref[sub]
        cum_t = exact(-step_t * rate, low, NT)
        both_wide = widen(jnp.concatenate([cum_t, step_t], axis=0), twice)
        cum_wide, step_wide = both_wide[:, :VW], both_wide[:, VW:]
        growth = jnp.exp(cum_wide)
        rest = jnp.exp(cum_wide[Q - 1 :, :] - cum_wide)
        x, g = x_ref[rows, :], g_ref[rows, :]
        xf, gf = x.astype(f32), g.astype(f32)
        b_mat, c_mat = bc_ref[rows, :STATE], bc_ref[rows, STATE:]
        state, nxt, grad = held[k], held[k + 1], grads[k]
        state_b, grad_b = state.astype(bf16), grad.astype(bf16)

        scores = jnp.where(mask, dot(c_mat, b_mat, NT), 0.0)
        mixed, moved = [], []
        pairs = jnp.zeros((Q, Q), f32)
        out_sum = jnp.zeros((Q, EACH), f32)
        in_sum = jnp.zeros((EACH, Q), f32)
        for e in range(EACH):
            cut = slice(e * HEAD_DIM, (e + 1) * HEAD_DIM)
            first = slice(e * HEAD_DIM, e * HEAD_DIM + 1)
            fade = jnp.exp(jnp.minimum(cum_wide[:, first] - cum_t[e : e + 1, :], 0.0))
            weight = scores * fade
            step_row = step_t[e : e + 1, :]
            mixing = (weight * step_row).astype(bf16)
            mixed.append(dot(mixing, x[:, cut], NN))
            moved.append(dot(mixing, g[:, cut], TN))
            outer = dot(g[:, cut], x[:, cut], NT)
            pairs = pairs + outer * fade * step_row
            both = weight * outer
            in_sum = in_sum + jnp.where(row == e, jnp.sum(both, axis=0, keepdims=True), 0.0)
            out_sum = out_sum + jnp.where(
                lane == e, jnp.sum(both * step_row, axis=1, keepdims=True), 0.0
            )
        pairs = jnp.where(mask, pairs, 0.0).astype(bf16)

        from_state = growth * dot(c_mat, state_b, NT)
        from_later = rest * dot(b_mat, grad_b, NT)
        y_ref[rows, :] = (
            jnp.concatenate(mixed, axis=1) + from_state + gain_wide * xf
        ).astype(bf16)
        back_ref[rows, :VW] = (
            jnp.concatenate(moved, axis=1) + step_wide * from_later + gain_wide * gf
        ).astype(bf16)
        back_ref[rows, VW : VW + STATE] = (
            dot(pairs, c_mat, TN) + dot((xf * (rest * step_wide)).astype(bf16), grad_b, NN)
        ).astype(bf16)
        back_ref[rows, VW + STATE :] = (
            dot(pairs, b_mat, NN) + dot((gf * growth).astype(bf16), state_b, NN)
        ).astype(bf16)

        direct = in_sum + dot(spread.astype(bf16), (xf * from_later).astype(bf16), NT)
        out_t = dot(spread.astype(bf16), (gf * from_state).astype(bf16), NT)
        crossing = dot(spread, jnp.sum(grad * nxt, axis=1, keepdims=True), NN, HI)
        d_decay = (
            dot(out_sum, low, TN, HI) + exact(out_t - direct * step_t, low, NN) + crossing
        )
        d_step = (direct - rate * d_decay) * sig_ref[sub]
        dstep_ref[:, rows] = jnp.concatenate(
            [d_step, jnp.zeros((STEPS - EACH, Q), f32)], axis=0
        ).astype(bf16)


def both_bc(back_ref, pair_ref):
    return (back_ref[:, VW:].astype(f32) + pair_ref[:, VW:].astype(f32)).astype(bf16)


def fetch_blocks(at_ref, offsets, hid_ref, blocks, sems):
    copies = []
    for i in range(blocks.shape[0]):
        lanes = pl.ds(pl.multiple_of(at_ref[14 + offsets[i]] * FEAT, FEAT), FEAT)
        copies.append(pltpu.make_async_copy(hid_ref.at[:, :, lanes], blocks.at[i], sems.at[i]))
        copies[-1].start()
    return copies


def write_terms(copies, blocks, main, steps, outs):
    for i, out_ref in enumerate(outs):
        copies[i].wait()
        block = blocks[i].reshape(-1, FEAT)
        out_ref[:FEAT, :] = dot(block, main, TN).astype(bf16)
        out_ref[FEAT:, :FEAT] = dot(steps, block, NN).astype(bf16)
        out_ref[FEAT:, FEAT:] = jnp.zeros((STEPS, MAIN - FEAT), bf16)


def first_kernel(at_ref, back_ref, pair_ref, own_ref, other_ref, hid_ref, main_ref, steps_ref, *refs):
    outs, blocks, sems = refs[:-2], refs[-2], refs[-1]
    copies = fetch_blocks(at_ref, FIRST, hid_ref, blocks, sems)
    bc = (back_ref[:, VW:].astype(f32) + pair_ref[:, VW:].astype(f32)).astype(bf16)
    main = jnp.concatenate([back_ref[:, :VW], pair_ref[:, :VW], bc], axis=1)
    half = STEPS // 2
    steps = jnp.concatenate(
        [own_ref[...].astype(f32)[:half], other_ref[...].astype(f32)[:half]], axis=0
    ).astype(bf16)
    eye = (iota((STEPS, STATE), 0) == iota((STEPS, STATE), 1)).astype(bf16)
    main_ref[:, :MAIN] = main
    main_ref[:, MAIN:] = dot(steps, eye, TN).astype(bf16)
    steps_ref[...] = steps
    write_terms(copies, blocks, main, steps, outs)


def term_kernel(at_ref, main_ref, steps_ref, hid_ref, *refs):
    outs, blocks, sems = refs[:-2], refs[-2], refs[-1]
    copies = fetch_blocks(at_ref, LATER, hid_ref, blocks, sems)
    write_terms(copies, blocks, main_ref[:, :MAIN], steps_ref[...], outs)


def input_kernel(
    at_ref, main_ref, w_ref, a_ref, b_ref, a_first_ref, b_first_ref, weights, sems
):
    k = pl.program_id(0)
    x_first, y_first = at_ref[6], at_ref[10]

    def fetch(i):
        return pltpu.make_async_copy(
            w_ref.at[:, i * FEAT : (i + 1) * FEAT], weights.at[i, :COLS], sems.at[i]
        )

    @pl.when(k == 0)
    def _():
        for i in range(NZ):
            fetch(i).start()
            weights[i, COLS:] = jnp.zeros((MAIN + STATE - COLS, FEAT), bf16)

    for i in range(NZ):

        @pl.when(k == i)
        def _():
            fetch(i).wait()

    size = a_ref.shape[3]
    total = dot(main_ref[...], weights[k], NN).astype(bf16).reshape(2, 2, size, FEAT)
    x_at, yl_at = k // 2, k % 2
    a_ref[0, 0] = total[:, 0]
    b_ref[:, 0, 0] = total[:, 1]

    @pl.when(x_at == x_first)
    def _():
        a_first_ref[yl_at] = total[:, 0]

    for i in range(2):

        @pl.when(y_first == 2 * i + yl_at)
        def _():
            b_first_ref[x_at] = total[i, 1]


def hop_kernel(hop, final, at_ref, *refs):
    count = 4
    x, y = at_ref[0], at_ref[1]
    ins, held, sems = refs[: 2 * count], refs[-2 * count - 1 : -1], refs[-1]
    outs = list(refs[2 * count : -2 * count - 1])
    copies = []
    for i in range(2 * count):
        source = ins[i]
        if i == 1:
            source = source.at[at_ref[6 + hop]]
        if i == 3:
            source = source.at[at_ref[10 + hop]]
        copies.append(pltpu.make_async_copy(source, held[i], sems.at[i]))
        copies[-1].start()
    for i in range(count):
        copies[2 * i].wait()
        copies[2 * i + 1].wait()
        value = (held[2 * i][...].astype(f32) + held[2 * i + 1][...].astype(f32)).astype(bf16)
        if final:
            held[2 * i][...] = value
        else:
            outs.pop(0)[...] = value
    if final:
        for i in range(NY):
            at = (y + i) & (NY - 1)
            outs[i][...] = held[0][(at & 1) * 2 + (at >> 1)]
            outs[NY + i][...] = held[2][(x + i) & (NX - 1)]
        half = FEAT // 2
        for i in range(2):
            for j in range(2):
                at = pl.multiple_of(((y >> 1) ^ j) * half, half)
                out_ref = outs[2 * i + j - 4]
                out_ref[:half, :] = held[4 + 2 * i][pl.ds(at, half), :]
                out_ref[half:, :half] = held[4 + 2 * i][FEAT:, pl.ds(at, half)]
                out_ref[half:, half:] = jnp.zeros((STEPS, MAIN - half), bf16)


def close_kernel(at_ref, *refs):
    a_refs, b_refs, keep_ref, give_ref = refs[:NY], refs[NY : NY + NX], refs[-2], refs[-1]
    sums = []
    for parts in (a_refs, b_refs):
        total = parts[0][...].astype(f32)
        for part in parts[1:]:
            total = total + part[...].astype(f32)
        sums.append(total)
    mine = at_ref[5] == 0
    keep_ref[...] = jnp.where(mine, sums[0], sums[1]).astype(bf16)
    give_ref[...] = jnp.where(mine, sums[1], sums[0]).astype(bf16)


def cores_kernel(at_ref, own_ref, pair_ref, out_ref):
    c = at_ref[5]
    for i in range(2):
        part = slice(i * 128, (i + 1) * 128)
        out_ref[:, pl.ds(pl.multiple_of((2 * i + c) * 128, 128), 128)] = own_ref[:, part]
        out_ref[:, pl.ds(pl.multiple_of((2 * i + 1 - c) * 128, 128), 128)] = pair_ref[:, part]


def heads_kernel(at_ref, own_ref, pair_ref, cross_ref, out_ref):
    yh, c = at_ref[4], at_ref[5]

    def to(first, second, value):
        lanes = pl.ds(pl.multiple_of((first * 2 + second) * VW, VW), VW)
        out_ref[:, lanes] = value

    to(yh, c, own_ref[c])
    to(1 - yh, c, pair_ref[c])
    to(yh, 1 - c, cross_ref[0])
    to(1 - yh, 1 - c, cross_ref[1])


def pick(value, at, dim):
    return lax.dynamic_index_in_dim(value, at, dim, False)


def tie(*values):
    return lax.optimization_barrier(values)


FIRST, LATER = (4, 5), (3, 6, 2, 7, 1, 0)
LONG = pl.CostEstimate(flops=10 * 2**30, bytes_accessed=32 * 2**20, transcendentals=0)
TINY = pl.CostEstimate(flops=1024, bytes_accessed=1024, transcendentals=0)


def local(hidden, value_proj, state_proj, step_proj, step_bias, decay_rate, skip_gain, out_grad):
    z, yh, c, x, yl = (lax.axis_index(a) for a in ("z", "yh", "c", "x", "yl"))
    y = yh * 2 + yl
    way = 1 - 2 * c
    tok = hidden.shape[0]
    tokens = 4 * tok
    blocks = tokens // Q

    def x_at(hop):
        return (x - way * hop) % NX

    def y_at(hop):
        return (y - way * hop) % NY

    places = jnp.stack(
        [x, y, z, way, yh, c]
        + [x_at(i) for i in range(1, 5)]
        + [y_at(i) for i in range(1, 5)]
        + [(z + i) % NZ for i in range(NZ)]
    ).astype(jnp.int32)
    heads = jnp.stack(
        [
            lax.dynamic_slice_in_dim(v, (yh * 2 + c) * EACH, EACH, 0)
            for v in (step_bias, decay_rate, skip_gain)
        ],
        axis=1,
    )

    value_t, state_t, step_tr = value_proj.T, state_proj.T, step_proj.T
    none = jnp.zeros((EACH, value_proj.shape[0]), bf16)

    def chosen(which):
        def some(array, wide, core):
            return lax.dynamic_slice_in_dim(array, (which * 2 + core) * wide, wide, 0)

        return jnp.concatenate(
            [
                some(value_t, VW, c), some(value_t, VW, 1 - c), state_t,
                some(step_tr, EACH, c), none, some(step_tr, EACH, 1 - c), none,
            ],
            axis=0,
        )

    hidden, given = tie(hidden, chosen(1 - yh))
    mine, theirs = chosen(yh), shift(given, "yh", 1, 2)
    chunk = jnp.where(
        yh == 0,
        jnp.concatenate([mine, theirs], axis=1),
        jnp.concatenate([theirs, mine], axis=1),
    )
    parts = hidden.reshape(tok, 2, 2, 128)
    keep = pick(parts, c, 2).reshape(tok, FEAT)
    got = swap(pick(parts, 1 - c, 2).reshape(tok, FEAT))
    first = jnp.where(c == 0, keep, got)
    second = jnp.where(c == 0, got, keep)

    def pairwise(own, pair, place, dim):
        return jnp.where(
            place == 0, jnp.stack([own, pair], dim), jnp.stack([pair, own], dim)
        )

    out_grad, chunk = tie(out_grad, chunk)
    cot = out_grad.reshape(tok, 2, 2, VW)
    cot = pairwise(pick(cot, c, 2), swap(pick(cot, 1 - c, 2)), c, 0)

    brought = [lax.all_gather(chunk[:SPLIT], "z")] if SPLIT else []
    ring = chunk[SPLIT:]
    weights = [ring, shift(ring, "z", 1, NZ), shift(ring, "z", -1, NZ)]
    a_blocks = [jnp.stack([first] + [shift(first, ("yh", "yl"), i, NY) for i in range(1, NY)])]
    b_blocks = [jnp.stack([second] + [shift(second, "x", i, NX) for i in range(1, NX)])]
    weights[1], weights[2], a_blocks[0], b_blocks[0], cot = tie(
        weights[1], weights[2], a_blocks[0], b_blocks[0], cot
    )
    cot = pairwise(pick(cot, yh, 2), shift(pick(cot, 1 - yh, 2), "yh", 1, 2), yh, 0)
    cot = cot.reshape(tokens, VW)
    for hop in range(1, 4):
        weights.append(shift(weights[-2], "z", 1, NZ))
        if hop < 3:
            weights.append(shift(weights[-2], "z", -1, NZ))
        a_blocks.append(both_x(a_blocks[-1]))
        b_blocks.append(both_y(b_blocks[-1]))
        if hop == 1:
            a_blocks[-1], b_blocks[-1], cot = tie(a_blocks[-1], b_blocks[-1], cot)
        if hop < 3:
            weights[-1], weights[-2], a_blocks[-1], b_blocks[-1] = tie(
                weights[-1], weights[-2], a_blocks[-1], b_blocks[-1]
            )

    def whole(*shape):
        return pl.BlockSpec(shape, lambda *k: (0,) * len(shape))

    def shaped(dtype, *shape):
        return jax.ShapeDtypeStruct(shape, dtype)

    wide = NZ * FEAT
    in_hbm = pl.BlockSpec(memory_space=pltpu.HBM)
    in_vmem = pl.BlockSpec(memory_space=pltpu.VMEM)
    in_smem = pl.BlockSpec(memory_space=pltpu.SMEM)
    hid, whole_w, p_own, p_send = pl.pallas_call(
        project_kernel,
        in_specs=[in_smem] + [in_hbm] * (NX + NY + NZ + len(brought)),
        out_specs=[in_hbm, in_hbm, in_vmem, in_vmem],
        out_shape=[
            shaped(bf16, 4, tok, wide), shaped(bf16, COLS, wide),
            shaped(f32, tokens, VW), shaped(f32, tokens + 2 * STEPS, VW + BC),
        ],
        scratch_shapes=[
            pltpu.VMEM((4, tok, wide), bf16), pltpu.VMEM((COLS, wide), bf16),
            pltpu.SemaphoreType.DMA((2 * NX * NY + 2 * NZ + 2,)),
        ],
        compiler_params=ALL,
        cost_estimate=LONG,
        name="project",
    )(places, *a_blocks, *b_blocks, *weights, *brought)
    p_recv = swap(p_send)

    states = shaped(f32, blocks, VW, STATE)
    by_lanes = shaped(f32, blocks, EACH, Q)
    packed = shaped(bf16, VW + STEPS, STATE)
    values, bc, step, sig, fresh, seeds, lasts, keep, give = pl.pallas_call(
        state_kernel,
        in_specs=[in_smem] + [in_vmem] * 5,
        out_shape=[
            shaped(bf16, tokens, VW), shaped(bf16, tokens, BC), by_lanes, by_lanes,
            states, states, shaped(f32, VW, blocks), packed, packed,
        ],
        compiler_params=ALL,
        name="states",
    )(places, p_own, p_send, p_recv, cot, heads)

    def along(packed, by):
        pairs = [
            (i * 2 + core, (i + by * (1 - 2 * core)) * 2 + core)
            for i in range(NZ)
            for core in range(2)
            if 0 <= i + by * (1 - 2 * core) < NZ
        ]
        return lax.ppermute(packed, ("z", "c"), pairs)

    def joined(near, far, split=False):
        return pl.pallas_call(
            window_kernel,
            out_shape=[packed] * 2 if split else shaped(bf16, 2, VW + STEPS, STATE),
            compiler_params=vmem(2),
            cost_estimate=TINY,
            name="window",
        )(near, far)

    start = jnp.stack([keep, swap(give)])
    window = joined(along(start, 1), along(start, 2))
    window = joined(window, along(window, 2))
    kept, given = joined(window, along(window, 4), True)
    other_way = swap(given)

    each = 2

    def rows(width):
        return pl.BlockSpec((each * Q, width), lambda k: (k, 0))

    lanes = pl.BlockSpec((each, EACH, Q), lambda k: (k, 0, 0))
    mixed, back, steps = pl.pallas_call(
        scan_kernel,
        grid=(blocks // each,),
        in_specs=[
            in_smem, rows(VW), rows(BC), rows(VW), lanes, lanes, whole(EACH, 3),
            whole(blocks, VW, STATE), whole(blocks, VW, STATE), whole(VW, blocks),
            whole(VW + STEPS, STATE), whole(VW + STEPS, STATE),
        ],
        out_specs=[
            rows(VW), rows(VW + BC), pl.BlockSpec((STEPS, each * Q), lambda k: (0, k)),
        ],
        out_shape=[
            shaped(bf16, tokens, VW), shaped(bf16, tokens, VW + BC), shaped(bf16, STEPS, tokens),
        ],
        scratch_shapes=[
            pltpu.VMEM((blocks + 1, VW, STATE), f32), pltpu.VMEM((blocks, VW, STATE), f32),
        ],
        compiler_params=ALL,
        name="scan",
    )(
        places, values, bc, cot, step, sig, heads, fresh, seeds, lasts, kept, other_way,
    )

    back_pair, steps_pair = swap(back), swap(steps)

    def fetched(count):
        return [pltpu.VMEM((count, 4, tok, FEAT), bf16), pltpu.SemaphoreType.DMA((count,))]

    grad_block = shaped(bf16, FEAT + STEPS, MAIN)
    main, both_steps, up, down = pl.pallas_call(
        first_kernel,
        in_specs=[in_smem] + [in_vmem] * 4 + [in_hbm],
        out_shape=[shaped(bf16, tokens, MAIN + STATE), shaped(bf16, STEPS, tokens)]
        + [grad_block] * 2,
        scratch_shapes=fetched(2),
        compiler_params=ALL,
        cost_estimate=TINY,
        name="first",
    )(places, back, back_pair, steps, steps_pair, hid)
    add_3, add_6, add_2, add_7, add_1, add_0 = pl.pallas_call(
        term_kernel,
        in_specs=[in_smem, in_vmem, in_vmem, in_hbm],
        out_shape=[grad_block] * 6,
        scratch_shapes=fetched(6),
        compiler_params=ALL,
        cost_estimate=LONG,
        name="term",
    )(places, main, both_steps, hid)

    def add_hop(hop, a_sum, b_sum, *sums):
        final = hop == 3
        tables = [a_sum, a_part, b_sum, b_part, *sums]
        wide_block, block, grad = (NX, tok, FEAT), (tok, FEAT), (FEAT + STEPS, MAIN)
        shapes = [wide_block] * 4 + [grad] * 4
        outs = [wide_block] * 2 + [grad] * 2
        if final:
            outs = [block] * (NX + NY) + [(FEAT // 2 + STEPS, MAIN)] * 4
        return pl.pallas_call(
            lambda *refs: hop_kernel(hop, final, *refs),
            in_specs=[in_smem] + [in_hbm] * len(tables),
            out_shape=[shaped(bf16, *shape) for shape in outs],
            scratch_shapes=[pltpu.VMEM(shape, bf16) for shape in shapes]
            + [pltpu.SemaphoreType.DMA((len(tables),))],
            compiler_params=vmem(10),
            cost_estimate=TINY,
            name="hop",
        )(places, *tables)

    def more(sums, *parts):
        total = sums.astype(f32)
        for part in parts:
            total = total + part.astype(f32)
        return total

    a_part, b_part, a_sum, b_sum = pl.pallas_call(
        input_kernel,
        grid=(NZ,),
        in_specs=[in_smem, whole(tokens, MAIN + STATE), in_hbm],
        out_specs=[
            pl.BlockSpec((1, 1, 2, tok, FEAT), lambda k: (k // 2, k % 2, 0, 0, 0)),
            pl.BlockSpec((2, 1, 1, tok, FEAT), lambda k: (0, k % 2, k // 2, 0, 0)),
            whole(2, 2, tok, FEAT), whole(NX, tok, FEAT),
        ],
        out_shape=[
            shaped(bf16, NX, 2, 2, tok, FEAT), shaped(bf16, 2, 2, NX, tok, FEAT),
            shaped(bf16, 2, 2, tok, FEAT), shaped(bf16, NX, tok, FEAT),
        ],
        scratch_shapes=[
            pltpu.VMEM((NZ, MAIN + STATE, FEAT), bf16), pltpu.SemaphoreType.DMA((NZ,)),
        ],
        compiler_params=ALL,
        cost_estimate=LONG,
        name="input",
    )(places, main, whole_w)
    mixed = mixed.reshape(2, 2, tok, VW)
    heads_own = pick(mixed, yh, 0)
    pair = shift(pick(mixed, 1 - yh, 0), "yh", 1, 2)
    a_sum, b_sum, pair = tie(a_sum, b_sum, pair)
    crossed = swap(jnp.stack([pick(heads_own, 1 - c, 0), pick(pair, 1 - c, 0)]))
    a_part = a_part.reshape(NX, NY, tok, FEAT)
    b_part = b_part.reshape(NY, NX, tok, FEAT)
    a_sum = a_sum.reshape(NY, tok, FEAT)

    for hop in range(1, 4):
        a_sum, b_sum, up, down, *last = add_hop(
            hop, both_x(a_sum), both_y(b_sum),
            shift(up, "z", 1, NZ), (add_3, add_2, add_1)[hop - 1],
            shift(down, "z", -1, NZ), (add_6, add_7, add_0)[hop - 1],
        )
        if hop == 1:
            a_sum, b_sum, crossed = tie(a_sum, b_sum, crossed)
    last = [a_sum, b_sum, up, down] + last
    ends = last[NX + NY :]
    mixer_out = pl.pallas_call(
        heads_kernel,
        in_specs=[in_smem, in_vmem, in_vmem, in_vmem],
        out_shape=shaped(bf16, tok, 4 * VW),
        compiler_params=vmem(4),
        cost_estimate=TINY,
        name="by_head",
    )(places, heads_own, pair, crossed)
    across = [(2 * i + j, 2 * ((i + 1) % NZ) + 1 - j) for i in range(NZ) for j in range(2)]
    own = more(ends[2], shift(ends[0], "z", 1, NZ))
    other = more(
        shift(ends[3], "yh", 1, 2), lax.ppermute(ends[1], ("z", "yh"), across)
    )
    a_last = [last[0]] + [shift(last[i], ("yh", "yl"), i, NY) for i in range(1, NY)]
    b_last = [last[NY]] + [shift(last[NY + i], "x", i, NX) for i in range(1, NX)]
    keep, give = pl.pallas_call(
        close_kernel,
        in_specs=[in_smem] + [in_vmem] * (NX + NY),
        out_shape=[shaped(bf16, tok, FEAT)] * 2,
        compiler_params=vmem(4),
        cost_estimate=TINY,
        name="close",
    )(places, *a_last, *b_last)
    hidden_grad = pl.pallas_call(
        cores_kernel,
        in_specs=[in_smem, in_vmem, in_vmem],
        out_shape=shaped(bf16, tok, 2 * FEAT),
        compiler_params=vmem(3),
        cost_estimate=TINY,
        name="by_core",
    )(places, keep, swap(give))

    half = FEAT // 2
    own_step, other_step = own[half:, :half], other[half:, :half]
    own, other = own[:half], other[:half]
    state_grad = own[:, 2 * VW :] + other[:, 2 * VW :]

    def ordered(own, other, wide, gap):
        def cores(value):
            mine, pair = value[:, :wide], value[:, gap : gap + wide]
            return jnp.where(
                c == 0,
                jnp.concatenate([mine, pair], axis=1),
                jnp.concatenate([pair, mine], axis=1),
            )

        own, other = cores(own), cores(other)
        return jnp.where(
            yh == 0,
            jnp.concatenate([own, other], axis=1),
            jnp.concatenate([other, own], axis=1),
        )

    value_grad = ordered(own, other, VW, VW)
    step_grad = ordered(own_step.T, other_step.T, EACH, STEPS // 2)
    return mixer_out, hidden_grad, value_grad, state_grad, step_grad


def solution(mesh):
    fine = Mesh(mesh.devices.reshape(NZ, 2, 2, NX, 2), ("z", "yh", "c", "x", "yl"))
    split = P(("z", "yh", "c"), ("x", "yl"))
    by_head = P(("x", "yl"))
    return jax.shard_map(
        local,
        mesh=fine,
        in_specs=(split,) * 4 + (by_head,) * 3 + (split,),
        out_specs=(split,) * 5,
        check_vma=False,
    )
```

```python
import jax
import jax.numpy as jnp
from jax import lax
from jax.experimental import pallas as pl
from jax.experimental.pallas import tpu as pltpu
from jax.sharding import Mesh, PartitionSpec as P

HEAD_DIM = 64
STATE = 128
Q = 128
EACH = 4
VW = EACH * HEAD_DIM
BC = 2 * STATE
MAIN = 2 * VW + BC
STEPS = 16
COLS = MAIN + STEPS
FEAT = 256
NZ, NX, NY = 8, 4, 4
f32, bf16 = jnp.float32, jnp.bfloat16
HI = lax.Precision.HIGHEST


def vmem(mebibytes):
    return pltpu.CompilerParams(vmem_limit_bytes=mebibytes * 1024 * 1024)


ALL = vmem(60)


def shift(value, axis, by, count, wrap=True):
    pairs = [(i, (i + by) % count) for i in range(count) if wrap or 0 <= i + by < count]
    return lax.ppermute(value, axis, pairs)


def both_x(value):
    pairs = [(c * NX + i, c * NX + (i + 1 - 2 * c) % NX) for c in range(2) for i in range(NX)]
    return lax.ppermute(value, ("c", "x"), pairs)


def both_y(value):
    def at(c, y):
        return (y // 2) * 4 + c * 2 + y % 2

    pairs = [(at(c, y), at(c, (y + 1 - 2 * c) % NY)) for c in range(2) for y in range(NY)]
    return lax.ppermute(value, ("yh", "c", "yl"), pairs)


def swap(value):
    return shift(value, "c", 1, 2)


def dot(left, right, dims, precision=None):
    return lax.dot_general(
        left, right, (dims, ((), ())), preferred_element_type=f32, precision=precision
    )


NN, NT, TN = ((1,), (0,)), ((1,), (1,)), ((0,), (0,))


def iota(shape, dim):
    return lax.broadcasted_iota(jnp.int32, shape, dim)


def consts():
    low = (iota((Q, Q), 0) >= iota((Q, Q), 1)).astype(f32)
    spread = (iota((EACH, VW), 1) // HEAD_DIM == iota((EACH, VW), 0)).astype(f32)
    return low, spread


def pieces(rows):
    high = rows.astype(bf16).astype(f32)
    mid = (rows - high).astype(bf16).astype(f32)
    return jnp.concatenate([high, mid, rows - high - mid], axis=0).astype(bf16)


def exact(rows, right, dims):
    n = rows.shape[0]
    out = dot(pieces(rows), right.astype(bf16), dims)
    return out[:n] + out[n : 2 * n] + out[2 * n :]


def widen(rows, right):
    right = right.astype(bf16)
    return dot(pieces(rows), jnp.concatenate([right] * 3, axis=0), TN)


def project_kernel(at_ref, *refs):
    x, y, z, way = (at_ref[i] for i in range(4))
    a_refs, b_refs, w_refs = refs[:NX], refs[NX : NX + NY], refs[NX + NY : NX + NY + NZ]
    hid_out, w_out, own_out, send_out, hid, weights, own, send, sems = refs[-9:]
    tok = hid.shape[1]
    started = []

    def copy(source, target):
        one = pltpu.make_async_copy(source, target, sems.at[len(started)])
        one.start()
        started.append(one)
        return one

    def place(source, x_at, y_at, core):
        x_at, y_at = x_at & (NX - 1), y_at & (NY - 1)
        lanes = pl.ds(pl.multiple_of((2 * x_at + (y_at & 1)) * FEAT, FEAT), FEAT)
        return copy(source, hid.at[(y_at >> 1) * 2 + core, :, lanes])

    ready = []
    for i in range(NZ):
        z_at = (z + offset(i)) & (NZ - 1)
        lanes = pl.ds(pl.multiple_of(z_at * FEAT, FEAT), FEAT)
        ready.append(copy(w_refs[i], weights.at[:, lanes]))
    every = [(j, i) for j in range(NX) for i in range(NY)]
    ready += [place(a_refs[j].at[i], x - way * j, y - i, 0) for j, i in every]
    later = [place(b_refs[i].at[j], x - j, y - way * i, 1) for j, i in every]
    out = []
    for i in (0, 2, 1, 3):
        if i < 2:
            for one in ready if i == 0 else later:
                one.wait()
        if i == 0:
            out.append(copy(weights, w_out))
        block = hid[i]
        rows = slice(i * tok, (i + 1) * tok)
        out.append(copy(hid.at[i], hid_out.at[i]))
        send[rows, VW:] = dot(block, weights[2 * VW : MAIN, :], NT)
        send[rows, :VW] = dot(block, weights[VW : 2 * VW, :], NT)
        base = 4 * tok + STEPS * (i // 2)
        send[base : base + STEPS, i % 2 * tok : (i % 2 + 1) * tok] = dot(
            weights[MAIN:, :], block, NT
        )
        out.append(copy(send.at[rows], send_out.at[rows]))
        own[rows, :] = dot(block, weights[:VW, :], NT)
        out.append(copy(own.at[rows], own_out.at[rows]))
    out.append(copy(send.at[4 * tok :], send_out.at[4 * tok :]))
    for one in out:
        one.wait()


def offset(i):
    return i // 2 if i % 2 == 0 else -(i + 1) // 2


def state_kernel(
    at_ref, own_ref, send_ref, recv_ref, g_ref, head_ref,
    x_ref, bc_ref, step_ref, sig_ref, fresh_ref, seed_ref, last_ref, keep_ref, give_ref,
):
    tokens = x_ref.shape[0]
    count = tokens // Q
    low, spread = consts()
    bias, rate = head_ref[:, 0:1], head_ref[:, 1:2]
    pre = []
    for i in range(2):
        base = tokens + i * STEPS
        mine = send_ref[base : base + EACH, :]
        pair = recv_ref[base + STEPS // 2 : base + STEPS // 2 + EACH, :]
        rows = mine + pair + bias
        pre += [rows[:, k * Q : (k + 1) * Q] for k in range(rows.shape[1] // Q)]
    pre = jnp.concatenate(pre, axis=0)
    small = jnp.exp(-jnp.abs(pre))
    above = 1.0 + small
    log_above = jnp.where(
        above == 1.0, small, jnp.log(above) * (small / jnp.where(above == 1.0, 1.0, above - 1.0))
    )
    step = jnp.maximum(pre, 0.0) + log_above
    sig = jnp.where(pre >= 0.0, 1.0, small) / above
    for k in range(count):
        step_ref[k] = step[k * EACH : (k + 1) * EACH]
        sig_ref[k] = sig[k * EACH : (k + 1) * EACH]
    cum = exact(-step * jnp.concatenate([rate] * count, axis=0), low, NT)
    twice = jnp.concatenate(
        [jnp.concatenate([spread, jnp.zeros_like(spread)], axis=1),
         jnp.concatenate([jnp.zeros_like(spread), spread], axis=1)], axis=0)
    lane = iota((EACH, count), 1)
    ends = jnp.zeros((EACH, count), f32)
    for k in range(count):
        rows = slice(k * Q, (k + 1) * Q)
        x = (own_ref[rows, :] + recv_ref[rows, :VW]).astype(bf16)
        bc = (send_ref[rows, VW:] + recv_ref[rows, VW:]).astype(bf16)
        x_ref[rows, :] = x
        bc_ref[rows, :] = bc
        here = cum[k * EACH : (k + 1) * EACH]
        last = here[:, Q - 1 :]
        ends = ends + jnp.where(lane == k, last, 0.0)
        rest = jnp.exp(last - here) * step[k * EACH : (k + 1) * EACH]
        both = widen(jnp.concatenate([rest, jnp.exp(here)], axis=0), twice)
        tail = (x.astype(f32) * both[:, :VW]).astype(bf16)
        grown = (g_ref[rows, :].astype(f32) * both[:, VW:]).astype(bf16)
        fresh_ref[k] = dot(tail, bc[:, :STATE], TN)
        seed_ref[k] = dot(grown, bc[:, STATE:], TN)
    lasts = dot(spread, jnp.exp(ends), TN, HI)
    last_ref[...] = lasts
    state = jnp.zeros((VW, STATE), f32)
    grad = jnp.zeros((VW, STATE), f32)
    for k in range(count):
        state = lasts[:, k : k + 1] * state + fresh_ref[k]
        back = count - 1 - k
        grad = lasts[:, back : back + 1] * grad + seed_ref[back]
    eye = (iota((EACH, STATE), 0) == iota((EACH, STATE), 1)).astype(f32)
    total = jnp.exp(jnp.sum(ends, axis=1, keepdims=True))
    parts = split_decay(dot(jnp.broadcast_to(total, (EACH, STEPS)), eye, TN, HI)).astype(bf16)
    up_core = at_ref[5] == 0
    keep_ref[:VW] = jnp.where(up_core, state, grad).astype(bf16)
    give_ref[:VW] = jnp.where(up_core, grad, state).astype(bf16)
    keep_ref[VW:] = parts
    give_ref[VW:] = parts


def split_decay(decay):
    high = decay.astype(bf16).astype(f32)
    mid = (decay - high).astype(bf16).astype(f32)
    least = decay - high - mid
    row = iota((STEPS, STATE), 0)
    return jnp.where(row == 0, high, jnp.where(row == 1, mid, jnp.where(row == 2, least, 0.0)))


def window_kernel(near_ref, far_ref, *out_refs):
    spread = (iota((VW, STATE), 0) // HEAD_DIM == iota((VW, STATE), 1)).astype(bf16)
    for i in range(2):
        out_ref = out_refs[i] if len(out_refs) == 2 else out_refs[0].at[i]
        near = near_ref[i, VW:]
        column = jnp.sum(dot(spread, near, NT), axis=1, keepdims=True)
        out_ref[:VW] = (
            near_ref[i, :VW].astype(f32) + column * far_ref[i, :VW].astype(f32)
        ).astype(bf16)
        decay = jnp.sum(near.astype(f32), axis=0, keepdims=True) * jnp.sum(
            far_ref[i, VW:].astype(f32), axis=0, keepdims=True
        )
        out_ref[VW:] = split_decay(jnp.broadcast_to(decay, (STEPS, STATE))).astype(bf16)


def inside_kernel(x_ref, bc_ref, g_ref, step_ref, head_ref, out_ref, direct_ref, decay_ref):
    low, spread = consts()
    mask = low > 0.0
    lane = iota((Q, EACH), 1)
    row = iota((EACH, Q), 0)
    rate = head_ref[:, 1:2]
    gain_wide = jnp.sum(head_ref[:, 2:3] * spread, axis=0, keepdims=True)
    for sub in range(step_ref.shape[0]):
        rows = slice(sub * Q, (sub + 1) * Q)
        step_t = step_ref[sub]
        cum_t = exact(-step_t * rate, low, NT)
        cum_wide = widen(cum_t, spread)
        x, g = x_ref[rows, :], g_ref[rows, :]
        b_mat, c_mat = bc_ref[rows, :STATE], bc_ref[rows, STATE:]
        scores = jnp.where(mask, dot(c_mat, b_mat, NT), 0.0)
        mixed, moved = [], []
        pairs = jnp.zeros((Q, Q), f32)
        out_sum = jnp.zeros((Q, EACH), f32)
        in_sum = jnp.zeros((EACH, Q), f32)
        for e in range(EACH):
            cut = slice(e * HEAD_DIM, (e + 1) * HEAD_DIM)
            first = slice(e * HEAD_DIM, e * HEAD_DIM + 1)
            fade = jnp.exp(jnp.minimum(cum_wide[:, first] - cum_t[e : e + 1, :], 0.0))
            weight = scores * fade
            step_row = step_t[e : e + 1, :]
            mixing = (weight * step_row).astype(bf16)
            mixed.append(dot(mixing, x[:, cut], NN))
            moved.append(dot(mixing, g[:, cut], TN))
            outer = dot(g[:, cut], x[:, cut], NT)
            pairs = pairs + outer * fade * step_row
            both = weight * outer
            in_sum = in_sum + jnp.where(row == e, jnp.sum(both, axis=0, keepdims=True), 0.0)
            out_sum = out_sum + jnp.where(
                lane == e, jnp.sum(both * step_row, axis=1, keepdims=True), 0.0
            )
        pairs = jnp.where(mask, pairs, 0.0).astype(bf16)
        out_ref[rows, :VW] = jnp.concatenate(mixed, axis=1) + gain_wide * x.astype(f32)
        out_ref[rows, VW : 2 * VW] = jnp.concatenate(moved, axis=1) + gain_wide * g.astype(f32)
        out_ref[rows, 2 * VW : 2 * VW + STATE] = dot(pairs, c_mat, TN)
        out_ref[rows, 2 * VW + STATE :] = dot(pairs, b_mat, NN)
        direct_ref[sub] = in_sum
        decay_ref[sub] = dot(out_sum, low, TN, HI) - exact(in_sum * step_t, low, NN)


def scan_kernel(
    at_ref, x_ref, bc_ref, g_ref, step_ref, sig_ref, head_ref, part_ref, direct_ref, decay_ref,
    fresh_ref, seed_ref, last_ref, kept_ref, other_ref,
    y_ref, back_ref, dstep_ref, held, grads,
):
    at = pl.program_id(0)
    count = fresh_ref.shape[0]

    @pl.when(at == 0)
    def _():
        lasts = last_ref[...]
        kept, other = kept_ref[:VW].astype(f32), other_ref[:VW].astype(f32)
        up_core = at_ref[5] == 0
        state, grad = jnp.where(up_core, kept, other), jnp.where(up_core, other, kept)
        for k in range(count):
            held[k] = state
            state = lasts[:, k : k + 1] * state + fresh_ref[k]
            back = count - 1 - k
            grads[back] = grad
            grad = lasts[:, back : back + 1] * grad + seed_ref[back]
        held[count] = state

    low, spread = consts()
    zero = jnp.zeros_like(spread)
    twice = jnp.concatenate(
        [jnp.concatenate([spread, zero], axis=1), jnp.concatenate([zero, spread], axis=1)], axis=0)
    rate = head_ref[:, 1:2]
    ones = spread.astype(bf16)
    for sub in range(step_ref.shape[0]):
        k = at * step_ref.shape[0] + sub
        rows = slice(sub * Q, (sub + 1) * Q)
        step_t = step_ref[sub]
        cum_t = exact(-step_t * rate, low, NT)
        both_wide = widen(jnp.concatenate([cum_t, step_t], axis=0), twice)
        cum_wide, step_wide = both_wide[:, :VW], both_wide[:, VW:]
        growth = jnp.exp(cum_wide)
        rest = jnp.exp(cum_wide[Q - 1 :, :] - cum_wide)
        xf, gf = x_ref[rows, :].astype(f32), g_ref[rows, :].astype(f32)
        b_mat, c_mat = bc_ref[rows, :STATE], bc_ref[rows, STATE:]
        state, nxt, grad = held[k], held[k + 1], grads[k]
        state_b, grad_b = state.astype(bf16), grad.astype(bf16)
        from_state = growth * dot(c_mat, state_b, NT)
        from_later = rest * dot(b_mat, grad_b, NT)
        y_ref[rows, :] = (part_ref[rows, :VW] + from_state).astype(bf16)
        back_ref[rows, :VW] = (
            part_ref[rows, VW : 2 * VW] + step_wide * from_later
        ).astype(bf16)
        back_ref[rows, VW : VW + STATE] = (
            part_ref[rows, 2 * VW : 2 * VW + STATE]
            + dot((xf * (rest * step_wide)).astype(bf16), grad_b, NN)
        ).astype(bf16)
        back_ref[rows, VW + STATE :] = (
            part_ref[rows, 2 * VW + STATE :] + dot((gf * growth).astype(bf16), state_b, NN)
        ).astype(bf16)
        far = dot(ones, (xf * from_later).astype(bf16), NT)
        out_t = dot(ones, (gf * from_state).astype(bf16), NT)
        crossing = dot(spread, jnp.sum(grad * nxt, axis=1, keepdims=True), NN, HI)
        d_decay = decay_ref[sub] + exact(out_t - far * step_t, low, NN) + crossing
        d_step = (direct_ref[sub] + far - rate * d_decay) * sig_ref[sub]
        dstep_ref[:, rows] = jnp.concatenate(
            [d_step, jnp.zeros((STEPS - EACH, Q), f32)], axis=0
        ).astype(bf16)


def fetch_blocks(at_ref, offsets, hid_ref, blocks, sems):
    copies = []
    for i in range(blocks.shape[0]):
        lanes = pl.ds(pl.multiple_of(at_ref[14 + offsets[i]] * FEAT, FEAT), FEAT)
        copies.append(pltpu.make_async_copy(hid_ref.at[:, :, lanes], blocks.at[i], sems.at[i]))
        copies[-1].start()
    return copies


def write_terms(copies, blocks, main, steps, outs):
    for i, out_ref in enumerate(outs):
        copies[i].wait()
        block = blocks[i].reshape(-1, FEAT)
        out_ref[:FEAT, :] = dot(block, main, TN).astype(bf16)
        out_ref[FEAT:, :FEAT] = dot(steps, block, NN).astype(bf16)
        out_ref[FEAT:, FEAT:] = jnp.zeros((STEPS, MAIN - FEAT), bf16)


def first_kernel(at_ref, back_ref, pair_ref, own_ref, other_ref, hid_ref, main_ref, steps_ref, *refs):
    outs, blocks, sems = refs[:-2], refs[-2], refs[-1]
    copies = fetch_blocks(at_ref, FIRST, hid_ref, blocks, sems)
    bc = (back_ref[:, VW:].astype(f32) + pair_ref[:, VW:].astype(f32)).astype(bf16)
    main = jnp.concatenate([back_ref[:, :VW], pair_ref[:, :VW], bc], axis=1)
    half = STEPS // 2
    steps = jnp.concatenate(
        [own_ref[...].astype(f32)[:half], other_ref[...].astype(f32)[:half]], axis=0
    ).astype(bf16)
    eye = (iota((STEPS, STATE), 0) == iota((STEPS, STATE), 1)).astype(bf16)
    main_ref[:, :MAIN] = main
    main_ref[:, MAIN:] = dot(steps, eye, TN).astype(bf16)
    steps_ref[...] = steps
    write_terms(copies, blocks, main, steps, outs)


def term_kernel(at_ref, main_ref, steps_ref, hid_ref, *refs):
    outs, blocks, sems = refs[:-2], refs[-2], refs[-1]
    copies = fetch_blocks(at_ref, LATER, hid_ref, blocks, sems)
    write_terms(copies, blocks, main_ref[:, :MAIN], steps_ref[...], outs)


def input_kernel(
    at_ref, main_ref, w_ref, a_ref, b_ref, a_first_ref, b_first_ref, weights, sems
):
    k = pl.program_id(0)
    x_first, y_first = at_ref[6], at_ref[10]
    two = 2 * FEAT

    def fetch(i):
        return pltpu.make_async_copy(
            w_ref.at[:, i * two : (i + 1) * two], weights.at[i, :COLS], sems.at[i]
        )

    @pl.when(k == 0)
    def _():
        for i in range(NX):
            fetch(i).start()
            weights[i, COLS:] = jnp.zeros((MAIN + STATE - COLS, two), bf16)

    for i in range(NX):

        @pl.when(k == i)
        def _():
            fetch(i).wait()

    size = a_ref.shape[3]
    total = dot(main_ref[...], weights[k], NN).astype(bf16).reshape(2, 2, size, two)
    for yl in range(2):
        part = total[..., yl * FEAT : (yl + 1) * FEAT]
        a_ref[0, yl] = part[:, 0]
        b_ref[:, yl, 0] = part[:, 1]

        @pl.when(k == x_first)
        def _():
            a_first_ref[yl] = part[:, 0]

        for i in range(2):

            @pl.when(y_first == 2 * i + yl)
            def _():
                b_first_ref[k] = part[i, 1]


def hop_kernel(hop, final, at_ref, *refs):
    count = 4
    x, y = at_ref[0], at_ref[1]
    ins, held, sems = refs[: 2 * count], refs[-2 * count - 1 : -1], refs[-1]
    outs = list(refs[2 * count : -2 * count - 1])
    copies = []
    for i in range(2 * count):
        source = ins[i]
        if i == 1:
            source = source.at[at_ref[6 + hop]]
        if i == 3:
            source = source.at[at_ref[10 + hop]]
        copies.append(pltpu.make_async_copy(source, held[i], sems.at[i]))
        copies[-1].start()
    for i in range(count):
        copies[2 * i].wait()
        copies[2 * i + 1].wait()
        value = (held[2 * i][...].astype(f32) + held[2 * i + 1][...].astype(f32)).astype(bf16)
        if final:
            held[2 * i][...] = value
        else:
            outs.pop(0)[...] = value
    if final:
        for i in range(NY):
            at = (y + i) & (NY - 1)
            outs[i][...] = held[0][(at & 1) * 2 + (at >> 1)]
            outs[NY + i][...] = held[2][(x + i) & (NX - 1)]
        half = FEAT // 2
        for i in range(2):
            for j in range(2):
                at = pl.multiple_of(((y >> 1) ^ j) * half, half)
                out_ref = outs[2 * i + j - 4]
                out_ref[:half, :] = held[4 + 2 * i][pl.ds(at, half), :]
                out_ref[half:, :half] = held[4 + 2 * i][FEAT:, pl.ds(at, half)]
                out_ref[half:, half:] = jnp.zeros((STEPS, MAIN - half), bf16)


def close_kernel(at_ref, *refs):
    a_refs, b_refs, keep_ref, give_ref = refs[:NY], refs[NY : NY + NX], refs[-2], refs[-1]
    sums = []
    for parts in (a_refs, b_refs):
        total = parts[0][...].astype(f32)
        for part in parts[1:]:
            total = total + part[...].astype(f32)
        sums.append(total)
    mine = at_ref[5] == 0
    keep_ref[...] = jnp.where(mine, sums[0], sums[1]).astype(bf16)
    give_ref[...] = jnp.where(mine, sums[1], sums[0]).astype(bf16)


def cores_kernel(at_ref, own_ref, pair_ref, out_ref):
    c = at_ref[5]
    for i in range(2):
        part = slice(i * 128, (i + 1) * 128)
        out_ref[:, pl.ds(pl.multiple_of((2 * i + c) * 128, 128), 128)] = own_ref[:, part]
        out_ref[:, pl.ds(pl.multiple_of((2 * i + 1 - c) * 128, 128), 128)] = pair_ref[:, part]


def heads_kernel(at_ref, own_ref, pair_ref, cross_ref, out_ref):
    yh, c = at_ref[4], at_ref[5]

    def to(first, second, value):
        lanes = pl.ds(pl.multiple_of((first * 2 + second) * VW, VW), VW)
        out_ref[:, lanes] = value

    to(yh, c, own_ref[c])
    to(1 - yh, c, pair_ref[c])
    to(yh, 1 - c, cross_ref[0])
    to(1 - yh, 1 - c, cross_ref[1])


def pick(value, at, dim):
    return lax.dynamic_index_in_dim(value, at, dim, False)


def tie(*values):
    return lax.optimization_barrier(values)


FIRST, LATER = (4, 5), (3, 6, 2, 7, 1, 0)
LONG = pl.CostEstimate(flops=10 * 2**30, bytes_accessed=32 * 2**20, transcendentals=0)
TINY = pl.CostEstimate(flops=1024, bytes_accessed=1024, transcendentals=0)


def local(hidden, value_proj, state_proj, step_proj, step_bias, decay_rate, skip_gain, out_grad):
    z, yh, c, x, yl = (lax.axis_index(a) for a in ("z", "yh", "c", "x", "yl"))
    y = yh * 2 + yl
    way = 1 - 2 * c
    tok = hidden.shape[0]
    tokens = 4 * tok
    blocks = tokens // Q

    def x_at(hop):
        return (x - way * hop) % NX

    def y_at(hop):
        return (y - way * hop) % NY

    places = jnp.stack(
        [x, y, z, way, yh, c]
        + [x_at(i) for i in range(1, 5)]
        + [y_at(i) for i in range(1, 5)]
        + [(z + i) % NZ for i in range(NZ)]
    ).astype(jnp.int32)
    heads = jnp.stack(
        [
            lax.dynamic_slice_in_dim(v, (yh * 2 + c) * EACH, EACH, 0)
            for v in (step_bias, decay_rate, skip_gain)
        ],
        axis=1,
    )

    value_t, state_t, step_tr = value_proj.T, state_proj.T, step_proj.T
    none = jnp.zeros((EACH, value_proj.shape[0]), bf16)

    def chosen(which):
        def some(array, wide, core):
            return lax.dynamic_slice_in_dim(array, (which * 2 + core) * wide, wide, 0)

        return jnp.concatenate(
            [
                some(value_t, VW, c), some(value_t, VW, 1 - c), state_t,
                some(step_tr, EACH, c), none, some(step_tr, EACH, 1 - c), none,
            ],
            axis=0,
        )

    hidden, given = tie(hidden, chosen(1 - yh))
    mine, theirs = chosen(yh), shift(given, "yh", 1, 2)
    chunk = jnp.where(
        yh == 0,
        jnp.concatenate([mine, theirs], axis=1),
        jnp.concatenate([theirs, mine], axis=1),
    )
    parts = hidden.reshape(tok, 2, 2, 128)
    keep = pick(parts, c, 2).reshape(tok, FEAT)
    got = swap(pick(parts, 1 - c, 2).reshape(tok, FEAT))
    first = jnp.where(c == 0, keep, got)
    second = jnp.where(c == 0, got, keep)

    def pairwise(own, pair, place, dim):
        return jnp.where(
            place == 0, jnp.stack([own, pair], dim), jnp.stack([pair, own], dim)
        )

    out_grad, chunk = tie(out_grad, chunk)
    cot = out_grad.reshape(tok, 2, 2, VW)
    cot = pairwise(pick(cot, c, 2), swap(pick(cot, 1 - c, 2)), c, 0)

    weights = [chunk, shift(chunk, "z", 1, NZ), shift(chunk, "z", -1, NZ)]
    a_blocks = [jnp.stack([first] + [shift(first, ("yh", "yl"), i, NY) for i in range(1, NY)])]
    b_blocks = [jnp.stack([second] + [shift(second, "x", i, NX) for i in range(1, NX)])]
    weights[1], weights[2], a_blocks[0], b_blocks[0], cot = tie(
        weights[1], weights[2], a_blocks[0], b_blocks[0], cot
    )
    cot = pairwise(pick(cot, yh, 2), shift(pick(cot, 1 - yh, 2), "yh", 1, 2), yh, 0)
    cot = cot.reshape(tokens, VW)
    for hop in range(1, 4):
        weights.append(shift(weights[-2], "z", 1, NZ))
        if hop < 3:
            weights.append(shift(weights[-2], "z", -1, NZ))
        a_blocks.append(both_x(a_blocks[-1]))
        b_blocks.append(both_y(b_blocks[-1]))
        if hop == 1:
            a_blocks[-1], b_blocks[-1], cot, heads, places = tie(
                a_blocks[-1], b_blocks[-1], cot, heads, places
            )
        if hop < 3:
            weights[-1], weights[-2], a_blocks[-1], b_blocks[-1] = tie(
                weights[-1], weights[-2], a_blocks[-1], b_blocks[-1]
            )

    def whole(*shape):
        return pl.BlockSpec(shape, lambda *k: (0,) * len(shape))

    def shaped(dtype, *shape):
        return jax.ShapeDtypeStruct(shape, dtype)

    wide = NZ * FEAT
    in_hbm = pl.BlockSpec(memory_space=pltpu.HBM)
    in_vmem = pl.BlockSpec(memory_space=pltpu.VMEM)
    in_smem = pl.BlockSpec(memory_space=pltpu.SMEM)
    hid, whole_w, p_own, p_send = pl.pallas_call(
        project_kernel,
        in_specs=[in_smem] + [in_hbm] * (NX + NY + NZ),
        out_specs=[in_hbm] * 4,
        out_shape=[
            shaped(bf16, 4, tok, wide), shaped(bf16, COLS, wide),
            shaped(f32, tokens, VW), shaped(f32, tokens + 2 * STEPS, VW + BC),
        ],
        scratch_shapes=[
            pltpu.VMEM((4, tok, wide), bf16), pltpu.VMEM((COLS, wide), bf16),
            pltpu.VMEM((tokens, VW), f32), pltpu.VMEM((tokens + 2 * STEPS, VW + BC), f32),
            pltpu.SemaphoreType.DMA((2 * NX * NY + NZ + 14,)),
        ],
        compiler_params=ALL,
        cost_estimate=LONG,
        name="project",
    )(places, *a_blocks, *b_blocks, *weights)
    p_recv = swap(p_send)

    states = shaped(f32, blocks, VW, STATE)
    by_lanes = shaped(f32, blocks, EACH, Q)
    packed = shaped(bf16, VW + STEPS, STATE)
    values, bc, step, sig, fresh, seeds, lasts, keep, give = pl.pallas_call(
        state_kernel,
        in_specs=[in_smem] + [in_vmem] * 5,
        out_shape=[
            shaped(bf16, tokens, VW), shaped(bf16, tokens, BC), by_lanes, by_lanes,
            states, states, shaped(f32, VW, blocks), packed, packed,
        ],
        compiler_params=ALL,
        name="states",
    )(places, p_own, p_send, p_recv, cot, heads)

    def along(packed, by):
        pairs = [
            (i * 2 + core, (i + by * (1 - 2 * core)) * 2 + core)
            for i in range(NZ)
            for core in range(2)
            if 0 <= i + by * (1 - 2 * core) < NZ
        ]
        return lax.ppermute(packed, ("z", "c"), pairs)

    def joined(near, far, split=False):
        return pl.pallas_call(
            window_kernel,
            out_shape=[packed] * 2 if split else shaped(bf16, 2, VW + STEPS, STATE),
            compiler_params=vmem(2),
            cost_estimate=TINY,
            name="window",
        )(near, far)

    each = 2

    def rows(width):
        return pl.BlockSpec((each * Q, width), lambda k: (k, 0))

    lanes = pl.BlockSpec((each, EACH, Q), lambda k: (k, 0, 0))
    inside, direct, decays = pl.pallas_call(
        inside_kernel,
        grid=(blocks // each,),
        in_specs=[rows(VW), rows(BC), rows(VW), lanes, whole(EACH, 3)],
        out_specs=[rows(2 * VW + BC), lanes, lanes],
        out_shape=[shaped(f32, tokens, 2 * VW + BC), by_lanes, by_lanes],
        compiler_params=ALL,
        cost_estimate=LONG,
        name="inside",
    )(values, bc, cot, step, heads)
    start = jnp.stack([keep, swap(give)])
    window = joined(along(start, 1), along(start, 2))
    window, inside = tie(window, inside)
    window = joined(window, along(window, 2))
    kept, given = joined(window, along(window, 4), True)
    other_way = swap(given)

    mixed, back, steps = pl.pallas_call(
        scan_kernel,
        grid=(blocks // each,),
        in_specs=[
            in_smem, rows(VW), rows(BC), rows(VW), lanes, lanes, whole(EACH, 3),
            rows(2 * VW + BC), lanes, lanes,
            whole(blocks, VW, STATE), whole(blocks, VW, STATE), whole(VW, blocks),
            whole(VW + STEPS, STATE), whole(VW + STEPS, STATE),
        ],
        out_specs=[
            rows(VW), rows(VW + BC), pl.BlockSpec((STEPS, each * Q), lambda k: (0, k)),
        ],
        out_shape=[
            shaped(bf16, tokens, VW), shaped(bf16, tokens, VW + BC), shaped(bf16, STEPS, tokens),
        ],
        scratch_shapes=[
            pltpu.VMEM((blocks + 1, VW, STATE), f32), pltpu.VMEM((blocks, VW, STATE), f32),
        ],
        compiler_params=ALL,
        name="scan",
    )(
        places, values, bc, cot, step, sig, heads, inside, direct, decays,
        fresh, seeds, lasts, kept, other_way,
    )

    back_pair, steps_pair = swap(back), swap(steps)

    def fetched(count):
        return [pltpu.VMEM((count, 4, tok, FEAT), bf16), pltpu.SemaphoreType.DMA((count,))]

    grad_block = shaped(bf16, FEAT + STEPS, MAIN)
    main, both_steps, up, down = pl.pallas_call(
        first_kernel,
        in_specs=[in_smem] + [in_vmem] * 4 + [in_hbm],
        out_shape=[shaped(bf16, tokens, MAIN + STATE), shaped(bf16, STEPS, tokens)]
        + [grad_block] * 2,
        scratch_shapes=fetched(2),
        compiler_params=ALL,
        cost_estimate=TINY,
        name="first",
    )(places, back, back_pair, steps, steps_pair, hid)
    add_3, add_6, add_2, add_7, add_1, add_0 = pl.pallas_call(
        term_kernel,
        in_specs=[in_smem, in_vmem, in_vmem, in_hbm],
        out_shape=[grad_block] * 6,
        scratch_shapes=fetched(6),
        compiler_params=ALL,
        cost_estimate=LONG,
        name="term",
    )(places, main, both_steps, hid)

    def add_hop(hop, a_sum, b_sum, *sums):
        final = hop == 3
        tables = [a_sum, a_part, b_sum, b_part, *sums]
        wide_block, block, grad = (NX, tok, FEAT), (tok, FEAT), (FEAT + STEPS, MAIN)
        shapes = [wide_block] * 4 + [grad] * 4
        outs = [wide_block] * 2 + [grad] * 2
        if final:
            outs = [block] * (NX + NY) + [(FEAT // 2 + STEPS, MAIN)] * 4
        return pl.pallas_call(
            lambda *refs: hop_kernel(hop, final, *refs),
            in_specs=[in_smem] + [in_hbm] * len(tables),
            out_shape=[shaped(bf16, *shape) for shape in outs],
            scratch_shapes=[pltpu.VMEM(shape, bf16) for shape in shapes]
            + [pltpu.SemaphoreType.DMA((len(tables),))],
            compiler_params=vmem(10),
            cost_estimate=TINY,
            name="hop",
        )(places, *tables)

    def more(sums, *parts):
        total = sums.astype(f32)
        for part in parts:
            total = total + part.astype(f32)
        return total

    a_part, b_part, a_sum, b_sum = pl.pallas_call(
        input_kernel,
        grid=(NX,),
        in_specs=[in_smem, whole(tokens, MAIN + STATE), in_hbm],
        out_specs=[
            pl.BlockSpec((1, 2, 2, tok, FEAT), lambda k: (k, 0, 0, 0, 0)),
            pl.BlockSpec((2, 2, 1, tok, FEAT), lambda k: (0, 0, k, 0, 0)),
            whole(2, 2, tok, FEAT), whole(NX, tok, FEAT),
        ],
        out_shape=[
            shaped(bf16, NX, 2, 2, tok, FEAT), shaped(bf16, 2, 2, NX, tok, FEAT),
            shaped(bf16, 2, 2, tok, FEAT), shaped(bf16, NX, tok, FEAT),
        ],
        scratch_shapes=[
            pltpu.VMEM((NX, MAIN + STATE, 2 * FEAT), bf16), pltpu.SemaphoreType.DMA((NX,)),
        ],
        compiler_params=ALL,
        cost_estimate=LONG,
        name="input",
    )(places, main, whole_w)
    mixed = mixed.reshape(2, 2, tok, VW)
    heads_own = pick(mixed, yh, 0)
    pair = shift(pick(mixed, 1 - yh, 0), "yh", 1, 2)
    a_sum, b_sum, pair = tie(a_sum, b_sum, pair)
    crossed = swap(jnp.stack([pick(heads_own, 1 - c, 0), pick(pair, 1 - c, 0)]))
    a_part = a_part.reshape(NX, NY, tok, FEAT)
    b_part = b_part.reshape(NY, NX, tok, FEAT)
    a_sum = a_sum.reshape(NY, tok, FEAT)

    for hop in range(1, 4):
        a_sum, b_sum, up, down, *last = add_hop(
            hop, both_x(a_sum), both_y(b_sum),
            shift(up, "z", 1, NZ), (add_3, add_2, add_1)[hop - 1],
            shift(down, "z", -1, NZ), (add_6, add_7, add_0)[hop - 1],
        )
        if hop == 1:
            a_sum, b_sum, crossed = tie(a_sum, b_sum, crossed)
    last = [a_sum, b_sum, up, down] + last
    ends = last[NX + NY :]
    mixer_out = pl.pallas_call(
        heads_kernel,
        in_specs=[in_smem, in_vmem, in_vmem, in_vmem],
        out_shape=shaped(bf16, tok, 4 * VW),
        compiler_params=vmem(4),
        cost_estimate=TINY,
        name="by_head",
    )(places, heads_own, pair, crossed)
    across = [(2 * i + j, 2 * ((i + 1) % NZ) + 1 - j) for i in range(NZ) for j in range(2)]
    own = more(ends[2], shift(ends[0], "z", 1, NZ))
    other = more(
        shift(ends[3], "yh", 1, 2), lax.ppermute(ends[1], ("z", "yh"), across)
    )
    a_last = [last[0]] + [shift(last[i], ("yh", "yl"), i, NY) for i in range(1, NY)]
    b_last = [last[NY]] + [shift(last[NY + i], "x", i, NX) for i in range(1, NX)]
    keep, give = pl.pallas_call(
        close_kernel,
        in_specs=[in_smem] + [in_vmem] * (NX + NY),
        out_shape=[shaped(bf16, tok, FEAT)] * 2,
        compiler_params=vmem(4),
        cost_estimate=TINY,
        name="close",
    )(places, *a_last, *b_last)
    hidden_grad = pl.pallas_call(
        cores_kernel,
        in_specs=[in_smem, in_vmem, in_vmem],
        out_shape=shaped(bf16, tok, 2 * FEAT),
        compiler_params=vmem(3),
        cost_estimate=TINY,
        name="by_core",
    )(places, keep, swap(give))

    half = FEAT // 2
    own_step, other_step = own[half:, :half], other[half:, :half]
    own, other = own[:half], other[:half]
    state_grad = own[:, 2 * VW :] + other[:, 2 * VW :]

    def ordered(own, other, wide, gap):
        def cores(value):
            mine, pair = value[:, :wide], value[:, gap : gap + wide]
            return jnp.where(
                c == 0,
                jnp.concatenate([mine, pair], axis=1),
                jnp.concatenate([pair, mine], axis=1),
            )

        own, other = cores(own), cores(other)
        return jnp.where(
            yh == 0,
            jnp.concatenate([own, other], axis=1),
            jnp.concatenate([other, own], axis=1),
        )

    value_grad = ordered(own, other, VW, VW)
    step_grad = ordered(own_step.T, other_step.T, EACH, STEPS // 2)
    return mixer_out, hidden_grad, value_grad, state_grad, step_grad


def solution(mesh):
    fine = Mesh(mesh.devices.reshape(NZ, 2, 2, NX, 2), ("z", "yh", "c", "x", "yl"))
    split = P(("z", "yh", "c"), ("x", "yl"))
    by_head = P(("x", "yl"))
    return jax.shard_map(
        local,
        mesh=fine,
        in_specs=(split,) * 4 + (by_head,) * 3 + (split,),
        out_specs=(split,) * 5,
        check_vma=False,
    )
```

```python
import jax
import jax.numpy as jnp
from jax import lax
from jax.experimental import pallas as pl
from jax.experimental.pallas import tpu as pltpu
from jax.sharding import Mesh, PartitionSpec as P

HEAD_DIM = 64
STATE = 128
Q = 128
EACH = 4
VW = EACH * HEAD_DIM
BC = 2 * STATE
MAIN = 2 * VW + BC
STEPS = 16
COLS = MAIN + STEPS
FEAT = 256
NZ, NX, NY = 8, 4, 4
SPLIT = 0
f32, bf16 = jnp.float32, jnp.bfloat16
HI = lax.Precision.HIGHEST


def vmem(mebibytes):
    return pltpu.CompilerParams(vmem_limit_bytes=mebibytes * 1024 * 1024)


ALL = vmem(60)


def shift(value, axis, by, count, wrap=True):
    pairs = [(i, (i + by) % count) for i in range(count) if wrap or 0 <= i + by < count]
    return lax.ppermute(value, axis, pairs)


def both_x(value):
    pairs = [(c * NX + i, c * NX + (i + 1 - 2 * c) % NX) for c in range(2) for i in range(NX)]
    return lax.ppermute(value, ("c", "x"), pairs)


def both_y(value):
    def at(c, y):
        return (y // 2) * 4 + c * 2 + y % 2

    pairs = [(at(c, y), at(c, (y + 1 - 2 * c) % NY)) for c in range(2) for y in range(NY)]
    return lax.ppermute(value, ("yh", "c", "yl"), pairs)


def swap(value):
    return shift(value, "c", 1, 2)


def dot(left, right, dims, precision=None):
    return lax.dot_general(
        left, right, (dims, ((), ())), preferred_element_type=f32, precision=precision
    )


NN, NT, TN = ((1,), (0,)), ((1,), (1,)), ((0,), (0,))


def iota(shape, dim):
    return lax.broadcasted_iota(jnp.int32, shape, dim)


def consts():
    low = (iota((Q, Q), 0) >= iota((Q, Q), 1)).astype(f32)
    spread = (iota((EACH, VW), 1) // HEAD_DIM == iota((EACH, VW), 0)).astype(f32)
    return low, spread


def pieces(rows):
    high = rows.astype(bf16).astype(f32)
    mid = (rows - high).astype(bf16).astype(f32)
    return jnp.concatenate([high, mid, rows - high - mid], axis=0).astype(bf16)


def exact(rows, right, dims):
    n = rows.shape[0]
    out = dot(pieces(rows), right.astype(bf16), dims)
    return out[:n] + out[n : 2 * n] + out[2 * n :]


def widen(rows, right):
    right = right.astype(bf16)
    return dot(pieces(rows), jnp.concatenate([right] * 3, axis=0), TN)


def project_kernel(at_ref, *refs):
    x, y, z, way = (at_ref[i] for i in range(4))
    a_refs, b_refs, w_refs = refs[:NX], refs[NX : NX + NY], refs[NX + NY : NX + NY + NZ]
    hid_out, w_out, own_ref, send_ref, hid, weights, sems = refs[-7:]
    tok = hid.shape[1]
    copies = []

    def copy(source, target):
        copies.append(pltpu.make_async_copy(source, target, sems.at[len(copies)]))
        copies[-1].start()

    def place(source, x_at, y_at, core):
        x_at, y_at = x_at & (NX - 1), y_at & (NY - 1)
        lanes = pl.ds(pl.multiple_of((2 * x_at + (y_at & 1)) * FEAT, FEAT), FEAT)
        copy(source, hid.at[(y_at >> 1) * 2 + core, :, lanes])

    for j in range(NX):
        for i in range(NY):
            place(a_refs[j].at[i], x - way * j, y - i, 0)
            place(b_refs[i].at[j], x - j, y - way * i, 1)
    for i in range(NZ):
        z_at = (z + offset(i)) & (NZ - 1)
        lanes = pl.ds(pl.multiple_of(z_at * FEAT, FEAT), FEAT)
        copy(w_refs[i], weights.at[SPLIT:, lanes])
        if SPLIT:
            part_ref = refs[NX + NY + NZ]
            copy(part_ref.at[i], weights.at[:SPLIT, i * FEAT : (i + 1) * FEAT])
    for one in copies:
        one.wait()
    hid_back = pltpu.make_async_copy(hid, hid_out, sems.at[len(copies)])
    w_back = pltpu.make_async_copy(weights, w_out, sems.at[len(copies) + 1])
    hid_back.start()
    w_back.start()
    block = hid[...].reshape(4 * tok, NZ * FEAT)
    send_ref[: 4 * tok, VW:] = dot(block, weights[2 * VW : MAIN, :], NT)
    send_ref[: 4 * tok, :VW] = dot(block, weights[VW : 2 * VW, :], NT)
    steps = dot(weights[MAIN:, :], block, NT)
    send_ref[4 * tok : 4 * tok + STEPS, :] = steps[:, : 2 * tok]
    send_ref[4 * tok + STEPS :, :] = steps[:, 2 * tok :]
    own_ref[...] = dot(block, weights[:VW, :], NT)
    hid_back.wait()
    w_back.wait()


def offset(i):
    return i // 2 if i % 2 == 0 else -(i + 1) // 2


def state_kernel(
    at_ref, own_ref, send_ref, recv_ref, g_ref, head_ref,
    x_ref, bc_ref, step_ref, sig_ref, fresh_ref, seed_ref, last_ref, keep_ref, give_ref,
):
    tokens = x_ref.shape[0]
    count = tokens // Q
    low, spread = consts()
    bias, rate = head_ref[:, 0:1], head_ref[:, 1:2]
    pre = []
    for i in range(2):
        base = tokens + i * STEPS
        mine = send_ref[base : base + EACH, :]
        pair = recv_ref[base + STEPS // 2 : base + STEPS // 2 + EACH, :]
        rows = mine + pair + bias
        pre += [rows[:, k * Q : (k + 1) * Q] for k in range(rows.shape[1] // Q)]
    pre = jnp.concatenate(pre, axis=0)
    small = jnp.exp(-jnp.abs(pre))
    above = 1.0 + small
    log_above = jnp.where(
        above == 1.0, small, jnp.log(above) * (small / jnp.where(above == 1.0, 1.0, above - 1.0))
    )
    step = jnp.maximum(pre, 0.0) + log_above
    sig = jnp.where(pre >= 0.0, 1.0, small) / above
    for k in range(count):
        step_ref[k] = step[k * EACH : (k + 1) * EACH]
        sig_ref[k] = sig[k * EACH : (k + 1) * EACH]
    cum = exact(-step * jnp.concatenate([rate] * count, axis=0), low, NT)
    twice = jnp.concatenate(
        [jnp.concatenate([spread, jnp.zeros_like(spread)], axis=1),
         jnp.concatenate([jnp.zeros_like(spread), spread], axis=1)], axis=0)
    lane = iota((EACH, count), 1)
    ends = jnp.zeros((EACH, count), f32)
    for k in range(count):
        rows = slice(k * Q, (k + 1) * Q)
        x = (own_ref[rows, :] + recv_ref[rows, :VW]).astype(bf16)
        bc = (send_ref[rows, VW:] + recv_ref[rows, VW:]).astype(bf16)
        x_ref[rows, :] = x
        bc_ref[rows, :] = bc
        here = cum[k * EACH : (k + 1) * EACH]
        last = here[:, Q - 1 :]
        ends = ends + jnp.where(lane == k, last, 0.0)
        rest = jnp.exp(last - here) * step[k * EACH : (k + 1) * EACH]
        both = widen(jnp.concatenate([rest, jnp.exp(here)], axis=0), twice)
        tail = (x.astype(f32) * both[:, :VW]).astype(bf16)
        grown = (g_ref[rows, :].astype(f32) * both[:, VW:]).astype(bf16)
        fresh_ref[k] = dot(tail, bc[:, :STATE], TN)
        seed_ref[k] = dot(grown, bc[:, STATE:], TN)
    lasts = dot(spread, jnp.exp(ends), TN, HI)
    last_ref[...] = lasts
    state = jnp.zeros((VW, STATE), f32)
    grad = jnp.zeros((VW, STATE), f32)
    for k in range(count):
        state = lasts[:, k : k + 1] * state + fresh_ref[k]
        back = count - 1 - k
        grad = lasts[:, back : back + 1] * grad + seed_ref[back]
    eye = (iota((EACH, STATE), 0) == iota((EACH, STATE), 1)).astype(f32)
    total = jnp.exp(jnp.sum(ends, axis=1, keepdims=True))
    parts = split_decay(dot(jnp.broadcast_to(total, (EACH, STEPS)), eye, TN, HI)).astype(bf16)
    up_core = at_ref[5] == 0
    keep_ref[:VW] = jnp.where(up_core, state, grad).astype(bf16)
    give_ref[:VW] = jnp.where(up_core, grad, state).astype(bf16)
    keep_ref[VW:] = parts
    give_ref[VW:] = parts


def split_decay(decay):
    high = decay.astype(bf16).astype(f32)
    mid = (decay - high).astype(bf16).astype(f32)
    least = decay - high - mid
    row = iota((STEPS, STATE), 0)
    return jnp.where(row == 0, high, jnp.where(row == 1, mid, jnp.where(row == 2, least, 0.0)))


def window_kernel(near_ref, far_ref, *out_refs):
    spread = (iota((VW, STATE), 0) // HEAD_DIM == iota((VW, STATE), 1)).astype(bf16)
    for i in range(2):
        out_ref = out_refs[i] if len(out_refs) == 2 else out_refs[0].at[i]
        near = near_ref[i, VW:]
        column = jnp.sum(dot(spread, near, NT), axis=1, keepdims=True)
        out_ref[:VW] = (
            near_ref[i, :VW].astype(f32) + column * far_ref[i, :VW].astype(f32)
        ).astype(bf16)
        decay = jnp.sum(near.astype(f32), axis=0, keepdims=True) * jnp.sum(
            far_ref[i, VW:].astype(f32), axis=0, keepdims=True
        )
        out_ref[VW:] = split_decay(jnp.broadcast_to(decay, (STEPS, STATE))).astype(bf16)


def scan_kernel(
    at_ref, x_ref, bc_ref, g_ref, step_ref, sig_ref, head_ref,
    fresh_ref, seed_ref, last_ref, kept_ref, other_ref,
    y_ref, back_ref, dstep_ref, held, grads,
):
    at = pl.program_id(0)
    count = fresh_ref.shape[0]

    @pl.when(at == 0)
    def _():
        lasts = last_ref[...]
        kept, other = kept_ref[:VW].astype(f32), other_ref[:VW].astype(f32)
        up_core = at_ref[5] == 0
        state, grad = jnp.where(up_core, kept, other), jnp.where(up_core, other, kept)
        for k in range(count):
            held[k] = state
            state = lasts[:, k : k + 1] * state + fresh_ref[k]
            back = count - 1 - k
            grads[back] = grad
            grad = lasts[:, back : back + 1] * grad + seed_ref[back]
        held[count] = state

    low, spread = consts()
    mask = low > 0.0
    zero = jnp.zeros_like(spread)
    twice = jnp.concatenate(
        [jnp.concatenate([spread, zero], axis=1), jnp.concatenate([zero, spread], axis=1)], axis=0)
    lane = iota((Q, EACH), 1)
    row = iota((EACH, Q), 0)
    rate = head_ref[:, 1:2]
    gain_wide = jnp.sum(head_ref[:, 2:3] * spread, axis=0, keepdims=True)
    for sub in range(step_ref.shape[0]):
        k = at * step_ref.shape[0] + sub
        rows = slice(sub * Q, (sub + 1) * Q)
        step_t = step_ref[sub]
        cum_t = exact(-step_t * rate, low, NT)
        both_wide = widen(jnp.concatenate([cum_t, step_t], axis=0), twice)
        cum_wide, step_wide = both_wide[:, :VW], both_wide[:, VW:]
        growth = jnp.exp(cum_wide)
        rest = jnp.exp(cum_wide[Q - 1 :, :] - cum_wide)
        x, g = x_ref[rows, :], g_ref[rows, :]
        xf, gf = x.astype(f32), g.astype(f32)
        b_mat, c_mat = bc_ref[rows, :STATE], bc_ref[rows, STATE:]
        state, nxt, grad = held[k], held[k + 1], grads[k]
        state_b, grad_b = state.astype(bf16), grad.astype(bf16)

        scores = jnp.where(mask, dot(c_mat, b_mat, NT), 0.0)
        mixed, moved = [], []
        pairs = jnp.zeros((Q, Q), f32)
        out_sum = jnp.zeros((Q, EACH), f32)
        in_sum = jnp.zeros((EACH, Q), f32)
        for e in range(EACH):
            cut = slice(e * HEAD_DIM, (e + 1) * HEAD_DIM)
            first = slice(e * HEAD_DIM, e * HEAD_DIM + 1)
            fade = jnp.exp(jnp.minimum(cum_wide[:, first] - cum_t[e : e + 1, :], 0.0))
            weight = scores * fade
            step_row = step_t[e : e + 1, :]
            mixing = (weight * step_row).astype(bf16)
            mixed.append(dot(mixing, x[:, cut], NN))
            moved.append(dot(mixing, g[:, cut], TN))
            outer = dot(g[:, cut], x[:, cut], NT)
            pairs = pairs + outer * fade * step_row
            both = weight * outer
            in_sum = in_sum + jnp.where(row == e, jnp.sum(both, axis=0, keepdims=True), 0.0)
            out_sum = out_sum + jnp.where(
                lane == e, jnp.sum(both * step_row, axis=1, keepdims=True), 0.0
            )
        pairs = jnp.where(mask, pairs, 0.0).astype(bf16)

        from_state = growth * dot(c_mat, state_b, NT)
        from_later = rest * dot(b_mat, grad_b, NT)
        y_ref[rows, :] = (
            jnp.concatenate(mixed, axis=1) + from_state + gain_wide * xf
        ).astype(bf16)
        back_ref[rows, :VW] = (
            jnp.concatenate(moved, axis=1) + step_wide * from_later + gain_wide * gf
        ).astype(bf16)
        back_ref[rows, VW : VW + STATE] = (
            dot(pairs, c_mat, TN) + dot((xf * (rest * step_wide)).astype(bf16), grad_b, NN)
        ).astype(bf16)
        back_ref[rows, VW + STATE :] = (
            dot(pairs, b_mat, NN) + dot((gf * growth).astype(bf16), state_b, NN)
        ).astype(bf16)

        direct = in_sum + dot(spread.astype(bf16), (xf * from_later).astype(bf16), NT)
        out_t = dot(spread.astype(bf16), (gf * from_state).astype(bf16), NT)
        crossing = dot(spread, jnp.sum(grad * nxt, axis=1, keepdims=True), NN, HI)
        d_decay = (
            dot(out_sum, low, TN, HI) + exact(out_t - direct * step_t, low, NN) + crossing
        )
        d_step = (direct - rate * d_decay) * sig_ref[sub]
        dstep_ref[:, rows] = jnp.concatenate(
            [d_step, jnp.zeros((STEPS - EACH, Q), f32)], axis=0
        ).astype(bf16)


def both_bc(back_ref, pair_ref):
    return (back_ref[:, VW:].astype(f32) + pair_ref[:, VW:].astype(f32)).astype(bf16)


def fetch_blocks(at_ref, offsets, hid_ref, blocks, sems):
    copies = []
    for i in range(blocks.shape[0]):
        lanes = pl.ds(pl.multiple_of(at_ref[14 + offsets[i]] * FEAT, FEAT), FEAT)
        copies.append(pltpu.make_async_copy(hid_ref.at[:, :, lanes], blocks.at[i], sems.at[i]))
        copies[-1].start()
    return copies


def write_terms(copies, blocks, main, steps, outs):
    for i, out_ref in enumerate(outs):
        copies[i].wait()
        block = blocks[i].reshape(-1, FEAT)
        out_ref[:FEAT, :] = dot(block, main, TN).astype(bf16)
        out_ref[FEAT:, :FEAT] = dot(steps, block, NN).astype(bf16)
        out_ref[FEAT:, FEAT:] = jnp.zeros((STEPS, MAIN - FEAT), bf16)


def first_kernel(at_ref, back_ref, pair_ref, own_ref, other_ref, hid_ref, main_ref, steps_ref, *refs):
    outs, blocks, sems = refs[:-2], refs[-2], refs[-1]
    copies = fetch_blocks(at_ref, FIRST, hid_ref, blocks, sems)
    bc = (back_ref[:, VW:].astype(f32) + pair_ref[:, VW:].astype(f32)).astype(bf16)
    main = jnp.concatenate([back_ref[:, :VW], pair_ref[:, :VW], bc], axis=1)
    half = STEPS // 2
    steps = jnp.concatenate(
        [own_ref[...].astype(f32)[:half], other_ref[...].astype(f32)[:half]], axis=0
    ).astype(bf16)
    eye = (iota((STEPS, STATE), 0) == iota((STEPS, STATE), 1)).astype(bf16)
    main_ref[:, :MAIN] = main
    main_ref[:, MAIN:] = dot(steps, eye, TN).astype(bf16)
    steps_ref[...] = steps
    write_terms(copies, blocks, main, steps, outs)


def term_kernel(at_ref, main_ref, steps_ref, hid_ref, *refs):
    outs, blocks, sems = refs[:-2], refs[-2], refs[-1]
    copies = fetch_blocks(at_ref, LATER, hid_ref, blocks, sems)
    write_terms(copies, blocks, main_ref[:, :MAIN], steps_ref[...], outs)


def input_kernel(
    at_ref, main_ref, w_ref, a_ref, b_ref, a_first_ref, b_first_ref, weights, sems
):
    k = pl.program_id(0)
    x_first, y_first = at_ref[6], at_ref[10]
    two = 2 * FEAT

    def fetch(i):
        return pltpu.make_async_copy(
            w_ref.at[:, i * two : (i + 1) * two], weights.at[i, :COLS], sems.at[i]
        )

    @pl.when(k == 0)
    def _():
        for i in range(NX):
            fetch(i).start()
            weights[i, COLS:] = jnp.zeros((MAIN + STATE - COLS, two), bf16)

    for i in range(NX):

        @pl.when(k == i)
        def _():
            fetch(i).wait()

    size = a_ref.shape[3]
    total = dot(main_ref[...], weights[k], NN).astype(bf16).reshape(2, 2, size, two)
    for yl in range(2):
        part = total[..., yl * FEAT : (yl + 1) * FEAT]
        a_ref[0, yl] = part[:, 0]
        b_ref[:, yl, 0] = part[:, 1]

        @pl.when(k == x_first)
        def _():
            a_first_ref[yl] = part[:, 0]

        for i in range(2):

            @pl.when(y_first == 2 * i + yl)
            def _():
                b_first_ref[k] = part[i, 1]


def hop_kernel(hop, final, at_ref, *refs):
    count = 4
    x, y = at_ref[0], at_ref[1]
    ins, held, sems = refs[: 2 * count], refs[-2 * count - 1 : -1], refs[-1]
    outs = list(refs[2 * count : -2 * count - 1])
    copies = []
    for i in range(2 * count):
        source = ins[i]
        if i == 1:
            source = source.at[at_ref[6 + hop]]
        if i == 3:
            source = source.at[at_ref[10 + hop]]
        copies.append(pltpu.make_async_copy(source, held[i], sems.at[i]))
        copies[-1].start()
    for i in range(count):
        copies[2 * i].wait()
        copies[2 * i + 1].wait()
        value = (held[2 * i][...].astype(f32) + held[2 * i + 1][...].astype(f32)).astype(bf16)
        if final:
            held[2 * i][...] = value
        else:
            outs.pop(0)[...] = value
    if final:
        for i in range(NY):
            at = (y + i) & (NY - 1)
            outs[i][...] = held[0][(at & 1) * 2 + (at >> 1)]
            outs[NY + i][...] = held[2][(x + i) & (NX - 1)]
        half = FEAT // 2
        for i in range(2):
            for j in range(2):
                at = pl.multiple_of(((y >> 1) ^ j) * half, half)
                out_ref = outs[2 * i + j - 4]
                out_ref[:half, :] = held[4 + 2 * i][pl.ds(at, half), :]
                out_ref[half:, :half] = held[4 + 2 * i][FEAT:, pl.ds(at, half)]
                out_ref[half:, half:] = jnp.zeros((STEPS, MAIN - half), bf16)


def close_kernel(at_ref, *refs):
    a_refs, b_refs, keep_ref, give_ref = refs[:NY], refs[NY : NY + NX], refs[-2], refs[-1]
    sums = []
    for parts in (a_refs, b_refs):
        total = parts[0][...].astype(f32)
        for part in parts[1:]:
            total = total + part[...].astype(f32)
        sums.append(total)
    mine = at_ref[5] == 0
    keep_ref[...] = jnp.where(mine, sums[0], sums[1]).astype(bf16)
    give_ref[...] = jnp.where(mine, sums[1], sums[0]).astype(bf16)


def cores_kernel(at_ref, own_ref, pair_ref, out_ref):
    c = at_ref[5]
    for i in range(2):
        part = slice(i * 128, (i + 1) * 128)
        out_ref[:, pl.ds(pl.multiple_of((2 * i + c) * 128, 128), 128)] = own_ref[:, part]
        out_ref[:, pl.ds(pl.multiple_of((2 * i + 1 - c) * 128, 128), 128)] = pair_ref[:, part]


def heads_kernel(at_ref, own_ref, pair_ref, cross_ref, out_ref):
    yh, c = at_ref[4], at_ref[5]

    def to(first, second, value):
        lanes = pl.ds(pl.multiple_of((first * 2 + second) * VW, VW), VW)
        out_ref[:, lanes] = value

    to(yh, c, own_ref[c])
    to(1 - yh, c, pair_ref[c])
    to(yh, 1 - c, cross_ref[0])
    to(1 - yh, 1 - c, cross_ref[1])


def pick(value, at, dim):
    return lax.dynamic_index_in_dim(value, at, dim, False)


def tie(*values):
    return lax.optimization_barrier(values)


FIRST, LATER = (4, 5), (3, 6, 2, 7, 1, 0)
LONG = pl.CostEstimate(flops=10 * 2**30, bytes_accessed=32 * 2**20, transcendentals=0)
TINY = pl.CostEstimate(flops=1024, bytes_accessed=1024, transcendentals=0)


def local(hidden, value_proj, state_proj, step_proj, step_bias, decay_rate, skip_gain, out_grad):
    z, yh, c, x, yl = (lax.axis_index(a) for a in ("z", "yh", "c", "x", "yl"))
    y = yh * 2 + yl
    way = 1 - 2 * c
    tok = hidden.shape[0]
    tokens = 4 * tok
    blocks = tokens // Q

    def x_at(hop):
        return (x - way * hop) % NX

    def y_at(hop):
        return (y - way * hop) % NY

    places = jnp.stack(
        [x, y, z, way, yh, c]
        + [x_at(i) for i in range(1, 5)]
        + [y_at(i) for i in range(1, 5)]
        + [(z + i) % NZ for i in range(NZ)]
    ).astype(jnp.int32)
    heads = jnp.stack(
        [
            lax.dynamic_slice_in_dim(v, (yh * 2 + c) * EACH, EACH, 0)
            for v in (step_bias, decay_rate, skip_gain)
        ],
        axis=1,
    )

    value_t, state_t, step_tr = value_proj.T, state_proj.T, step_proj.T
    none = jnp.zeros((EACH, value_proj.shape[0]), bf16)

    def chosen(which):
        def some(array, wide, core):
            return lax.dynamic_slice_in_dim(array, (which * 2 + core) * wide, wide, 0)

        return jnp.concatenate(
            [
                some(value_t, VW, c), some(value_t, VW, 1 - c), state_t,
                some(step_tr, EACH, c), none, some(step_tr, EACH, 1 - c), none,
            ],
            axis=0,
        )

    hidden, given = tie(hidden, chosen(1 - yh))
    mine, theirs = chosen(yh), shift(given, "yh", 1, 2)
    chunk = jnp.where(
        yh == 0,
        jnp.concatenate([mine, theirs], axis=1),
        jnp.concatenate([theirs, mine], axis=1),
    )
    parts = hidden.reshape(tok, 2, 2, 128)
    keep = pick(parts, c, 2).reshape(tok, FEAT)
    got = swap(pick(parts, 1 - c, 2).reshape(tok, FEAT))
    first = jnp.where(c == 0, keep, got)
    second = jnp.where(c == 0, got, keep)

    def pairwise(own, pair, place, dim):
        return jnp.where(
            place == 0, jnp.stack([own, pair], dim), jnp.stack([pair, own], dim)
        )

    out_grad, chunk = tie(out_grad, chunk)
    cot = out_grad.reshape(tok, 2, 2, VW)
    cot = pairwise(pick(cot, c, 2), swap(pick(cot, 1 - c, 2)), c, 0)

    brought = [lax.all_gather(chunk[:SPLIT], "z")] if SPLIT else []
    ring = chunk[SPLIT:]
    weights = [ring, shift(ring, "z", 1, NZ), shift(ring, "z", -1, NZ)]
    a_blocks = [jnp.stack([first] + [shift(first, ("yh", "yl"), i, NY) for i in range(1, NY)])]
    b_blocks = [jnp.stack([second] + [shift(second, "x", i, NX) for i in range(1, NX)])]
    weights[1], weights[2], a_blocks[0], b_blocks[0], cot = tie(
        weights[1], weights[2], a_blocks[0], b_blocks[0], cot
    )
    cot = pairwise(pick(cot, yh, 2), shift(pick(cot, 1 - yh, 2), "yh", 1, 2), yh, 0)
    cot = cot.reshape(tokens, VW)
    for hop in range(1, 4):
        weights.append(shift(weights[-2], "z", 1, NZ))
        if hop < 3:
            weights.append(shift(weights[-2], "z", -1, NZ))
        a_blocks.append(both_x(a_blocks[-1]))
        b_blocks.append(both_y(b_blocks[-1]))
        if hop == 1:
            a_blocks[-1], b_blocks[-1], cot, heads, places = tie(
                a_blocks[-1], b_blocks[-1], cot, heads, places
            )
        if hop < 3:
            weights[-1], weights[-2], a_blocks[-1], b_blocks[-1] = tie(
                weights[-1], weights[-2], a_blocks[-1], b_blocks[-1]
            )

    def whole(*shape):
        return pl.BlockSpec(shape, lambda *k: (0,) * len(shape))

    def shaped(dtype, *shape):
        return jax.ShapeDtypeStruct(shape, dtype)

    wide = NZ * FEAT
    in_hbm = pl.BlockSpec(memory_space=pltpu.HBM)
    in_vmem = pl.BlockSpec(memory_space=pltpu.VMEM)
    in_smem = pl.BlockSpec(memory_space=pltpu.SMEM)
    hid, whole_w, p_own, p_send = pl.pallas_call(
        project_kernel,
        in_specs=[in_smem] + [in_hbm] * (NX + NY + NZ + len(brought)),
        out_specs=[in_hbm, in_hbm, in_vmem, in_vmem],
        out_shape=[
            shaped(bf16, 4, tok, wide), shaped(bf16, COLS, wide),
            shaped(f32, tokens, VW), shaped(f32, tokens + 2 * STEPS, VW + BC),
        ],
        scratch_shapes=[
            pltpu.VMEM((4, tok, wide), bf16), pltpu.VMEM((COLS, wide), bf16),
            pltpu.SemaphoreType.DMA((2 * NX * NY + 2 * NZ + 2,)),
        ],
        compiler_params=ALL,
        cost_estimate=LONG,
        name="project",
    )(places, *a_blocks, *b_blocks, *weights, *brought)
    p_recv = swap(p_send)

    states = shaped(f32, blocks, VW, STATE)
    by_lanes = shaped(f32, blocks, EACH, Q)
    packed = shaped(bf16, VW + STEPS, STATE)
    values, bc, step, sig, fresh, seeds, lasts, keep, give = pl.pallas_call(
        state_kernel,
        in_specs=[in_smem] + [in_vmem] * 5,
        out_shape=[
            shaped(bf16, tokens, VW), shaped(bf16, tokens, BC), by_lanes, by_lanes,
            states, states, shaped(f32, VW, blocks), packed, packed,
        ],
        compiler_params=ALL,
        name="states",
    )(places, p_own, p_send, p_recv, cot, heads)

    def along(packed, by):
        pairs = [
            (i * 2 + core, (i + by * (1 - 2 * core)) * 2 + core)
            for i in range(NZ)
            for core in range(2)
            if 0 <= i + by * (1 - 2 * core) < NZ
        ]
        return lax.ppermute(packed, ("z", "c"), pairs)

    def joined(near, far, split=False):
        return pl.pallas_call(
            window_kernel,
            out_shape=[packed] * 2 if split else shaped(bf16, 2, VW + STEPS, STATE),
            compiler_params=vmem(2),
            cost_estimate=TINY,
            name="window",
        )(near, far)

    start = jnp.stack([keep, swap(give)])
    window = joined(along(start, 1), along(start, 2))
    window = joined(window, along(window, 2))
    kept, given = joined(window, along(window, 4), True)
    other_way = swap(given)

    each = 2

    def rows(width):
        return pl.BlockSpec((each * Q, width), lambda k: (k, 0))

    lanes = pl.BlockSpec((each, EACH, Q), lambda k: (k, 0, 0))
    mixed, back, steps = pl.pallas_call(
        scan_kernel,
        grid=(blocks // each,),
        in_specs=[
            in_smem, rows(VW), rows(BC), rows(VW), lanes, lanes, whole(EACH, 3),
            whole(blocks, VW, STATE), whole(blocks, VW, STATE), whole(VW, blocks),
            whole(VW + STEPS, STATE), whole(VW + STEPS, STATE),
        ],
        out_specs=[
            rows(VW), rows(VW + BC), pl.BlockSpec((STEPS, each * Q), lambda k: (0, k)),
        ],
        out_shape=[
            shaped(bf16, tokens, VW), shaped(bf16, tokens, VW + BC), shaped(bf16, STEPS, tokens),
        ],
        scratch_shapes=[
            pltpu.VMEM((blocks + 1, VW, STATE), f32), pltpu.VMEM((blocks, VW, STATE), f32),
        ],
        compiler_params=ALL,
        name="scan",
    )(
        places, values, bc, cot, step, sig, heads, fresh, seeds, lasts, kept, other_way,
    )

    back_pair, steps_pair = swap(back), swap(steps)

    def fetched(count):
        return [pltpu.VMEM((count, 4, tok, FEAT), bf16), pltpu.SemaphoreType.DMA((count,))]

    grad_block = shaped(bf16, FEAT + STEPS, MAIN)
    main, both_steps, up, down = pl.pallas_call(
        first_kernel,
        in_specs=[in_smem] + [in_vmem] * 4 + [in_hbm],
        out_shape=[shaped(bf16, tokens, MAIN + STATE), shaped(bf16, STEPS, tokens)]
        + [grad_block] * 2,
        scratch_shapes=fetched(2),
        compiler_params=ALL,
        cost_estimate=TINY,
        name="first",
    )(places, back, back_pair, steps, steps_pair, hid)
    add_3, add_6, add_2, add_7, add_1, add_0 = pl.pallas_call(
        term_kernel,
        in_specs=[in_smem, in_vmem, in_vmem, in_hbm],
        out_shape=[grad_block] * 6,
        scratch_shapes=fetched(6),
        compiler_params=vmem(10),
        cost_estimate=LONG,
        name="term",
    )(places, main, both_steps, hid)

    def add_hop(hop, a_sum, b_sum, *sums):
        final = hop == 3
        tables = [a_sum, a_part, b_sum, b_part, *sums]
        wide_block, block, grad = (NX, tok, FEAT), (tok, FEAT), (FEAT + STEPS, MAIN)
        shapes = [wide_block] * 4 + [grad] * 4
        outs = [wide_block] * 2 + [grad] * 2
        if final:
            outs = [block] * (NX + NY) + [(FEAT // 2 + STEPS, MAIN)] * 4
        return pl.pallas_call(
            lambda *refs: hop_kernel(hop, final, *refs),
            in_specs=[in_smem] + [in_hbm] * len(tables),
            out_shape=[shaped(bf16, *shape) for shape in outs],
            scratch_shapes=[pltpu.VMEM(shape, bf16) for shape in shapes]
            + [pltpu.SemaphoreType.DMA((len(tables),))],
            compiler_params=vmem(10),
            cost_estimate=TINY,
            name="hop",
        )(places, *tables)

    def more(sums, *parts):
        total = sums.astype(f32)
        for part in parts:
            total = total + part.astype(f32)
        return total

    a_part, b_part, a_sum, b_sum = pl.pallas_call(
        input_kernel,
        grid=(NX,),
        in_specs=[in_smem, whole(tokens, MAIN + STATE), in_hbm],
        out_specs=[
            pl.BlockSpec((1, 2, 2, tok, FEAT), lambda k: (k, 0, 0, 0, 0)),
            pl.BlockSpec((2, 2, 1, tok, FEAT), lambda k: (0, 0, k, 0, 0)),
            whole(2, 2, tok, FEAT), whole(NX, tok, FEAT),
        ],
        out_shape=[
            shaped(bf16, NX, 2, 2, tok, FEAT), shaped(bf16, 2, 2, NX, tok, FEAT),
            shaped(bf16, 2, 2, tok, FEAT), shaped(bf16, NX, tok, FEAT),
        ],
        scratch_shapes=[
            pltpu.VMEM((NX, MAIN + STATE, 2 * FEAT), bf16), pltpu.SemaphoreType.DMA((NX,)),
        ],
        compiler_params=ALL,
        cost_estimate=LONG,
        name="input",
    )(places, main, whole_w)
    mixed = mixed.reshape(2, 2, tok, VW)
    heads_own = pick(mixed, yh, 0)
    pair = shift(pick(mixed, 1 - yh, 0), "yh", 1, 2)
    a_sum, b_sum, pair = tie(a_sum, b_sum, pair)
    crossed = swap(jnp.stack([pick(heads_own, 1 - c, 0), pick(pair, 1 - c, 0)]))
    a_part = a_part.reshape(NX, NY, tok, FEAT)
    b_part = b_part.reshape(NY, NX, tok, FEAT)
    a_sum = a_sum.reshape(NY, tok, FEAT)

    for hop in range(1, 4):
        a_sum, b_sum, up, down, *last = add_hop(
            hop, both_x(a_sum), both_y(b_sum),
            shift(up, "z", 1, NZ), (add_3, add_2, add_1)[hop - 1],
            shift(down, "z", -1, NZ), (add_6, add_7, add_0)[hop - 1],
        )
        if hop == 1:
            a_sum, b_sum, crossed = tie(a_sum, b_sum, crossed)
    last = [a_sum, b_sum, up, down] + last
    ends = last[NX + NY :]
    mixer_out = pl.pallas_call(
        heads_kernel,
        in_specs=[in_smem, in_vmem, in_vmem, in_vmem],
        out_shape=shaped(bf16, tok, 4 * VW),
        compiler_params=vmem(4),
        cost_estimate=TINY,
        name="by_head",
    )(places, heads_own, pair, crossed)
    across = [(2 * i + j, 2 * ((i + 1) % NZ) + 1 - j) for i in range(NZ) for j in range(2)]
    own = more(ends[2], shift(ends[0], "z", 1, NZ))
    other = more(
        shift(ends[3], "yh", 1, 2), lax.ppermute(ends[1], ("z", "yh"), across)
    )
    a_last = [last[0]] + [shift(last[i], ("yh", "yl"), i, NY) for i in range(1, NY)]
    b_last = [last[NY]] + [shift(last[NY + i], "x", i, NX) for i in range(1, NX)]
    keep, give = pl.pallas_call(
        close_kernel,
        in_specs=[in_smem] + [in_vmem] * (NX + NY),
        out_shape=[shaped(bf16, tok, FEAT)] * 2,
        compiler_params=vmem(4),
        cost_estimate=TINY,
        name="close",
    )(places, *a_last, *b_last)
    hidden_grad = pl.pallas_call(
        cores_kernel,
        in_specs=[in_smem, in_vmem, in_vmem],
        out_shape=shaped(bf16, tok, 2 * FEAT),
        compiler_params=vmem(3),
        cost_estimate=TINY,
        name="by_core",
    )(places, keep, swap(give))

    half = FEAT // 2
    own_step, other_step = own[half:, :half], other[half:, :half]
    own, other = own[:half], other[:half]
    state_grad = own[:, 2 * VW :] + other[:, 2 * VW :]

    def ordered(own, other, wide, gap):
        def cores(value):
            mine, pair = value[:, :wide], value[:, gap : gap + wide]
            return jnp.where(
                c == 0,
                jnp.concatenate([mine, pair], axis=1),
                jnp.concatenate([pair, mine], axis=1),
            )

        own, other = cores(own), cores(other)
        return jnp.where(
            yh == 0,
            jnp.concatenate([own, other], axis=1),
            jnp.concatenate([other, own], axis=1),
        )

    value_grad = ordered(own, other, VW, VW)
    step_grad = ordered(own_step.T, other_step.T, EACH, STEPS // 2)
    return mixer_out, hidden_grad, value_grad, state_grad, step_grad


def solution(mesh):
    fine = Mesh(mesh.devices.reshape(NZ, 2, 2, NX, 2), ("z", "yh", "c", "x", "yl"))
    split = P(("z", "yh", "c"), ("x", "yl"))
    by_head = P(("x", "yl"))
    return jax.shard_map(
        local,
        mesh=fine,
        in_specs=(split,) * 4 + (by_head,) * 3 + (split,),
        out_specs=(split,) * 5,
        check_vma=False,
    )
```

```python
import jax
import jax.numpy as jnp
from jax import lax
from jax.experimental import pallas as pl
from jax.experimental.pallas import tpu as pltpu
from jax.sharding import Mesh, PartitionSpec as P

HEAD_DIM = 64
STATE = 128
Q = 128
EACH = 4
VW = EACH * HEAD_DIM
BC = 2 * STATE
MAIN = 2 * VW + BC
STEPS = 16
COLS = MAIN + STEPS
FEAT = 256
NZ, NX, NY = 8, 4, 4
SPLIT = 0
f32, bf16 = jnp.float32, jnp.bfloat16
HI = lax.Precision.HIGHEST


def vmem(mebibytes):
    return pltpu.CompilerParams(vmem_limit_bytes=mebibytes * 1024 * 1024)


ALL = vmem(60)


def shift(value, axis, by, count, wrap=True):
    pairs = [(i, (i + by) % count) for i in range(count) if wrap or 0 <= i + by < count]
    return lax.ppermute(value, axis, pairs)


def both_x(value):
    pairs = [(c * NX + i, c * NX + (i + 1 - 2 * c) % NX) for c in range(2) for i in range(NX)]
    return lax.ppermute(value, ("c", "x"), pairs)


def both_y(value):
    def at(c, y):
        return (y // 2) * 4 + c * 2 + y % 2

    pairs = [(at(c, y), at(c, (y + 1 - 2 * c) % NY)) for c in range(2) for y in range(NY)]
    return lax.ppermute(value, ("yh", "c", "yl"), pairs)


def swap(value):
    return shift(value, "c", 1, 2)


def dot(left, right, dims, precision=None):
    return lax.dot_general(
        left, right, (dims, ((), ())), preferred_element_type=f32, precision=precision
    )


NN, NT, TN = ((1,), (0,)), ((1,), (1,)), ((0,), (0,))


def iota(shape, dim):
    return lax.broadcasted_iota(jnp.int32, shape, dim)


def consts():
    low = (iota((Q, Q), 0) >= iota((Q, Q), 1)).astype(f32)
    spread = (iota((EACH, VW), 1) // HEAD_DIM == iota((EACH, VW), 0)).astype(f32)
    return low, spread


def pieces(rows):
    high = rows.astype(bf16).astype(f32)
    mid = (rows - high).astype(bf16).astype(f32)
    return jnp.concatenate([high, mid, rows - high - mid], axis=0).astype(bf16)


def exact(rows, right, dims):
    n = rows.shape[0]
    out = dot(pieces(rows), right.astype(bf16), dims)
    return out[:n] + out[n : 2 * n] + out[2 * n :]


def widen(rows, right):
    right = right.astype(bf16)
    return dot(pieces(rows), jnp.concatenate([right] * 3, axis=0), TN)


def project_kernel(at_ref, *refs):
    x, y, z, way = (at_ref[i] for i in range(4))
    a_refs, b_refs, w_refs = refs[:NX], refs[NX : NX + NY], refs[NX + NY : NX + NY + NZ]
    hid_out, w_out, own_ref, send_ref, hid, weights, sems = refs[-7:]
    tok = hid.shape[1]
    copies = []

    def copy(source, target):
        copies.append(pltpu.make_async_copy(source, target, sems.at[len(copies)]))
        copies[-1].start()

    def place(source, x_at, y_at, core):
        x_at, y_at = x_at & (NX - 1), y_at & (NY - 1)
        lanes = pl.ds(pl.multiple_of((2 * x_at + (y_at & 1)) * FEAT, FEAT), FEAT)
        copy(source, hid.at[(y_at >> 1) * 2 + core, :, lanes])

    for j in range(NX):
        for i in range(NY):
            place(a_refs[j].at[i], x - way * j, y - i, 0)
            place(b_refs[i].at[j], x - j, y - way * i, 1)
    for i in range(NZ):
        z_at = (z + offset(i)) & (NZ - 1)
        lanes = pl.ds(pl.multiple_of(z_at * FEAT, FEAT), FEAT)
        copy(w_refs[i], weights.at[SPLIT:, lanes])
        if SPLIT:
            part_ref = refs[NX + NY + NZ]
            copy(part_ref.at[i], weights.at[:SPLIT, i * FEAT : (i + 1) * FEAT])
    for one in copies:
        one.wait()
    hid_back = pltpu.make_async_copy(hid, hid_out, sems.at[len(copies)])
    w_back = pltpu.make_async_copy(weights, w_out, sems.at[len(copies) + 1])
    hid_back.start()
    w_back.start()
    block = hid[...].reshape(4 * tok, NZ * FEAT)
    send_ref[: 4 * tok, VW:] = dot(block, weights[2 * VW : MAIN, :], NT)
    send_ref[: 4 * tok, :VW] = dot(block, weights[VW : 2 * VW, :], NT)
    steps = dot(weights[MAIN:, :], block, NT)
    send_ref[4 * tok : 4 * tok + STEPS, :] = steps[:, : 2 * tok]
    send_ref[4 * tok + STEPS :, :] = steps[:, 2 * tok :]
    own_ref[...] = dot(block, weights[:VW, :], NT)
    hid_back.wait()
    w_back.wait()


def offset(i):
    return i // 2 if i % 2 == 0 else -(i + 1) // 2


def state_kernel(
    at_ref, own_ref, send_ref, recv_ref, g_ref, head_ref,
    x_ref, bc_ref, step_ref, sig_ref, fresh_ref, seed_ref, last_ref, keep_ref, give_ref,
):
    tokens = x_ref.shape[0]
    count = tokens // Q
    low, spread = consts()
    bias, rate = head_ref[:, 0:1], head_ref[:, 1:2]
    pre = []
    for i in range(2):
        base = tokens + i * STEPS
        mine = send_ref[base : base + EACH, :]
        pair = recv_ref[base + STEPS // 2 : base + STEPS // 2 + EACH, :]
        rows = mine + pair + bias
        pre += [rows[:, k * Q : (k + 1) * Q] for k in range(rows.shape[1] // Q)]
    pre = jnp.concatenate(pre, axis=0)
    small = jnp.exp(-jnp.abs(pre))
    above = 1.0 + small
    log_above = jnp.where(
        above == 1.0, small, jnp.log(above) * (small / jnp.where(above == 1.0, 1.0, above - 1.0))
    )
    step = jnp.maximum(pre, 0.0) + log_above
    sig = jnp.where(pre >= 0.0, 1.0, small) / above
    for k in range(count):
        step_ref[k] = step[k * EACH : (k + 1) * EACH]
        sig_ref[k] = sig[k * EACH : (k + 1) * EACH]
    cum = exact(-step * jnp.concatenate([rate] * count, axis=0), low, NT)
    twice = jnp.concatenate(
        [jnp.concatenate([spread, jnp.zeros_like(spread)], axis=1),
         jnp.concatenate([jnp.zeros_like(spread), spread], axis=1)], axis=0)
    lane = iota((EACH, count), 1)
    ends = jnp.zeros((EACH, count), f32)
    for k in range(count):
        rows = slice(k * Q, (k + 1) * Q)
        x = (own_ref[rows, :] + recv_ref[rows, :VW]).astype(bf16)
        bc = (send_ref[rows, VW:] + recv_ref[rows, VW:]).astype(bf16)
        x_ref[rows, :] = x
        bc_ref[rows, :] = bc
        here = cum[k * EACH : (k + 1) * EACH]
        last = here[:, Q - 1 :]
        ends = ends + jnp.where(lane == k, last, 0.0)
        rest = jnp.exp(last - here) * step[k * EACH : (k + 1) * EACH]
        both = widen(jnp.concatenate([rest, jnp.exp(here)], axis=0), twice)
        tail = (x.astype(f32) * both[:, :VW]).astype(bf16)
        grown = (g_ref[rows, :].astype(f32) * both[:, VW:]).astype(bf16)
        fresh_ref[k] = dot(tail, bc[:, :STATE], TN)
        seed_ref[k] = dot(grown, bc[:, STATE:], TN)
    lasts = dot(spread, jnp.exp(ends), TN, HI)
    last_ref[...] = lasts
    state = jnp.zeros((VW, STATE), f32)
    grad = jnp.zeros((VW, STATE), f32)
    for k in range(count):
        state = lasts[:, k : k + 1] * state + fresh_ref[k]
        back = count - 1 - k
        grad = lasts[:, back : back + 1] * grad + seed_ref[back]
    eye = (iota((EACH, STATE), 0) == iota((EACH, STATE), 1)).astype(f32)
    total = jnp.exp(jnp.sum(ends, axis=1, keepdims=True))
    parts = split_decay(dot(jnp.broadcast_to(total, (EACH, STEPS)), eye, TN, HI)).astype(bf16)
    up_core = at_ref[5] == 0
    keep_ref[:VW] = jnp.where(up_core, state, grad).astype(bf16)
    give_ref[:VW] = jnp.where(up_core, grad, state).astype(bf16)
    keep_ref[VW:] = parts
    give_ref[VW:] = parts


def split_decay(decay):
    high = decay.astype(bf16).astype(f32)
    mid = (decay - high).astype(bf16).astype(f32)
    least = decay - high - mid
    row = iota((STEPS, STATE), 0)
    return jnp.where(row == 0, high, jnp.where(row == 1, mid, jnp.where(row == 2, least, 0.0)))


def window_kernel(near_ref, far_ref, *out_refs):
    spread = (iota((VW, STATE), 0) // HEAD_DIM == iota((VW, STATE), 1)).astype(bf16)
    for i in range(2):
        out_ref = out_refs[i] if len(out_refs) == 2 else out_refs[0].at[i]
        near = near_ref[i, VW:]
        column = jnp.sum(dot(spread, near, NT), axis=1, keepdims=True)
        out_ref[:VW] = (
            near_ref[i, :VW].astype(f32) + column * far_ref[i, :VW].astype(f32)
        ).astype(bf16)
        decay = jnp.sum(near.astype(f32), axis=0, keepdims=True) * jnp.sum(
            far_ref[i, VW:].astype(f32), axis=0, keepdims=True
        )
        out_ref[VW:] = split_decay(jnp.broadcast_to(decay, (STEPS, STATE))).astype(bf16)


def scan_kernel(
    at_ref, x_ref, bc_ref, g_ref, step_ref, sig_ref, head_ref,
    fresh_ref, seed_ref, last_ref, kept_ref, other_ref,
    y_ref, back_ref, dstep_ref, held, grads,
):
    at = pl.program_id(0)
    count = fresh_ref.shape[0]

    @pl.when(at == 0)
    def _():
        lasts = last_ref[...]
        kept, other = kept_ref[:VW].astype(f32), other_ref[:VW].astype(f32)
        up_core = at_ref[5] == 0
        state, grad = jnp.where(up_core, kept, other), jnp.where(up_core, other, kept)
        for k in range(count):
            held[k] = state
            state = lasts[:, k : k + 1] * state + fresh_ref[k]
            back = count - 1 - k
            grads[back] = grad
            grad = lasts[:, back : back + 1] * grad + seed_ref[back]
        held[count] = state

    low, spread = consts()
    mask = low > 0.0
    zero = jnp.zeros_like(spread)
    twice = jnp.concatenate(
        [jnp.concatenate([spread, zero], axis=1), jnp.concatenate([zero, spread], axis=1)], axis=0)
    lane = iota((Q, EACH), 1)
    row = iota((EACH, Q), 0)
    rate = head_ref[:, 1:2]
    gain_wide = jnp.sum(head_ref[:, 2:3] * spread, axis=0, keepdims=True)
    for sub in range(step_ref.shape[0]):
        k = at * step_ref.shape[0] + sub
        rows = slice(sub * Q, (sub + 1) * Q)
        step_t = step_ref[sub]
        cum_t = exact(-step_t * rate, low, NT)
        both_wide = widen(jnp.concatenate([cum_t, step_t], axis=0), twice)
        cum_wide, step_wide = both_wide[:, :VW], both_wide[:, VW:]
        growth = jnp.exp(cum_wide)
        rest = jnp.exp(cum_wide[Q - 1 :, :] - cum_wide)
        x, g = x_ref[rows, :], g_ref[rows, :]
        xf, gf = x.astype(f32), g.astype(f32)
        b_mat, c_mat = bc_ref[rows, :STATE], bc_ref[rows, STATE:]
        state, nxt, grad = held[k], held[k + 1], grads[k]
        state_b, grad_b = state.astype(bf16), grad.astype(bf16)

        scores = jnp.where(mask, dot(c_mat, b_mat, NT), 0.0)
        mixed, moved = [], []
        pairs = jnp.zeros((Q, Q), f32)
        out_sum = jnp.zeros((Q, EACH), f32)
        in_sum = jnp.zeros((EACH, Q), f32)
        for e in range(EACH):
            cut = slice(e * HEAD_DIM, (e + 1) * HEAD_DIM)
            first = slice(e * HEAD_DIM, e * HEAD_DIM + 1)
            fade = jnp.exp(jnp.minimum(cum_wide[:, first] - cum_t[e : e + 1, :], 0.0))
            weight = scores * fade
            step_row = step_t[e : e + 1, :]
            mixing = (weight * step_row).astype(bf16)
            mixed.append(dot(mixing, x[:, cut], NN))
            moved.append(dot(mixing, g[:, cut], TN))
            outer = dot(g[:, cut], x[:, cut], NT)
            pairs = pairs + outer * fade * step_row
            both = weight * outer
            in_sum = in_sum + jnp.where(row == e, jnp.sum(both, axis=0, keepdims=True), 0.0)
            out_sum = out_sum + jnp.where(
                lane == e, jnp.sum(both * step_row, axis=1, keepdims=True), 0.0
            )
        pairs = jnp.where(mask, pairs, 0.0).astype(bf16)

        from_state = growth * dot(c_mat, state_b, NT)
        from_later = rest * dot(b_mat, grad_b, NT)
        y_ref[rows, :] = (
            jnp.concatenate(mixed, axis=1) + from_state + gain_wide * xf
        ).astype(bf16)
        back_ref[rows, :VW] = (
            jnp.concatenate(moved, axis=1) + step_wide * from_later + gain_wide * gf
        ).astype(bf16)
        back_ref[rows, VW : VW + STATE] = (
            dot(pairs, c_mat, TN) + dot((xf * (rest * step_wide)).astype(bf16), grad_b, NN)
        ).astype(bf16)
        back_ref[rows, VW + STATE :] = (
            dot(pairs, b_mat, NN) + dot((gf * growth).astype(bf16), state_b, NN)
        ).astype(bf16)

        direct = in_sum + dot(spread.astype(bf16), (xf * from_later).astype(bf16), NT)
        out_t = dot(spread.astype(bf16), (gf * from_state).astype(bf16), NT)
        crossing = dot(spread, jnp.sum(grad * nxt, axis=1, keepdims=True), NN, HI)
        d_decay = (
            dot(out_sum, low, TN, HI) + exact(out_t - direct * step_t, low, NN) + crossing
        )
        d_step = (direct - rate * d_decay) * sig_ref[sub]
        dstep_ref[:, rows] = jnp.concatenate(
            [d_step, jnp.zeros((STEPS - EACH, Q), f32)], axis=0
        ).astype(bf16)


def both_bc(back_ref, pair_ref):
    return (back_ref[:, VW:].astype(f32) + pair_ref[:, VW:].astype(f32)).astype(bf16)


def fetch_blocks(at_ref, offsets, hid_ref, blocks, sems):
    copies = []
    for i in range(blocks.shape[0]):
        lanes = pl.ds(pl.multiple_of(at_ref[14 + offsets[i]] * FEAT, FEAT), FEAT)
        copies.append(pltpu.make_async_copy(hid_ref.at[:, :, lanes], blocks.at[i], sems.at[i]))
        copies[-1].start()
    return copies


def write_terms(copies, blocks, main, steps, outs):
    for i, out_ref in enumerate(outs):
        copies[i].wait()
        block = blocks[i].reshape(-1, FEAT)
        out_ref[:FEAT, :] = dot(block, main, TN).astype(bf16)
        out_ref[FEAT:, :FEAT] = dot(steps, block, NN).astype(bf16)
        out_ref[FEAT:, FEAT:] = jnp.zeros((STEPS, MAIN - FEAT), bf16)


def first_kernel(at_ref, back_ref, pair_ref, own_ref, other_ref, hid_ref, main_ref, steps_ref, *refs):
    outs, blocks, sems = refs[:-2], refs[-2], refs[-1]
    copies = fetch_blocks(at_ref, FIRST, hid_ref, blocks, sems)
    bc = (back_ref[:, VW:].astype(f32) + pair_ref[:, VW:].astype(f32)).astype(bf16)
    main = jnp.concatenate([back_ref[:, :VW], pair_ref[:, :VW], bc], axis=1)
    half = STEPS // 2
    steps = jnp.concatenate(
        [own_ref[...].astype(f32)[:half], other_ref[...].astype(f32)[:half]], axis=0
    ).astype(bf16)
    eye = (iota((STEPS, STATE), 0) == iota((STEPS, STATE), 1)).astype(bf16)
    main_ref[:, :MAIN] = main
    main_ref[:, MAIN:] = dot(steps, eye, TN).astype(bf16)
    steps_ref[...] = steps
    write_terms(copies, blocks, main, steps, outs)


def term_kernel(at_ref, main_ref, steps_ref, hid_ref, *refs):
    outs, blocks, sems = refs[:-2], refs[-2], refs[-1]
    copies = fetch_blocks(at_ref, LATER, hid_ref, blocks, sems)
    write_terms(copies, blocks, main_ref[:, :MAIN], steps_ref[...], outs)


def input_kernel(
    at_ref, main_ref, w_ref, a_ref, b_ref, a_first_ref, b_first_ref, weights, sems
):
    k = pl.program_id(0)
    x_first, y_first = at_ref[6], at_ref[10]
    two = 2 * FEAT

    def fetch(i):
        return pltpu.make_async_copy(
            w_ref.at[:, i * two : (i + 1) * two], weights.at[i, :COLS], sems.at[i]
        )

    @pl.when(k == 0)
    def _():
        for i in range(NX):
            fetch(i).start()
            weights[i, COLS:] = jnp.zeros((MAIN + STATE - COLS, two), bf16)

    for i in range(NX):

        @pl.when(k == i)
        def _():
            fetch(i).wait()

    size = a_ref.shape[3]
    total = dot(main_ref[...], weights[k], NN).astype(bf16).reshape(2, 2, size, two)
    for yl in range(2):
        part = total[..., yl * FEAT : (yl + 1) * FEAT]
        a_ref[0, yl] = part[:, 0]
        b_ref[:, yl, 0] = part[:, 1]

        @pl.when(k == x_first)
        def _():
            a_first_ref[yl] = part[:, 0]

        for i in range(2):

            @pl.when(y_first == 2 * i + yl)
            def _():
                b_first_ref[k] = part[i, 1]


def hop_kernel(hop, final, at_ref, *refs):
    count = 4
    x, y = at_ref[0], at_ref[1]
    ins, held, sems = refs[: 2 * count], refs[-2 * count - 1 : -1], refs[-1]
    outs = list(refs[2 * count : -2 * count - 1])
    copies = []
    for i in range(2 * count):
        source = ins[i]
        if i == 1:
            source = source.at[at_ref[6 + hop]]
        if i == 3:
            source = source.at[at_ref[10 + hop]]
        copies.append(pltpu.make_async_copy(source, held[i], sems.at[i]))
        copies[-1].start()
    for i in range(count):
        copies[2 * i].wait()
        copies[2 * i + 1].wait()
        value = (held[2 * i][...].astype(f32) + held[2 * i + 1][...].astype(f32)).astype(bf16)
        if final:
            held[2 * i][...] = value
        else:
            outs.pop(0)[...] = value
    if final:
        for i in range(NY):
            at = (y + i) & (NY - 1)
            outs[i][...] = held[0][(at & 1) * 2 + (at >> 1)]
            outs[NY + i][...] = held[2][(x + i) & (NX - 1)]
        half = FEAT // 2
        for i in range(2):
            for j in range(2):
                at = pl.multiple_of(((y >> 1) ^ j) * half, half)
                out_ref = outs[2 * i + j - 4]
                out_ref[:half, :] = held[4 + 2 * i][pl.ds(at, half), :]
                out_ref[half:, :half] = held[4 + 2 * i][FEAT:, pl.ds(at, half)]
                out_ref[half:, half:] = jnp.zeros((STEPS, MAIN - half), bf16)


def close_kernel(at_ref, *refs):
    a_refs, b_refs, keep_ref, give_ref = refs[:NY], refs[NY : NY + NX], refs[-2], refs[-1]
    sums = []
    for parts in (a_refs, b_refs):
        total = parts[0][...].astype(f32)
        for part in parts[1:]:
            total = total + part[...].astype(f32)
        sums.append(total)
    mine = at_ref[5] == 0
    keep_ref[...] = jnp.where(mine, sums[0], sums[1]).astype(bf16)
    give_ref[...] = jnp.where(mine, sums[1], sums[0]).astype(bf16)


def cores_kernel(at_ref, own_ref, pair_ref, out_ref):
    c = at_ref[5]
    for i in range(2):
        part = slice(i * 128, (i + 1) * 128)
        out_ref[:, pl.ds(pl.multiple_of((2 * i + c) * 128, 128), 128)] = own_ref[:, part]
        out_ref[:, pl.ds(pl.multiple_of((2 * i + 1 - c) * 128, 128), 128)] = pair_ref[:, part]


def heads_kernel(at_ref, own_ref, pair_ref, cross_ref, out_ref):
    yh, c = at_ref[4], at_ref[5]

    def to(first, second, value):
        lanes = pl.ds(pl.multiple_of((first * 2 + second) * VW, VW), VW)
        out_ref[:, lanes] = value

    to(yh, c, own_ref[c])
    to(1 - yh, c, pair_ref[c])
    to(yh, 1 - c, cross_ref[0])
    to(1 - yh, 1 - c, cross_ref[1])


def pick(value, at, dim):
    return lax.dynamic_index_in_dim(value, at, dim, False)


def tie(*values):
    return lax.optimization_barrier(values)


FIRST, LATER = (4, 5), (3, 6, 2, 7, 1, 0)
LONG = pl.CostEstimate(flops=10 * 2**30, bytes_accessed=32 * 2**20, transcendentals=0)
TINY = pl.CostEstimate(flops=1024, bytes_accessed=1024, transcendentals=0)


def local(hidden, value_proj, state_proj, step_proj, step_bias, decay_rate, skip_gain, out_grad):
    z, yh, c, x, yl = (lax.axis_index(a) for a in ("z", "yh", "c", "x", "yl"))
    y = yh * 2 + yl
    way = 1 - 2 * c
    tok = hidden.shape[0]
    tokens = 4 * tok
    blocks = tokens // Q

    def x_at(hop):
        return (x - way * hop) % NX

    def y_at(hop):
        return (y - way * hop) % NY

    places = jnp.stack(
        [x, y, z, way, yh, c]
        + [x_at(i) for i in range(1, 5)]
        + [y_at(i) for i in range(1, 5)]
        + [(z + i) % NZ for i in range(NZ)]
    ).astype(jnp.int32)
    heads = jnp.stack(
        [
            lax.dynamic_slice_in_dim(v, (yh * 2 + c) * EACH, EACH, 0)
            for v in (step_bias, decay_rate, skip_gain)
        ],
        axis=1,
    )

    value_t, state_t, step_tr = value_proj.T, state_proj.T, step_proj.T
    none = jnp.zeros((EACH, value_proj.shape[0]), bf16)

    def chosen(which):
        def some(array, wide, core):
            return lax.dynamic_slice_in_dim(array, (which * 2 + core) * wide, wide, 0)

        return jnp.concatenate(
            [
                some(value_t, VW, c), some(value_t, VW, 1 - c), state_t,
                some(step_tr, EACH, c), none, some(step_tr, EACH, 1 - c), none,
            ],
            axis=0,
        )

    hidden, given = tie(hidden, chosen(1 - yh))
    mine, theirs = chosen(yh), shift(given, "yh", 1, 2)
    chunk = jnp.where(
        yh == 0,
        jnp.concatenate([mine, theirs], axis=1),
        jnp.concatenate([theirs, mine], axis=1),
    )
    parts = hidden.reshape(tok, 2, 2, 128)
    keep = pick(parts, c, 2).reshape(tok, FEAT)
    got = swap(pick(parts, 1 - c, 2).reshape(tok, FEAT))
    first = jnp.where(c == 0, keep, got)
    second = jnp.where(c == 0, got, keep)

    def pairwise(own, pair, place, dim):
        return jnp.where(
            place == 0, jnp.stack([own, pair], dim), jnp.stack([pair, own], dim)
        )

    out_grad, chunk = tie(out_grad, chunk)
    cot = out_grad.reshape(tok, 2, 2, VW)
    cot = pairwise(pick(cot, c, 2), swap(pick(cot, 1 - c, 2)), c, 0)

    brought = [lax.all_gather(chunk[:SPLIT], "z")] if SPLIT else []
    ring = chunk[SPLIT:]
    weights = [ring, shift(ring, "z", 1, NZ), shift(ring, "z", -1, NZ)]
    a_blocks = [jnp.stack([first] + [shift(first, ("yh", "yl"), i, NY) for i in range(1, NY)])]
    b_blocks = [jnp.stack([second] + [shift(second, "x", i, NX) for i in range(1, NX)])]
    weights[1], weights[2], a_blocks[0], b_blocks[0], cot = tie(
        weights[1], weights[2], a_blocks[0], b_blocks[0], cot
    )
    cot = pairwise(pick(cot, yh, 2), shift(pick(cot, 1 - yh, 2), "yh", 1, 2), yh, 0)
    cot = cot.reshape(tokens, VW)
    for hop in range(1, 4):
        weights.append(shift(weights[-2], "z", 1, NZ))
        if hop < 3:
            weights.append(shift(weights[-2], "z", -1, NZ))
        a_blocks.append(both_x(a_blocks[-1]))
        b_blocks.append(both_y(b_blocks[-1]))
        if hop == 1:
            a_blocks[-1], b_blocks[-1], cot = tie(a_blocks[-1], b_blocks[-1], cot)
        if hop < 3:
            weights[-1], weights[-2], a_blocks[-1], b_blocks[-1] = tie(
                weights[-1], weights[-2], a_blocks[-1], b_blocks[-1]
            )

    def whole(*shape):
        return pl.BlockSpec(shape, lambda *k: (0,) * len(shape))

    def shaped(dtype, *shape):
        return jax.ShapeDtypeStruct(shape, dtype)

    wide = NZ * FEAT
    in_hbm = pl.BlockSpec(memory_space=pltpu.HBM)
    in_vmem = pl.BlockSpec(memory_space=pltpu.VMEM)
    in_smem = pl.BlockSpec(memory_space=pltpu.SMEM)
    hid, whole_w, p_own, p_send = pl.pallas_call(
        project_kernel,
        in_specs=[in_smem] + [in_hbm] * (NX + NY + NZ + len(brought)),
        out_specs=[in_hbm, in_hbm, in_vmem, in_vmem],
        out_shape=[
            shaped(bf16, 4, tok, wide), shaped(bf16, COLS, wide),
            shaped(f32, tokens, VW), shaped(f32, tokens + 2 * STEPS, VW + BC),
        ],
        scratch_shapes=[
            pltpu.VMEM((4, tok, wide), bf16), pltpu.VMEM((COLS, wide), bf16),
            pltpu.SemaphoreType.DMA((2 * NX * NY + 2 * NZ + 2,)),
        ],
        compiler_params=ALL,
        cost_estimate=LONG,
        name="project",
    )(places, *a_blocks, *b_blocks, *weights, *brought)
    p_recv = swap(p_send)

    states = shaped(f32, blocks, VW, STATE)
    by_lanes = shaped(f32, blocks, EACH, Q)
    packed = shaped(bf16, VW + STEPS, STATE)
    values, bc, step, sig, fresh, seeds, lasts, keep, give = pl.pallas_call(
        state_kernel,
        in_specs=[in_smem] + [in_vmem] * 5,
        out_shape=[
            shaped(bf16, tokens, VW), shaped(bf16, tokens, BC), by_lanes, by_lanes,
            states, states, shaped(f32, VW, blocks), packed, packed,
        ],
        compiler_params=ALL,
        name="states",
    )(places, p_own, p_send, p_recv, cot, heads)

    def along(packed, by):
        pairs = [
            (i * 2 + core, (i + by * (1 - 2 * core)) * 2 + core)
            for i in range(NZ)
            for core in range(2)
            if 0 <= i + by * (1 - 2 * core) < NZ
        ]
        return lax.ppermute(packed, ("z", "c"), pairs)

    def joined(near, far, split=False):
        return pl.pallas_call(
            window_kernel,
            out_shape=[packed] * 2 if split else shaped(bf16, 2, VW + STEPS, STATE),
            compiler_params=vmem(2),
            cost_estimate=TINY,
            name="window",
        )(near, far)

    start = jnp.stack([keep, swap(give)])
    window = joined(along(start, 1), along(start, 2))
    window = joined(window, along(window, 2))
    kept, given = joined(window, along(window, 4), True)
    other_way = swap(given)

    each = 2

    def rows(width):
        return pl.BlockSpec((each * Q, width), lambda k: (k, 0))

    lanes = pl.BlockSpec((each, EACH, Q), lambda k: (k, 0, 0))
    mixed, back, steps = pl.pallas_call(
        scan_kernel,
        grid=(blocks // each,),
        in_specs=[
            in_smem, rows(VW), rows(BC), rows(VW), lanes, lanes, whole(EACH, 3),
            whole(blocks, VW, STATE), whole(blocks, VW, STATE), whole(VW, blocks),
            whole(VW + STEPS, STATE), whole(VW + STEPS, STATE),
        ],
        out_specs=[
            rows(VW), rows(VW + BC), pl.BlockSpec((STEPS, each * Q), lambda k: (0, k)),
        ],
        out_shape=[
            shaped(bf16, tokens, VW), shaped(bf16, tokens, VW + BC), shaped(bf16, STEPS, tokens),
        ],
        scratch_shapes=[
            pltpu.VMEM((blocks + 1, VW, STATE), f32), pltpu.VMEM((blocks, VW, STATE), f32),
        ],
        compiler_params=ALL,
        name="scan",
    )(
        places, values, bc, cot, step, sig, heads, fresh, seeds, lasts, kept, other_way,
    )

    back_pair, steps_pair = swap(back), swap(steps)

    def fetched(count):
        return [pltpu.VMEM((count, 4, tok, FEAT), bf16), pltpu.SemaphoreType.DMA((count,))]

    grad_block = shaped(bf16, FEAT + STEPS, MAIN)
    main, both_steps, up, down = pl.pallas_call(
        first_kernel,
        in_specs=[in_smem] + [in_vmem] * 4 + [in_hbm],
        out_shape=[shaped(bf16, tokens, MAIN + STATE), shaped(bf16, STEPS, tokens)]
        + [grad_block] * 2,
        scratch_shapes=fetched(2),
        compiler_params=ALL,
        cost_estimate=TINY,
        name="first",
    )(places, back, back_pair, steps, steps_pair, hid)
    add_3, add_6, add_2, add_7, add_1, add_0 = pl.pallas_call(
        term_kernel,
        in_specs=[in_smem, in_vmem, in_vmem, in_hbm],
        out_shape=[grad_block] * 6,
        scratch_shapes=fetched(6),
        compiler_params=vmem(10),
        cost_estimate=LONG,
        name="term",
    )(places, main, both_steps, hid)

    def add_hop(hop, a_sum, b_sum, *sums):
        final = hop == 3
        tables = [a_sum, a_part, b_sum, b_part, *sums]
        wide_block, block, grad = (NX, tok, FEAT), (tok, FEAT), (FEAT + STEPS, MAIN)
        shapes = [wide_block] * 4 + [grad] * 4
        outs = [wide_block] * 2 + [grad] * 2
        if final:
            outs = [block] * (NX + NY) + [(FEAT // 2 + STEPS, MAIN)] * 4
        return pl.pallas_call(
            lambda *refs: hop_kernel(hop, final, *refs),
            in_specs=[in_smem] + [in_hbm] * len(tables),
            out_shape=[shaped(bf16, *shape) for shape in outs],
            scratch_shapes=[pltpu.VMEM(shape, bf16) for shape in shapes]
            + [pltpu.SemaphoreType.DMA((len(tables),))],
            compiler_params=vmem(10),
            cost_estimate=TINY,
            name="hop",
        )(places, *tables)

    def more(sums, *parts):
        total = sums.astype(f32)
        for part in parts:
            total = total + part.astype(f32)
        return total

    a_part, b_part, a_sum, b_sum = pl.pallas_call(
        input_kernel,
        grid=(NX,),
        in_specs=[in_smem, whole(tokens, MAIN + STATE), in_hbm],
        out_specs=[
            pl.BlockSpec((1, 2, 2, tok, FEAT), lambda k: (k, 0, 0, 0, 0)),
            pl.BlockSpec((2, 2, 1, tok, FEAT), lambda k: (0, 0, k, 0, 0)),
            whole(2, 2, tok, FEAT), whole(NX, tok, FEAT),
        ],
        out_shape=[
            shaped(bf16, NX, 2, 2, tok, FEAT), shaped(bf16, 2, 2, NX, tok, FEAT),
            shaped(bf16, 2, 2, tok, FEAT), shaped(bf16, NX, tok, FEAT),
        ],
        scratch_shapes=[
            pltpu.VMEM((NX, MAIN + STATE, 2 * FEAT), bf16), pltpu.SemaphoreType.DMA((NX,)),
        ],
        compiler_params=ALL,
        cost_estimate=LONG,
        name="input",
    )(places, main, whole_w)
    mixed = mixed.reshape(2, 2, tok, VW)
    heads_own = pick(mixed, yh, 0)
    pair = shift(pick(mixed, 1 - yh, 0), "yh", 1, 2)
    a_sum, b_sum, pair = tie(a_sum, b_sum, pair)
    crossed = swap(jnp.stack([pick(heads_own, 1 - c, 0), pick(pair, 1 - c, 0)]))
    a_part = a_part.reshape(NX, NY, tok, FEAT)
    b_part = b_part.reshape(NY, NX, tok, FEAT)
    a_sum = a_sum.reshape(NY, tok, FEAT)

    for hop in range(1, 4):
        a_sum, b_sum, up, down, *last = add_hop(
            hop, both_x(a_sum), both_y(b_sum),
            shift(up, "z", 1, NZ), (add_3, add_2, add_1)[hop - 1],
            shift(down, "z", -1, NZ), (add_6, add_7, add_0)[hop - 1],
        )
        if hop == 1:
            a_sum, b_sum, crossed = tie(a_sum, b_sum, crossed)
    last = [a_sum, b_sum, up, down] + last
    ends = last[NX + NY :]
    mixer_out = pl.pallas_call(
        heads_kernel,
        in_specs=[in_smem, in_vmem, in_vmem, in_vmem],
        out_shape=shaped(bf16, tok, 4 * VW),
        compiler_params=vmem(4),
        cost_estimate=TINY,
        name="by_head",
    )(places, heads_own, pair, crossed)
    across = [(2 * i + j, 2 * ((i + 1) % NZ) + 1 - j) for i in range(NZ) for j in range(2)]
    own = more(ends[2], shift(ends[0], "z", 1, NZ))
    other = more(
        shift(ends[3], "yh", 1, 2), lax.ppermute(ends[1], ("z", "yh"), across)
    )
    a_last = [last[0]] + [shift(last[i], ("yh", "yl"), i, NY) for i in range(1, NY)]
    b_last = [last[NY]] + [shift(last[NY + i], "x", i, NX) for i in range(1, NX)]
    keep, give = pl.pallas_call(
        close_kernel,
        in_specs=[in_smem] + [in_vmem] * (NX + NY),
        out_shape=[shaped(bf16, tok, FEAT)] * 2,
        compiler_params=vmem(4),
        cost_estimate=TINY,
        name="close",
    )(places, *a_last, *b_last)
    hidden_grad = pl.pallas_call(
        cores_kernel,
        in_specs=[in_smem, in_vmem, in_vmem],
        out_shape=shaped(bf16, tok, 2 * FEAT),
        compiler_params=vmem(3),
        cost_estimate=TINY,
        name="by_core",
    )(places, keep, swap(give))

    half = FEAT // 2
    own_step, other_step = own[half:, :half], other[half:, :half]
    own, other = own[:half], other[:half]
    state_grad = own[:, 2 * VW :] + other[:, 2 * VW :]

    def ordered(own, other, wide, gap):
        def cores(value):
            mine, pair = value[:, :wide], value[:, gap : gap + wide]
            return jnp.where(
                c == 0,
                jnp.concatenate([mine, pair], axis=1),
                jnp.concatenate([pair, mine], axis=1),
            )

        own, other = cores(own), cores(other)
        return jnp.where(
            yh == 0,
            jnp.concatenate([own, other], axis=1),
            jnp.concatenate([other, own], axis=1),
        )

    value_grad = ordered(own, other, VW, VW)
    step_grad = ordered(own_step.T, other_step.T, EACH, STEPS // 2)
    return mixer_out, hidden_grad, value_grad, state_grad, step_grad


def solution(mesh):
    fine = Mesh(mesh.devices.reshape(NZ, 2, 2, NX, 2), ("z", "yh", "c", "x", "yl"))
    split = P(("z", "yh", "c"), ("x", "yl"))
    by_head = P(("x", "yl"))
    return jax.shard_map(
        local,
        mesh=fine,
        in_specs=(split,) * 4 + (by_head,) * 3 + (split,),
        out_specs=(split,) * 5,
        check_vma=False,
    )
```

```python
import jax
import jax.numpy as jnp
from jax import lax
from jax.experimental import pallas as pl
from jax.experimental.pallas import tpu as pltpu
from jax.sharding import Mesh, PartitionSpec as P

HEAD_DIM = 64
STATE = 128
Q = 128
EACH = 4
VW = EACH * HEAD_DIM
BC = 2 * STATE
MAIN = 2 * VW + BC
STEPS = 16
COLS = MAIN + STEPS
FEAT = 256
NZ, NX, NY = 8, 4, 4
SPLIT = 0
f32, bf16 = jnp.float32, jnp.bfloat16
HI = lax.Precision.HIGHEST


def vmem(mebibytes):
    return pltpu.CompilerParams(vmem_limit_bytes=mebibytes * 1024 * 1024)


ALL = vmem(60)


def shift(value, axis, by, count, wrap=True):
    pairs = [(i, (i + by) % count) for i in range(count) if wrap or 0 <= i + by < count]
    return lax.ppermute(value, axis, pairs)


def both_x(value):
    pairs = [(c * NX + i, c * NX + (i + 1 - 2 * c) % NX) for c in range(2) for i in range(NX)]
    return lax.ppermute(value, ("c", "x"), pairs)


def both_y(value):
    def at(c, y):
        return (y // 2) * 4 + c * 2 + y % 2

    pairs = [(at(c, y), at(c, (y + 1 - 2 * c) % NY)) for c in range(2) for y in range(NY)]
    return lax.ppermute(value, ("yh", "c", "yl"), pairs)


def swap(value):
    return shift(value, "c", 1, 2)


def dot(left, right, dims, precision=None):
    return lax.dot_general(
        left, right, (dims, ((), ())), preferred_element_type=f32, precision=precision
    )


NN, NT, TN = ((1,), (0,)), ((1,), (1,)), ((0,), (0,))


def iota(shape, dim):
    return lax.broadcasted_iota(jnp.int32, shape, dim)


def consts():
    low = (iota((Q, Q), 0) >= iota((Q, Q), 1)).astype(f32)
    spread = (iota((EACH, VW), 1) // HEAD_DIM == iota((EACH, VW), 0)).astype(f32)
    return low, spread


def pieces(rows):
    high = rows.astype(bf16).astype(f32)
    mid = (rows - high).astype(bf16).astype(f32)
    return jnp.concatenate([high, mid, rows - high - mid], axis=0).astype(bf16)


def exact(rows, right, dims):
    n = rows.shape[0]
    out = dot(pieces(rows), right.astype(bf16), dims)
    return out[:n] + out[n : 2 * n] + out[2 * n :]


def widen(rows, right):
    right = right.astype(bf16)
    return dot(pieces(rows), jnp.concatenate([right] * 3, axis=0), TN)


def project_kernel(at_ref, *refs):
    x, y, z, way = (at_ref[i] for i in range(4))
    a_refs, b_refs, w_refs = refs[:NX], refs[NX : NX + NY], refs[NX + NY : NX + NY + NZ]
    hid_out, w_out, own_ref, send_ref, hid, weights, sems = refs[-7:]
    tok = hid.shape[1]
    copies = []

    def copy(source, target):
        copies.append(pltpu.make_async_copy(source, target, sems.at[len(copies)]))
        copies[-1].start()

    def place(source, x_at, y_at, core):
        x_at, y_at = x_at & (NX - 1), y_at & (NY - 1)
        lanes = pl.ds(pl.multiple_of((2 * x_at + (y_at & 1)) * FEAT, FEAT), FEAT)
        copy(source, hid.at[(y_at >> 1) * 2 + core, :, lanes])

    for j in range(NX):
        for i in range(NY):
            place(a_refs[j].at[i], x - way * j, y - i, 0)
            place(b_refs[i].at[j], x - j, y - way * i, 1)
    for i in range(NZ):
        z_at = (z + offset(i)) & (NZ - 1)
        lanes = pl.ds(pl.multiple_of(z_at * FEAT, FEAT), FEAT)
        copy(w_refs[i], weights.at[SPLIT:, lanes])
        if SPLIT:
            part_ref = refs[NX + NY + NZ]
            copy(part_ref.at[i], weights.at[:SPLIT, i * FEAT : (i + 1) * FEAT])
    for one in copies:
        one.wait()
    hid_back = pltpu.make_async_copy(hid, hid_out, sems.at[len(copies)])
    w_back = pltpu.make_async_copy(weights, w_out, sems.at[len(copies) + 1])
    hid_back.start()
    w_back.start()
    block = hid[...].reshape(4 * tok, NZ * FEAT)
    send_ref[: 4 * tok, VW:] = dot(block, weights[2 * VW : MAIN, :], NT)
    send_ref[: 4 * tok, :VW] = dot(block, weights[VW : 2 * VW, :], NT)
    steps = dot(weights[MAIN:, :], block, NT)
    send_ref[4 * tok : 4 * tok + STEPS, :] = steps[:, : 2 * tok]
    send_ref[4 * tok + STEPS :, :] = steps[:, 2 * tok :]
    own_ref[...] = dot(block, weights[:VW, :], NT)
    hid_back.wait()
    w_back.wait()


def offset(i):
    return i // 2 if i % 2 == 0 else -(i + 1) // 2


def state_kernel(
    at_ref, own_ref, send_ref, recv_ref, g_ref, head_ref,
    x_ref, bc_ref, step_ref, sig_ref, fresh_ref, seed_ref, last_ref, keep_ref, give_ref,
):
    tokens = x_ref.shape[0]
    count = tokens // Q
    low, spread = consts()
    bias, rate = head_ref[:, 0:1], head_ref[:, 1:2]
    pre = []
    for i in range(2):
        base = tokens + i * STEPS
        mine = send_ref[base : base + EACH, :]
        pair = recv_ref[base + STEPS // 2 : base + STEPS // 2 + EACH, :]
        rows = mine + pair + bias
        pre += [rows[:, k * Q : (k + 1) * Q] for k in range(rows.shape[1] // Q)]
    pre = jnp.concatenate(pre, axis=0)
    small = jnp.exp(-jnp.abs(pre))
    above = 1.0 + small
    log_above = jnp.where(
        above == 1.0, small, jnp.log(above) * (small / jnp.where(above == 1.0, 1.0, above - 1.0))
    )
    step = jnp.maximum(pre, 0.0) + log_above
    sig = jnp.where(pre >= 0.0, 1.0, small) / above
    for k in range(count):
        step_ref[k] = step[k * EACH : (k + 1) * EACH]
        sig_ref[k] = sig[k * EACH : (k + 1) * EACH]
    cum = exact(-step * jnp.concatenate([rate] * count, axis=0), low, NT)
    twice = jnp.concatenate(
        [jnp.concatenate([spread, jnp.zeros_like(spread)], axis=1),
         jnp.concatenate([jnp.zeros_like(spread), spread], axis=1)], axis=0)
    lane = iota((EACH, count), 1)
    ends = jnp.zeros((EACH, count), f32)
    for k in range(count):
        rows = slice(k * Q, (k + 1) * Q)
        x = (own_ref[rows, :] + recv_ref[rows, :VW]).astype(bf16)
        bc = (send_ref[rows, VW:] + recv_ref[rows, VW:]).astype(bf16)
        x_ref[rows, :] = x
        bc_ref[rows, :] = bc
        here = cum[k * EACH : (k + 1) * EACH]
        last = here[:, Q - 1 :]
        ends = ends + jnp.where(lane == k, last, 0.0)
        rest = jnp.exp(last - here) * step[k * EACH : (k + 1) * EACH]
        both = widen(jnp.concatenate([rest, jnp.exp(here)], axis=0), twice)
        tail = (x.astype(f32) * both[:, :VW]).astype(bf16)
        grown = (g_ref[rows, :].astype(f32) * both[:, VW:]).astype(bf16)
        fresh_ref[k] = dot(tail, bc[:, :STATE], TN)
        seed_ref[k] = dot(grown, bc[:, STATE:], TN)
    lasts = dot(spread, jnp.exp(ends), TN, HI)
    last_ref[...] = lasts
    state = jnp.zeros((VW, STATE), f32)
    grad = jnp.zeros((VW, STATE), f32)
    for k in range(count):
        state = lasts[:, k : k + 1] * state + fresh_ref[k]
        back = count - 1 - k
        grad = lasts[:, back : back + 1] * grad + seed_ref[back]
    eye = (iota((EACH, STATE), 0) == iota((EACH, STATE), 1)).astype(f32)
    total = jnp.exp(jnp.sum(ends, axis=1, keepdims=True))
    parts = split_decay(dot(jnp.broadcast_to(total, (EACH, STEPS)), eye, TN, HI)).astype(bf16)
    up_core = at_ref[5] == 0
    keep_ref[:VW] = jnp.where(up_core, state, grad).astype(bf16)
    give_ref[:VW] = jnp.where(up_core, grad, state).astype(bf16)
    keep_ref[VW:] = parts
    give_ref[VW:] = parts


def split_decay(decay):
    high = decay.astype(bf16).astype(f32)
    mid = (decay - high).astype(bf16).astype(f32)
    least = decay - high - mid
    row = iota((STEPS, STATE), 0)
    return jnp.where(row == 0, high, jnp.where(row == 1, mid, jnp.where(row == 2, least, 0.0)))


def window_kernel(near_ref, far_ref, *out_refs):
    spread = (iota((VW, STATE), 0) // HEAD_DIM == iota((VW, STATE), 1)).astype(bf16)
    for i in range(2):
        out_ref = out_refs[i] if len(out_refs) == 2 else out_refs[0].at[i]
        near = near_ref[i, VW:]
        column = jnp.sum(dot(spread, near, NT), axis=1, keepdims=True)
        out_ref[:VW] = (
            near_ref[i, :VW].astype(f32) + column * far_ref[i, :VW].astype(f32)
        ).astype(bf16)
        decay = jnp.sum(near.astype(f32), axis=0, keepdims=True) * jnp.sum(
            far_ref[i, VW:].astype(f32), axis=0, keepdims=True
        )
        out_ref[VW:] = split_decay(jnp.broadcast_to(decay, (STEPS, STATE))).astype(bf16)


def scan_kernel(
    at_ref, x_ref, bc_ref, g_ref, step_ref, sig_ref, head_ref,
    fresh_ref, seed_ref, last_ref, kept_ref, other_ref,
    y_ref, back_ref, dstep_ref, held, grads,
):
    at = pl.program_id(0)
    count = fresh_ref.shape[0]

    @pl.when(at == 0)
    def _():
        lasts = last_ref[...]
        kept, other = kept_ref[:VW].astype(f32), other_ref[:VW].astype(f32)
        up_core = at_ref[5] == 0
        state, grad = jnp.where(up_core, kept, other), jnp.where(up_core, other, kept)
        for k in range(count):
            held[k] = state
            state = lasts[:, k : k + 1] * state + fresh_ref[k]
            back = count - 1 - k
            grads[back] = grad
            grad = lasts[:, back : back + 1] * grad + seed_ref[back]
        held[count] = state

    low, spread = consts()
    mask = low > 0.0
    zero = jnp.zeros_like(spread)
    twice = jnp.concatenate(
        [jnp.concatenate([spread, zero], axis=1), jnp.concatenate([zero, spread], axis=1)], axis=0)
    lane = iota((Q, EACH), 1)
    row = iota((EACH, Q), 0)
    rate = head_ref[:, 1:2]
    gain_wide = jnp.sum(head_ref[:, 2:3] * spread, axis=0, keepdims=True)
    for sub in range(step_ref.shape[0]):
        k = at * step_ref.shape[0] + sub
        rows = slice(sub * Q, (sub + 1) * Q)
        step_t = step_ref[sub]
        cum_t = exact(-step_t * rate, low, NT)
        both_wide = widen(jnp.concatenate([cum_t, step_t], axis=0), twice)
        cum_wide, step_wide = both_wide[:, :VW], both_wide[:, VW:]
        growth = jnp.exp(cum_wide)
        rest = jnp.exp(cum_wide[Q - 1 :, :] - cum_wide)
        x, g = x_ref[rows, :], g_ref[rows, :]
        xf, gf = x.astype(f32), g.astype(f32)
        b_mat, c_mat = bc_ref[rows, :STATE], bc_ref[rows, STATE:]
        state, nxt, grad = held[k], held[k + 1], grads[k]
        state_b, grad_b = state.astype(bf16), grad.astype(bf16)

        scores = jnp.where(mask, dot(c_mat, b_mat, NT), 0.0)
        mixed, moved = [], []
        pairs = jnp.zeros((Q, Q), f32)
        out_sum = jnp.zeros((Q, EACH), f32)
        in_sum = jnp.zeros((EACH, Q), f32)
        for e in range(EACH):
            cut = slice(e * HEAD_DIM, (e + 1) * HEAD_DIM)
            first = slice(e * HEAD_DIM, e * HEAD_DIM + 1)
            fade = jnp.exp(jnp.minimum(cum_wide[:, first] - cum_t[e : e + 1, :], 0.0))
            weight = scores * fade
            step_row = step_t[e : e + 1, :]
            mixing = (weight * step_row).astype(bf16)
            mixed.append(dot(mixing, x[:, cut], NN))
            moved.append(dot(mixing, g[:, cut], TN))
            outer = dot(g[:, cut], x[:, cut], NT)
            pairs = pairs + outer * fade * step_row
            both = weight * outer
            in_sum = in_sum + jnp.where(row == e, jnp.sum(both, axis=0, keepdims=True), 0.0)
            out_sum = out_sum + jnp.where(
                lane == e, jnp.sum(both * step_row, axis=1, keepdims=True), 0.0
            )
        pairs = jnp.where(mask, pairs, 0.0).astype(bf16)

        from_state = growth * dot(c_mat, state_b, NT)
        from_later = rest * dot(b_mat, grad_b, NT)
        y_ref[rows, :] = (
            jnp.concatenate(mixed, axis=1) + from_state + gain_wide * xf
        ).astype(bf16)
        back_ref[rows, :VW] = (
            jnp.concatenate(moved, axis=1) + step_wide * from_later + gain_wide * gf
        ).astype(bf16)
        back_ref[rows, VW : VW + STATE] = (
            dot(pairs, c_mat, TN) + dot((xf * (rest * step_wide)).astype(bf16), grad_b, NN)
        ).astype(bf16)
        back_ref[rows, VW + STATE :] = (
            dot(pairs, b_mat, NN) + dot((gf * growth).astype(bf16), state_b, NN)
        ).astype(bf16)

        direct = in_sum + dot(spread.astype(bf16), (xf * from_later).astype(bf16), NT)
        out_t = dot(spread.astype(bf16), (gf * from_state).astype(bf16), NT)
        crossing = dot(spread, jnp.sum(grad * nxt, axis=1, keepdims=True), NN, HI)
        d_decay = (
            dot(out_sum, low, TN, HI) + exact(out_t - direct * step_t, low, NN) + crossing
        )
        d_step = (direct - rate * d_decay) * sig_ref[sub]
        dstep_ref[:, rows] = jnp.concatenate(
            [d_step, jnp.zeros((STEPS - EACH, Q), f32)], axis=0
        ).astype(bf16)


def both_bc(back_ref, pair_ref):
    return (back_ref[:, VW:].astype(f32) + pair_ref[:, VW:].astype(f32)).astype(bf16)


def fetch_blocks(at_ref, offsets, hid_ref, blocks, sems):
    copies = []
    for i in range(blocks.shape[0]):
        lanes = pl.ds(pl.multiple_of(at_ref[14 + offsets[i]] * FEAT, FEAT), FEAT)
        copies.append(pltpu.make_async_copy(hid_ref.at[:, :, lanes], blocks.at[i], sems.at[i]))
        copies[-1].start()
    return copies


def write_terms(copies, blocks, main, steps, outs):
    for i, out_ref in enumerate(outs):
        copies[i].wait()
        block = blocks[i].reshape(-1, FEAT)
        out_ref[:FEAT, :] = dot(block, main, TN).astype(bf16)
        out_ref[FEAT:, :FEAT] = dot(steps, block, NN).astype(bf16)
        out_ref[FEAT:, FEAT:] = jnp.zeros((STEPS, MAIN - FEAT), bf16)


def first_kernel(at_ref, back_ref, pair_ref, own_ref, other_ref, hid_ref, main_ref, steps_ref, *refs):
    outs, blocks, sems = refs[:-2], refs[-2], refs[-1]
    copies = fetch_blocks(at_ref, FIRST, hid_ref, blocks, sems)
    bc = (back_ref[:, VW:].astype(f32) + pair_ref[:, VW:].astype(f32)).astype(bf16)
    main = jnp.concatenate([back_ref[:, :VW], pair_ref[:, :VW], bc], axis=1)
    half = STEPS // 2
    steps = jnp.concatenate(
        [own_ref[...].astype(f32)[:half], other_ref[...].astype(f32)[:half]], axis=0
    ).astype(bf16)
    eye = (iota((STEPS, STATE), 0) == iota((STEPS, STATE), 1)).astype(bf16)
    main_ref[:, :MAIN] = main
    main_ref[:, MAIN:] = dot(steps, eye, TN).astype(bf16)
    steps_ref[...] = steps
    write_terms(copies, blocks, main, steps, outs)


def term_kernel(at_ref, main_ref, steps_ref, hid_ref, *refs):
    outs, blocks, sems = refs[:-2], refs[-2], refs[-1]
    copies = fetch_blocks(at_ref, LATER, hid_ref, blocks, sems)
    write_terms(copies, blocks, main_ref[:, :MAIN], steps_ref[...], outs)


def input_kernel(
    at_ref, main_ref, w_ref, a_ref, b_ref, a_first_ref, b_first_ref, weights, sems
):
    k = pl.program_id(0)
    x_first, y_first = at_ref[6], at_ref[10]

    def fetch(i):
        return pltpu.make_async_copy(
            w_ref.at[:, i * FEAT : (i + 1) * FEAT], weights.at[i, :COLS], sems.at[i]
        )

    @pl.when(k == 0)
    def _():
        for i in range(NZ):
            fetch(i).start()
            weights[i, COLS:] = jnp.zeros((MAIN + STATE - COLS, FEAT), bf16)

    for i in range(NZ):

        @pl.when(k == i)
        def _():
            fetch(i).wait()

    size = a_ref.shape[3]
    total = dot(main_ref[...], weights[k], NN).astype(bf16).reshape(2, 2, size, FEAT)
    x_at, yl_at = k // 2, k % 2
    a_ref[0, 0] = total[:, 0]
    b_ref[:, 0, 0] = total[:, 1]

    @pl.when(x_at == x_first)
    def _():
        a_first_ref[yl_at] = total[:, 0]

    for i in range(2):

        @pl.when(y_first == 2 * i + yl_at)
        def _():
            b_first_ref[x_at] = total[i, 1]


def hop_kernel(hop, final, at_ref, *refs):
    count = 4
    x, y = at_ref[0], at_ref[1]
    ins, held, sems = refs[: 2 * count], refs[-2 * count - 1 : -1], refs[-1]
    outs = list(refs[2 * count : -2 * count - 1])
    copies = []
    for i in range(2 * count):
        source = ins[i]
        if i == 1:
            source = source.at[at_ref[6 + hop]]
        if i == 3:
            source = source.at[at_ref[10 + hop]]
        copies.append(pltpu.make_async_copy(source, held[i], sems.at[i]))
        copies[-1].start()
    for i in range(count):
        copies[2 * i].wait()
        copies[2 * i + 1].wait()
        value = (held[2 * i][...].astype(f32) + held[2 * i + 1][...].astype(f32)).astype(bf16)
        if final:
            held[2 * i][...] = value
        else:
            outs.pop(0)[...] = value
    if final:
        for i in range(NY):
            at = (y + i) & (NY - 1)
            outs[i][...] = held[0][(at & 1) * 2 + (at >> 1)]
            outs[NY + i][...] = held[2][(x + i) & (NX - 1)]
        half = FEAT // 2
        for i in range(2):
            for j in range(2):
                at = pl.multiple_of(((y >> 1) ^ j) * half, half)
                out_ref = outs[2 * i + j - 4]
                out_ref[:half, :] = held[4 + 2 * i][pl.ds(at, half), :]
                out_ref[half:, :half] = held[4 + 2 * i][FEAT:, pl.ds(at, half)]
                out_ref[half:, half:] = jnp.zeros((STEPS, MAIN - half), bf16)


def close_kernel(at_ref, *refs):
    a_refs, b_refs, keep_ref, give_ref = refs[:NY], refs[NY : NY + NX], refs[-2], refs[-1]
    sums = []
    for parts in (a_refs, b_refs):
        total = parts[0][...].astype(f32)
        for part in parts[1:]:
            total = total + part[...].astype(f32)
        sums.append(total)
    mine = at_ref[5] == 0
    keep_ref[...] = jnp.where(mine, sums[0], sums[1]).astype(bf16)
    give_ref[...] = jnp.where(mine, sums[1], sums[0]).astype(bf16)


def cores_kernel(at_ref, own_ref, pair_ref, out_ref):
    c = at_ref[5]
    for i in range(2):
        part = slice(i * 128, (i + 1) * 128)
        out_ref[:, pl.ds(pl.multiple_of((2 * i + c) * 128, 128), 128)] = own_ref[:, part]
        out_ref[:, pl.ds(pl.multiple_of((2 * i + 1 - c) * 128, 128), 128)] = pair_ref[:, part]


def heads_kernel(at_ref, own_ref, pair_ref, cross_ref, out_ref):
    yh, c = at_ref[4], at_ref[5]

    def to(first, second, value):
        lanes = pl.ds(pl.multiple_of((first * 2 + second) * VW, VW), VW)
        out_ref[:, lanes] = value

    to(yh, c, own_ref[c])
    to(1 - yh, c, pair_ref[c])
    to(yh, 1 - c, cross_ref[0])
    to(1 - yh, 1 - c, cross_ref[1])


def pick(value, at, dim):
    return lax.dynamic_index_in_dim(value, at, dim, False)


def tie(*values):
    return lax.optimization_barrier(values)


FIRST, LATER = (4, 5), (3, 6, 2, 7, 1, 0)
LONG = pl.CostEstimate(flops=10 * 2**30, bytes_accessed=32 * 2**20, transcendentals=0)
TINY = pl.CostEstimate(flops=1024, bytes_accessed=1024, transcendentals=0)


def local(hidden, value_proj, state_proj, step_proj, step_bias, decay_rate, skip_gain, out_grad):
    z, yh, c, x, yl = (lax.axis_index(a) for a in ("z", "yh", "c", "x", "yl"))
    y = yh * 2 + yl
    way = 1 - 2 * c
    tok = hidden.shape[0]
    tokens = 4 * tok
    blocks = tokens // Q

    def x_at(hop):
        return (x - way * hop) % NX

    def y_at(hop):
        return (y - way * hop) % NY

    places = jnp.stack(
        [x, y, z, way, yh, c]
        + [x_at(i) for i in range(1, 5)]
        + [y_at(i) for i in range(1, 5)]
        + [(z + i) % NZ for i in range(NZ)]
    ).astype(jnp.int32)
    heads = jnp.stack(
        [
            lax.dynamic_slice_in_dim(v, (yh * 2 + c) * EACH, EACH, 0)
            for v in (step_bias, decay_rate, skip_gain)
        ],
        axis=1,
    )

    value_t, state_t, step_tr = value_proj.T, state_proj.T, step_proj.T
    none = jnp.zeros((EACH, value_proj.shape[0]), bf16)

    def chosen(which):
        def some(array, wide, core):
            return lax.dynamic_slice_in_dim(array, (which * 2 + core) * wide, wide, 0)

        return jnp.concatenate(
            [
                some(value_t, VW, c), some(value_t, VW, 1 - c), state_t,
                some(step_tr, EACH, c), none, some(step_tr, EACH, 1 - c), none,
            ],
            axis=0,
        )

    hidden, given = tie(hidden, chosen(1 - yh))
    mine, theirs = chosen(yh), shift(given, "yh", 1, 2)
    chunk = jnp.where(
        yh == 0,
        jnp.concatenate([mine, theirs], axis=1),
        jnp.concatenate([theirs, mine], axis=1),
    )
    parts = hidden.reshape(tok, 2, 2, 128)
    keep = pick(parts, c, 2).reshape(tok, FEAT)
    got = swap(pick(parts, 1 - c, 2).reshape(tok, FEAT))
    first = jnp.where(c == 0, keep, got)
    second = jnp.where(c == 0, got, keep)

    def pairwise(own, pair, place, dim):
        return jnp.where(
            place == 0, jnp.stack([own, pair], dim), jnp.stack([pair, own], dim)
        )

    out_grad, chunk = tie(out_grad, chunk)
    cot = out_grad.reshape(tok, 2, 2, VW)
    cot = pairwise(pick(cot, c, 2), swap(pick(cot, 1 - c, 2)), c, 0)

    brought = [lax.all_gather(chunk[:SPLIT], "z")] if SPLIT else []
    ring = chunk[SPLIT:]
    weights = [ring, shift(ring, "z", 1, NZ), shift(ring, "z", -1, NZ)]
    a_blocks = [jnp.stack([first] + [shift(first, ("yh", "yl"), i, NY) for i in range(1, NY)])]
    b_blocks = [jnp.stack([second] + [shift(second, "x", i, NX) for i in range(1, NX)])]
    weights[1], weights[2], a_blocks[0], b_blocks[0], cot = tie(
        weights[1], weights[2], a_blocks[0], b_blocks[0], cot
    )
    cot = pairwise(pick(cot, yh, 2), shift(pick(cot, 1 - yh, 2), "yh", 1, 2), yh, 0)
    cot = cot.reshape(tokens, VW)
    for hop in range(1, 4):
        weights.append(shift(weights[-2], "z", 1, NZ))
        if hop < 3:
            weights.append(shift(weights[-2], "z", -1, NZ))
        a_blocks.append(both_x(a_blocks[-1]))
        b_blocks.append(both_y(b_blocks[-1]))
        if hop == 1:
            a_blocks[-1], b_blocks[-1], cot = tie(a_blocks[-1], b_blocks[-1], cot)
        if hop < 3:
            weights[-1], weights[-2], a_blocks[-1], b_blocks[-1] = tie(
                weights[-1], weights[-2], a_blocks[-1], b_blocks[-1]
            )

    def whole(*shape):
        return pl.BlockSpec(shape, lambda *k: (0,) * len(shape))

    def shaped(dtype, *shape):
        return jax.ShapeDtypeStruct(shape, dtype)

    wide = NZ * FEAT
    in_hbm = pl.BlockSpec(memory_space=pltpu.HBM)
    in_vmem = pl.BlockSpec(memory_space=pltpu.VMEM)
    in_smem = pl.BlockSpec(memory_space=pltpu.SMEM)
    hid, whole_w, p_own, p_send = pl.pallas_call(
        project_kernel,
        in_specs=[in_smem] + [in_hbm] * (NX + NY + NZ + len(brought)),
        out_specs=[in_hbm, in_hbm, in_vmem, in_vmem],
        out_shape=[
            shaped(bf16, 4, tok, wide), shaped(bf16, COLS, wide),
            shaped(f32, tokens, VW), shaped(f32, tokens + 2 * STEPS, VW + BC),
        ],
        scratch_shapes=[
            pltpu.VMEM((4, tok, wide), bf16), pltpu.VMEM((COLS, wide), bf16),
            pltpu.SemaphoreType.DMA((2 * NX * NY + 2 * NZ + 2,)),
        ],
        compiler_params=ALL,
        cost_estimate=LONG,
        name="project",
    )(places, *a_blocks, *b_blocks, *weights, *brought)
    p_recv = swap(p_send)

    states = shaped(f32, blocks, VW, STATE)
    by_lanes = shaped(f32, blocks, EACH, Q)
    packed = shaped(bf16, VW + STEPS, STATE)
    values, bc, step, sig, fresh, seeds, lasts, keep, give = pl.pallas_call(
        state_kernel,
        in_specs=[in_smem] + [in_vmem] * 5,
        out_shape=[
            shaped(bf16, tokens, VW), shaped(bf16, tokens, BC), by_lanes, by_lanes,
            states, states, shaped(f32, VW, blocks), packed, packed,
        ],
        compiler_params=ALL,
        name="states",
    )(places, p_own, p_send, p_recv, cot, heads)

    def along(packed, by):
        pairs = [
            (i * 2 + core, (i + by * (1 - 2 * core)) * 2 + core)
            for i in range(NZ)
            for core in range(2)
            if 0 <= i + by * (1 - 2 * core) < NZ
        ]
        return lax.ppermute(packed, ("z", "c"), pairs)

    def joined(near, far, split=False):
        return pl.pallas_call(
            window_kernel,
            out_shape=[packed] * 2 if split else shaped(bf16, 2, VW + STEPS, STATE),
            compiler_params=vmem(2),
            cost_estimate=TINY,
            name="window",
        )(near, far)

    start = jnp.stack([keep, swap(give)])
    window = joined(along(start, 1), along(start, 2))
    window = joined(window, along(window, 2))
    kept, given = joined(window, along(window, 4), True)
    other_way = swap(given)

    each = 2

    def rows(width):
        return pl.BlockSpec((each * Q, width), lambda k: (k, 0))

    lanes = pl.BlockSpec((each, EACH, Q), lambda k: (k, 0, 0))
    mixed, back, steps = pl.pallas_call(
        scan_kernel,
        grid=(blocks // each,),
        in_specs=[
            in_smem, rows(VW), rows(BC), rows(VW), lanes, lanes, whole(EACH, 3),
            whole(blocks, VW, STATE), whole(blocks, VW, STATE), whole(VW, blocks),
            whole(VW + STEPS, STATE), whole(VW + STEPS, STATE),
        ],
        out_specs=[
            rows(VW), rows(VW + BC), pl.BlockSpec((STEPS, each * Q), lambda k: (0, k)),
        ],
        out_shape=[
            shaped(bf16, tokens, VW), shaped(bf16, tokens, VW + BC), shaped(bf16, STEPS, tokens),
        ],
        scratch_shapes=[
            pltpu.VMEM((blocks + 1, VW, STATE), f32), pltpu.VMEM((blocks, VW, STATE), f32),
        ],
        compiler_params=ALL,
        name="scan",
    )(
        places, values, bc, cot, step, sig, heads, fresh, seeds, lasts, kept, other_way,
    )

    back_pair, steps_pair = swap(back), swap(steps)

    def fetched(count):
        return [pltpu.VMEM((count, 4, tok, FEAT), bf16), pltpu.SemaphoreType.DMA((count,))]

    grad_block = shaped(bf16, FEAT + STEPS, MAIN)
    main, both_steps, up, down = pl.pallas_call(
        first_kernel,
        in_specs=[in_smem] + [in_vmem] * 4 + [in_hbm],
        out_shape=[shaped(bf16, tokens, MAIN + STATE), shaped(bf16, STEPS, tokens)]
        + [grad_block] * 2,
        scratch_shapes=fetched(2),
        compiler_params=ALL,
        cost_estimate=TINY,
        name="first",
    )(places, back, back_pair, steps, steps_pair, hid)
    add_3, add_6, add_2, add_7, add_1, add_0 = pl.pallas_call(
        term_kernel,
        in_specs=[in_smem, in_vmem, in_vmem, in_hbm],
        out_shape=[grad_block] * 6,
        scratch_shapes=fetched(6),
        compiler_params=vmem(10),
        cost_estimate=LONG,
        name="term",
    )(places, main, both_steps, hid)

    def add_hop(hop, a_sum, b_sum, *sums):
        final = hop == 3
        tables = [a_sum, a_part, b_sum, b_part, *sums]
        wide_block, block, grad = (NX, tok, FEAT), (tok, FEAT), (FEAT + STEPS, MAIN)
        shapes = [wide_block] * 4 + [grad] * 4
        outs = [wide_block] * 2 + [grad] * 2
        if final:
            outs = [block] * (NX + NY) + [(FEAT // 2 + STEPS, MAIN)] * 4
        return pl.pallas_call(
            lambda *refs: hop_kernel(hop, final, *refs),
            in_specs=[in_smem] + [in_hbm] * len(tables),
            out_shape=[shaped(bf16, *shape) for shape in outs],
            scratch_shapes=[pltpu.VMEM(shape, bf16) for shape in shapes]
            + [pltpu.SemaphoreType.DMA((len(tables),))],
            compiler_params=vmem(10),
            cost_estimate=TINY,
            name="hop",
        )(places, *tables)

    def more(sums, *parts):
        total = sums.astype(f32)
        for part in parts:
            total = total + part.astype(f32)
        return total

    a_part, b_part, a_sum, b_sum = pl.pallas_call(
        input_kernel,
        grid=(NZ,),
        in_specs=[in_smem, whole(tokens, MAIN + STATE), in_hbm],
        out_specs=[
            pl.BlockSpec((1, 1, 2, tok, FEAT), lambda k: (k // 2, k % 2, 0, 0, 0)),
            pl.BlockSpec((2, 1, 1, tok, FEAT), lambda k: (0, k % 2, k // 2, 0, 0)),
            whole(2, 2, tok, FEAT), whole(NX, tok, FEAT),
        ],
        out_shape=[
            shaped(bf16, NX, 2, 2, tok, FEAT), shaped(bf16, 2, 2, NX, tok, FEAT),
            shaped(bf16, 2, 2, tok, FEAT), shaped(bf16, NX, tok, FEAT),
        ],
        scratch_shapes=[
            pltpu.VMEM((NZ, MAIN + STATE, FEAT), bf16), pltpu.SemaphoreType.DMA((NZ,)),
        ],
        compiler_params=ALL,
        cost_estimate=LONG,
        name="input",
    )(places, main, whole_w)
    mixed = mixed.reshape(2, 2, tok, VW)
    heads_own = pick(mixed, yh, 0)
    pair = shift(pick(mixed, 1 - yh, 0), "yh", 1, 2)
    a_sum, b_sum, pair = tie(a_sum, b_sum, pair)
    crossed = swap(jnp.stack([pick(heads_own, 1 - c, 0), pick(pair, 1 - c, 0)]))
    a_part = a_part.reshape(NX, NY, tok, FEAT)
    b_part = b_part.reshape(NY, NX, tok, FEAT)
    a_sum = a_sum.reshape(NY, tok, FEAT)

    for hop in range(1, 4):
        a_sum, b_sum, up, down, *last = add_hop(
            hop, both_x(a_sum), both_y(b_sum),
            shift(up, "z", 1, NZ), (add_3, add_2, add_1)[hop - 1],
            shift(down, "z", -1, NZ), (add_6, add_7, add_0)[hop - 1],
        )
        if hop == 1:
            a_sum, b_sum, crossed = tie(a_sum, b_sum, crossed)
    last = [a_sum, b_sum, up, down] + last
    ends = last[NX + NY :]
    mixer_out = pl.pallas_call(
        heads_kernel,
        in_specs=[in_smem, in_vmem, in_vmem, in_vmem],
        out_shape=shaped(bf16, tok, 4 * VW),
        compiler_params=vmem(4),
        cost_estimate=TINY,
        name="by_head",
    )(places, heads_own, pair, crossed)
    across = [(2 * i + j, 2 * ((i + 1) % NZ) + 1 - j) for i in range(NZ) for j in range(2)]
    own = more(ends[2], shift(ends[0], "z", 1, NZ))
    other = more(
        shift(ends[3], "yh", 1, 2), lax.ppermute(ends[1], ("z", "yh"), across)
    )
    a_last = [last[0]] + [shift(last[i], ("yh", "yl"), i, NY) for i in range(1, NY)]
    b_last = [last[NY]] + [shift(last[NY + i], "x", i, NX) for i in range(1, NX)]
    keep, give = pl.pallas_call(
        close_kernel,
        in_specs=[in_smem] + [in_vmem] * (NX + NY),
        out_shape=[shaped(bf16, tok, FEAT)] * 2,
        compiler_params=vmem(4),
        cost_estimate=TINY,
        name="close",
    )(places, *a_last, *b_last)
    hidden_grad = pl.pallas_call(
        cores_kernel,
        in_specs=[in_smem, in_vmem, in_vmem],
        out_shape=shaped(bf16, tok, 2 * FEAT),
        compiler_params=vmem(3),
        cost_estimate=TINY,
        name="by_core",
    )(places, keep, swap(give))

    half = FEAT // 2
    own_step, other_step = own[half:, :half], other[half:, :half]
    own, other = own[:half], other[:half]
    state_grad = own[:, 2 * VW :] + other[:, 2 * VW :]

    def ordered(own, other, wide, gap):
        def cores(value):
            mine, pair = value[:, :wide], value[:, gap : gap + wide]
            return jnp.where(
                c == 0,
                jnp.concatenate([mine, pair], axis=1),
                jnp.concatenate([pair, mine], axis=1),
            )

        own, other = cores(own), cores(other)
        return jnp.where(
            yh == 0,
            jnp.concatenate([own, other], axis=1),
            jnp.concatenate([other, own], axis=1),
        )

    value_grad = ordered(own, other, VW, VW)
    step_grad = ordered(own_step.T, other_step.T, EACH, STEPS // 2)
    return mixer_out, hidden_grad, value_grad, state_grad, step_grad


def solution(mesh):
    fine = Mesh(mesh.devices.reshape(NZ, 2, 2, NX, 2), ("z", "yh", "c", "x", "yl"))
    split = P(("z", "yh", "c"), ("x", "yl"))
    by_head = P(("x", "yl"))
    return jax.shard_map(
        local,
        mesh=fine,
        in_specs=(split,) * 4 + (by_head,) * 3 + (split,),
        out_specs=(split,) * 5,
        check_vma=False,
    )
```
